32 devices in a mesh: grp: 2 (over y), row: 4 (over z), col: 2 (over x), pair: 2 (over core).
Axes of the slice: x: 2, y: 2, z: 4, core: 2. Of those that a mesh axis runs over, the one named last changes fastest.
Arguments:
- features_in: bfloat16 [128, 32, 512], P('grp', 'row', ('col', 'pair')), parts along dimension 0, may hold values from -8 to 8
- filters_one: bfloat16 [64, 3, 3, 64], replicated, may hold values from -0.25 to 0.25
- filters_two: bfloat16 [512, 3, 3, 256], P('row'), may hold values from -0.125 to 0.125
- out_grad: bfloat16 [1024, 128, 8], P(('grp', 'row'), ('col', 'pair')), parts along dimension 0, may hold values from -24 to 24
Outputs:
- input_grad: bfloat16 [128, 32, 512], P('grp', 'row', ('col', 'pair')), parts along dimension 0
- grad_one: float32 [128, 3, 3, 64], P('grp'), parts along dimension 0
- grad_two: float32 [1024, 3, 3, 256], P(('grp', 'row')), parts along dimension 0
The draws below stay inside these ranges and needn't reach their ends.
There are 2 independent parts, one for each index of `grp`. The reference program is written for one: setup_inputs(seed, part) draws one part's arguments, and reference() takes and returns one part's arrays. A program takes and returns all parts, laid end to end along the dimension named above; an argument that names none is the same for every part. Nothing has to cross between parts.
All inputs are finite; a program needn't handle non-finite values.
Results may differ from the reference program's by a relative error of at most 0.015.
Values may be sent and summed in bfloat16 or wider, within the bound.
No kernel may reach another device: no remote copies, remote signals or barrier semaphores. Data moves between devices by JAX's collectives and lax.ppermute only.
A program may use at most 64 MiB of HBM per device.

```python
import math
import jax
import jax.numpy as jnp
from jax import lax

C1 = 64
F2 = 512
C2 = 256
H = 32
W = 512
H2 = 8
W2 = 128


def mixed_field(key, shape, base_scale):
    values = jax.random.normal(jax.random.fold_in(key, 13), shape, jnp.float32)
    return (jnp.clip(values, -6.0, 6.0) * base_scale).astype(jnp.bfloat16)


def draw_features_in(key, part):
    return mixed_field(key, (C1, H, W), 1.0)


def draw_out_grad(key, part):
    return mixed_field(key, (F2, W2, H2), 3.0)


def level_of(stream_key, extent, split, low, top_value):
    level, own = 1.0, jax.random.fold_in(stream_key, 6)
    for position, shards_of in split:
        heights = jnp.exp(jax.random.uniform(jax.random.fold_in(own, position), (shards_of,), jnp.float32, low / len(split), top_value / len(split)))
        level = level * jnp.repeat(heights, extent[position] // shards_of).reshape([-1 if axis == position else 1 for axis in range(len(extent))])
    return level


def noise(stream_key, shape, width, most, pieces=(), held_as=jnp.bfloat16):
    entries = jax.random.normal(stream_key, shape, jnp.float32) * width
    if len(pieces) > 0:
        entries = level_of(stream_key, shape, pieces, -0.22, 0.18) * entries
    return jnp.clip(entries, min=-most, max=most).astype(held_as)


def setup_inputs(seed: int = 0, part: int = 0) -> dict:
    splits = jax.random.split(jax.random.key(seed), 5)
    own_keys = jax.random.split(jax.random.fold_in(splits[4], part), 5)
    features_in = draw_features_in(jax.random.fold_in(jax.random.fold_in(splits[4], part), 71), part)
    filters_one = noise(splits[1], (C1, 3, 3, C1), (9 * C1) ** -0.5, 0.25)
    filters_two = noise(splits[2], (F2, 3, 3, C2), (9 * C2) ** -0.5, 0.125, ((0, 4),))
    out_grad = draw_out_grad(jax.random.fold_in(jax.random.fold_in(splits[4], part), 71), part)
    return dict(features_in=features_in, filters_one=filters_one, filters_two=filters_two, out_grad=out_grad)


def conv_same(values, kernel):
    return lax.conv_general_dilated(values.astype(jnp.float32)[None], kernel.astype(jnp.float32), (1, 1), ((1, 1), (1, 1)), dimension_numbers=('NCHW', 'OHWI', 'NCHW'), precision=lax.Precision.HIGHEST)[0]

def conv_back(gradient, kernel):
    flipped = jnp.transpose(kernel[:, ::-1, ::-1, :], (3, 1, 2, 0))
    return conv_same(gradient, flipped)

def filter_grad(gradient, values):
    padded = jnp.pad(values.astype(jnp.float32), ((0, 0), (1, 1), (1, 1)))
    row_count, col_count = (gradient.shape[1], gradient.shape[2])
    wide_grad = gradient.astype(jnp.float32)
    tap_list = []
    for row_tap in range(3):
        tap_row = []
        for col_tap in range(3):
            window = padded[:, row_tap:row_tap + row_count, col_tap:col_tap + col_count]
            tap_row.append(jnp.einsum('ohw,chw->oc', wide_grad, window, precision=lax.Precision.HIGHEST))
        tap_list.append(jnp.stack(tap_row, 1))
    return jnp.stack(tap_list, 1)

def silu_slope(values):
    sigmoid_value = jax.nn.sigmoid(values)
    return sigmoid_value * (1.0 + values * (1.0 - sigmoid_value))

def pool_map(active):
    channels, row_count, col_count = active.shape
    folded = active.reshape(channels, row_count // 4, 2, 2, col_count // 4, 2, 2).mean(axis=(3, 6))
    return jnp.transpose(folded, (0, 2, 4, 1, 3)).reshape(channels * 4, row_count // 4, col_count // 4)

def unpool_map(gradient):
    quad_count, row_count, col_count = gradient.shape
    ordered = jnp.transpose(gradient.reshape(quad_count // 4, 2, 2, row_count, col_count), (0, 3, 1, 4, 2))
    spread = jnp.broadcast_to(ordered[:, :, :, None, :, :, None], (quad_count // 4, row_count, 2, 2, col_count, 2, 2)) * 0.25
    return spread.reshape(quad_count // 4, row_count * 4, col_count * 4)

def reference(features_in, filters_one, filters_two, out_grad):
    pre_one = conv_same(features_in, filters_one)
    pooled = pool_map(jax.nn.silu(pre_one)).astype(jnp.bfloat16)
    pre_two = conv_same(pooled, filters_two)
    grad_pre_two = (jnp.transpose(out_grad, (0, 2, 1)).astype(jnp.float32) * silu_slope(pre_two)).astype(jnp.bfloat16)
    grad_two = filter_grad(grad_pre_two, pooled) / math.sqrt(H2 * W2)
    grad_pooled = conv_back(grad_pre_two, filters_two)
    grad_pre_one = (unpool_map(grad_pooled) * silu_slope(pre_one)).astype(jnp.bfloat16)
    grad_one = filter_grad(grad_pre_one, features_in) / math.sqrt(H * W)
    input_grad = conv_back(grad_pre_one, filters_one).astype(jnp.bfloat16)
    return (input_grad, grad_one, grad_two)
```

```python
import math

import jax
import jax.numpy as jnp
from jax import lax
from jax.sharding import PartitionSpec as P

BF16 = jnp.bfloat16
F32 = jnp.float32
COLS = ("col", "pair")
HALO = 3
PIXEL_HALO = 4 * HALO + 1
GRAD_HALO = HALO - 1


def shift_pair(tail, head, axis):
    count = lax.axis_size(axis)
    ends = count - 1
    before = lax.ppermute(tail, axis, [(i, i + 1) for i in range(ends)])
    after = lax.ppermute(head, axis, [(i + 1, i) for i in range(ends)])
    return before, after


def conv_valid(padded, kernel):
    return lax.conv_general_dilated(
        padded[None],
        kernel,
        (1, 1),
        "VALID",
        dimension_numbers=("NCHW", "OHWI", "NCHW"),
        preferred_element_type=F32,
    )[0]


def flip_kernel(kernel):
    return jnp.transpose(kernel[:, ::-1, ::-1, :], (3, 1, 2, 0))


def silu_slope(values):
    sigmoid_value = jax.nn.sigmoid(values)
    return sigmoid_value * (1.0 + values * (1.0 - sigmoid_value))


def tap_grads(gradient, padded):
    row_count, col_count = gradient.shape[1:]
    return jnp.stack(
        [
            jnp.stack(
                [
                    jnp.einsum(
                        "ohw,chw->oc",
                        gradient,
                        padded[:, i : i + row_count, j : j + col_count],
                        preferred_element_type=F32,
                    )
                    for j in range(3)
                ],
                1,
            )
            for i in range(3)
        ],
        1,
    )


def pool_columns(active):
    channels, row_count, col_count = active.shape
    folded = active.reshape(channels, row_count // 4, 2, 2, col_count // 4, 2, 2).mean(axis=(3, 6))
    return jnp.transpose(folded, (0, 2, 4, 3, 1)).reshape(
        channels * 4, col_count // 4, row_count // 4
    )


def half_grid(gradient):
    quads, col_count, row_count = gradient.shape
    ordered = jnp.transpose(
        gradient.reshape(quads // 4, 2, 2, col_count, row_count), (0, 4, 1, 3, 2)
    )
    return ordered.reshape(quads // 4, row_count * 2, col_count * 2)


def sum_all(values, axis):
    count = lax.axis_size(axis)
    shape = values.shape
    parts = values.reshape(count, -1).astype(BF16)
    mine = lax.all_to_all(parts, axis, 0, 0, tiled=True).astype(F32).sum(0)
    copies = jnp.broadcast_to(mine.astype(BF16)[None], (count, mine.shape[0]))
    return lax.all_to_all(copies, axis, 0, 0, tiled=True).astype(F32).reshape(shape)


def local(features_in, filters_one, filters_two, out_grad):
    channels, band_rows, strip_cols = features_in.shape
    filters, own_cols, pooled_rows = out_grad.shape
    bands = lax.axis_size("row")
    strips = lax.axis_size(COLS)
    band = lax.axis_index("row")
    strip = lax.axis_index(COLS)
    height, width = band_rows * bands, strip_cols * strips

    split = channels * band_rows * PIXEL_HALO

    def packed(cells, grads):
        return jnp.concatenate([cells.reshape(-1), grads.reshape(-1)])

    def unpacked(flat):
        return (
            flat[:split].reshape(channels, band_rows, PIXEL_HALO),
            flat[split:].reshape(filters, GRAD_HALO, pooled_rows),
        )

    before, after = shift_pair(
        packed(features_in[:, :, -PIXEL_HALO:], out_grad[:, -GRAD_HALO:]),
        packed(features_in[:, :, :PIXEL_HALO], out_grad[:, :GRAD_HALO]),
        COLS,
    )
    (cells_before, grads_before), (cells_after, grads_after) = unpacked(before), unpacked(after)
    cells = jnp.concatenate([cells_before, features_in, cells_after], 2)
    out_wide = jnp.concatenate([grads_before, out_grad, grads_after], 1)
    above, below = shift_pair(cells[:, -2:], cells[:, :2], "row")
    cells = jnp.concatenate([above, cells, below], 1)

    pre_one = conv_valid(cells, filters_one)
    pooled = pool_columns(jax.nn.silu(pre_one[:, 1:-1]))
    column = strip * own_cols - HALO + jnp.arange(own_cols + 2 * HALO)
    inside = (column >= 0) & (column < own_cols * strips)
    pooled = jnp.where(inside[None, :, None], pooled, 0.0).astype(BF16)
    copies = jnp.broadcast_to(pooled[None], (bands,) + pooled.shape)
    gathered = lax.all_to_all(copies, "row", 0, 0, tiled=True)
    quads, wide_cols, _ = pooled.shape
    column_strip = jnp.transpose(gathered, (1, 2, 0, 3)).reshape(quads, wide_cols, pooled_rows)
    strip_padded = jnp.pad(column_strip, ((0, 0), (0, 0), (1, 1)))

    swapped = jnp.transpose(filters_two, (0, 2, 1, 3))
    pre_two = conv_valid(strip_padded, swapped)
    grad_pre_two = (out_wide.astype(F32) * silu_slope(pre_two)).astype(BF16)
    padded_grad = jnp.pad(grad_pre_two, ((0, 0), (0, 0), (1, 1)))
    spread = conv_valid(padded_grad, flip_kernel(swapped))
    half = jnp.pad(half_grid(spread.astype(BF16))[:, :, 1:-1], ((0, 0), (1, 1), (0, 0)))
    half_rows = band_rows // 2
    terms = jnp.stack([half[:, b * half_rows : (b + 1) * half_rows + 2] for b in range(bands)])
    grad_half = lax.all_to_all(terms, "row", 0, 0, tiled=True).astype(F32).sum(0)

    local_two = jnp.transpose(
        tap_grads(
            grad_pre_two[:, GRAD_HALO:-GRAD_HALO], strip_padded[:, GRAD_HALO:-GRAD_HALO]
        ),
        (0, 2, 1, 3),
    )

    pixel = strip * strip_cols - 2 + jnp.arange(strip_cols + 4)
    keep = (pixel >= 0) & (pixel < width)
    upsampled = jnp.repeat(jnp.repeat(grad_half, 2, 1), 2, 2) * 0.25
    upsampled = jnp.where(keep[None, None], upsampled, 0.0)[:, 1:-1, 1:-1]
    border = PIXEL_HALO - 2
    slope = silu_slope(pre_one[:, :, border:-border])
    grad_pre_one = (upsampled * slope).astype(BF16)
    inner = PIXEL_HALO - 1
    local_one = tap_grads(grad_pre_one[:, 1:-1, 1:-1], cells[:, 1:-1, inner:-inner])
    input_grad = conv_valid(grad_pre_one, flip_kernel(filters_one)).astype(BF16)

    grad_two = sum_all(local_two, COLS) / math.sqrt(pooled_rows * own_cols * strips)
    grad_one = sum_all(local_one, ("row",) + COLS) / math.sqrt(height * width)
    return (input_grad, grad_one, grad_two)


def solution(mesh):
    in_specs = (
        P("grp", "row", ("col", "pair")),
        P(),
        P("row", None, None, None),
        P(("grp", "row"), ("col", "pair"), None),
    )
    out_specs = (
        P("grp", "row", ("col", "pair")),
        P("grp", None, None, None),
        P(("grp", "row"), None, None, None),
    )
    return jax.shard_map(local, mesh=mesh, in_specs=in_specs, out_specs=out_specs, check_vma=False)
```

```python
import functools
import math

import jax
import jax.numpy as jnp
from jax import lax
from jax.experimental import pallas as pl
from jax.experimental.pallas import tpu as pltpu
from jax.sharding import PartitionSpec as P

BF16 = jnp.bfloat16
F32 = jnp.float32
COLS = ("col", "pair")
EVERY = ("row", "col", "pair")
REACH = 3
PITCH = 48
SENT = 40


def dot(a, b, contract):
    return lax.dot_general(a, b, ((contract[:1], contract[1:]), ((), ())), preferred_element_type=F32)


def whole_call(body, outs, operands, flops, scalars=1, scratch=()):
    specs = [
        pl.BlockSpec(memory_space=pltpu.SMEM if n < scalars else pltpu.VMEM)
        for n in range(len(operands))
    ]
    moved = sum(math.prod(a.shape) * a.dtype.itemsize for a in tuple(operands[scalars:]) + tuple(outs))
    return pl.pallas_call(
        body,
        out_shape=outs,
        in_specs=specs,
        out_specs=[pl.BlockSpec(memory_space=pltpu.VMEM) for _ in outs],
        scratch_shapes=list(scratch),
        cost_estimate=pl.CostEstimate(flops=flops, bytes_accessed=moved, transcendentals=0),
        compiler_params=pltpu.CompilerParams(vmem_limit_bytes=40 * 1024 * 1024),
    )(*operands)


def shaped(shape, dtype=BF16):
    return jax.ShapeDtypeStruct(shape, dtype)


def roll(values, amount, axis):
    return pltpu.roll(values, amount % values.shape[axis], axis)


def sigmoid(values):
    return 1.0 / (1.0 + jnp.exp(-values))


def slope_of(values, sig):
    return sig * (1.0 + values * (1.0 - sig))


def pool_matrix(strip, total):
    row = lax.broadcasted_iota(jnp.int32, (2 * PITCH, 256), 0)
    lane = lax.broadcasted_iota(jnp.int32, (2 * PITCH, 256), 1)
    half = (row >= PITCH).astype(jnp.int32)
    v = row - half * PITCH
    first = 4 * (v - REACH) + 2 * half
    near = jnp.bitwise_and(lane - first, 255) < 2
    place = strip * 32 + v - REACH
    keep = near & (v < 32 + 2 * REACH) & (place >= 0) & (place < total)
    return jnp.where(keep, 0.25, 0.0).astype(BF16)


def order_matrix():
    row = lax.broadcasted_iota(jnp.int32, (256, 256), 0)
    lane = lax.broadcasted_iota(jnp.int32, (256, 256), 1)
    j, i, c = row >> 7, (row >> 6) & 1, row & 63
    return jnp.where(lane == 4 * c + 2 * i + j, 1.0, 0.0).astype(BF16)


def layer_one(info, x_ref, a_ref, b_ref, w_ref, pooled_ref, slope_ref, wide_ref, *, total):
    strip = info[0]
    lane = lax.broadcasted_iota(jnp.int32, x_ref.shape, 2)
    from_a = (lane >= 64).astype(jnp.int32) == (strip & 1)
    halo = jnp.where(from_a, a_ref[...].astype(F32), b_ref[...].astype(F32))
    wide_ref[:, :, :128] = x_ref[...]
    wide_ref[:, :, 128:] = halo.astype(BF16)
    weights = jnp.concatenate([w_ref[0], w_ref[1], w_ref[2]], axis=1)
    rows = slope_ref.shape[0]
    halves, held = [], None
    for h in range(rows):
        y = dot(weights, wide_ref[h : h + 3].reshape(192, 256), (1, 0))
        pre = roll(y[:64], 1, 1) + y[64:128] + roll(y[128:], -1, 1)
        sig = sigmoid(pre)
        slope_ref[h] = slope_of(pre, sig).astype(BF16)
        if 1 <= h <= rows - 2:
            active = pre * sig
            if h % 2:
                held = active
            else:
                halves.append((held + active).astype(BF16))
    pooled = dot(pool_matrix(strip, total), jnp.concatenate(halves, 0), (1, 1))
    stacked = jnp.concatenate(
        [
            jnp.concatenate(
                [pooled[:PITCH, u * 128 : u * 128 + 128], pooled[PITCH:, u * 128 : u * 128 + 128]], 1
            )
            for u in range(2)
        ],
        0,
    ).astype(BF16)
    ordered = dot(stacked, order_matrix(), (1, 0)).astype(BF16)
    for u in range(2):
        pooled_ref[u] = ordered[u * PITCH : u * PITCH + SENT]


def layer_two(info, og_ref, w_ref, *refs, bands):
    pieces, refs = refs[:bands], refs[bands:]
    terms, refs = refs[:bands], refs[bands:]
    map_ref, cat_ref, grad_ref, spread_ref = refs
    band = info[0]
    rows, _, filters = og_ref.shape
    count = rows * PITCH
    map_ref[0] = jnp.zeros((PITCH, 256), BF16)
    map_ref[rows + 1] = jnp.zeros((PITCH, 256), BF16)
    blank = jnp.zeros((PITCH - SENT, 256), BF16)
    for k in range(bands):
        for t in range(2):
            map_ref[1 + 2 * (band ^ k) + t] = jnp.concatenate([pieces[k][t], blank], 0)
    y = None
    for i in range(3):
        part = dot(map_ref[i : i + rows].reshape(count, 256), w_ref[i], (1, 1))
        y = part if y is None else y + part
    pre = roll(y[:, :filters], 1, 0) + y[:, filters : 2 * filters] + roll(y[:, 2 * filters :], -1, 0)
    grad = og_ref[...].reshape(count, filters).astype(F32) * slope_of(pre, sigmoid(pre))
    grad = grad.astype(BF16)
    grad_ref[0] = jnp.zeros((PITCH, filters), BF16)
    grad_ref[rows + 1] = jnp.zeros((PITCH, filters), BF16)
    grad_ref[1 : rows + 1] = grad.reshape(rows, PITCH, filters)
    z = None
    for i in range(3):
        weights = jnp.concatenate([w_ref[i, j * filters : (j + 1) * filters] for j in range(3)], 1)
        part = dot(grad_ref[2 - i : 2 - i + rows].reshape(count, filters), weights, (1, 0))
        z = part if z is None else z + part
    spread = roll(z[:, :256], -1, 0) + z[:, 256:512] + roll(z[:, 512:], 1, 0)
    spread_ref[0] = jnp.zeros((PITCH, 256), F32)
    spread_ref[rows + 1] = jnp.zeros((PITCH, 256), F32)
    spread_ref[1 : rows + 1] = spread.reshape(rows, PITCH, 256)
    lower = (lax.broadcasted_iota(jnp.int32, (PITCH, 256), 1) & 2) == 0
    for k in range(bands):
        first = 2 * (band ^ k)
        for t in range(2):
            terms[k][t] = spread_ref[first + 1 + t][:SENT].astype(BF16)
        edge = jnp.where(lower, spread_ref[first + 3], spread_ref[first])
        terms[k][2] = edge[:SENT].astype(BF16)
    wide = grad.astype(F32)
    v = lax.broadcasted_iota(jnp.int32, (rows, PITCH, filters), 1).reshape(count, filters)
    wide = jnp.where((v >= REACH) & (v < REACH + 32), wide, 0.0)
    cat_ref[...] = jnp.concatenate([roll(wide, -1, 0), wide, roll(wide, 1, 0)], 1).astype(BF16)


def filter_two_grads(info, map_ref, cat_ref, keep_ref, send_ref, all_ref):
    pair = info[0]
    rows = map_ref.shape[0] - 2
    taps = cat_ref.shape[1]
    for i in range(3):
        part = dot(cat_ref[...], map_ref[i : i + rows].reshape(rows * PITCH, 256), (0, 0))
        all_ref[i * taps : (i + 1) * taps] = part.astype(BF16)
    half = keep_ref.shape[0]
    keep_ref[...] = all_ref[pl.ds(pl.multiple_of(pair * half, 16), half)]
    send_ref[...] = all_ref[pl.ds(pl.multiple_of((1 - pair) * half, 16), half)]


def grad_pre_one(info, *refs, bands, total):
    terms, (slope_ref, wide_ref, g_ref, part_ref) = refs[:bands], refs[bands:]
    strip = info[0]
    summed = terms[0][...].astype(F32)
    for k in range(1, bands):
        summed = summed + terms[k][...].astype(F32)
    blank = jnp.zeros((PITCH - SENT, 256), F32)
    stacked = jnp.concatenate([p for t in range(3) for p in (summed[t], blank)], 0).astype(BF16)
    ordered = dot(stacked, order_matrix(), (1, 1)).astype(BF16)
    pool = pool_matrix(strip, total)
    ups = []
    for t in range(3):
        block = ordered[t * PITCH : (t + 1) * PITCH]
        ups.append(dot(jnp.concatenate([block[:, :128], block[:, 128:]], 0), pool, (0, 0)))
    quads = [ups[0][:64], ups[0][64:], ups[1][:64], ups[1][64:]]
    rows = [ups[2][64:]] + [quads[h // 2] for h in range(8)] + [ups[2][:64]]
    acc = None
    own = lax.broadcasted_iota(jnp.int32, (64, 256), 1) < 128
    for h in range(10):
        g = (rows[h] * slope_ref[h].astype(F32)).astype(BF16)
        g_ref[h] = g
        if 1 <= h <= 8:
            mine = jnp.where(own, g.astype(F32), 0.0)
            cat = jnp.concatenate([roll(mine, -1, 1), mine, roll(mine, 1, 1)], 0).astype(BF16)
            part = dot(cat, wide_ref[h : h + 3].reshape(192, 256), (1, 1))
            acc = part if acc is None else acc + part
    part_ref[:192] = acc[:, :128].astype(BF16)
    tail = jnp.concatenate([acc[:96, 128:], acc[96:, 128:]], 1)
    part_ref[192:288] = tail.astype(BF16)
    rest = part_ref.shape[0] - 288
    if rest:
        part_ref[288:] = jnp.zeros((rest, 128), BF16)


def layer_one_back(g_ref, w_ref, out_ref):
    rows = []
    for h in range(8):
        z = dot(w_ref[...], g_ref[h : h + 3].reshape(192, 256), (1, 0))
        rows.append((roll(z[:64], -1, 1) + z[64:128] + roll(z[128:], 1, 1))[:, :128])
    out_ref[...] = jnp.swapaxes(jnp.stack(rows, 0), 0, 1).astype(BF16)


def sum_and_copy(parts_ref, out_ref):
    count = parts_ref.shape[0]
    total = parts_ref[0].astype(F32)
    for n in range(1, count):
        total = total + parts_ref[n].astype(F32)
    for n in range(count):
        out_ref[n] = total.astype(BF16)


def unpack_one(flat_ref, out_ref, *, scale):
    out_ref[0] = flat_ref[:192, :64].astype(F32) * scale
    out_ref[1] = flat_ref[:192, 64:].astype(F32) * scale
    out_ref[2, :96] = flat_ref[192:288, :64].astype(F32) * scale
    out_ref[2, 96:] = flat_ref[192:288, 64:].astype(F32) * scale


def even_swap(values, axis, count):
    return lax.ppermute(values, axis, [(n, n ^ 1) for n in range(count)])


def odd_swap(values, axis, count):
    steps = [(n, n + 1) for n in range(1, count - 1, 2)]
    return lax.ppermute(values, axis, steps + [(b, a) for a, b in steps])


def xor_swap(values, axis, count, k):
    return lax.ppermute(values, axis, [(n, n ^ k) for n in range(count)])


def border_swap(head, tail, axis, place):
    count = lax.axis_size(axis)
    even = place % 2 == 0
    first = even_swap(jnp.where(even, tail, head), axis, count)
    second = odd_swap(jnp.where(even, head, tail), axis, count)
    return jnp.where(even, second, first), jnp.where(even, first, second)


def local(features_in, filters_one, filters_two, out_grad):
    channels, band_rows, strip_cols = features_in.shape
    filters, own_cols, pooled_rows = out_grad.shape
    bands = lax.axis_size("row")
    strips = lax.axis_size(COLS)
    band = lax.axis_index("row")
    strip = lax.axis_index(COLS)
    pair = lax.axis_index("pair")
    height, width = band_rows * bands, strip_cols * strips
    total = own_cols * strips
    at_strip = jnp.stack([strip]).astype(jnp.int32)
    at_band = jnp.stack([band]).astype(jnp.int32)
    at_pair = jnp.stack([pair]).astype(jnp.int32)

    taps_one = jnp.transpose(filters_one, (1, 2, 0, 3)).reshape(3, 3 * channels, channels)
    back_one = jnp.transpose(filters_one[:, ::-1], (2, 3, 1, 0)).reshape(3 * channels, 3 * channels)
    taps_two = jnp.transpose(filters_two, (1, 2, 0, 3)).reshape(3, 3 * filters, 4 * channels)

    x = jnp.transpose(features_in, (1, 0, 2))
    above, below = border_swap(x[:2], x[-2:], "row", band)
    x = jnp.concatenate([above, x, below], 0)
    side_a = even_swap(x, COLS, strips)
    side_b = odd_swap(x, COLS, strips)
    rows_wide = band_rows + 2
    pooled, slope, wide = whole_call(
        functools.partial(layer_one, total=total),
        [
            shaped((2, SENT, 4 * channels)),
            shaped((rows_wide, channels, 256)),
            shaped((rows_wide + 2, channels, 256)),
        ],
        [at_strip, x, side_a, side_b, taps_one],
        2 * rows_wide * 192 * 192 * 256,
    )
    pieces = [pooled] + [xor_swap(pooled, "row", bands, k) for k in range(1, bands)]

    og = jnp.transpose(out_grad, (1, 2, 0))
    before, after = border_swap(og[: REACH - 1], og[-(REACH - 1) :], COLS, strip)
    og = jnp.concatenate([before, og, after], 0)
    og = jnp.pad(og, ((1, PITCH - own_cols - 2 * REACH + 1), (0, 0), (0, 0)))
    og = jnp.transpose(og, (1, 0, 2))

    count = pooled_rows * PITCH
    *terms, pooled_map, grad_cat = whole_call(
        functools.partial(layer_two, bands=bands),
        [shaped((3, SENT, 4 * channels))] * bands
        + [shaped((pooled_rows + 2, PITCH, 4 * channels)), shaped((count, 3 * filters))],
        [at_band, og, taps_two] + pieces,
        4 * count * 9 * filters * 4 * channels,
        scratch=[
            pltpu.VMEM((pooled_rows + 2, PITCH, filters), BF16),
            pltpu.VMEM((pooled_rows + 2, PITCH, 4 * channels), F32),
        ],
    )
    received = [terms[0]] + [xor_swap(terms[k], "row", bands, k) for k in range(1, bands)]

    half = 9 * filters // 2
    keep, send = whole_call(
        filter_two_grads,
        [shaped((half, 4 * channels))] * 2,
        [at_pair, pooled_map, grad_cat],
        2 * count * 9 * filters * 4 * channels,
        scratch=[pltpu.VMEM((2 * half, 4 * channels), BF16)],
    )
    part = keep.astype(F32) + even_swap(send, "pair", 2).astype(F32)
    step = 1
    while step < lax.axis_size("col"):
        sent = part.astype(BF16)
        part = sent.astype(F32) + xor_swap(sent, "col", lax.axis_size("col"), step).astype(F32)
        step *= 2
    mine = part.astype(BF16)
    other = even_swap(mine, "pair", 2)
    grad_two = jnp.concatenate([jnp.where(pair == 0, mine, other), jnp.where(pair == 0, other, mine)], 0)
    grad_two = grad_two.astype(F32) * (1.0 / math.sqrt(pooled_rows * total))
    grad_two = jnp.transpose(grad_two.reshape(3, 3, filters, 4 * channels), (2, 0, 1, 3))

    devices = lax.axis_size(EVERY)
    share = -(-288 // (8 * devices)) * 8
    g, part_one = whole_call(
        functools.partial(grad_pre_one, bands=bands, total=total),
        [shaped((rows_wide, channels, 256)), shaped((devices * share, 128))],
        [at_strip] + received + [slope, wide],
        2 * 8 * 192 * 192 * 256,
    )
    parts = lax.all_to_all(part_one.reshape(devices, share, 128), EVERY, 0, 0, tiled=True)
    (copies,) = whole_call(sum_and_copy, [shaped((devices, share, 128))], [parts], 1, scalars=0)
    flat = lax.all_to_all(copies, EVERY, 0, 0, tiled=True).reshape(devices * share, 128)
    (grad_one,) = whole_call(
        functools.partial(unpack_one, scale=1.0 / math.sqrt(height * width)),
        [shaped((3, 3 * channels, channels), F32)],
        [flat],
        1,
        scalars=0,
    )
    grad_one = jnp.transpose(grad_one.reshape(3, 3, channels, channels), (2, 0, 1, 3))
    (input_grad,) = whole_call(
        layer_one_back, [shaped(features_in.shape)], [g, back_one], 2 * 8 * 192 * 192 * 256, scalars=0
    )
    return (input_grad, grad_one, grad_two)


def solution(mesh):
    in_specs = (
        P("grp", "row", ("col", "pair")),
        P(),
        P("row", None, None, None),
        P(("grp", "row"), ("col", "pair"), None),
    )
    out_specs = (
        P("grp", "row", ("col", "pair")),
        P("grp", None, None, None),
        P(("grp", "row"), None, None, None),
    )
    return jax.shard_map(local, mesh=mesh, in_specs=in_specs, out_specs=out_specs, check_vma=False)
```

```python
import functools
import math

import jax
import jax.numpy as jnp
from jax import lax
from jax.experimental import pallas as pl
from jax.experimental.pallas import tpu as pltpu
from jax.sharding import PartitionSpec as P

BF16 = jnp.bfloat16
F32 = jnp.float32
COLS = ("col", "pair")
REACH = 3
PITCH = 48
SENT = 40


def dot(a, b, contract):
    return lax.dot_general(a, b, ((contract[:1], contract[1:]), ((), ())), preferred_element_type=F32)


def whole_call(body, outs, operands, flops, scalars=1, scratch=()):
    specs = [
        pl.BlockSpec(memory_space=pltpu.SMEM if n < scalars else pltpu.VMEM)
        for n in range(len(operands))
    ]
    sizes = [math.prod(a.shape) * a.dtype.itemsize for a in tuple(operands[scalars:]) + tuple(outs)]
    moved = sum(sizes) if flops else 0
    return pl.pallas_call(
        body,
        out_shape=outs,
        in_specs=specs,
        out_specs=[pl.BlockSpec(memory_space=pltpu.VMEM) for _ in outs],
        scratch_shapes=list(scratch),
        cost_estimate=pl.CostEstimate(flops=flops, bytes_accessed=moved, transcendentals=0),
        compiler_params=pltpu.CompilerParams(vmem_limit_bytes=40 * 1024 * 1024),
    )(*operands)


def shaped(shape, dtype=BF16):
    return jax.ShapeDtypeStruct(shape, dtype)


def roll(values, amount, axis):
    return pltpu.roll(values, amount % values.shape[axis], axis)


def sigmoid(values):
    return 1.0 / (1.0 + jnp.exp(-values))


def slope_of(values, sig):
    return sig * (1.0 + values * (1.0 - sig))


def pool_matrix(strip, total):
    row = lax.broadcasted_iota(jnp.int32, (2 * PITCH, 256), 0)
    lane = lax.broadcasted_iota(jnp.int32, (2 * PITCH, 256), 1)
    half = (row >= PITCH).astype(jnp.int32)
    v = row - half * PITCH
    first = 4 * (v - REACH) + 2 * half
    near = jnp.bitwise_and(lane - first, 255) < 2
    place = strip * 32 + v - REACH
    keep = near & (v < 32 + 2 * REACH) & (place >= 0) & (place < total)
    return jnp.where(keep, 0.25, 0.0).astype(BF16)


def order_matrix():
    row = lax.broadcasted_iota(jnp.int32, (256, 256), 0)
    lane = lax.broadcasted_iota(jnp.int32, (256, 256), 1)
    j, i, c = row >> 7, (row >> 6) & 1, row & 63
    return jnp.where(lane == 4 * c + 2 * i + j, 1.0, 0.0).astype(BF16)


def layer_one(
    info, x_ref, above_ref, below_ref, a_ref, b_ref, w_ref, pooled_ref, slope_ref, wide_ref, *, total
):
    strip = info[0]
    band_rows = x_ref.shape[0]
    lane = lax.broadcasted_iota(jnp.int32, wide_ref.shape[:2] + (128,), 2)
    from_a = (lane >= 64).astype(jnp.int32) == (strip & 1)
    sides = a_ref[: band_rows + 4].astype(F32), b_ref[: band_rows + 4].astype(F32)
    halo = jnp.where(from_a, *sides)
    wide_ref[:2, :, :128] = above_ref[...]
    wide_ref[2 : band_rows + 2, :, :128] = x_ref[...]
    wide_ref[band_rows + 2 :, :, :128] = below_ref[...]
    wide_ref[:, :, 128:] = halo.astype(BF16)
    weights = jnp.concatenate([w_ref[0], w_ref[1], w_ref[2]], axis=1)
    rows = slope_ref.shape[0]
    halves, held = [], None
    for h in range(rows):
        y = dot(weights, wide_ref[h : h + 3].reshape(192, 256), (1, 0))
        pre = roll(y[:64], 1, 1) + y[64:128] + roll(y[128:], -1, 1)
        sig = sigmoid(pre)
        slope_ref[h] = slope_of(pre, sig).astype(BF16)
        if 1 <= h <= rows - 2:
            active = pre * sig
            if h % 2:
                held = active
            else:
                halves.append((held + active).astype(BF16))
    pooled = dot(pool_matrix(strip, total), jnp.concatenate(halves, 0), (1, 1))
    stacked = jnp.concatenate(
        [
            jnp.concatenate(
                [pooled[:PITCH, u * 128 : u * 128 + 128], pooled[PITCH:, u * 128 : u * 128 + 128]], 1
            )
            for u in range(2)
        ],
        0,
    ).astype(BF16)
    ordered = dot(stacked, order_matrix(), (1, 0)).astype(BF16)
    for u in range(2):
        pooled_ref[u] = ordered[u * PITCH : u * PITCH + SENT]


def layer_two(info, og_ref, w_ref, *refs, bands):
    pieces, refs = refs[:bands], refs[bands:]
    terms, refs = refs[:bands], refs[bands:]
    map_ref, cat_ref, grad_ref, spread_ref = refs
    band = info[0]
    rows, _, filters = og_ref.shape
    count = rows * PITCH
    map_ref[0] = jnp.zeros((PITCH, 256), BF16)
    map_ref[rows + 1] = jnp.zeros((PITCH, 256), BF16)
    blank = jnp.zeros((PITCH - SENT, 256), BF16)
    for k in range(bands):
        for t in range(2):
            map_ref[1 + 2 * (band ^ k) + t] = jnp.concatenate([pieces[k][t], blank], 0)
    y = None
    for i in range(3):
        part = dot(map_ref[i : i + rows].reshape(count, 256), w_ref[i], (1, 1))
        y = part if y is None else y + part
    pre = roll(y[:, :filters], 1, 0) + y[:, filters : 2 * filters] + roll(y[:, 2 * filters :], -1, 0)
    grad = og_ref[...].reshape(count, filters).astype(F32) * slope_of(pre, sigmoid(pre))
    grad = grad.astype(BF16)
    grad_ref[0] = jnp.zeros((PITCH, filters), BF16)
    grad_ref[rows + 1] = jnp.zeros((PITCH, filters), BF16)
    grad_ref[1 : rows + 1] = grad.reshape(rows, PITCH, filters)
    z = None
    for i in range(3):
        weights = jnp.concatenate([w_ref[i, j * filters : (j + 1) * filters] for j in range(3)], 1)
        part = dot(grad_ref[2 - i : 2 - i + rows].reshape(count, filters), weights, (1, 0))
        z = part if z is None else z + part
    spread = roll(z[:, :256], -1, 0) + z[:, 256:512] + roll(z[:, 512:], 1, 0)
    spread_ref[0] = jnp.zeros((PITCH, 256), F32)
    spread_ref[rows + 1] = jnp.zeros((PITCH, 256), F32)
    spread_ref[1 : rows + 1] = spread.reshape(rows, PITCH, 256)
    lower = (lax.broadcasted_iota(jnp.int32, (PITCH, 256), 1) & 2) == 0
    for k in range(bands):
        first = 2 * (band ^ k)
        for t in range(2):
            terms[k][t] = spread_ref[first + 1 + t][:SENT].astype(BF16)
        edge = jnp.where(lower, spread_ref[first + 3], spread_ref[first])
        terms[k][2] = edge[:SENT].astype(BF16)
    wide = grad.astype(F32)
    v = lax.broadcasted_iota(jnp.int32, (rows, PITCH, filters), 1).reshape(count, filters)
    wide = jnp.where((v >= REACH) & (v < REACH + 32), wide, 0.0)
    cat_ref[...] = jnp.concatenate([roll(wide, -1, 0), wide, roll(wide, 1, 0)], 1).astype(BF16)


def filter_two_grads(info, map_ref, cat_ref, keep_ref, send_ref, all_ref):
    pair = info[0]
    rows = map_ref.shape[0] - 2
    taps = cat_ref.shape[1]
    for i in range(3):
        part = dot(cat_ref[...], map_ref[i : i + rows].reshape(rows * PITCH, 256), (0, 0))
        all_ref[i * taps : (i + 1) * taps] = part.astype(BF16)
    half = keep_ref.shape[0]
    keep_ref[...] = all_ref[pl.ds(pl.multiple_of(pair * half, 16), half)]
    send_ref[...] = all_ref[pl.ds(pl.multiple_of((1 - pair) * half, 16), half)]


def add_after(a_ref, b_ref, after_ref, out_ref):
    out_ref[...] = (a_ref[...].astype(F32) + b_ref[...].astype(F32)).astype(BF16)


def grad_pre_one(info, *refs, bands, total):
    terms, refs = refs[:bands], refs[bands:]
    slope_ref, wide_ref, g_ref, keep_ref, send_ref, part_ref = refs
    strip, pair = info[0], info[1]
    summed = terms[0][...].astype(F32)
    for k in range(1, bands):
        summed = summed + terms[k][...].astype(F32)
    blank = jnp.zeros((PITCH - SENT, 256), F32)
    stacked = jnp.concatenate([p for t in range(3) for p in (summed[t], blank)], 0).astype(BF16)
    ordered = dot(stacked, order_matrix(), (1, 1)).astype(BF16)
    pool = pool_matrix(strip, total)
    ups = []
    for t in range(3):
        block = ordered[t * PITCH : (t + 1) * PITCH]
        ups.append(dot(jnp.concatenate([block[:, :128], block[:, 128:]], 0), pool, (0, 0)))
    quads = [ups[0][:64], ups[0][64:], ups[1][:64], ups[1][64:]]
    rows = [ups[2][64:]] + [quads[h // 2] for h in range(8)] + [ups[2][:64]]
    acc = None
    own = lax.broadcasted_iota(jnp.int32, (64, 256), 1) < 128
    for h in range(10):
        g = (rows[h] * slope_ref[h].astype(F32)).astype(BF16)
        g_ref[h] = g
        if 1 <= h <= 8:
            mine = jnp.where(own, g.astype(F32), 0.0)
            cat = jnp.concatenate([roll(mine, -1, 1), mine, roll(mine, 1, 1)], 0).astype(BF16)
            part = dot(cat, wide_ref[h : h + 3].reshape(192, 256), (1, 1))
            acc = part if acc is None else acc + part
    part_ref[:192] = acc[:, :128].astype(BF16)
    tail = jnp.concatenate([acc[:96, 128:], acc[96:, 128:]], 1)
    part_ref[192:] = tail.astype(BF16)
    half = keep_ref.shape[0]
    keep_ref[...] = part_ref[pl.ds(pl.multiple_of(pair * half, 16), half)]
    send_ref[...] = part_ref[pl.ds(pl.multiple_of((1 - pair) * half, 16), half)]


def layer_one_back(g_ref, w_ref, out_ref):
    rows = []
    for h in range(8):
        z = dot(w_ref[...], g_ref[h : h + 3].reshape(192, 256), (1, 0))
        rows.append((roll(z[:64], -1, 1) + z[64:128] + roll(z[128:], 1, 1))[:, :128])
    out_ref[...] = jnp.swapaxes(jnp.stack(rows, 0), 0, 1).astype(BF16)


def unpack_one(info, mine_ref, other_ref, out_ref, flat_ref, *, scale):
    pair, half = info[1], mine_ref.shape[0]
    flat_ref[pl.ds(pl.multiple_of(pair * half, 16), half)] = mine_ref[...]
    flat_ref[pl.ds(pl.multiple_of((1 - pair) * half, 16), half)] = other_ref[...]
    flat = flat_ref[...].astype(F32) * scale
    out_ref[0] = flat[:192, :64]
    out_ref[1] = flat[:192, 64:]
    out_ref[2, :96] = flat[192:, :64]
    out_ref[2, 96:] = flat[192:, 64:]


def even_swap(values, axis, count):
    return lax.ppermute(values, axis, [(n, n ^ 1) for n in range(count)])


def odd_swap(values, axis, count):
    steps = [(n, n + 1) for n in range(1, count - 1, 2)]
    return lax.ppermute(values, axis, steps + [(b, a) for a, b in steps])


def xor_swap(values, axis, count, k):
    return lax.ppermute(values, axis, [(n, n ^ k) for n in range(count)])


def border_swap(head, tail, axis, place):
    count = lax.axis_size(axis)
    even = place % 2 == 0
    first = even_swap(jnp.where(even, tail, head), axis, count)
    second = odd_swap(jnp.where(even, head, tail), axis, count)
    return jnp.where(even, second, first), jnp.where(even, first, second)


def sum_cols(part):
    count, step = lax.axis_size("col"), 1
    while step < count:
        sent = part.astype(BF16)
        part = sent.astype(F32) + xor_swap(sent, "col", count, step).astype(F32)
        step *= 2
    return part


def local(features_in, filters_one, filters_two, out_grad):
    channels, band_rows, strip_cols = features_in.shape
    filters, own_cols, pooled_rows = out_grad.shape
    bands = lax.axis_size("row")
    strips = lax.axis_size(COLS)
    band = lax.axis_index("row")
    strip = lax.axis_index(COLS)
    pair = lax.axis_index("pair")
    height, width = band_rows * bands, strip_cols * strips
    total = own_cols * strips
    at_strip = jnp.stack([strip]).astype(jnp.int32)
    at_band = jnp.stack([band]).astype(jnp.int32)
    at_pair = jnp.stack([pair]).astype(jnp.int32)
    at_place = jnp.stack([strip, pair]).astype(jnp.int32)

    taps_one = jnp.transpose(filters_one, (1, 2, 0, 3)).reshape(3, 3 * channels, channels)
    back_one = jnp.transpose(filters_one[:, ::-1], (2, 3, 1, 0)).reshape(3 * channels, 3 * channels)
    taps_two = jnp.transpose(filters_two, (1, 2, 0, 3)).reshape(3, 3 * filters, 4 * channels)

    x = jnp.transpose(features_in, (1, 0, 2))
    above, below = border_swap(x[:2], x[-2:], "row", band)
    og = jnp.transpose(out_grad, (1, 2, 0))
    edge = REACH - 1
    head, tail = (
        jnp.pad(e.reshape(-1, 128), ((0, channels - e.size // 128), (0, 0)))[None]
        for e in (og[:edge], og[-edge:])
    )
    even = strip % 2 == 0
    side_a = even_swap(jnp.concatenate([above, x, below, jnp.where(even, tail, head)], 0), COLS, strips)
    side_b = odd_swap(jnp.concatenate([above, x, below, jnp.where(even, head, tail)], 0), COLS, strips)
    rows_wide = band_rows + 2
    pooled, slope, wide = whole_call(
        functools.partial(layer_one, total=total),
        [
            shaped((2, SENT, 4 * channels)),
            shaped((rows_wide, channels, 256)),
            shaped((rows_wide + 2, channels, 256)),
        ],
        [at_strip, x, above, below, side_a, side_b, taps_one],
        2 * rows_wide * 192 * 192 * 256,
    )
    pieces = [pooled] + [xor_swap(pooled, "row", bands, k) for k in range(1, bands)]

    ends = [side[-1].reshape(-1)[: og[:edge].size].reshape(og[:edge].shape) for side in (side_a, side_b)]
    before, after = jnp.where(even, ends[1], ends[0]), jnp.where(even, ends[0], ends[1])
    og = jnp.concatenate([before, og, after], 0)
    og = jnp.pad(og, ((1, PITCH - own_cols - 2 * REACH + 1), (0, 0), (0, 0)))
    og = jnp.transpose(og, (1, 0, 2))

    count = pooled_rows * PITCH
    *terms, pooled_map, grad_cat = whole_call(
        functools.partial(layer_two, bands=bands),
        [shaped((3, SENT, 4 * channels))] * bands
        + [shaped((pooled_rows + 2, PITCH, 4 * channels)), shaped((count, 3 * filters))],
        [at_band, og, taps_two] + pieces,
        4 * count * 9 * filters * 4 * channels,
        scratch=[
            pltpu.VMEM((pooled_rows + 2, PITCH, filters), BF16),
            pltpu.VMEM((pooled_rows + 2, PITCH, 4 * channels), F32),
        ],
    )
    received = [terms[0]] + [xor_swap(terms[k], "row", bands, k) for k in range(1, bands)]

    half = 9 * filters // 2
    keep_two, send_two = whole_call(
        filter_two_grads,
        [shaped((half, 4 * channels))] * 2,
        [at_pair, pooled_map, grad_cat],
        0,
        scratch=[pltpu.VMEM((2 * half, 4 * channels), BF16)],
    )
    swapped = even_swap(send_two, "pair", 2)
    share = 9 * channels * channels // 256
    g, keep, send = whole_call(
        functools.partial(grad_pre_one, bands=bands, total=total),
        [shaped((rows_wide, channels, 256))] + [shaped((share, 128))] * 2,
        [at_place] + received + [slope, wide],
        2 * 8 * 192 * 192 * 256,
        scratch=[pltpu.VMEM((2 * share, 128), BF16)],
    )
    (part_two,) = whole_call(
        add_after, [shaped(keep_two.shape)], [keep_two, swapped, keep], 0, scalars=0
    )
    mine = sum_cols(part_two).astype(BF16)
    other = even_swap(mine, "pair", 2)
    grad_two = jnp.concatenate([jnp.where(pair == 0, mine, other), jnp.where(pair == 0, other, mine)], 0)
    grad_two = grad_two.astype(F32) * (1.0 / math.sqrt(pooled_rows * total))
    grad_two = jnp.transpose(grad_two.reshape(3, 3, filters, 4 * channels), (2, 0, 1, 3))

    part = sum_cols(keep.astype(F32) + even_swap(send, "pair", 2).astype(F32)).astype(BF16)
    terms = [part.astype(F32)] + [xor_swap(part, "row", bands, k).astype(F32) for k in range(1, bands)]
    while len(terms) > 1:
        terms = [a + b for a, b in zip(terms[::2], terms[1::2])]
    mine = terms[0].astype(BF16)
    other = even_swap(mine, "pair", 2)
    (grad_one,) = whole_call(
        functools.partial(unpack_one, scale=1.0 / math.sqrt(height * width)),
        [shaped((3, 3 * channels, channels), F32)],
        [at_place, mine, other],
        1,
        scratch=[pltpu.VMEM((2 * share, 128), BF16)],
    )
    grad_one = jnp.transpose(grad_one.reshape(3, 3, channels, channels), (2, 0, 1, 3))
    (input_grad,) = whole_call(
        layer_one_back, [shaped(features_in.shape)], [g, back_one], 2 * 8 * 192 * 192 * 256, scalars=0
    )
    return (input_grad, grad_one, grad_two)


def solution(mesh):
    in_specs = (
        P("grp", "row", ("col", "pair")),
        P(),
        P("row", None, None, None),
        P(("grp", "row"), ("col", "pair"), None),
    )
    out_specs = (
        P("grp", "row", ("col", "pair")),
        P("grp", None, None, None),
        P(("grp", "row"), None, None, None),
    )
    return jax.shard_map(local, mesh=mesh, in_specs=in_specs, out_specs=out_specs, check_vma=False)
```

```python
import functools
import math

import jax
import jax.numpy as jnp
from jax import lax
from jax.experimental import pallas as pl
from jax.experimental.pallas import tpu as pltpu
from jax.sharding import PartitionSpec as P

BF16 = jnp.bfloat16
F32 = jnp.float32
COLS = ("col", "pair")
REACH = 3
PITCH = 48
SENT = 40


def dot(a, b, contract):
    return lax.dot_general(a, b, ((contract[:1], contract[1:]), ((), ())), preferred_element_type=F32)


def whole_call(body, outs, operands, flops, scalars=1, scratch=()):
    specs = [
        pl.BlockSpec(memory_space=pltpu.SMEM if n < scalars else pltpu.VMEM)
        for n in range(len(operands))
    ]
    sizes = [math.prod(a.shape) * a.dtype.itemsize for a in tuple(operands[scalars:]) + tuple(outs)]
    moved = sum(sizes) if flops else 0
    return pl.pallas_call(
        body,
        out_shape=outs,
        in_specs=specs,
        out_specs=[pl.BlockSpec(memory_space=pltpu.VMEM) for _ in outs],
        scratch_shapes=list(scratch),
        cost_estimate=pl.CostEstimate(flops=flops, bytes_accessed=moved, transcendentals=0),
        compiler_params=pltpu.CompilerParams(vmem_limit_bytes=40 * 1024 * 1024),
    )(*operands)


def shaped(shape, dtype=BF16):
    return jax.ShapeDtypeStruct(shape, dtype)


def roll(values, amount, axis):
    return pltpu.roll(values, amount % values.shape[axis], axis)


def sigmoid(values):
    return 1.0 / (1.0 + jnp.exp(-values))


def slope_of(values, sig):
    return sig * (1.0 + values * (1.0 - sig))


def pool_matrix(strip, total, back=False):
    row = lax.broadcasted_iota(jnp.int32, (2 * PITCH, 256), 0)
    lane = lax.broadcasted_iota(jnp.int32, (2 * PITCH, 256), 1)
    half = (row >= PITCH).astype(jnp.int32)
    n = row - half * PITCH
    if back:
        v, most = jnp.where((n == 32) & (half == 1), -1, n), 33
    else:
        v, most = n - REACH, 32 + 2 * REACH
    near = jnp.bitwise_and(lane - 4 * v - 2 * half, 255) < 2
    place = strip * 32 + v
    keep = near & (n < most) & (place >= 0) & (place < total)
    return jnp.where(keep, 0.25, 0.0).astype(BF16)


def order_matrix():
    row = lax.broadcasted_iota(jnp.int32, (256, 256), 0)
    lane = lax.broadcasted_iota(jnp.int32, (256, 256), 1)
    j, i, c = row >> 7, (row >> 6) & 1, row & 63
    return jnp.where(lane == 4 * c + 2 * i + j, 1.0, 0.0).astype(BF16)


def pack_sides(info, x_ref, above_ref, below_ref, head_ref, tail_ref, a_ref, b_ref):
    even = (info[0] & 1) == 0
    rows = [above_ref[...]] + [x_ref[h] for h in range(x_ref.shape[0])] + [below_ref[...]]
    lane = lax.broadcasted_iota(jnp.int32, (64, 128), 1)
    tiles = [[jnp.zeros((64, 128), F32)] * 2 for _ in range(2)]
    for r, row in enumerate(rows):
        wide, slot = row.astype(F32), r % 8
        for side, shift in enumerate((16 * slot, 16 * slot + 16)):
            here = (lane >> 4) == slot
            tiles[side][r // 8] = jnp.where(here, roll(wide, shift, 1), tiles[side][r // 8])
    head, tail = tiles
    for t in range(2):
        a_ref[64 * t : 64 * t + 64] = jnp.where(even, tail[t], head[t]).astype(BF16)
        b_ref[64 * t : 64 * t + 64] = jnp.where(even, head[t], tail[t]).astype(BF16)
    first, last = head_ref[...].astype(F32), tail_ref[...].astype(F32)
    a_ref[128:] = jnp.where(even, last, first).astype(BF16)
    b_ref[128:] = jnp.where(even, first, last).astype(BF16)


def layer_one(
    info, x_ref, above_ref, below_ref, a_ref, b_ref, w_ref, pooled_ref, slope_ref, wide_ref, *, total
):
    strip = info[0]
    band_rows = x_ref.shape[0]
    even = (strip & 1) == 0
    lane = lax.broadcasted_iota(jnp.int32, (64, 128), 1)
    sides = [ref[:128].astype(F32) for ref in (a_ref, b_ref)]
    after, before = jnp.where(even, *sides), jnp.where(even, *sides[::-1])
    for r in range(band_rows + 2):
        tile, slot = 64 * (r // 8), r % 8
        right = roll(after[tile : tile + 64], -16 * slot, 1)
        left = roll(before[tile : tile + 64], -16 * slot - 16, 1)
        halo = jnp.where(lane < 16, right, jnp.where(lane >= 112, left, 0.0))
        wide_ref[r, :, 128:] = halo.astype(BF16)
    wide_ref[0, :, :128] = above_ref[...]
    wide_ref[1 : band_rows + 1, :, :128] = x_ref[...]
    wide_ref[band_rows + 1, :, :128] = below_ref[...]
    weights = jnp.concatenate([w_ref[0], w_ref[1], w_ref[2]], axis=1)
    rows = slope_ref.shape[0]
    halves, held = [], None
    for h in range(rows):
        y = dot(weights, wide_ref[h : h + 3].reshape(192, 256), (1, 0))
        pre = roll(y[:64], 1, 1) + y[64:128] + roll(y[128:], -1, 1)
        sig = sigmoid(pre)
        slope_ref[h] = slope_of(pre, sig).astype(BF16)
        active = pre * sig
        if h % 2:
            halves.append((held + active).astype(BF16))
        else:
            held = active
    pooled = dot(pool_matrix(strip, total), jnp.concatenate(halves, 0), (1, 1))
    stacked = jnp.concatenate(
        [
            jnp.concatenate(
                [pooled[:PITCH, u * 128 : u * 128 + 128], pooled[PITCH:, u * 128 : u * 128 + 128]], 1
            )
            for u in range(2)
        ],
        0,
    ).astype(BF16)
    ordered = dot(stacked, order_matrix(), (1, 0)).astype(BF16)
    for u in range(2):
        pooled_ref[u] = ordered[u * PITCH : u * PITCH + SENT]


def layer_two(info, og_ref, w_ref, *refs, bands):
    pieces, refs = refs[:bands], refs[bands:]
    terms, refs = refs[:bands], refs[bands:]
    map_ref, cat_ref, grad_ref, spread_ref = refs
    band = info[0]
    rows, _, filters = og_ref.shape
    count = rows * PITCH
    map_ref[0] = jnp.zeros((PITCH, 256), BF16)
    map_ref[rows + 1] = jnp.zeros((PITCH, 256), BF16)
    blank = jnp.zeros((PITCH - SENT, 256), BF16)
    for k in range(bands):
        for t in range(2):
            map_ref[1 + 2 * (band ^ k) + t] = jnp.concatenate([pieces[k][t], blank], 0)
    y = None
    for i in range(3):
        part = dot(map_ref[i : i + rows].reshape(count, 256), w_ref[i], (1, 1))
        y = part if y is None else y + part
    pre = roll(y[:, :filters], 1, 0) + y[:, filters : 2 * filters] + roll(y[:, 2 * filters :], -1, 0)
    grad = og_ref[...].reshape(count, filters).astype(F32) * slope_of(pre, sigmoid(pre))
    grad = grad.astype(BF16)
    grad_ref[0] = jnp.zeros((PITCH, filters), BF16)
    grad_ref[rows + 1] = jnp.zeros((PITCH, filters), BF16)
    grad_ref[1 : rows + 1] = grad.reshape(rows, PITCH, filters)
    z = None
    for i in range(3):
        weights = jnp.concatenate([w_ref[i, j * filters : (j + 1) * filters] for j in range(3)], 1)
        part = dot(grad_ref[2 - i : 2 - i + rows].reshape(count, filters), weights, (1, 0))
        z = part if z is None else z + part
    spread = roll(z[:, :256], -1 - REACH, 0) + roll(z[:, 256:512], -REACH, 0) + roll(z[:, 512:], 1 - REACH, 0)
    n = lax.broadcasted_iota(jnp.int32, (rows, PITCH, 256), 1).reshape(count, 256)
    odd = (lax.broadcasted_iota(jnp.int32, (count, 256), 1) & 1) == 1
    spread = jnp.where((n == 32) & odd, roll(spread, 33, 0), spread)
    spread = jnp.where(n == 33, roll(spread, 33 - 32 - PITCH, 0), spread)
    spread_ref[...] = spread.astype(BF16).reshape(rows, PITCH, 256)
    for k in range(bands):
        first = 2 * (band ^ k)
        terms[k][...] = jnp.concatenate([spread_ref[first, :40], spread_ref[first + 1, :32]], 0)
    wide = grad.astype(F32)
    v = lax.broadcasted_iota(jnp.int32, (rows, PITCH, filters), 1).reshape(count, filters)
    wide = jnp.where((v >= REACH) & (v < REACH + 32), wide, 0.0)
    cat_ref[...] = jnp.concatenate([roll(wide, -1, 0), wide, roll(wide, 1, 0)], 1).astype(BF16)


def filter_two_grads(info, map_ref, cat_ref, keep_ref, send_ref, all_ref):
    pair = info[0]
    rows = map_ref.shape[0] - 2
    taps = cat_ref.shape[1]
    for i in range(3):
        part = dot(cat_ref[...], map_ref[i : i + rows].reshape(rows * PITCH, 256), (0, 0))
        all_ref[i * taps : (i + 1) * taps] = part.astype(BF16)
    half = keep_ref.shape[0]
    keep_ref[...] = all_ref[pl.ds(pl.multiple_of(pair * half, 16), half)]
    send_ref[...] = all_ref[pl.ds(pl.multiple_of((1 - pair) * half, 16), half)]


def add_after(a_ref, b_ref, *refs):
    out_ref = refs[-1]
    out_ref[...] = (a_ref[...].astype(F32) + b_ref[...].astype(F32)).astype(BF16)


def grad_pre_one(info, *refs, bands, total):
    terms, refs = refs[:bands], refs[bands:]
    slope_ref, wide_ref, g_ref, a_ref, b_ref, keep_ref, send_ref, part_ref = refs
    strip, pair = info[0], info[1]
    summed = terms[0][...].astype(F32)
    for k in range(1, bands):
        summed = summed + terms[k][...].astype(F32)
    blank = jnp.zeros((8, 256), F32)
    ends = summed[32:40]
    blocks = [summed[:32], ends, blank, summed[40:], roll(ends, -1, 0), blank]
    ordered = dot(jnp.concatenate(blocks, 0).astype(BF16), order_matrix(), (1, 1)).astype(BF16)
    pool = pool_matrix(strip, total, back=True)
    acc = None
    own = lax.broadcasted_iota(jnp.int32, (64, 256), 1) < 128
    for u in range(2):
        block = ordered[u * PITCH : (u + 1) * PITCH]
        up = dot(jnp.concatenate([block[:, :128], block[:, 128:]], 0), pool, (0, 0))
        for i in range(4):
            h = 4 * u + i
            g = (up[64 * (i // 2) : 64 * (i // 2) + 64] * slope_ref[h].astype(F32)).astype(BF16)
            g_ref[h] = g
            mine = jnp.where(own, g.astype(F32), 0.0)
            cat = jnp.concatenate([roll(mine, -1, 1), mine, roll(mine, 1, 1)], 0).astype(BF16)
            part = dot(cat, wide_ref[h : h + 3].reshape(192, 256), (1, 1))
            acc = part if acc is None else acc + part
    even = (info[2] & 1) == 0
    first, last = g_ref[0].astype(F32), g_ref[7].astype(F32)
    a_ref[...] = jnp.where(even, last, first).astype(BF16)
    b_ref[...] = jnp.where(even, first, last).astype(BF16)
    part_ref[:192] = acc[:, :128].astype(BF16)
    tail = jnp.concatenate([acc[:96, 128:], acc[96:, 128:]], 1)
    part_ref[192:] = tail.astype(BF16)
    half = keep_ref.shape[0]
    keep_ref[...] = part_ref[pl.ds(pl.multiple_of(pair * half, 16), half)]
    send_ref[...] = part_ref[pl.ds(pl.multiple_of((1 - pair) * half, 16), half)]


def layer_one_back(info, g_ref, a_ref, b_ref, w_ref, out_ref):
    even = (info[2] & 1) == 0
    sides = a_ref[...].astype(F32), b_ref[...].astype(F32)
    below, above = jnp.where(even, *sides).astype(BF16), jnp.where(even, *sides[::-1]).astype(BF16)
    lines = [above] + [g_ref[h] for h in range(8)] + [below]
    rows = []
    for h in range(8):
        z = dot(w_ref[...], jnp.concatenate(lines[h : h + 3], 0), (1, 0))
        rows.append((roll(z[:64], -1, 1) + z[64:128] + roll(z[128:], 1, 1))[:, :128])
    out_ref[...] = jnp.swapaxes(jnp.stack(rows, 0), 0, 1).astype(BF16)


def unpack_one(info, mine_ref, other_ref, out_ref, flat_ref, *, scale):
    pair, half = info[1], mine_ref.shape[0]
    flat_ref[pl.ds(pl.multiple_of(pair * half, 16), half)] = mine_ref[...]
    flat_ref[pl.ds(pl.multiple_of((1 - pair) * half, 16), half)] = other_ref[...]
    flat = flat_ref[...].astype(F32) * scale
    out_ref[0] = flat[:192, :64]
    out_ref[1] = flat[:192, 64:]
    out_ref[2, :96] = flat[192:, :64]
    out_ref[2, 96:] = flat[192:, 64:]


def even_swap(values, axis, count):
    return lax.ppermute(values, axis, [(n, n ^ 1) for n in range(count)])


def odd_swap(values, axis, count):
    steps = [(n, n + 1) for n in range(1, count - 1, 2)]
    return lax.ppermute(values, axis, steps + [(b, a) for a, b in steps])


def xor_swap(values, axis, count, k):
    return lax.ppermute(values, axis, [(n, n ^ k) for n in range(count)])


def border_swap(head, tail, axis, place):
    count = lax.axis_size(axis)
    even = place % 2 == 0
    first = even_swap(jnp.where(even, tail, head), axis, count)
    second = odd_swap(jnp.where(even, head, tail), axis, count)
    return jnp.where(even, second, first), jnp.where(even, first, second)


def added(a, b, *after):
    (total,) = whole_call(add_after, [shaped(a.shape)], [a, b, *after], 0, scalars=0)
    return total


def sum_cols(part, after=()):
    count, step = lax.axis_size("col"), 1
    while step < count:
        other = xor_swap(part, "col", count, step)
        step *= 2
        if after and step >= count:
            part = added(part, other, *after)
        else:
            part = (part.astype(F32) + other.astype(F32)).astype(BF16)
    return part


def local(features_in, filters_one, filters_two, out_grad):
    channels, band_rows, strip_cols = features_in.shape
    filters, own_cols, pooled_rows = out_grad.shape
    bands = lax.axis_size("row")
    strips = lax.axis_size(COLS)
    band = lax.axis_index("row")
    strip = lax.axis_index(COLS)
    pair = lax.axis_index("pair")
    height, width = band_rows * bands, strip_cols * strips
    total = own_cols * strips
    at_band = jnp.stack([band]).astype(jnp.int32)
    at_pair = jnp.stack([pair]).astype(jnp.int32)
    at_place = jnp.stack([strip, pair, band]).astype(jnp.int32)

    taps_one = jnp.transpose(filters_one, (1, 2, 0, 3)).reshape(3, 3 * channels, channels)
    back_one = jnp.transpose(filters_one[:, ::-1], (2, 3, 1, 0)).reshape(3 * channels, 3 * channels)
    taps_two = jnp.transpose(filters_two, (1, 2, 0, 3)).reshape(3, 3 * filters, 4 * channels)

    above, below = border_swap(features_in[:, 0], features_in[:, -1], "row", band)
    x = jnp.transpose(features_in, (1, 0, 2))
    og = jnp.transpose(out_grad, (1, 2, 0))
    edge = REACH - 1
    head, tail = (e.reshape(-1, 128) for e in (og[:edge], og[-edge:]))
    to_a, to_b = whole_call(
        pack_sides,
        [shaped((2 * channels + head.shape[0], 128))] * 2,
        [at_place, x, above, below, head, tail],
        1,
    )
    side_a, side_b = even_swap(to_a, COLS, strips), odd_swap(to_b, COLS, strips)
    pooled, slope, wide = whole_call(
        functools.partial(layer_one, total=total),
        [
            shaped((2, SENT, 4 * channels)),
            shaped((band_rows, channels, 256)),
            shaped((band_rows + 2, channels, 256)),
        ],
        [at_place, x, above, below, side_a, side_b, taps_one],
        2 * band_rows * 192 * 192 * 256,
    )
    pieces = [pooled] + [xor_swap(pooled, "row", bands, k) for k in range(1, bands)]

    even = strip % 2 == 0
    ends = [side[2 * channels :].reshape(og[:edge].shape) for side in (side_a, side_b)]
    before, after = jnp.where(even, ends[1], ends[0]), jnp.where(even, ends[0], ends[1])
    og = jnp.concatenate([before, og, after], 0)
    og = jnp.pad(og, ((1, PITCH - own_cols - 2 * REACH + 1), (0, 0), (0, 0)))
    og = jnp.transpose(og, (1, 0, 2))

    count = pooled_rows * PITCH
    *terms, pooled_map, grad_cat = whole_call(
        functools.partial(layer_two, bands=bands),
        [shaped((72, 4 * channels))] * bands
        + [shaped((pooled_rows + 2, PITCH, 4 * channels)), shaped((count, 3 * filters))],
        [at_band, og, taps_two] + pieces,
        4 * count * 9 * filters * 4 * channels,
        scratch=[
            pltpu.VMEM((pooled_rows + 2, PITCH, filters), BF16),
            pltpu.VMEM((pooled_rows, PITCH, 4 * channels), BF16),
        ],
    )
    received = [terms[0]] + [xor_swap(terms[k], "row", bands, k) for k in range(1, bands)]

    half = 9 * filters // 2
    keep_two, send_two = whole_call(
        filter_two_grads,
        [shaped((half, 4 * channels))] * 2,
        [at_pair, pooled_map, grad_cat],
        0,
        scratch=[pltpu.VMEM((2 * half, 4 * channels), BF16)],
    )
    swapped = even_swap(send_two, "pair", 2)
    share = 9 * channels * channels // 256
    g, up_a, up_b, keep, send = whole_call(
        functools.partial(grad_pre_one, bands=bands, total=total),
        [shaped((band_rows, channels, 256))]
        + [shaped((channels, 256))] * 2
        + [shaped((share, 128))] * 2,
        [at_place] + received + [slope, wide],
        2 * 8 * 192 * 192 * 256,
        scratch=[pltpu.VMEM((2 * share, 128), BF16)],
    )
    part = sum_cols((keep.astype(F32) + even_swap(send, "pair", 2).astype(F32)).astype(BF16))
    part_two = added(keep_two, swapped, part)
    terms = [part.astype(F32)] + [xor_swap(part, "row", bands, k).astype(F32) for k in range(1, bands)]
    while len(terms) > 1:
        terms = [a + b for a, b in zip(terms[::2], terms[1::2])]
    mine = terms[0].astype(BF16)
    other = even_swap(mine, "pair", 2)
    (input_grad,) = whole_call(
        layer_one_back,
        [shaped(features_in.shape)],
        [at_place, g, even_swap(up_a, "row", bands), odd_swap(up_b, "row", bands), back_one],
        2 * band_rows * 192 * 192 * 256,
    )
    mine_two = sum_cols(part_two, after=(mine, input_grad))
    other_two = even_swap(mine_two, "pair", 2)
    first, second = jnp.where(pair == 0, mine_two, other_two), jnp.where(pair == 0, other_two, mine_two)
    grad_two = jnp.concatenate([first, second], 0)
    grad_two = grad_two.astype(F32) * (1.0 / math.sqrt(pooled_rows * total))
    grad_two = jnp.transpose(grad_two.reshape(3, 3, filters, 4 * channels), (2, 0, 1, 3))
    (grad_one,) = whole_call(
        functools.partial(unpack_one, scale=1.0 / math.sqrt(height * width)),
        [shaped((3, 3 * channels, channels), F32)],
        [at_place, mine, other],
        1,
        scratch=[pltpu.VMEM((2 * share, 128), BF16)],
    )
    grad_one = jnp.transpose(grad_one.reshape(3, 3, channels, channels), (2, 0, 1, 3))
    return (input_grad, grad_one, grad_two)


def solution(mesh):
    in_specs = (
        P("grp", "row", ("col", "pair")),
        P(),
        P("row", None, None, None),
        P(("grp", "row"), ("col", "pair"), None),
    )
    out_specs = (
        P("grp", "row", ("col", "pair")),
        P("grp", None, None, None),
        P(("grp", "row"), None, None, None),
    )
    return jax.shard_map(local, mesh=mesh, in_specs=in_specs, out_specs=out_specs, check_vma=False)
```

```python
import functools
import math

import jax
import jax.numpy as jnp
from jax import lax
from jax.experimental import pallas as pl
from jax.experimental.pallas import tpu as pltpu
from jax.sharding import PartitionSpec as P

BF16 = jnp.bfloat16
F32 = jnp.float32
COLS = ("col", "pair")
REACH = 3
PITCH = 48
SENT = 40


def dot(a, b, contract):
    return lax.dot_general(a, b, ((contract[:1], contract[1:]), ((), ())), preferred_element_type=F32)


def whole_call(body, outs, operands, flops, scalars=1, scratch=(), after=0):
    specs = [
        pl.BlockSpec(memory_space=pltpu.SMEM if n < scalars else pltpu.VMEM)
        for n in range(len(operands) - after)
    ] + [pl.BlockSpec(memory_space=pl.ANY)] * after
    sizes = [math.prod(a.shape) * a.dtype.itemsize for a in tuple(operands[scalars:]) + tuple(outs)]
    moved = sum(sizes) if flops else 0
    return pl.pallas_call(
        body,
        out_shape=outs,
        in_specs=specs,
        out_specs=[pl.BlockSpec(memory_space=pltpu.VMEM) for _ in outs],
        scratch_shapes=list(scratch),
        cost_estimate=pl.CostEstimate(flops=flops, bytes_accessed=moved, transcendentals=0),
        compiler_params=pltpu.CompilerParams(vmem_limit_bytes=40 * 1024 * 1024),
    )(*operands)


def shaped(shape, dtype=BF16):
    return jax.ShapeDtypeStruct(shape, dtype)


def roll(values, amount, axis):
    return pltpu.roll(values, amount % values.shape[axis], axis)


def sigmoid(values):
    return 1.0 / (1.0 + jnp.exp(-values))


def slope_of(values, sig):
    return sig * (1.0 + values * (1.0 - sig))


def pool_matrix(strip, total, back=False):
    row = lax.broadcasted_iota(jnp.int32, (2 * PITCH, 256), 0)
    lane = lax.broadcasted_iota(jnp.int32, (2 * PITCH, 256), 1)
    half = (row >= PITCH).astype(jnp.int32)
    n = row - half * PITCH
    if back:
        v, most = jnp.where((n == 32) & (half == 1), -1, n), 33
    else:
        v, most = n - REACH, 32 + 2 * REACH
    near = jnp.bitwise_and(lane - 4 * v - 2 * half, 255) < 2
    place = strip * 32 + v
    keep = near & (n < most) & (place >= 0) & (place < total)
    return jnp.where(keep, 0.25, 0.0).astype(BF16)


def order_matrix():
    row = lax.broadcasted_iota(jnp.int32, (256, 256), 0)
    lane = lax.broadcasted_iota(jnp.int32, (256, 256), 1)
    j, i, c = row >> 7, (row >> 6) & 1, row & 63
    return jnp.where(lane == 4 * c + 2 * i + j, 1.0, 0.0).astype(BF16)


def split_rows(info, x_ref, w_ref, rows_ref, a_ref, b_ref, joined_ref):
    even = (info[2] & 1) == 0
    rows = jnp.swapaxes(x_ref[...].astype(F32), 0, 1)
    rows_ref[...] = rows.astype(BF16)
    first, last = rows[0], rows[-1]
    a_ref[...] = jnp.where(even, last, first).astype(BF16)
    b_ref[...] = jnp.where(even, first, last).astype(BF16)
    joined_ref[...] = jnp.concatenate([w_ref[0], w_ref[1], w_ref[2]], axis=1)


def pack_sides(info, x_ref, above_ref, below_ref, head_ref, tail_ref, a_ref, b_ref):
    even = (info[0] & 1) == 0
    rows = [above_ref[...]] + [x_ref[h] for h in range(x_ref.shape[0])] + [below_ref[...]]
    slot = lax.broadcasted_iota(jnp.int32, (64, 128), 1) >> 4
    blank = jnp.zeros((64, 128), F32)
    heads, tails = [blank, blank], [blank, blank]
    for r, row in enumerate(rows):
        turned = roll(row.astype(F32), 16 * (r % 8), 1)
        heads[r // 8] = jnp.where(slot == r % 8, turned, heads[r // 8])
        tails[r // 8] = jnp.where(slot == (r - 1) % 8, turned, tails[r // 8])
    for t in range(2):
        a_ref[64 * t : 64 * t + 64] = jnp.where(even, tails[t], heads[t]).astype(BF16)
        b_ref[64 * t : 64 * t + 64] = jnp.where(even, heads[t], tails[t]).astype(BF16)
    first, last = head_ref[...].astype(F32), tail_ref[...].astype(F32)
    a_ref[128:] = jnp.where(even, last, first).astype(BF16)
    b_ref[128:] = jnp.where(even, first, last).astype(BF16)


def layer_one(
    info, x_ref, above_ref, below_ref, a_ref, b_ref, w_ref, pooled_ref, slope_ref, wide_ref, *, total
):
    strip = info[0]
    band_rows = x_ref.shape[0]
    slot = lax.broadcasted_iota(jnp.int32, (128, 128), 1) >> 4
    sides = [ref[:128].astype(F32) for ref in (a_ref, b_ref)]
    from_a = ((slot ^ strip) & 1) == 0
    packed = jnp.where(from_a, *sides), jnp.where(from_a, *sides[::-1])
    for r in range(band_rows + 2):
        tile = 64 * (r // 8)
        wide_ref[r, :, 128:] = roll(packed[r % 2][tile : tile + 64], -16 * (r % 8), 1).astype(BF16)
    wide_ref[0, :, :128] = above_ref[...]
    wide_ref[1 : band_rows + 1, :, :128] = x_ref[...]
    wide_ref[band_rows + 1, :, :128] = below_ref[...]
    weights = w_ref[...]
    rows = slope_ref.shape[0]
    halves, held = [], None
    for h in range(rows):
        y = dot(weights, wide_ref[h : h + 3].reshape(192, 256), (1, 0))
        pre = roll(y[:64], 1, 1) + y[64:128] + roll(y[128:], -1, 1)
        sig = sigmoid(pre)
        slope_ref[h] = slope_of(pre, sig).astype(BF16)
        active = pre * sig
        if h % 2:
            halves.append((held + active).astype(BF16))
        else:
            held = active
    pooled = dot(pool_matrix(strip, total), jnp.concatenate(halves, 0), (1, 1))
    stacked = jnp.concatenate(
        [
            jnp.concatenate(
                [pooled[:PITCH, u * 128 : u * 128 + 128], pooled[PITCH:, u * 128 : u * 128 + 128]], 1
            )
            for u in range(2)
        ],
        0,
    ).astype(BF16)
    ordered = dot(stacked, order_matrix(), (1, 0)).astype(BF16)
    for u in range(2):
        pooled_ref[u] = ordered[u * PITCH : u * PITCH + SENT]


def layer_two(info, og_ref, w_ref, *refs, bands):
    pieces, refs = refs[:bands], refs[bands:]
    terms, refs = refs[:bands], refs[bands:]
    map_ref, own_ref, grad_ref, spread_ref = refs
    band = info[2]
    rows, _, filters = og_ref.shape
    count = rows * PITCH
    map_ref[0] = jnp.zeros((PITCH, 256), BF16)
    map_ref[rows + 1] = jnp.zeros((PITCH, 256), BF16)
    blank = jnp.zeros((PITCH - SENT, 256), BF16)
    for k in range(bands):
        for t in range(2):
            map_ref[1 + 2 * (band ^ k) + t] = jnp.concatenate([pieces[k][t], blank], 0)
    y = None
    for i in range(3):
        part = dot(map_ref[i : i + rows].reshape(count, 256), w_ref[i], (1, 1))
        y = part if y is None else y + part
    pre = roll(y[:, :filters], 1, 0) + y[:, filters : 2 * filters] + roll(y[:, 2 * filters :], -1, 0)
    grad = og_ref[...].reshape(count, filters).astype(F32) * slope_of(pre, sigmoid(pre))
    grad = grad.astype(BF16)
    own_ref[...] = grad
    grad_ref[0] = jnp.zeros((PITCH, filters), BF16)
    grad_ref[rows + 1] = jnp.zeros((PITCH, filters), BF16)
    grad_ref[1 : rows + 1] = grad.reshape(rows, PITCH, filters)
    z = None
    for i in range(3):
        weights = jnp.concatenate([w_ref[i, j * filters : (j + 1) * filters] for j in range(3)], 1)
        part = dot(grad_ref[2 - i : 2 - i + rows].reshape(count, filters), weights, (1, 0))
        z = part if z is None else z + part
    spread = roll(z[:, :256], -1 - REACH, 0) + roll(z[:, 256:512], -REACH, 0) + roll(z[:, 512:], 1 - REACH, 0)
    n = lax.broadcasted_iota(jnp.int32, (rows, PITCH, 256), 1).reshape(count, 256)
    odd = (lax.broadcasted_iota(jnp.int32, (count, 256), 1) & 1) == 1
    spread = jnp.where((n == 32) & odd, roll(spread, 33, 0), spread)
    spread = jnp.where(n == 33, roll(spread, 33 - 32 - PITCH, 0), spread)
    spread_ref[...] = spread.astype(BF16).reshape(rows, PITCH, 256)
    for k in range(bands):
        first = 2 * (band ^ k)
        terms[k][...] = jnp.concatenate([spread_ref[first, :40], spread_ref[first + 1, :32]], 0)


def filter_two_grads(info, map_ref, own_ref, keep_ref, send_ref, all_ref):
    pair = info[1]
    rows = map_ref.shape[0] - 2
    count, filters = own_ref.shape
    v = lax.broadcasted_iota(jnp.int32, (rows, PITCH, filters), 1).reshape(count, filters)
    wide = jnp.where((v >= REACH) & (v < REACH + 32), own_ref[...].astype(F32), 0.0)
    cat = jnp.concatenate([roll(wide, -1, 0), wide, roll(wide, 1, 0)], 1).astype(BF16)
    taps = 3 * filters
    for i in range(3):
        part = dot(cat, map_ref[i : i + rows].reshape(rows * PITCH, 256), (0, 0))
        all_ref[i * taps : (i + 1) * taps] = part.astype(BF16)
    half = keep_ref.shape[0]
    keep_ref[...] = all_ref[pl.ds(pl.multiple_of(pair * half, 16), half)]
    send_ref[...] = all_ref[pl.ds(pl.multiple_of((1 - pair) * half, 16), half)]


def add_after(a_ref, b_ref, *refs):
    out_ref = refs[-1]
    out_ref[...] = (a_ref[...].astype(F32) + b_ref[...].astype(F32)).astype(BF16)


def grad_pre_one(info, *refs, bands, total):
    terms, refs = refs[:bands], refs[bands:]
    slope_ref, wide_ref, g_ref, a_ref, b_ref, keep_ref, send_ref, part_ref = refs
    strip, pair = info[0], info[1]
    summed = terms[0][...].astype(F32)
    for k in range(1, bands):
        summed = summed + terms[k][...].astype(F32)
    blank = jnp.zeros((8, 256), F32)
    ends = summed[32:40]
    blocks = [summed[:32], ends, blank, summed[40:], roll(ends, -1, 0), blank]
    ordered = dot(jnp.concatenate(blocks, 0).astype(BF16), order_matrix(), (1, 1)).astype(BF16)
    pool = pool_matrix(strip, total, back=True)
    acc = None
    own = lax.broadcasted_iota(jnp.int32, (64, 256), 1) < 128
    for u in range(2):
        block = ordered[u * PITCH : (u + 1) * PITCH]
        up = dot(jnp.concatenate([block[:, :128], block[:, 128:]], 0), pool, (0, 0))
        for i in range(4):
            h = 4 * u + i
            g = (up[64 * (i // 2) : 64 * (i // 2) + 64] * slope_ref[h].astype(F32)).astype(BF16)
            g_ref[h] = g
            mine = jnp.where(own, g.astype(F32), 0.0)
            cat = jnp.concatenate([roll(mine, -1, 1), mine, roll(mine, 1, 1)], 0).astype(BF16)
            part = dot(cat, wide_ref[h : h + 3].reshape(192, 256), (1, 1))
            acc = part if acc is None else acc + part
    even = (info[2] & 1) == 0
    first, last = g_ref[0].astype(F32), g_ref[7].astype(F32)
    a_ref[...] = jnp.where(even, last, first).astype(BF16)
    b_ref[...] = jnp.where(even, first, last).astype(BF16)
    part_ref[:192] = acc[:, :128].astype(BF16)
    tail = jnp.concatenate([acc[:96, 128:], acc[96:, 128:]], 1)
    part_ref[192:] = tail.astype(BF16)
    half = keep_ref.shape[0]
    keep_ref[...] = part_ref[pl.ds(pl.multiple_of(pair * half, 16), half)]
    send_ref[...] = part_ref[pl.ds(pl.multiple_of((1 - pair) * half, 16), half)]


def layer_one_back(info, g_ref, a_ref, b_ref, w_ref, out_ref, *, bands):
    band = info[2]
    even = (band & 1) == 0
    inner = (band > 0) & (band < bands - 1)
    sides = a_ref[...].astype(F32), jnp.where(inner, b_ref[...].astype(F32), 0.0)
    below, above = jnp.where(even, *sides).astype(BF16), jnp.where(even, *sides[::-1]).astype(BF16)
    lines = [above] + [g_ref[h] for h in range(8)] + [below]
    rows = []
    for h in range(8):
        z = dot(w_ref[...], jnp.concatenate(lines[h : h + 3], 0), (1, 0))
        rows.append((roll(z[:64], -1, 1) + z[64:128] + roll(z[128:], 1, 1))[:, :128])
    out_ref[...] = jnp.swapaxes(jnp.stack(rows, 0), 0, 1).astype(BF16)


def unpack_one(info, mine_ref, other_ref, out_ref, flat_ref, *, scale):
    pair, half = info[1], mine_ref.shape[0]
    flat_ref[pl.ds(pl.multiple_of(pair * half, 16), half)] = mine_ref[...]
    flat_ref[pl.ds(pl.multiple_of((1 - pair) * half, 16), half)] = other_ref[...]
    flat = flat_ref[...].astype(F32) * scale
    out_ref[0] = flat[:192, :64]
    out_ref[1] = flat[:192, 64:]
    out_ref[2, :96] = flat[192:, :64]
    out_ref[2, 96:] = flat[192:, 64:]


def even_swap(values, axis, count):
    return lax.ppermute(values, axis, [(n, n ^ 1) for n in range(count)])


def odd_swap(values, axis, count):
    return lax.ppermute(values, axis, [(n, (n - 1 if n % 2 == 0 else n + 1) % count) for n in range(count)])


def inner_swap(values, axis, count):
    steps = [(n, n - 1 if n % 2 == 0 else n + 1) for n in range(1, count - 1)]
    return lax.ppermute(values, axis, steps + [(0, 0), (count - 1, count - 1)])


def xor_swap(values, axis, count, k):
    return lax.ppermute(values, axis, [(n, n ^ k) for n in range(count)])


def row_swaps(values, bands):
    order = sorted(range(1, bands), key=lambda k: (k < bands // 2, k))
    moved = {k: xor_swap(values[k], "row", bands, k) for k in order}
    return [moved[k] for k in range(1, bands)]


def added(a, b, *after):
    (total,) = whole_call(add_after, [shaped(a.shape)], [a, b, *after], 0, scalars=0, after=len(after))
    return total


def sum_cols(part, after=()):
    count, step = lax.axis_size("col"), 1
    while step < count:
        other = xor_swap(part, "col", count, step)
        step *= 2
        if after and step >= count:
            part = added(part, other, *after)
        else:
            part = (part.astype(F32) + other.astype(F32)).astype(BF16)
    return part


def local(features_in, filters_one, filters_two, out_grad):
    channels, band_rows, strip_cols = features_in.shape
    filters, own_cols, pooled_rows = out_grad.shape
    bands = lax.axis_size("row")
    strips = lax.axis_size(COLS)
    band = lax.axis_index("row")
    strip = lax.axis_index(COLS)
    pair = lax.axis_index("pair")
    height, width = band_rows * bands, strip_cols * strips
    total = own_cols * strips
    at_place = jnp.stack([strip, pair, band]).astype(jnp.int32)

    taps_one = jnp.transpose(filters_one, (1, 2, 0, 3)).reshape(3, 3 * channels, channels)
    back_one = jnp.transpose(filters_one[:, ::-1], (2, 3, 1, 0)).reshape(3 * channels, 3 * channels)
    taps_two = jnp.transpose(filters_two, (1, 2, 0, 3)).reshape(3, 3 * filters, 4 * channels)

    x, to_a, to_b, joined_one = whole_call(
        split_rows,
        [shaped((band_rows, channels, strip_cols))]
        + [shaped((channels, strip_cols))] * 2
        + [shaped((3 * channels, 3 * channels))],
        [at_place, features_in, taps_one],
        1,
    )
    side_a, side_b = even_swap(to_a, "row", bands), inner_swap(to_b, "row", bands)
    even = band % 2 == 0
    above, below = jnp.where(even, side_b, side_a), jnp.where(even, side_a, side_b)
    above, below = jnp.where(band == 0, 0, above), jnp.where(band == bands - 1, 0, below)
    og = jnp.transpose(out_grad, (1, 2, 0))
    edge = REACH - 1
    head, tail = (e.reshape(-1, 128) for e in (og[:edge], og[-edge:]))
    to_a, to_b = whole_call(
        pack_sides,
        [shaped((2 * channels + head.shape[0], 128))] * 2,
        [at_place, x, above, below, head, tail],
        1,
    )
    side_a, side_b = even_swap(to_a, COLS, strips), odd_swap(to_b, COLS, strips)
    side_b = jnp.where((strip == 0) | (strip == strips - 1), 0, side_b)
    pooled, slope, wide = whole_call(
        functools.partial(layer_one, total=total),
        [
            shaped((2, SENT, 4 * channels)),
            shaped((band_rows, channels, 256)),
            shaped((band_rows + 2, channels, 256)),
        ],
        [at_place, x, above, below, side_a, side_b, joined_one],
        2 * band_rows * 192 * 192 * 256,
    )
    pieces = [pooled] + row_swaps([pooled] * bands, bands)

    even = strip % 2 == 0
    ends = [side[2 * channels :].reshape(og[:edge].shape) for side in (side_a, side_b)]
    before, after = jnp.where(even, ends[1], ends[0]), jnp.where(even, ends[0], ends[1])
    og = jnp.concatenate([before, og, after], 0)
    og = jnp.pad(og, ((1, PITCH - own_cols - 2 * REACH + 1), (0, 0), (0, 0)))
    og = jnp.transpose(og, (1, 0, 2))

    count = pooled_rows * PITCH
    *terms, pooled_map, own_grad = whole_call(
        functools.partial(layer_two, bands=bands),
        [shaped((72, 4 * channels))] * bands
        + [shaped((pooled_rows + 2, PITCH, 4 * channels)), shaped((count, filters))],
        [at_place, og, taps_two] + pieces,
        4 * count * 9 * filters * 4 * channels,
        scratch=[
            pltpu.VMEM((pooled_rows + 2, PITCH, filters), BF16),
            pltpu.VMEM((pooled_rows, PITCH, 4 * channels), BF16),
        ],
    )
    received = [terms[0]] + row_swaps(terms, bands)

    half = 9 * filters // 2
    keep_two, send_two = whole_call(
        filter_two_grads,
        [shaped((half, 4 * channels))] * 2,
        [at_place, pooled_map, own_grad],
        0,
        scratch=[pltpu.VMEM((2 * half, 4 * channels), BF16)],
    )
    swapped = even_swap(send_two, "pair", 2)
    share = 9 * channels * channels // 256
    g, up_a, up_b, keep, send = whole_call(
        functools.partial(grad_pre_one, bands=bands, total=total),
        [shaped((band_rows, channels, 256))]
        + [shaped((channels, 256))] * 2
        + [shaped((share, 128))] * 2,
        [at_place] + received + [slope, wide],
        2 * 8 * 192 * 192 * 256,
        scratch=[pltpu.VMEM((2 * share, 128), BF16)],
    )
    part_two = added(keep_two, swapped, keep)
    part = added(keep, even_swap(send, "pair", 2), part_two)
    terms = [t.astype(F32) for t in [part] + row_swaps([part] * bands, bands)]
    while len(terms) > 1:
        terms = [a + b for a, b in zip(terms[::2], terms[1::2])]
    part = terms[0].astype(BF16)
    (input_grad,) = whole_call(
        functools.partial(layer_one_back, bands=bands),
        [shaped(features_in.shape)],
        [at_place, g, even_swap(up_a, "row", bands), inner_swap(up_b, "row", bands), back_one],
        2 * band_rows * 192 * 192 * 256,
    )
    mine = sum_cols(part)
    other = even_swap(mine, "pair", 2)
    mine_two = sum_cols(part_two, after=(part, input_grad))
    other_two = even_swap(mine_two, "pair", 2)
    first, second = jnp.where(pair == 0, mine_two, other_two), jnp.where(pair == 0, other_two, mine_two)
    grad_two = jnp.concatenate([first, second], 0)
    grad_two = grad_two.astype(F32) * (1.0 / math.sqrt(pooled_rows * total))
    grad_two = jnp.transpose(grad_two.reshape(3, 3, filters, 4 * channels), (2, 0, 1, 3))
    (grad_one,) = whole_call(
        functools.partial(unpack_one, scale=1.0 / math.sqrt(height * width)),
        [shaped((3, 3 * channels, channels), F32)],
        [at_place, mine, other],
        1,
        scratch=[pltpu.VMEM((2 * share, 128), BF16)],
    )
    grad_one = jnp.transpose(grad_one.reshape(3, 3, channels, channels), (2, 0, 1, 3))
    return (input_grad, grad_one, grad_two)


def solution(mesh):
    in_specs = (
        P("grp", "row", ("col", "pair")),
        P(),
        P("row", None, None, None),
        P(("grp", "row"), ("col", "pair"), None),
    )
    out_specs = (
        P("grp", "row", ("col", "pair")),
        P("grp", None, None, None),
        P(("grp", "row"), None, None, None),
    )
    return jax.shard_map(local, mesh=mesh, in_specs=in_specs, out_specs=out_specs, check_vma=False)
```

```python
import functools
import math

import jax
import jax.numpy as jnp
from jax import lax
from jax.experimental import pallas as pl
from jax.experimental.pallas import tpu as pltpu
from jax.sharding import PartitionSpec as P

BF16 = jnp.bfloat16
F32 = jnp.float32
COLS = ("col", "pair")
REACH = 3
PITCH = 48
SENT = 40


def dot(a, b, contract):
    return lax.dot_general(a, b, ((contract[:1], contract[1:]), ((), ())), preferred_element_type=F32)


def whole_call(body, outs, operands, flops, scalars=1, scratch=(), after=0, held=0):
    specs = [
        pl.BlockSpec(memory_space=pltpu.SMEM if n < scalars else pltpu.HBM if n < scalars + held else pltpu.VMEM)
        for n in range(len(operands) - after)
    ] + [pl.BlockSpec(memory_space=pl.ANY)] * after
    sizes = [math.prod(a.shape) * a.dtype.itemsize for a in tuple(operands[scalars:]) + tuple(outs)]
    moved = sum(sizes) if flops else 0
    return pl.pallas_call(
        body,
        out_shape=outs,
        in_specs=specs,
        out_specs=[pl.BlockSpec(memory_space=pltpu.VMEM) for _ in outs],
        scratch_shapes=list(scratch),
        cost_estimate=pl.CostEstimate(flops=flops, bytes_accessed=moved, transcendentals=0),
        compiler_params=pltpu.CompilerParams(vmem_limit_bytes=40 * 1024 * 1024),
    )(*operands)


def shaped(shape, dtype=BF16):
    return jax.ShapeDtypeStruct(shape, dtype)


def roll(values, amount, axis):
    return pltpu.roll(values, amount % values.shape[axis], axis)


def sigmoid(values):
    return 1.0 / (1.0 + jnp.exp(-values))


def slope_of(values, sig):
    return sig * (1.0 + values * (1.0 - sig))


def pool_matrix(strip, total, back=False):
    row = lax.broadcasted_iota(jnp.int32, (2 * PITCH, 256), 0)
    lane = lax.broadcasted_iota(jnp.int32, (2 * PITCH, 256), 1)
    half = (row >= PITCH).astype(jnp.int32)
    n = row - half * PITCH
    if back:
        v, most = jnp.where((n == 32) & (half == 1), -1, n), 33
    else:
        v, most = n - REACH, 32 + 2 * REACH
    near = jnp.bitwise_and(lane - 4 * v - 2 * half, 255) < 2
    place = strip * 32 + v
    keep = near & (n < most) & (place >= 0) & (place < total)
    return jnp.where(keep, 0.25, 0.0).astype(BF16)


def order_matrix():
    row = lax.broadcasted_iota(jnp.int32, (256, 256), 0)
    lane = lax.broadcasted_iota(jnp.int32, (256, 256), 1)
    j, i, c = row >> 7, (row >> 6) & 1, row & 63
    return jnp.where(lane == 4 * c + 2 * i + j, 1.0, 0.0).astype(BF16)


def matrices(info, _, pool_ref, back_ref, order_ref, *, total):
    pool_ref[...] = pool_matrix(info[0], total)
    back_ref[...] = pool_matrix(info[0], total, back=True)
    order_ref[...] = order_matrix()


def split_rows(
    info, x_hbm, w_hbm, og_hbm, rows_ref, a_ref, b_ref, joined_ref, head_ref, tail_ref, x_ref, w_ref, sems
):
    edge = head_ref.shape[0]
    copies = [
        pltpu.make_async_copy(source, target, sems.at[n])
        for n, (source, target) in enumerate(
            [
                (x_hbm, x_ref),
                (w_hbm, w_ref),
                (og_hbm.at[pl.ds(0, edge)], head_ref),
                (og_hbm.at[pl.ds(og_hbm.shape[0] - edge, edge)], tail_ref),
            ]
        )
    ]
    for copy in copies:
        copy.start()
    copies[0].wait()
    even = (info[2] & 1) == 0
    rows = jnp.swapaxes(x_ref[...].astype(F32), 0, 1)
    rows_ref[...] = rows.astype(BF16)
    first, last = rows[0], rows[-1]
    a_ref[...] = jnp.where(even, last, first).astype(BF16)
    b_ref[...] = jnp.where(even, first, last).astype(BF16)
    for copy in copies[1:]:
        copy.wait()
    joined_ref[...] = jnp.concatenate([w_ref[0], w_ref[1], w_ref[2]], axis=1)


def beside(a_ref, b_ref, place, count):
    even = (place & 1) == 0
    a = a_ref[...].astype(F32)
    b = jnp.where((place > 0) & (place < count - 1), b_ref[...].astype(F32), 0.0)
    return jnp.where(even, b, a).astype(BF16), jnp.where(even, a, b).astype(BF16)


def pack_sides(
    info, x_ref, up_a_ref, up_b_ref, head_ref, tail_ref, a_ref, b_ref, above_ref, below_ref, *, bands
):
    even = (info[0] & 1) == 0
    above_ref[...], below_ref[...] = beside(up_a_ref, up_b_ref, info[2], bands)
    rows = [above_ref[...]] + [x_ref[h] for h in range(x_ref.shape[0])] + [below_ref[...]]
    slot = lax.broadcasted_iota(jnp.int32, (64, 128), 1) >> 4
    blank = jnp.zeros((64, 128), F32)
    heads, tails = [blank, blank], [blank, blank]
    for r, row in enumerate(rows):
        turned = roll(row.astype(F32), 16 * (r % 8), 1)
        heads[r // 8] = jnp.where(slot == r % 8, turned, heads[r // 8])
        tails[r // 8] = jnp.where(slot == (r - 1) % 8, turned, tails[r // 8])
    for t in range(2):
        a_ref[64 * t : 64 * t + 64] = jnp.where(even, tails[t], heads[t]).astype(BF16)
        b_ref[64 * t : 64 * t + 64] = jnp.where(even, heads[t], tails[t]).astype(BF16)
    first, last = head_ref[...].astype(F32), tail_ref[...].astype(F32)
    a_ref[128:] = jnp.where(even, last, first).astype(BF16)
    b_ref[128:] = jnp.where(even, first, last).astype(BF16)


def layer_one(
    info,
    x_ref,
    above_ref,
    below_ref,
    a_ref,
    b_ref,
    w_ref,
    pool_ref,
    order_ref,
    pooled_ref,
    slope_ref,
    wide_ref,
    *,
    strips,
):
    strip = info[0]
    band_rows = x_ref.shape[0]
    slot = lax.broadcasted_iota(jnp.int32, (128, 128), 1) >> 4
    inner = (strip > 0) & (strip < strips - 1)
    sides = a_ref[:128].astype(F32), jnp.where(inner, b_ref[:128].astype(F32), 0.0)
    from_a = ((slot ^ strip) & 1) == 0
    packed = jnp.where(from_a, *sides), jnp.where(from_a, *sides[::-1])
    for r in range(band_rows + 2):
        tile = 64 * (r // 8)
        wide_ref[r, :, 128:] = roll(packed[r % 2][tile : tile + 64], -16 * (r % 8), 1).astype(BF16)
    wide_ref[0, :, :128] = above_ref[...]
    wide_ref[1 : band_rows + 1, :, :128] = x_ref[...]
    wide_ref[band_rows + 1, :, :128] = below_ref[...]
    weights = w_ref[...]
    rows = slope_ref.shape[0]
    halves, held = [], None
    for h in range(rows):
        y = dot(weights, wide_ref[h : h + 3].reshape(192, 256), (1, 0))
        pre = roll(y[:64], 1, 1) + y[64:128] + roll(y[128:], -1, 1)
        sig = sigmoid(pre)
        slope_ref[h] = slope_of(pre, sig).astype(BF16)
        active = pre * sig
        if h % 2:
            halves.append((held + active).astype(BF16))
        else:
            held = active
    pooled = dot(pool_ref[...], jnp.concatenate(halves, 0), (1, 1))
    stacked = jnp.concatenate(
        [
            jnp.concatenate(
                [pooled[:PITCH, u * 128 : u * 128 + 128], pooled[PITCH:, u * 128 : u * 128 + 128]], 1
            )
            for u in range(2)
        ],
        0,
    ).astype(BF16)
    ordered = dot(stacked, order_ref[...], (1, 0)).astype(BF16)
    for u in range(2):
        pooled_ref[u] = ordered[u * PITCH : u * PITCH + SENT]


def layer_two(info, og_ref, w_ref, *refs, bands):
    pieces, refs = refs[:bands], refs[bands:]
    terms, refs = refs[:bands], refs[bands:]
    map_ref, grad_ref, pack_ref = refs
    band = info[2]
    rows, _, filters = og_ref.shape
    count = rows * PITCH
    map_ref[0] = jnp.zeros((PITCH, 256), BF16)
    map_ref[rows + 1] = jnp.zeros((PITCH, 256), BF16)
    blank = jnp.zeros((PITCH - SENT, 256), BF16)
    for k in range(bands):
        for t in range(2):
            map_ref[1 + 2 * (band ^ k) + t] = jnp.concatenate([pieces[k][t], blank], 0)
    y = None
    for i in range(3):
        part = dot(map_ref[i : i + rows].reshape(count, 256), w_ref[i], (1, 1))
        y = part if y is None else y + part
    pre = roll(y[:, :filters], 1, 0) + y[:, filters : 2 * filters] + roll(y[:, 2 * filters :], -1, 0)
    grad = og_ref[...].reshape(count, filters).astype(F32) * slope_of(pre, sigmoid(pre))
    grad = grad.astype(BF16)
    grad_ref[0] = jnp.zeros((PITCH, filters), BF16)
    grad_ref[rows + 1] = jnp.zeros((PITCH, filters), BF16)
    grad_ref[1 : rows + 1] = grad.reshape(rows, PITCH, filters)
    z = None
    for i in range(3):
        weights = jnp.concatenate([w_ref[i, j * filters : (j + 1) * filters] for j in range(3)], 1)
        part = dot(grad_ref[2 - i : 2 - i + rows].reshape(count, filters), weights, (1, 0))
        z = part if z is None else z + part
    spread = roll(z[:, :256], -1 - REACH, 0) + roll(z[:, 256:512], -REACH, 0) + roll(z[:, 512:], 1 - REACH, 0)
    spread = spread.reshape(rows, PITCH, 256)
    odd = (lax.broadcasted_iota(jnp.int32, (8, 256), 1) & 1) == 1
    row = lax.broadcasted_iota(jnp.int32, (8, 256), 0)
    ends = [jnp.where(odd, spread[u - 1, 47:48], spread[u, 32:33]) for u in range(rows)]
    for p in range(rows // 2):
        shared = jnp.where(row == 0, ends[2 * p], jnp.where(row == 1, ends[2 * p + 1], 0.0))
        pack_ref[p] = jnp.concatenate([spread[2 * p, :32], shared, spread[2 * p + 1, :32]], 0).astype(BF16)
    for k in range(bands):
        terms[k][...] = pack_ref[band ^ k]


def filter_two_grads(info, map_ref, grad_ref, _, keep_ref, send_ref, all_ref):
    pair = info[1]
    rows = map_ref.shape[0] - 2
    filters = grad_ref.shape[2]
    v = lax.broadcasted_iota(jnp.int32, (rows, PITCH, filters), 1)
    own = (v >= REACH) & (v < REACH + 32)
    wide = jnp.where(own, grad_ref[1 : rows + 1].astype(F32), 0.0).reshape(rows * PITCH, filters)
    cat = jnp.concatenate([roll(wide, -1, 0), wide, roll(wide, 1, 0)], 1).astype(BF16)
    taps = 3 * filters
    for i in range(3):
        part = dot(cat, map_ref[i : i + rows].reshape(rows * PITCH, 256), (0, 0))
        all_ref[i * taps : (i + 1) * taps] = part.astype(BF16)
    half = keep_ref.shape[0]
    keep_ref[...] = all_ref[pl.ds(pl.multiple_of(pair * half, 16), half)]
    send_ref[...] = all_ref[pl.ds(pl.multiple_of((1 - pair) * half, 16), half)]


def add_after(a_ref, b_ref, *refs):
    refs[-1][...] = (a_ref[...].astype(F32) + b_ref[...].astype(F32)).astype(BF16)


def add_and_pass(a_ref, b_ref, other_ref, out_ref, passed_ref):
    out_ref[...] = (a_ref[...].astype(F32) + b_ref[...].astype(F32)).astype(BF16)
    passed_ref[...] = other_ref[...]


def sum_rows(*refs):
    *terms, _, out_ref = refs
    terms = [t[...].astype(F32) for t in terms]
    while len(terms) > 1:
        terms = [a + b for a, b in zip(terms[::2], terms[1::2])]
    out_ref[...] = terms[0].astype(BF16)


def grad_pre_one(info, *refs, bands):
    terms, refs = refs[:bands], refs[bands:]
    slope_ref, wide_ref, pool_ref, order_ref, g_ref, a_ref, b_ref, keep_ref, send_ref, part_ref = refs
    pair = info[1]
    summed = terms[0][...].astype(F32)
    for k in range(1, bands):
        summed = summed + terms[k][...].astype(F32)
    blank = jnp.zeros((8, 256), F32)
    ends = summed[32:40]
    blocks = [summed[:32], ends, blank, summed[40:], roll(ends, -1, 0), blank]
    ordered = dot(jnp.concatenate(blocks, 0).astype(BF16), order_ref[...], (1, 1)).astype(BF16)
    pool = pool_ref[...]
    acc = None
    own = lax.broadcasted_iota(jnp.int32, (64, 256), 1) < 128
    for u in range(2):
        block = ordered[u * PITCH : (u + 1) * PITCH]
        up = dot(jnp.concatenate([block[:, :128], block[:, 128:]], 0), pool, (0, 0))
        for i in range(4):
            h = 4 * u + i
            g = (up[64 * (i // 2) : 64 * (i // 2) + 64] * slope_ref[h].astype(F32)).astype(BF16)
            g_ref[h] = g
            mine = jnp.where(own, g.astype(F32), 0.0)
            cat = jnp.concatenate([roll(mine, -1, 1), mine, roll(mine, 1, 1)], 0).astype(BF16)
            part = dot(cat, wide_ref[h : h + 3].reshape(192, 256), (1, 1))
            acc = part if acc is None else acc + part
    even = (info[2] & 1) == 0
    first, last = g_ref[0].astype(F32), g_ref[7].astype(F32)
    a_ref[...] = jnp.where(even, last, first).astype(BF16)
    b_ref[...] = jnp.where(even, first, last).astype(BF16)
    part_ref[:192] = acc[:, :128].astype(BF16)
    tail = jnp.concatenate([acc[:96, 128:], acc[96:, 128:]], 1)
    part_ref[192:] = tail.astype(BF16)
    half = keep_ref.shape[0]
    keep_ref[...] = part_ref[pl.ds(pl.multiple_of(pair * half, 16), half)]
    send_ref[...] = part_ref[pl.ds(pl.multiple_of((1 - pair) * half, 16), half)]


def layer_one_back(info, g_ref, a_ref, b_ref, w_ref, out_ref, done_ref, *, bands):
    above, below = beside(a_ref, b_ref, info[2], bands)
    done_ref[...] = jnp.zeros(done_ref.shape, F32)
    lines = [above] + [g_ref[h] for h in range(8)] + [below]
    rows = []
    for h in range(8):
        z = dot(w_ref[...], jnp.concatenate(lines[h : h + 3], 0), (1, 0))
        rows.append((roll(z[:64], -1, 1) + z[64:128] + roll(z[128:], 1, 1))[:, :128])
    out_ref[...] = jnp.swapaxes(jnp.stack(rows, 0), 0, 1).astype(BF16)


def unpack_one(info, mine_ref, other_ref, _, out_ref, flat_ref, *, scale):
    pair, half = info[1], mine_ref.shape[0]
    flat_ref[pl.ds(pl.multiple_of(pair * half, 16), half)] = mine_ref[...]
    flat_ref[pl.ds(pl.multiple_of((1 - pair) * half, 16), half)] = other_ref[...]
    flat = flat_ref[...].astype(F32) * scale
    out_ref[0] = flat[:192, :64]
    out_ref[1] = flat[:192, 64:]
    out_ref[2, :96] = flat[192:, :64]
    out_ref[2, 96:] = flat[192:, 64:]


def even_swap(values, axis, count):
    return lax.ppermute(values, axis, [(n, n ^ 1) for n in range(count)])


def odd_swap(values, axis, count):
    return lax.ppermute(values, axis, [(n, (n - 1 if n % 2 == 0 else n + 1) % count) for n in range(count)])


def xor_swap(values, axis, count, k):
    return lax.ppermute(values, axis, [(n, n ^ k) for n in range(count)])


def row_swaps(values, bands):
    order = sorted(range(1, bands), key=lambda k: (k < bands // 2, k))
    moved = {k: xor_swap(values[k], "row", bands, k) for k in order}
    return [moved[k] for k in range(1, bands)]


def added(a, b, *after):
    (total,) = whole_call(add_after, [shaped(a.shape)], [a, b, *after], 0, scalars=0, after=len(after))
    return total


def sum_cols(part, after=()):
    count, step = lax.axis_size("col"), 1
    while step < count:
        other = xor_swap(part, "col", count, step)
        step *= 2
        if after and step >= count:
            part = added(part, other, *after)
        else:
            part = (part.astype(F32) + other.astype(F32)).astype(BF16)
    return part


def local(features_in, filters_one, filters_two, out_grad):
    channels, band_rows, strip_cols = features_in.shape
    filters, own_cols, pooled_rows = out_grad.shape
    bands = lax.axis_size("row")
    strips = lax.axis_size(COLS)
    band = lax.axis_index("row")
    strip = lax.axis_index(COLS)
    pair = lax.axis_index("pair")
    height, width = band_rows * bands, strip_cols * strips
    total = own_cols * strips
    at_place = jnp.stack([strip, pair, band]).astype(jnp.int32)

    taps_one = jnp.transpose(filters_one, (1, 2, 0, 3)).reshape(3, 3 * channels, channels)
    back_one = jnp.transpose(filters_one[:, ::-1], (2, 3, 1, 0)).reshape(3 * channels, 3 * channels)
    taps_two = jnp.transpose(filters_two, (1, 2, 0, 3)).reshape(3, 3 * filters, 4 * channels)

    og = jnp.transpose(out_grad, (1, 2, 0))
    edge = REACH - 1
    x, to_a, to_b, joined_one, head, tail = whole_call(
        split_rows,
        [shaped((band_rows, channels, strip_cols))]
        + [shaped((channels, strip_cols))] * 2
        + [shaped((3 * channels, 3 * channels))]
        + [shaped((edge, pooled_rows, filters))] * 2,
        [at_place, features_in, taps_one, og],
        1,
        scratch=[
            pltpu.VMEM(features_in.shape, BF16),
            pltpu.VMEM(taps_one.shape, BF16),
            pltpu.SemaphoreType.DMA((4,)),
        ],
        held=3,
    )
    pool, pool_back, order = whole_call(
        functools.partial(matrices, total=total),
        [shaped((2 * PITCH, 256))] * 2 + [shaped((256, 256))],
        [at_place, to_a],
        10**8,
        after=1,
    )
    up_a, up_b = even_swap(to_a, "row", bands), odd_swap(to_b, "row", bands)
    head, tail = head.reshape(-1, 128), tail.reshape(-1, 128)
    to_a, to_b, above, below = whole_call(
        functools.partial(pack_sides, bands=bands),
        [shaped((2 * channels + head.shape[0], 128))] * 2 + [shaped((channels, strip_cols))] * 2,
        [at_place, x, up_a, up_b, head, tail],
        1,
    )
    side_a, side_b = even_swap(to_a, COLS, strips), odd_swap(to_b, COLS, strips)
    pooled, slope, wide = whole_call(
        functools.partial(layer_one, strips=strips),
        [
            shaped((2, SENT, 4 * channels)),
            shaped((band_rows, channels, 256)),
            shaped((band_rows + 2, channels, 256)),
        ],
        [at_place, x, above, below, side_a, side_b, joined_one, pool, order],
        2 * band_rows * 192 * 192 * 256,
    )
    pieces = [pooled] + row_swaps([pooled] * bands, bands)

    even = strip % 2 == 0
    ends = [side[2 * channels :].reshape(og[:edge].shape) for side in (side_a, side_b)]
    ends[1] = jnp.where((strip == 0) | (strip == strips - 1), 0, ends[1])
    before, after = jnp.where(even, ends[1], ends[0]), jnp.where(even, ends[0], ends[1])
    og = jnp.concatenate([before, og, after], 0)
    og = jnp.pad(og, ((1, PITCH - own_cols - 2 * REACH + 1), (0, 0), (0, 0)))
    og = jnp.transpose(og, (1, 0, 2))

    count = pooled_rows * PITCH
    *terms, pooled_map, grad_map = whole_call(
        functools.partial(layer_two, bands=bands),
        [shaped((72, 4 * channels))] * bands
        + [shaped((pooled_rows + 2, PITCH, 4 * channels)), shaped((pooled_rows + 2, PITCH, filters))],
        [at_place, og, taps_two] + pieces,
        4 * count * 9 * filters * 4 * channels,
        scratch=[pltpu.VMEM((bands, 72, 4 * channels), BF16)],
    )
    received = [terms[0]] + row_swaps(terms, bands)

    share = 9 * channels * channels // 256
    g, up_a, up_b, keep, send = whole_call(
        functools.partial(grad_pre_one, bands=bands),
        [shaped((band_rows, channels, 256))]
        + [shaped((channels, 256))] * 2
        + [shaped((share, 128))] * 2,
        [at_place] + received + [slope, wide, pool_back, order],
        2 * 8 * 192 * 192 * 256,
        scratch=[pltpu.VMEM((2 * share, 128), BF16)],
    )
    half = 9 * filters // 2
    keep_two, send_two = whole_call(
        filter_two_grads,
        [shaped((half, 4 * channels))] * 2,
        [at_place, pooled_map, grad_map, keep],
        0,
        scratch=[pltpu.VMEM((2 * half, 4 * channels), BF16)],
        after=1,
    )
    part = sum_cols(added(keep, even_swap(send, "pair", 2)))
    part_two, part = whole_call(
        add_and_pass,
        [shaped(keep_two.shape), shaped(part.shape)],
        [keep_two, even_swap(send_two, "pair", 2), part],
        0,
        scalars=0,
    )
    terms = [part] + row_swaps([part] * bands, bands)
    input_grad, done = whole_call(
        functools.partial(layer_one_back, bands=bands),
        [shaped(features_in.shape), shaped((8, 128), F32)],
        [at_place, g, even_swap(up_a, "row", bands), odd_swap(up_b, "row", bands), back_one],
        2 * band_rows * 192 * 192 * 256,
    )
    (mine,) = whole_call(sum_rows, [shaped(part.shape)], terms + [done], 0, scalars=0, after=1)
    other = even_swap(mine, "pair", 2)
    mine_two = sum_cols(part_two, after=(mine,))
    other_two = even_swap(mine_two, "pair", 2)
    first, second = jnp.where(pair == 0, mine_two, other_two), jnp.where(pair == 0, other_two, mine_two)
    grad_two = jnp.concatenate([first, second], 0)
    grad_two = grad_two.astype(F32) * (1.0 / math.sqrt(pooled_rows * total))
    grad_two = jnp.transpose(grad_two.reshape(3, 3, filters, 4 * channels), (2, 0, 1, 3))
    (grad_one,) = whole_call(
        functools.partial(unpack_one, scale=1.0 / math.sqrt(height * width)),
        [shaped((3, 3 * channels, channels), F32)],
        [at_place, mine, other, other_two],
        1,
        scratch=[pltpu.VMEM((2 * share, 128), BF16)],
        after=1,
    )
    grad_one = jnp.transpose(grad_one.reshape(3, 3, channels, channels), (2, 0, 1, 3))
    return (input_grad, grad_one, grad_two)


def solution(mesh):
    in_specs = (
        P("grp", "row", ("col", "pair")),
        P(),
        P("row", None, None, None),
        P(("grp", "row"), ("col", "pair"), None),
    )
    out_specs = (
        P("grp", "row", ("col", "pair")),
        P("grp", None, None, None),
        P(("grp", "row"), None, None, None),
    )
    return jax.shard_map(local, mesh=mesh, in_specs=in_specs, out_specs=out_specs, check_vma=False)
```

```python
import functools
import math

import jax
import jax.numpy as jnp
from jax import lax
from jax.experimental import pallas as pl
from jax.experimental.pallas import tpu as pltpu
from jax.sharding import PartitionSpec as P

BF16 = jnp.bfloat16
F32 = jnp.float32
COLS = ("col", "pair")
REACH = 3
TAIL = 80
PITCH = 48
SENT = 40


def dot(a, b, contract):
    return lax.dot_general(a, b, ((contract[:1], contract[1:]), ((), ())), preferred_element_type=F32)


def whole_call(body, outs, operands, flops, scalars=1, scratch=(), after=0, out_space=pltpu.VMEM):
    specs = [
        pl.BlockSpec(memory_space=pltpu.SMEM if n < scalars else pltpu.VMEM)
        for n in range(len(operands) - after)
    ] + [pl.BlockSpec(memory_space=pl.ANY)] * after
    sizes = [math.prod(a.shape) * a.dtype.itemsize for a in tuple(operands[scalars:]) + tuple(outs)]
    moved = sum(sizes) if flops else 0
    return pl.pallas_call(
        body,
        out_shape=outs,
        in_specs=specs,
        out_specs=[pl.BlockSpec(memory_space=out_space) for _ in outs],
        scratch_shapes=list(scratch),
        cost_estimate=pl.CostEstimate(flops=flops, bytes_accessed=moved, transcendentals=0),
        compiler_params=pltpu.CompilerParams(vmem_limit_bytes=40 * 1024 * 1024),
    )(*operands)


def shaped(shape, dtype=BF16):
    return jax.ShapeDtypeStruct(shape, dtype)


def roll(values, amount, axis):
    return pltpu.roll(values, amount % values.shape[axis], axis)


def sigmoid(values):
    return 1.0 / (1.0 + jnp.exp(-values))


def slope_of(values, sig):
    return sig * (1.0 + values * (1.0 - sig))


def pool_matrix(strip, total, back=False):
    row = lax.broadcasted_iota(jnp.int32, (2 * PITCH, 256), 0)
    lane = lax.broadcasted_iota(jnp.int32, (2 * PITCH, 256), 1)
    half = (row >= PITCH).astype(jnp.int32)
    n = row - half * PITCH
    if back:
        v, most = jnp.where((n == 32) & (half == 1), -1, n), 33
    else:
        v, most = n - REACH, 32 + 2 * REACH
    near = jnp.bitwise_and(lane - 4 * v - 2 * half, 255) < 2
    place = strip * 32 + v
    keep = near & (n < most) & (place >= 0) & (place < total)
    return jnp.where(keep, 0.25, 0.0).astype(BF16)


def order_matrix():
    row = lax.broadcasted_iota(jnp.int32, (256, 256), 0)
    lane = lax.broadcasted_iota(jnp.int32, (256, 256), 1)
    j, i, c = row >> 7, (row >> 6) & 1, row & 63
    return jnp.where(lane == 4 * c + 2 * i + j, 1.0, 0.0).astype(BF16)


def constants(info, w_ref, joined_ref, pool_ref, back_ref, order_ref, *, total):
    joined_ref[...] = jnp.concatenate([w_ref[0], w_ref[1], w_ref[2]], axis=1)
    pool_ref[...] = pool_matrix(info[0], total)
    back_ref[...] = pool_matrix(info[0], total, back=True)
    order_ref[...] = order_matrix()


def beside(a_ref, b_ref, place, count):
    even = (place & 1) == 0
    a = a_ref[...].astype(F32)
    b = jnp.where((place > 0) & (place < count - 1), b_ref[...].astype(F32), 0.0)
    return jnp.where(even, b, a).astype(BF16), jnp.where(even, a, b).astype(BF16)


def pack_sides(
    info, x_ref, up_a_ref, up_b_ref, head_ref, tail_ref, a_ref, b_ref, above_ref, below_ref, *, bands
):
    even = (info[0] & 1) == 0
    above_ref[...], below_ref[...] = beside(up_a_ref, up_b_ref, info[2], bands)
    rows = [above_ref[...]] + [x_ref[h] for h in range(x_ref.shape[0])] + [below_ref[...]]
    slot = lax.broadcasted_iota(jnp.int32, (64, 128), 1) >> 4
    blank = jnp.zeros((64, 128), F32)
    heads, tails = [blank, blank], [blank, blank]
    for r, row in enumerate(rows):
        turned = roll(row.astype(F32), 16 * (r % 8), 1)
        heads[r // 8] = jnp.where(slot == r % 8, turned, heads[r // 8])
        tails[r // 8] = jnp.where(slot == (r - 1) % 8, turned, tails[r // 8])
    for t in range(2):
        a_ref[64 * t : 64 * t + 64] = jnp.where(even, tails[t], heads[t]).astype(BF16)
        b_ref[64 * t : 64 * t + 64] = jnp.where(even, heads[t], tails[t]).astype(BF16)
    first, last = head_ref[...].astype(F32), tail_ref[...].astype(F32)
    a_ref[128:] = jnp.where(even, last, first).astype(BF16)
    b_ref[128:] = jnp.where(even, first, last).astype(BF16)


def layer_one(
    info,
    x_ref,
    above_ref,
    below_ref,
    a_ref,
    b_ref,
    w_ref,
    pool_ref,
    order_ref,
    pooled_ref,
    slope_ref,
    wide_ref,
    *,
    strips,
):
    strip = info[0]
    band_rows = x_ref.shape[0]
    slot = lax.broadcasted_iota(jnp.int32, (128, 128), 1) >> 4
    inner = (strip > 0) & (strip < strips - 1)
    sides = a_ref[:128].astype(F32), jnp.where(inner, b_ref[:128].astype(F32), 0.0)
    from_a = ((slot ^ strip) & 1) == 0
    packed = jnp.where(from_a, *sides), jnp.where(from_a, *sides[::-1])
    for r in range(band_rows + 2):
        tile = 64 * (r // 8)
        wide_ref[r, :, 128:] = roll(packed[r % 2][tile : tile + 64], -16 * (r % 8), 1).astype(BF16)
    wide_ref[0, :, :128] = above_ref[...]
    wide_ref[1 : band_rows + 1, :, :128] = x_ref[...]
    wide_ref[band_rows + 1, :, :128] = below_ref[...]
    weights = w_ref[...]
    rows = slope_ref.shape[0]
    halves, held = [], None
    for h in range(rows):
        y = dot(weights, wide_ref[h : h + 3].reshape(192, 256), (1, 0))
        pre = roll(y[:64], 1, 1) + y[64:128] + roll(y[128:], -1, 1)
        sig = sigmoid(pre)
        slope_ref[h] = slope_of(pre, sig).astype(BF16)
        active = pre * sig
        if h % 2:
            halves.append((held + active).astype(BF16))
        else:
            held = active
    pooled = dot(pool_ref[...], jnp.concatenate(halves, 0), (1, 1))
    stacked = jnp.concatenate(
        [
            jnp.concatenate(
                [pooled[:PITCH, u * 128 : u * 128 + 128], pooled[PITCH:, u * 128 : u * 128 + 128]], 1
            )
            for u in range(2)
        ],
        0,
    ).astype(BF16)
    ordered = dot(stacked, order_ref[...], (1, 0)).astype(BF16)
    for u in range(2):
        pooled_ref[u] = ordered[u * PITCH : u * PITCH + SENT]


def layer_two(info, og_ref, w_ref, *refs, bands):
    pieces, refs = refs[:bands], refs[bands:]
    terms, refs = refs[:bands], refs[bands:]
    map_ref, grad_ref, pack_ref = refs
    band = info[2]
    rows, _, filters = og_ref.shape
    count = rows * PITCH
    map_ref[0] = jnp.zeros((PITCH, 256), BF16)
    map_ref[rows + 1] = jnp.zeros((PITCH, 256), BF16)
    blank = jnp.zeros((PITCH - SENT, 256), BF16)
    for k in range(bands):
        for t in range(2):
            map_ref[1 + 2 * (band ^ k) + t] = jnp.concatenate([pieces[k][t], blank], 0)
    y = None
    for i in range(3):
        part = dot(map_ref[i : i + rows].reshape(count, 256), w_ref[i], (1, 1))
        y = part if y is None else y + part
    pre = roll(y[:, :filters], 1, 0) + y[:, filters : 2 * filters] + roll(y[:, 2 * filters :], -1, 0)
    grad = og_ref[...].reshape(count, filters).astype(F32) * slope_of(pre, sigmoid(pre))
    grad = grad.astype(BF16)
    grad_ref[0] = jnp.zeros((PITCH, filters), BF16)
    grad_ref[rows + 1] = jnp.zeros((PITCH, filters), BF16)
    grad_ref[1 : rows + 1] = grad.reshape(rows, PITCH, filters)
    z = None
    for i in range(3):
        weights = jnp.concatenate([w_ref[i, j * filters : (j + 1) * filters] for j in range(3)], 1)
        part = dot(grad_ref[2 - i : 2 - i + rows].reshape(count, filters), weights, (1, 0))
        z = part if z is None else z + part
    spread = roll(z[:, :256], -1 - REACH, 0) + roll(z[:, 256:512], -REACH, 0) + roll(z[:, 512:], 1 - REACH, 0)
    spread = spread.reshape(rows, PITCH, 256)
    odd = (lax.broadcasted_iota(jnp.int32, (8, 256), 1) & 1) == 1
    row = lax.broadcasted_iota(jnp.int32, (8, 256), 0)
    ends = [jnp.where(odd, spread[u - 1, 47:48], spread[u, 32:33]) for u in range(rows)]
    for p in range(rows // 2):
        shared = jnp.where(row == 0, ends[2 * p], jnp.where(row == 1, ends[2 * p + 1], 0.0))
        pack_ref[p] = jnp.concatenate([spread[2 * p, :32], shared, spread[2 * p + 1, :32]], 0).astype(BF16)
    for k in range(bands):
        terms[k][...] = pack_ref[band ^ k]


def filter_two_grads(info, map_ref, grad_ref, keep_ref, send_ref, all_ref):
    pair = info[1]
    rows = map_ref.shape[0] - 2
    filters = grad_ref.shape[2]
    v = lax.broadcasted_iota(jnp.int32, (rows, PITCH, filters), 1)
    own = (v >= REACH) & (v < REACH + 32)
    wide = jnp.where(own, grad_ref[1 : rows + 1].astype(F32), 0.0).reshape(rows * PITCH, filters)
    cat = jnp.concatenate([roll(wide, -1, 0), wide, roll(wide, 1, 0)], 1).astype(BF16)
    taps = 3 * filters
    for i in range(3):
        part = dot(cat, map_ref[i : i + rows].reshape(rows * PITCH, 256), (0, 0))
        all_ref[i * taps : (i + 1) * taps] = part.astype(BF16)
    half = keep_ref.shape[0]
    keep_ref[...] = all_ref[pl.ds(pl.multiple_of(pair * half, 16), half)]
    send_ref[...] = all_ref[pl.ds(pl.multiple_of((1 - pair) * half, 16), half)]


def add_after(a_ref, b_ref, *refs):
    refs[-1][...] = (a_ref[...].astype(F32) + b_ref[...].astype(F32)).astype(BF16)


def add_halves(a_ref, b_ref, two_ref, one_ref):
    half = two_ref.shape[0]
    total = (a_ref[...].astype(F32) + b_ref[...].astype(F32)).astype(BF16)
    two_ref[...] = total[:half]
    one_ref[...] = total[half:]


def add_joined(a_ref, b_ref, c_ref, d_ref, out_ref):
    half = a_ref.shape[0]
    out_ref[:half] = (a_ref[...].astype(F32) + b_ref[...].astype(F32)).astype(BF16)
    out_ref[half:] = (c_ref[...].astype(F32) + d_ref[...].astype(F32)).astype(BF16)


def grad_pre_one(info, *refs, bands):
    terms, refs = refs[:bands], refs[bands:]
    slope_ref, wide_ref, pool_ref, order_ref, keep_two_ref, send_two_ref, *refs = refs
    g_ref, a_ref, b_ref, keep_ref, send_ref, part_ref = refs
    pair = info[1]
    summed = terms[0][...].astype(F32)
    for k in range(1, bands):
        summed = summed + terms[k][...].astype(F32)
    blank = jnp.zeros((8, 256), F32)
    ends = summed[32:40]
    blocks = [summed[:32], ends, blank, summed[40:], roll(ends, -1, 0), blank]
    ordered = dot(jnp.concatenate(blocks, 0).astype(BF16), order_ref[...], (1, 1)).astype(BF16)
    pool = pool_ref[...]
    acc = None
    own = lax.broadcasted_iota(jnp.int32, (64, 256), 1) < 128
    for u in range(2):
        block = ordered[u * PITCH : (u + 1) * PITCH]
        up = dot(jnp.concatenate([block[:, :128], block[:, 128:]], 0), pool, (0, 0))
        for i in range(4):
            h = 4 * u + i
            g = (up[64 * (i // 2) : 64 * (i // 2) + 64] * slope_ref[h].astype(F32)).astype(BF16)
            g_ref[h] = g
            mine = jnp.where(own, g.astype(F32), 0.0)
            cat = jnp.concatenate([roll(mine, -1, 1), mine, roll(mine, 1, 1)], 0).astype(BF16)
            part = dot(cat, wide_ref[h : h + 3].reshape(192, 256), (1, 1))
            acc = part if acc is None else acc + part
    even = (info[2] & 1) == 0
    first, last = g_ref[0].astype(F32), g_ref[7].astype(F32)
    a_ref[...] = jnp.where(even, last, first).astype(BF16)
    b_ref[...] = jnp.where(even, first, last).astype(BF16)
    part_ref[:96] = jnp.concatenate([acc[:96, :128], acc[96:, :128]], 1)
    part_ref[96:] = jnp.concatenate([acc[48 * q : 48 * q + 48, 128:] for q in range(4)], 1)
    half = keep_two_ref.shape[0]
    blank = jnp.zeros((TAIL - 72, 256), F32)
    for ref, two_ref, place in ((keep_ref, keep_two_ref, pair), (send_ref, send_two_ref, 1 - pair)):
        ref[:half] = two_ref[...]
        mine = part_ref[pl.ds(pl.multiple_of(place * 72, 8), 72)]
        ref[half:] = jnp.concatenate([mine, blank], 0).astype(BF16)


def layer_one_back(info, g_ref, a_ref, b_ref, w_ref, out_ref, done_ref, *, bands):
    above, below = beside(a_ref, b_ref, info[2], bands)
    done_ref[...] = jnp.zeros(done_ref.shape, F32)
    lines = [above] + [g_ref[h] for h in range(8)] + [below]
    rows = []
    for h in range(8):
        z = dot(w_ref[...], jnp.concatenate(lines[h : h + 3], 0), (1, 0))
        rows.append((roll(z[:64], -1, 1) + z[64:128] + roll(z[128:], 1, 1))[:, :128])
    out_ref[...] = jnp.swapaxes(jnp.stack(rows, 0), 0, 1).astype(BF16)


def finish(info, mine_ref, other_ref, one_hbm, two_hbm, one_ref, two_ref, flat_ref, sems, *, scales):
    pair, half = info[1], mine_ref.shape[0] - TAIL
    copies = [pltpu.make_async_copy(one_ref, one_hbm, sems.at[0])]
    for ref, place in ((mine_ref, pair), (other_ref, 1 - pair)):
        flat_ref[pl.ds(pl.multiple_of(place * 72, 8), 72)] = ref[half : half + 72].astype(F32) * scales[0]
    one_ref[0, :96] = flat_ref[:96, :64]
    one_ref[1, :96] = flat_ref[:96, 64:128]
    one_ref[0, 96:] = flat_ref[:96, 128:192]
    one_ref[1, 96:] = flat_ref[:96, 192:]
    for q in range(4):
        one_ref[2, 48 * q : 48 * q + 48] = flat_ref[96:, 64 * q : 64 * q + 64]
    copies[0].start()
    for n, (ref, place) in enumerate(((mine_ref, pair), (other_ref, 1 - pair))):
        rows = pl.ds(pl.multiple_of(place * half, 16), half)
        two_ref[n] = ref[:half].astype(F32) * scales[1]
        copies.append(pltpu.make_async_copy(two_ref.at[n], two_hbm.at[rows], sems.at[1 + n]))
        copies[-1].start()
    for copy in copies:
        copy.wait()


def even_swap(values, axis, count):
    return lax.ppermute(values, axis, [(n, n ^ 1) for n in range(count)])


def odd_swap(values, axis, count):
    return lax.ppermute(values, axis, [(n, (n - 1 if n % 2 == 0 else n + 1) % count) for n in range(count)])


def xor_swap(values, axis, count, k):
    return lax.ppermute(values, axis, [(n, n ^ k) for n in range(count)])


def row_swaps(values, bands):
    order = sorted(range(1, bands), key=lambda k: (k < bands // 2, k))
    moved = {k: xor_swap(values[k], "row", bands, k) for k in order}
    return [moved[k] for k in range(1, bands)]


def added(a, b, *after):
    (total,) = whole_call(add_after, [shaped(a.shape)], [a, b, *after], 0, scalars=0, after=len(after))
    return total


def sum_but_last(part, axis, count):
    step = 1
    while 2 * step < count:
        part = added(part, xor_swap(part, axis, count, step))
        step *= 2
    return part, xor_swap(part, axis, count, step)


def local(features_in, filters_one, filters_two, out_grad):
    channels, band_rows, strip_cols = features_in.shape
    filters, own_cols, pooled_rows = out_grad.shape
    bands = lax.axis_size("row")
    strips = lax.axis_size(COLS)
    band = lax.axis_index("row")
    strip = lax.axis_index(COLS)
    pair = lax.axis_index("pair")
    height, width = band_rows * bands, strip_cols * strips
    total = own_cols * strips
    at_place = jnp.stack([strip, pair, band]).astype(jnp.int32)

    taps_one = jnp.transpose(filters_one, (1, 2, 0, 3)).reshape(3, 3 * channels, channels)
    back_one = jnp.transpose(filters_one[:, ::-1], (2, 3, 1, 0)).reshape(3 * channels, 3 * channels)
    taps_two = jnp.transpose(filters_two, (1, 2, 0, 3)).reshape(3, 3 * filters, 4 * channels)

    og = jnp.transpose(out_grad, (1, 2, 0))
    edge = REACH - 1
    x = jnp.transpose(features_in, (1, 0, 2))
    even = band % 2 == 0
    to_a, to_b = jnp.where(even, x[-1], x[0]), jnp.where(even, x[0], x[-1])
    head, tail = og[:edge], og[-edge:]
    joined_one, pool, pool_back, order = whole_call(
        functools.partial(constants, total=total),
        [shaped((3 * channels, 3 * channels))] + [shaped((2 * PITCH, 256))] * 2 + [shaped((256, 256))],
        [at_place, taps_one],
        10**8,
    )
    up_a, up_b = even_swap(to_a, "row", bands), odd_swap(to_b, "row", bands)
    head, tail = head.reshape(-1, 128), tail.reshape(-1, 128)
    to_a, to_b, above, below = whole_call(
        functools.partial(pack_sides, bands=bands),
        [shaped((2 * channels + head.shape[0], 128))] * 2 + [shaped((channels, strip_cols))] * 2,
        [at_place, x, up_a, up_b, head, tail],
        1,
    )
    side_a, side_b = even_swap(to_a, COLS, strips), odd_swap(to_b, COLS, strips)
    pooled, slope, wide = whole_call(
        functools.partial(layer_one, strips=strips),
        [
            shaped((2, SENT, 4 * channels)),
            shaped((band_rows, channels, 256)),
            shaped((band_rows + 2, channels, 256)),
        ],
        [at_place, x, above, below, side_a, side_b, joined_one, pool, order],
        2 * band_rows * 192 * 192 * 256,
    )
    pieces = [pooled] + row_swaps([pooled] * bands, bands)

    even = strip % 2 == 0
    ends = [side[2 * channels :].reshape(og[:edge].shape) for side in (side_a, side_b)]
    ends[1] = jnp.where((strip == 0) | (strip == strips - 1), 0, ends[1])
    before, after = jnp.where(even, ends[1], ends[0]), jnp.where(even, ends[0], ends[1])
    og = jnp.concatenate([before, og, after], 0)
    og = jnp.pad(og, ((1, PITCH - own_cols - 2 * REACH + 1), (0, 0), (0, 0)))
    og = jnp.transpose(og, (1, 0, 2))

    count = pooled_rows * PITCH
    *terms, pooled_map, grad_map = whole_call(
        functools.partial(layer_two, bands=bands),
        [shaped((72, 4 * channels))] * bands
        + [shaped((pooled_rows + 2, PITCH, 4 * channels)), shaped((pooled_rows + 2, PITCH, filters))],
        [at_place, og, taps_two] + pieces,
        4 * count * 9 * filters * 4 * channels,
        scratch=[pltpu.VMEM((bands, 72, 4 * channels), BF16)],
    )
    received = [terms[0]] + row_swaps(terms, bands)

    half = 9 * filters // 2
    keep_two, send_two = whole_call(
        filter_two_grads,
        [shaped((half, 4 * channels))] * 2,
        [at_place, pooled_map, grad_map],
        2 * count * 9 * filters * 4 * channels,
        scratch=[pltpu.VMEM((2 * half, 4 * channels), BF16)],
    )
    g, up_a, up_b, keep, send = whole_call(
        functools.partial(grad_pre_one, bands=bands),
        [shaped((band_rows, channels, 256))]
        + [shaped((channels, 256))] * 2
        + [shaped((half + TAIL, 256))] * 2,
        [at_place] + received + [slope, wide, pool_back, order, keep_two, send_two],
        2 * 8 * 192 * 192 * 256,
        scratch=[pltpu.VMEM((144, 256), F32)],
    )
    two, one = whole_call(
        add_halves,
        [shaped((half, 256)), shaped((TAIL, 256))],
        [keep, even_swap(send, "pair", 2)],
        0,
        scalars=0,
    )
    columns = lax.axis_size("col")
    two, two_more = sum_but_last(two, "col", columns)
    one, one_more = sum_but_last(one, "row", bands)
    input_grad, done = whole_call(
        functools.partial(layer_one_back, bands=bands),
        [shaped(features_in.shape), shaped((8, 128), F32)],
        [at_place, g, even_swap(up_a, "row", bands), odd_swap(up_b, "row", bands), back_one],
        2 * band_rows * 192 * 192 * 256,
    )
    one, one_more = sum_but_last(added(one, one_more, done), "col", columns)
    (mine,) = whole_call(
        add_joined, [shaped((half + TAIL, 256))], [two, two_more, one, one_more], 0, scalars=0
    )
    grad_one, grad_two = whole_call(
        functools.partial(
            finish,
            scales=(1.0 / math.sqrt(height * width), 1.0 / math.sqrt(pooled_rows * total)),
        ),
        [shaped((3, 3 * channels, channels), F32), shaped((2 * half, 256), F32)],
        [at_place, mine, even_swap(mine, "pair", 2)],
        1,
        scratch=[
            pltpu.VMEM((3, 3 * channels, channels), F32),
            pltpu.VMEM((2, half, 256), F32),
            pltpu.VMEM((144, 256), F32),
            pltpu.SemaphoreType.DMA((3,)),
        ],
        out_space=pl.ANY,
    )
    grad_two = jnp.transpose(grad_two.reshape(3, 3, filters, 4 * channels), (2, 0, 1, 3))
    grad_one = jnp.transpose(grad_one.reshape(3, 3, channels, channels), (2, 0, 1, 3))
    return (input_grad, grad_one, grad_two)


def solution(mesh):
    in_specs = (
        P("grp", "row", ("col", "pair")),
        P(),
        P("row", None, None, None),
        P(("grp", "row"), ("col", "pair"), None),
    )
    out_specs = (
        P("grp", "row", ("col", "pair")),
        P("grp", None, None, None),
        P(("grp", "row"), None, None, None),
    )
    return jax.shard_map(local, mesh=mesh, in_specs=in_specs, out_specs=out_specs, check_vma=False)
```

```python
import functools
import math

import jax
import jax.numpy as jnp
from jax import lax
from jax.experimental import pallas as pl
from jax.experimental.pallas import tpu as pltpu
from jax.sharding import PartitionSpec as P

BF16 = jnp.bfloat16
F32 = jnp.float32
COLS = ("col", "pair")
REACH = 3
TAIL = 80
PITCH = 48
SENT = 40


def dot(a, b, contract):
    return lax.dot_general(a, b, ((contract[:1], contract[1:]), ((), ())), preferred_element_type=F32)


def whole_call(body, outs, operands, flops, scalars=1, scratch=(), after=0, out_space=pltpu.VMEM):
    specs = [
        pl.BlockSpec(memory_space=pltpu.SMEM if n < scalars else pltpu.VMEM)
        for n in range(len(operands) - after)
    ] + [pl.BlockSpec(memory_space=pl.ANY)] * after
    sizes = [math.prod(a.shape) * a.dtype.itemsize for a in tuple(operands[scalars:]) + tuple(outs)]
    moved = sum(sizes) if flops else 0
    return pl.pallas_call(
        body,
        out_shape=outs,
        in_specs=specs,
        out_specs=[pl.BlockSpec(memory_space=out_space) for _ in outs],
        scratch_shapes=list(scratch),
        cost_estimate=pl.CostEstimate(flops=flops, bytes_accessed=moved, transcendentals=0),
        compiler_params=pltpu.CompilerParams(vmem_limit_bytes=40 * 1024 * 1024),
    )(*operands)


def shaped(shape, dtype=BF16):
    return jax.ShapeDtypeStruct(shape, dtype)


def roll(values, amount, axis):
    return pltpu.roll(values, amount % values.shape[axis], axis)


def sigmoid(values):
    return 0.5 + 0.5 * jnp.tanh(0.5 * values)


def slope_of(values, sig):
    return sig * (1.0 + values * (1.0 - sig))


def pool_matrix(strip, total, back=False):
    row = lax.broadcasted_iota(jnp.int32, (2 * PITCH, 256), 0)
    lane = lax.broadcasted_iota(jnp.int32, (2 * PITCH, 256), 1)
    half = (row >= PITCH).astype(jnp.int32)
    n = row - half * PITCH
    if back:
        v, most = jnp.where((n == 32) & (half == 1), -1, n), 33
    else:
        v, most = n - REACH, 32 + 2 * REACH
    near = jnp.bitwise_and(lane - 4 * v - 2 * half, 255) < 2
    place = strip * 32 + v
    keep = near & (n < most) & (place >= 0) & (place < total)
    return jnp.where(keep, 0.25, 0.0).astype(BF16)


def order_matrix():
    row = lax.broadcasted_iota(jnp.int32, (256, 256), 0)
    lane = lax.broadcasted_iota(jnp.int32, (256, 256), 1)
    j, i, c = row >> 7, (row >> 6) & 1, row & 63
    return jnp.where(lane == 4 * c + 2 * i + j, 1.0, 0.0).astype(BF16)


def constants(info, w_ref, joined_ref, pool_ref, back_ref, order_ref, *, total):
    joined_ref[...] = jnp.concatenate([w_ref[0], w_ref[1], w_ref[2]], axis=1)
    pool_ref[...] = pool_matrix(info[0], total)
    back_ref[...] = pool_matrix(info[0], total, back=True)
    order_ref[...] = order_matrix()


def beside(a_ref, b_ref, place, count):
    even = (place & 1) == 0
    a = a_ref[...].astype(F32)
    b = jnp.where((place > 0) & (place < count - 1), b_ref[...].astype(F32), 0.0)
    return jnp.where(even, b, a).astype(BF16), jnp.where(even, a, b).astype(BF16)


def pack_row(row, r, slot, head, tail):
    turned = roll(row.astype(F32), 16 * r, 1)
    return jnp.where(slot == r, turned, head), jnp.where(slot == (r - 1) % 8, turned, tail)


def pack_own(info, x_ref, head_ref, tail_ref, a_ref, b_ref):
    even = (info[0] & 1) == 0
    slot = lax.broadcasted_iota(jnp.int32, (64, 128), 1) >> 4
    head = tail = jnp.zeros((64, 128), F32)
    for r in range(x_ref.shape[0]):
        head, tail = pack_row(x_ref[r], r, slot, head, tail)
    a_ref[:64] = jnp.where(even, tail, head).astype(BF16)
    b_ref[:64] = jnp.where(even, head, tail).astype(BF16)
    first, last = head_ref[...].astype(F32), tail_ref[...].astype(F32)
    a_ref[64:] = jnp.where(even, last, first).astype(BF16)
    b_ref[64:] = jnp.where(even, first, last).astype(BF16)


def pack_borders(info, up_a_ref, up_b_ref, own_a_ref, own_b_ref, a_ref, b_ref, above_ref, below_ref, *, bands):
    even = (info[0] & 1) == 0
    above_ref[...], below_ref[...] = beside(up_a_ref, up_b_ref, info[2], bands)
    slot = lax.broadcasted_iota(jnp.int32, (64, 128), 1) >> 4
    head = tail = jnp.zeros((64, 128), F32)
    for r, ref in enumerate((above_ref, below_ref)):
        head, tail = pack_row(ref[...], r, slot, head, tail)
    a_ref[:64] = jnp.where(even, tail, head).astype(BF16)
    b_ref[:64] = jnp.where(even, head, tail).astype(BF16)
    a_ref[64:] = own_a_ref[...]
    b_ref[64:] = own_b_ref[...]


def layer_one(
    info,
    x_ref,
    above_ref,
    below_ref,
    a_ref,
    b_ref,
    w_ref,
    pool_ref,
    order_ref,
    pooled_ref,
    slope_ref,
    wide_ref,
    *,
    strips,
):
    strip = info[0]
    band_rows = x_ref.shape[0]
    slot = lax.broadcasted_iota(jnp.int32, (128, 128), 1) >> 4
    inner = (strip > 0) & (strip < strips - 1)
    sides = a_ref[:128].astype(F32), jnp.where(inner, b_ref[:128].astype(F32), 0.0)
    from_a = ((slot ^ strip) & 1) == 0
    packed = jnp.where(from_a, *sides), jnp.where(from_a, *sides[::-1])
    for r in range(band_rows):
        wide_ref[1 + r, :, 128:] = roll(packed[r % 2][64:], -16 * r, 1).astype(BF16)
    for r, place in enumerate((0, band_rows + 1)):
        wide_ref[place, :, 128:] = roll(packed[r][:64], -16 * r, 1).astype(BF16)
    wide_ref[0, :, :128] = above_ref[...]
    wide_ref[1 : band_rows + 1, :, :128] = x_ref[...]
    wide_ref[band_rows + 1, :, :128] = below_ref[...]
    weights = w_ref[...]
    rows = slope_ref.shape[0]
    halves, held = [], None
    for h in range(rows):
        y = dot(weights, wide_ref[h : h + 3].reshape(192, 256), (1, 0))
        pre = roll(y[:64], 1, 1) + y[64:128] + roll(y[128:], -1, 1)
        sig = sigmoid(pre)
        slope_ref[h] = slope_of(pre, sig).astype(BF16)
        active = pre * sig
        if h % 2:
            halves.append((held + active).astype(BF16))
        else:
            held = active
    pooled = dot(pool_ref[...], jnp.concatenate(halves, 0), (1, 1))
    stacked = jnp.concatenate(
        [
            jnp.concatenate(
                [pooled[:PITCH, u * 128 : u * 128 + 128], pooled[PITCH:, u * 128 : u * 128 + 128]], 1
            )
            for u in range(2)
        ],
        0,
    ).astype(BF16)
    ordered = dot(stacked, order_ref[...], (1, 0)).astype(BF16)
    for u in range(2):
        pooled_ref[u] = ordered[u * PITCH : u * PITCH + SENT]


def layer_two(info, og_ref, w_ref, *refs, bands):
    pieces, refs = refs[:bands], refs[bands:]
    terms, refs = refs[:bands], refs[bands:]
    map_ref, grad_ref, pack_ref = refs
    band = info[2]
    rows, _, filters = og_ref.shape
    count = rows * PITCH
    map_ref[0] = jnp.zeros((PITCH, 256), BF16)
    map_ref[rows + 1] = jnp.zeros((PITCH, 256), BF16)
    blank = jnp.zeros((PITCH - SENT, 256), BF16)
    for k in range(bands):
        for t in range(2):
            map_ref[1 + 2 * (band ^ k) + t] = jnp.concatenate([pieces[k][t], blank], 0)
    near = jnp.concatenate([map_ref[i : i + rows].reshape(count, 256) for i in range(3)], 1)
    y = dot(near, jnp.concatenate([w_ref[i] for i in range(3)], 1), (1, 1))
    pre = roll(y[:, :filters], 1, 0) + y[:, filters : 2 * filters] + roll(y[:, 2 * filters :], -1, 0)
    grad = og_ref[...].reshape(count, filters).astype(F32) * slope_of(pre, sigmoid(pre))
    grad = grad.astype(BF16)
    grad_ref[0] = jnp.zeros((PITCH, filters), BF16)
    grad_ref[rows + 1] = jnp.zeros((PITCH, filters), BF16)
    grad_ref[1 : rows + 1] = grad.reshape(rows, PITCH, filters)
    near = jnp.concatenate([grad_ref[2 - i : 2 - i + rows].reshape(count, filters) for i in range(3)], 1)
    weights = [
        jnp.concatenate([w_ref[i, j * filters : (j + 1) * filters] for j in range(3)], 1) for i in range(3)
    ]
    z = dot(near, jnp.concatenate(weights, 0), (1, 0))
    spread = roll(z[:, :256], -1 - REACH, 0) + roll(z[:, 256:512], -REACH, 0) + roll(z[:, 512:], 1 - REACH, 0)
    spread = spread.reshape(rows, PITCH, 256)
    odd = (lax.broadcasted_iota(jnp.int32, (8, 256), 1) & 1) == 1
    row = lax.broadcasted_iota(jnp.int32, (8, 256), 0)
    ends = [jnp.where(odd, spread[u - 1, 47:48], spread[u, 32:33]) for u in range(rows)]
    for p in range(rows // 2):
        shared = jnp.where(row == 0, ends[2 * p], jnp.where(row == 1, ends[2 * p + 1], 0.0))
        pack_ref[p] = jnp.concatenate([spread[2 * p, :32], shared, spread[2 * p + 1, :32]], 0).astype(BF16)
    for k in range(bands):
        terms[k][...] = pack_ref[band ^ k]


def filter_two_grads(info, map_ref, grad_ref, keep_ref, send_ref, all_ref):
    pair = info[1]
    rows = map_ref.shape[0] - 2
    filters = grad_ref.shape[2]
    v = lax.broadcasted_iota(jnp.int32, (rows, PITCH, filters), 1)
    own = (v >= REACH) & (v < REACH + 32)
    wide = jnp.where(own, grad_ref[1 : rows + 1].astype(F32), 0.0).reshape(rows * PITCH, filters)
    cat = jnp.concatenate([roll(wide, -1, 0), wide, roll(wide, 1, 0)], 1).astype(BF16)
    taps = 3 * filters
    for i in range(3):
        part = dot(cat, map_ref[i : i + rows].reshape(rows * PITCH, 256), (0, 0))
        all_ref[i * taps : (i + 1) * taps] = part.astype(BF16)
    half = keep_ref.shape[0]
    keep_ref[...] = all_ref[pl.ds(pl.multiple_of(pair * half, 16), half)]
    send_ref[...] = all_ref[pl.ds(pl.multiple_of((1 - pair) * half, 16), half)]


def add_after(a_ref, b_ref, *refs):
    refs[-1][...] = (a_ref[...].astype(F32) + b_ref[...].astype(F32)).astype(BF16)


def add_halves(a_ref, b_ref, two_ref, one_ref):
    half = two_ref.shape[0]
    total = (a_ref[...].astype(F32) + b_ref[...].astype(F32)).astype(BF16)
    two_ref[...] = total[:half]
    one_ref[...] = total[half:]


def add_joined(a_ref, b_ref, c_ref, d_ref, _, out_ref):
    half = a_ref.shape[0]
    out_ref[:half] = (a_ref[...].astype(F32) + b_ref[...].astype(F32)).astype(BF16)
    out_ref[half:] = (c_ref[...].astype(F32) + d_ref[...].astype(F32)).astype(BF16)


def grad_pre_one(info, *refs, bands):
    terms, refs = refs[:bands], refs[bands:]
    slope_ref, wide_ref, pool_ref, order_ref, keep_two_ref, send_two_ref, *refs = refs
    g_ref, a_ref, b_ref, keep_ref, send_ref, part_ref = refs
    pair = info[1]
    summed = terms[0][...].astype(F32)
    for k in range(1, bands):
        summed = summed + terms[k][...].astype(F32)
    blank = jnp.zeros((8, 256), F32)
    ends = summed[32:40]
    blocks = [summed[:32], ends, blank, summed[40:], roll(ends, -1, 0), blank]
    ordered = dot(jnp.concatenate(blocks, 0).astype(BF16), order_ref[...], (1, 1)).astype(BF16)
    pool = pool_ref[...]
    cats = []
    own = lax.broadcasted_iota(jnp.int32, (64, 256), 1) < 128
    for u in range(2):
        block = ordered[u * PITCH : (u + 1) * PITCH]
        up = dot(jnp.concatenate([block[:, :128], block[:, 128:]], 0), pool, (0, 0))
        for i in range(4):
            h = 4 * u + i
            g = (up[64 * (i // 2) : 64 * (i // 2) + 64] * slope_ref[h].astype(F32)).astype(BF16)
            g_ref[h] = g
            mine = jnp.where(own, g.astype(F32), 0.0)
            cats.append(jnp.concatenate([roll(mine, -1, 1), mine, roll(mine, 1, 1)], 0).astype(BF16))
    around = jnp.concatenate([wide_ref[h : h + 3].reshape(192, 256) for h in range(8)], 1)
    acc = dot(jnp.concatenate(cats, 1), around, (1, 1))
    even = (info[2] & 1) == 0
    first, last = g_ref[0].astype(F32), g_ref[7].astype(F32)
    a_ref[...] = jnp.where(even, last, first).astype(BF16)
    b_ref[...] = jnp.where(even, first, last).astype(BF16)
    part_ref[:96] = jnp.concatenate([acc[:96, :128], acc[96:, :128]], 1)
    part_ref[96:] = jnp.concatenate([acc[48 * q : 48 * q + 48, 128:] for q in range(4)], 1)
    half = keep_two_ref.shape[0]
    blank = jnp.zeros((TAIL - 72, 256), F32)
    for ref, two_ref, place in ((keep_ref, keep_two_ref, pair), (send_ref, send_two_ref, 1 - pair)):
        ref[:half] = two_ref[...]
        mine = part_ref[pl.ds(pl.multiple_of(place * 72, 8), 72)]
        ref[half:] = jnp.concatenate([mine, blank], 0).astype(BF16)


def layer_one_back(info, g_ref, a_ref, b_ref, w_ref, out_ref, done_ref, *, bands):
    above, below = beside(a_ref, b_ref, info[2], bands)
    done_ref[...] = jnp.zeros(done_ref.shape, F32)
    lines = [above] + [g_ref[h] for h in range(8)] + [below]
    rows = []
    for h in range(8):
        z = dot(w_ref[...], jnp.concatenate(lines[h : h + 3], 0), (1, 0))
        rows.append((roll(z[:64], -1, 1) + z[64:128] + roll(z[128:], 1, 1))[:, :128])
    out_ref[...] = jnp.swapaxes(jnp.stack(rows, 0), 0, 1).astype(BF16)


def finish(info, mine_ref, other_ref, one_hbm, two_hbm, one_ref, two_ref, flat_ref, sems, *, scales):
    pair, half = info[1], mine_ref.shape[0] - TAIL
    copies = [pltpu.make_async_copy(one_ref, one_hbm, sems.at[0])]
    for ref, place in ((mine_ref, pair), (other_ref, 1 - pair)):
        flat_ref[pl.ds(pl.multiple_of(place * 72, 8), 72)] = ref[half : half + 72].astype(F32) * scales[0]
    one_ref[0, :96] = flat_ref[:96, :64]
    one_ref[1, :96] = flat_ref[:96, 64:128]
    one_ref[0, 96:] = flat_ref[:96, 128:192]
    one_ref[1, 96:] = flat_ref[:96, 192:]
    for q in range(4):
        one_ref[2, 48 * q : 48 * q + 48] = flat_ref[96:, 64 * q : 64 * q + 64]
    copies[0].start()
    for n, (ref, place) in enumerate(((mine_ref, pair), (other_ref, 1 - pair))):
        rows = pl.ds(pl.multiple_of(place * half, 16), half)
        two_ref[n] = ref[:half].astype(F32) * scales[1]
        copies.append(pltpu.make_async_copy(two_ref.at[n], two_hbm.at[rows], sems.at[1 + n]))
        copies[-1].start()
    for copy in copies:
        copy.wait()


def even_swap(values, axis, count):
    return lax.ppermute(values, axis, [(n, n ^ 1) for n in range(count)])


def odd_swap(values, axis, count):
    return lax.ppermute(values, axis, [(n, (n - 1 if n % 2 == 0 else n + 1) % count) for n in range(count)])


def xor_swap(values, axis, count, k):
    return lax.ppermute(values, axis, [(n, n ^ k) for n in range(count)])


def row_swaps(values, bands):
    order = sorted(range(1, bands), key=lambda k: (k < bands // 2, k))
    moved = {k: xor_swap(values[k], "row", bands, k) for k in order}
    return [moved[k] for k in range(1, bands)]


def added(a, b, *after):
    (total,) = whole_call(add_after, [shaped(a.shape)], [a, b, *after], 0, scalars=0, after=len(after))
    return total


def sum_but_last(part, axis, count):
    step = 1
    while 2 * step < count:
        part = added(part, xor_swap(part, axis, count, step))
        step *= 2
    return part, xor_swap(part, axis, count, step)


def local(features_in, filters_one, filters_two, out_grad):
    channels, band_rows, strip_cols = features_in.shape
    filters, own_cols, pooled_rows = out_grad.shape
    bands = lax.axis_size("row")
    strips = lax.axis_size(COLS)
    band = lax.axis_index("row")
    strip = lax.axis_index(COLS)
    pair = lax.axis_index("pair")
    height, width = band_rows * bands, strip_cols * strips
    total = own_cols * strips
    at_place = jnp.stack([strip, pair, band]).astype(jnp.int32)

    taps_one = jnp.transpose(filters_one, (1, 2, 0, 3)).reshape(3, 3 * channels, channels)
    back_one = jnp.transpose(filters_one[:, ::-1], (2, 3, 1, 0)).reshape(3 * channels, 3 * channels)
    taps_two = jnp.transpose(filters_two, (1, 2, 0, 3)).reshape(3, 3 * filters, 4 * channels)

    og = jnp.transpose(out_grad, (1, 2, 0))
    edge = REACH - 1
    x = jnp.transpose(features_in, (1, 0, 2))
    even = band % 2 == 0
    to_a, to_b = jnp.where(even, x[-1], x[0]), jnp.where(even, x[0], x[-1])
    head, tail = og[:edge], og[-edge:]
    joined_one, pool, pool_back, order = whole_call(
        functools.partial(constants, total=total),
        [shaped((3 * channels, 3 * channels))] + [shaped((2 * PITCH, 256))] * 2 + [shaped((256, 256))],
        [at_place, taps_one],
        10**8,
    )
    head, tail = head.reshape(-1, 128), tail.reshape(-1, 128)
    own_a, own_b = whole_call(
        pack_own, [shaped((channels + head.shape[0], 128))] * 2, [at_place, x, head, tail], 10**8
    )
    to_a, to_b, above, below = whole_call(
        functools.partial(pack_borders, bands=bands),
        [shaped((2 * channels + head.shape[0], 128))] * 2 + [shaped((channels, strip_cols))] * 2,
        [at_place, even_swap(to_a, "row", bands), odd_swap(to_b, "row", bands), own_a, own_b],
        1,
    )
    side_a, side_b = even_swap(to_a, COLS, strips), odd_swap(to_b, COLS, strips)
    pooled, slope, wide = whole_call(
        functools.partial(layer_one, strips=strips),
        [
            shaped((2, SENT, 4 * channels)),
            shaped((band_rows, channels, 256)),
            shaped((band_rows + 2, channels, 256)),
        ],
        [at_place, x, above, below, side_a, side_b, joined_one, pool, order],
        2 * band_rows * 192 * 192 * 256,
    )
    pieces = [pooled] + row_swaps([pooled] * bands, bands)

    even = strip % 2 == 0
    ends = [side[2 * channels :].reshape(og[:edge].shape) for side in (side_a, side_b)]
    ends[1] = jnp.where((strip == 0) | (strip == strips - 1), 0, ends[1])
    before, after = jnp.where(even, ends[1], ends[0]), jnp.where(even, ends[0], ends[1])
    og = jnp.concatenate([before, og, after], 0)
    og = jnp.pad(og, ((1, PITCH - own_cols - 2 * REACH + 1), (0, 0), (0, 0)))
    og = jnp.transpose(og, (1, 0, 2))

    count = pooled_rows * PITCH
    *terms, pooled_map, grad_map = whole_call(
        functools.partial(layer_two, bands=bands),
        [shaped((72, 4 * channels))] * bands
        + [shaped((pooled_rows + 2, PITCH, 4 * channels)), shaped((pooled_rows + 2, PITCH, filters))],
        [at_place, og, taps_two] + pieces,
        4 * count * 9 * filters * 4 * channels,
        scratch=[pltpu.VMEM((bands, 72, 4 * channels), BF16)],
    )
    received = [terms[0]] + row_swaps(terms, bands)

    half = 9 * filters // 2
    keep_two, send_two = whole_call(
        filter_two_grads,
        [shaped((half, 4 * channels))] * 2,
        [at_place, pooled_map, grad_map],
        2 * count * 9 * filters * 4 * channels,
        scratch=[pltpu.VMEM((2 * half, 4 * channels), BF16)],
    )
    g, up_a, up_b, keep, send = whole_call(
        functools.partial(grad_pre_one, bands=bands),
        [shaped((band_rows, channels, 256))]
        + [shaped((channels, 256))] * 2
        + [shaped((half + TAIL, 256))] * 2,
        [at_place] + received + [slope, wide, pool_back, order, keep_two, send_two],
        2 * 8 * 192 * 192 * 256,
        scratch=[pltpu.VMEM((144, 256), F32)],
    )
    two, one = whole_call(
        add_halves,
        [shaped((half, 256)), shaped((TAIL, 256))],
        [keep, even_swap(send, "pair", 2)],
        0,
        scalars=0,
    )
    columns = lax.axis_size("col")
    two, two_more = sum_but_last(two, "col", columns)
    one, one_more = sum_but_last(one, "row", bands)
    input_grad, done = whole_call(
        functools.partial(layer_one_back, bands=bands),
        [shaped(features_in.shape), shaped((8, 128), F32)],
        [at_place, g, even_swap(up_a, "row", bands), odd_swap(up_b, "row", bands), back_one],
        2 * band_rows * 192 * 192 * 256,
    )
    one, one_more = sum_but_last(added(one, one_more), "col", columns)
    (mine,) = whole_call(
        add_joined,
        [shaped((half + TAIL, 256))],
        [two, two_more, one, one_more, done],
        0,
        scalars=0,
        after=1,
    )
    grad_one, grad_two = whole_call(
        functools.partial(
            finish,
            scales=(1.0 / math.sqrt(height * width), 1.0 / math.sqrt(pooled_rows * total)),
        ),
        [shaped((3, 3 * channels, channels), F32), shaped((2 * half, 256), F32)],
        [at_place, mine, even_swap(mine, "pair", 2)],
        1,
        scratch=[
            pltpu.VMEM((3, 3 * channels, channels), F32),
            pltpu.VMEM((2, half, 256), F32),
            pltpu.VMEM((144, 256), F32),
            pltpu.SemaphoreType.DMA((3,)),
        ],
        out_space=pl.ANY,
    )
    grad_two = jnp.transpose(grad_two.reshape(3, 3, filters, 4 * channels), (2, 0, 1, 3))
    grad_one = jnp.transpose(grad_one.reshape(3, 3, channels, channels), (2, 0, 1, 3))
    return (input_grad, grad_one, grad_two)


def solution(mesh):
    in_specs = (
        P("grp", "row", ("col", "pair")),
        P(),
        P("row", None, None, None),
        P(("grp", "row"), ("col", "pair"), None),
    )
    out_specs = (
        P("grp", "row", ("col", "pair")),
        P("grp", None, None, None),
        P(("grp", "row"), None, None, None),
    )
    return jax.shard_map(local, mesh=mesh, in_specs=in_specs, out_specs=out_specs, check_vma=False)
```

```python
import functools
import math

import jax
import jax.numpy as jnp
from jax import lax
from jax.experimental import pallas as pl
from jax.experimental.pallas import tpu as pltpu
from jax.sharding import PartitionSpec as P

BF16 = jnp.bfloat16
F32 = jnp.float32
COLS = ("col", "pair")
REACH = 3
TAIL = 80
PITCH = 48
SENT = 40


def dot(a, b, contract):
    return lax.dot_general(a, b, ((contract[:1], contract[1:]), ((), ())), preferred_element_type=F32)


def whole_call(body, outs, operands, flops, scratch=(), after=0, out_space=pltpu.VMEM):
    specs = [
        pl.BlockSpec(memory_space=pltpu.VMEM) for _ in range(len(operands) - after)
    ] + [pl.BlockSpec(memory_space=pl.ANY)] * after
    sizes = [math.prod(a.shape) * a.dtype.itemsize for a in tuple(operands) + tuple(outs)]
    moved = sum(sizes) if flops else 0
    return pl.pallas_call(
        body,
        out_shape=outs,
        in_specs=specs,
        out_specs=[pl.BlockSpec(memory_space=out_space) for _ in outs],
        scratch_shapes=list(scratch),
        cost_estimate=pl.CostEstimate(flops=flops, bytes_accessed=moved, transcendentals=0),
        compiler_params=pltpu.CompilerParams(vmem_limit_bytes=40 * 1024 * 1024),
    )(*operands)


def strip_index():
    return lax.axis_index("col") * lax.axis_size("pair") + lax.axis_index("pair")


def shaped(shape, dtype=BF16):
    return jax.ShapeDtypeStruct(shape, dtype)


def roll(values, amount, axis):
    return pltpu.roll(values, amount % values.shape[axis], axis)


def sigmoid(values):
    return 0.5 + 0.5 * jnp.tanh(0.5 * values)


def slope_of(values, sig):
    return sig * (1.0 + values * (1.0 - sig))


def pool_matrix(strip, total, back=False):
    row = lax.broadcasted_iota(jnp.int32, (2 * PITCH, 256), 0)
    lane = lax.broadcasted_iota(jnp.int32, (2 * PITCH, 256), 1)
    half = (row >= PITCH).astype(jnp.int32)
    n = row - half * PITCH
    if back:
        v, most = jnp.where((n == 32) & (half == 1), -1, n), 33
    else:
        v, most = n - REACH, 32 + 2 * REACH
    near = jnp.bitwise_and(lane - 4 * v - 2 * half, 255) < 2
    place = strip * 32 + v
    keep = near & (n < most) & (place >= 0) & (place < total)
    return jnp.where(keep, 0.25, 0.0).astype(BF16)


def order_matrix():
    row = lax.broadcasted_iota(jnp.int32, (256, 256), 0)
    lane = lax.broadcasted_iota(jnp.int32, (256, 256), 1)
    j, i, c = row >> 7, (row >> 6) & 1, row & 63
    return jnp.where(lane == 4 * c + 2 * i + j, 1.0, 0.0).astype(BF16)


def constants(w_ref, joined_ref, pool_ref, back_ref, order_ref, *, total):
    joined_ref[...] = jnp.concatenate([w_ref[0], w_ref[1], w_ref[2]], axis=1)
    pool_ref[...] = pool_matrix(strip_index(), total)
    back_ref[...] = pool_matrix(strip_index(), total, back=True)
    order_ref[...] = order_matrix()


def beside(a_ref, b_ref, place, count):
    even = (place & 1) == 0
    a = a_ref[...].astype(F32)
    b = jnp.where((place > 0) & (place < count - 1), b_ref[...].astype(F32), 0.0)
    return jnp.where(even, b, a).astype(BF16), jnp.where(even, a, b).astype(BF16)


def pack_row(row, r, slot, head, tail):
    turned = roll(row.astype(F32), 16 * r, 1)
    return jnp.where(slot == r, turned, head), jnp.where(slot == (r - 1) % 8, turned, tail)


def pack_own(x_ref, head_ref, tail_ref, a_ref, b_ref):
    even = (strip_index() & 1) == 0
    slot = lax.broadcasted_iota(jnp.int32, (64, 128), 1) >> 4
    head = tail = jnp.zeros((64, 128), F32)
    for r in range(x_ref.shape[0]):
        head, tail = pack_row(x_ref[r], r, slot, head, tail)
    a_ref[:64] = jnp.where(even, tail, head).astype(BF16)
    b_ref[:64] = jnp.where(even, head, tail).astype(BF16)
    first, last = head_ref[...].astype(F32), tail_ref[...].astype(F32)
    a_ref[64:] = jnp.where(even, last, first).astype(BF16)
    b_ref[64:] = jnp.where(even, first, last).astype(BF16)


def pack_borders(up_a_ref, up_b_ref, own_a_ref, own_b_ref, a_ref, b_ref, above_ref, below_ref, *, bands):
    even = (strip_index() & 1) == 0
    above_ref[...], below_ref[...] = beside(up_a_ref, up_b_ref, lax.axis_index("row"), bands)
    slot = lax.broadcasted_iota(jnp.int32, (64, 128), 1) >> 4
    head = tail = jnp.zeros((64, 128), F32)
    for r, ref in enumerate((above_ref, below_ref)):
        head, tail = pack_row(ref[...], r, slot, head, tail)
    a_ref[:64] = jnp.where(even, tail, head).astype(BF16)
    b_ref[:64] = jnp.where(even, head, tail).astype(BF16)
    a_ref[64:] = own_a_ref[...]
    b_ref[64:] = own_b_ref[...]


def layer_one(
    x_ref,
    above_ref,
    below_ref,
    a_ref,
    b_ref,
    w_ref,
    pool_ref,
    order_ref,
    pooled_ref,
    slope_ref,
    wide_ref,
    *,
    strips,
):
    strip = strip_index()
    band_rows = x_ref.shape[0]
    slot = lax.broadcasted_iota(jnp.int32, (128, 128), 1) >> 4
    inner = (strip > 0) & (strip < strips - 1)
    sides = a_ref[:128].astype(F32), jnp.where(inner, b_ref[:128].astype(F32), 0.0)
    from_a = ((slot ^ strip) & 1) == 0
    packed = jnp.where(from_a, *sides), jnp.where(from_a, *sides[::-1])
    for r in range(band_rows):
        wide_ref[1 + r, :, 128:] = roll(packed[r % 2][64:], -16 * r, 1).astype(BF16)
    for r, place in enumerate((0, band_rows + 1)):
        wide_ref[place, :, 128:] = roll(packed[r][:64], -16 * r, 1).astype(BF16)
    wide_ref[0, :, :128] = above_ref[...]
    wide_ref[1 : band_rows + 1, :, :128] = x_ref[...]
    wide_ref[band_rows + 1, :, :128] = below_ref[...]
    weights = w_ref[...]
    rows = slope_ref.shape[0]
    halves, held = [], None
    for h in range(rows):
        y = dot(weights, wide_ref[h : h + 3].reshape(192, 256), (1, 0))
        pre = roll(y[:64], 1, 1) + y[64:128] + roll(y[128:], -1, 1)
        sig = sigmoid(pre)
        slope_ref[h] = slope_of(pre, sig).astype(BF16)
        active = pre * sig
        if h % 2:
            halves.append((held + active).astype(BF16))
        else:
            held = active
    pooled = dot(pool_ref[...], jnp.concatenate(halves, 0), (1, 1))
    stacked = jnp.concatenate(
        [
            jnp.concatenate(
                [pooled[:PITCH, u * 128 : u * 128 + 128], pooled[PITCH:, u * 128 : u * 128 + 128]], 1
            )
            for u in range(2)
        ],
        0,
    ).astype(BF16)
    ordered = dot(stacked, order_ref[...], (1, 0)).astype(BF16)
    for u in range(2):
        pooled_ref[u] = ordered[u * PITCH : u * PITCH + SENT]


def layer_two(og_ref, w_ref, *refs, bands):
    pieces, refs = refs[:bands], refs[bands:]
    terms, refs = refs[:bands], refs[bands:]
    map_ref, grad_ref, pack_ref = refs
    band = lax.axis_index("row")
    rows, _, filters = og_ref.shape
    count = rows * PITCH
    map_ref[0] = jnp.zeros((PITCH, 256), BF16)
    map_ref[rows + 1] = jnp.zeros((PITCH, 256), BF16)
    blank = jnp.zeros((PITCH - SENT, 256), BF16)
    for k in range(bands):
        for t in range(2):
            map_ref[1 + 2 * (band ^ k) + t] = jnp.concatenate([pieces[k][t], blank], 0)
    near = jnp.concatenate([map_ref[i : i + rows].reshape(count, 256) for i in range(3)], 1)
    y = dot(near, jnp.concatenate([w_ref[i] for i in range(3)], 1), (1, 1))
    pre = roll(y[:, :filters], 1, 0) + y[:, filters : 2 * filters] + roll(y[:, 2 * filters :], -1, 0)
    grad = og_ref[...].reshape(count, filters).astype(F32) * slope_of(pre, sigmoid(pre))
    grad = grad.astype(BF16)
    grad_ref[0] = jnp.zeros((PITCH, filters), BF16)
    grad_ref[rows + 1] = jnp.zeros((PITCH, filters), BF16)
    grad_ref[1 : rows + 1] = grad.reshape(rows, PITCH, filters)
    near = jnp.concatenate([grad_ref[2 - i : 2 - i + rows].reshape(count, filters) for i in range(3)], 1)
    weights = [
        jnp.concatenate([w_ref[i, j * filters : (j + 1) * filters] for j in range(3)], 1) for i in range(3)
    ]
    z = dot(near, jnp.concatenate(weights, 0), (1, 0))
    spread = roll(z[:, :256], -1 - REACH, 0) + roll(z[:, 256:512], -REACH, 0) + roll(z[:, 512:], 1 - REACH, 0)
    spread = spread.reshape(rows, PITCH, 256)
    odd = (lax.broadcasted_iota(jnp.int32, (8, 256), 1) & 1) == 1
    row = lax.broadcasted_iota(jnp.int32, (8, 256), 0)
    ends = [jnp.where(odd, spread[u - 1, 47:48], spread[u, 32:33]) for u in range(rows)]
    for p in range(rows // 2):
        shared = jnp.where(row == 0, ends[2 * p], jnp.where(row == 1, ends[2 * p + 1], 0.0))
        pack_ref[p] = jnp.concatenate([spread[2 * p, :32], shared, spread[2 * p + 1, :32]], 0).astype(BF16)
    for k in range(bands):
        terms[k][...] = pack_ref[band ^ k]


def filter_two_grads(map_ref, grad_ref, keep_ref, send_ref, all_ref):
    pair = lax.axis_index("pair")
    rows = map_ref.shape[0] - 2
    filters = grad_ref.shape[2]
    v = lax.broadcasted_iota(jnp.int32, (rows, PITCH, filters), 1)
    own = (v >= REACH) & (v < REACH + 32)
    wide = jnp.where(own, grad_ref[1 : rows + 1].astype(F32), 0.0).reshape(rows * PITCH, filters)
    cat = jnp.concatenate([roll(wide, -1, 0), wide, roll(wide, 1, 0)], 1).astype(BF16)
    taps = 3 * filters
    for i in range(3):
        part = dot(cat, map_ref[i : i + rows].reshape(rows * PITCH, 256), (0, 0))
        all_ref[i * taps : (i + 1) * taps] = part.astype(BF16)
    half = keep_ref.shape[0]
    keep_ref[...] = all_ref[pl.ds(pl.multiple_of(pair * half, 16), half)]
    send_ref[...] = all_ref[pl.ds(pl.multiple_of((1 - pair) * half, 16), half)]


def add_after(a_ref, b_ref, *refs):
    refs[-1][...] = (a_ref[...].astype(F32) + b_ref[...].astype(F32)).astype(BF16)


def add_halves(a_ref, b_ref, two_ref, one_ref):
    half = two_ref.shape[0]
    total = (a_ref[...].astype(F32) + b_ref[...].astype(F32)).astype(BF16)
    two_ref[...] = total[:half]
    one_ref[...] = total[half:]


def add_joined(a_ref, b_ref, c_ref, d_ref, _, out_ref):
    half = a_ref.shape[0]
    out_ref[:half] = (a_ref[...].astype(F32) + b_ref[...].astype(F32)).astype(BF16)
    out_ref[half:] = (c_ref[...].astype(F32) + d_ref[...].astype(F32)).astype(BF16)


def grad_pre_one(*refs, bands):
    terms, refs = refs[:bands], refs[bands:]
    slope_ref, wide_ref, pool_ref, order_ref, keep_two_ref, send_two_ref, *refs = refs
    g_ref, a_ref, b_ref, keep_ref, send_ref, part_ref = refs
    pair = lax.axis_index("pair")
    summed = terms[0][...].astype(F32)
    for k in range(1, bands):
        summed = summed + terms[k][...].astype(F32)
    blank = jnp.zeros((8, 256), F32)
    ends = summed[32:40]
    blocks = [summed[:32], ends, blank, summed[40:], roll(ends, -1, 0), blank]
    ordered = dot(jnp.concatenate(blocks, 0).astype(BF16), order_ref[...], (1, 1)).astype(BF16)
    pool = pool_ref[...]
    cats = []
    own = lax.broadcasted_iota(jnp.int32, (64, 256), 1) < 128
    for u in range(2):
        block = ordered[u * PITCH : (u + 1) * PITCH]
        up = dot(jnp.concatenate([block[:, :128], block[:, 128:]], 0), pool, (0, 0))
        for i in range(4):
            h = 4 * u + i
            g = (up[64 * (i // 2) : 64 * (i // 2) + 64] * slope_ref[h].astype(F32)).astype(BF16)
            g_ref[h] = g
            mine = jnp.where(own, g.astype(F32), 0.0)
            cats.append(jnp.concatenate([roll(mine, -1, 1), mine, roll(mine, 1, 1)], 0).astype(BF16))
    around = jnp.concatenate([wide_ref[h : h + 3].reshape(192, 256) for h in range(8)], 1)
    acc = dot(jnp.concatenate(cats, 1), around, (1, 1))
    even = (lax.axis_index("row") & 1) == 0
    first, last = g_ref[0].astype(F32), g_ref[7].astype(F32)
    a_ref[...] = jnp.where(even, last, first).astype(BF16)
    b_ref[...] = jnp.where(even, first, last).astype(BF16)
    part_ref[:96] = jnp.concatenate([acc[:96, :128], acc[96:, :128]], 1)
    part_ref[96:] = jnp.concatenate([acc[48 * q : 48 * q + 48, 128:] for q in range(4)], 1)
    half = keep_two_ref.shape[0]
    blank = jnp.zeros((TAIL - 72, 256), F32)
    for ref, two_ref, place in ((keep_ref, keep_two_ref, pair), (send_ref, send_two_ref, 1 - pair)):
        ref[:half] = two_ref[...]
        mine = part_ref[pl.ds(pl.multiple_of(place * 72, 8), 72)]
        ref[half:] = jnp.concatenate([mine, blank], 0).astype(BF16)


def layer_one_back(g_ref, a_ref, b_ref, w_ref, out_ref, done_ref, *, bands):
    above, below = beside(a_ref, b_ref, lax.axis_index("row"), bands)
    done_ref[...] = jnp.zeros(done_ref.shape, F32)
    lines = [above] + [g_ref[h] for h in range(8)] + [below]
    rows = []
    for h in range(8):
        z = dot(w_ref[...], jnp.concatenate(lines[h : h + 3], 0), (1, 0))
        rows.append((roll(z[:64], -1, 1) + z[64:128] + roll(z[128:], 1, 1))[:, :128])
    out_ref[...] = jnp.swapaxes(jnp.stack(rows, 0), 0, 1).astype(BF16)


def finish(mine_ref, other_ref, one_hbm, two_hbm, one_ref, two_ref, flat_ref, sems, *, scales):
    pair, half = lax.axis_index("pair"), mine_ref.shape[0] - TAIL
    copies = [pltpu.make_async_copy(one_ref, one_hbm, sems.at[0])]
    for ref, place in ((mine_ref, pair), (other_ref, 1 - pair)):
        flat_ref[pl.ds(pl.multiple_of(place * 72, 8), 72)] = ref[half : half + 72].astype(F32) * scales[0]
    one_ref[0, :96] = flat_ref[:96, :64]
    one_ref[1, :96] = flat_ref[:96, 64:128]
    one_ref[0, 96:] = flat_ref[:96, 128:192]
    one_ref[1, 96:] = flat_ref[:96, 192:]
    for q in range(4):
        one_ref[2, 48 * q : 48 * q + 48] = flat_ref[96:, 64 * q : 64 * q + 64]
    copies[0].start()
    for n, (ref, place) in enumerate(((mine_ref, pair), (other_ref, 1 - pair))):
        rows = pl.ds(pl.multiple_of(place * half, 16), half)
        two_ref[n] = ref[:half].astype(F32) * scales[1]
        copies.append(pltpu.make_async_copy(two_ref.at[n], two_hbm.at[rows], sems.at[1 + n]))
        copies[-1].start()
    for copy in copies:
        copy.wait()


def even_swap(values, axis, count):
    return lax.ppermute(values, axis, [(n, n ^ 1) for n in range(count)])


def odd_swap(values, axis, count):
    return lax.ppermute(values, axis, [(n, (n - 1 if n % 2 == 0 else n + 1) % count) for n in range(count)])


def xor_swap(values, axis, count, k):
    return lax.ppermute(values, axis, [(n, n ^ k) for n in range(count)])


def row_swaps(values, bands):
    order = sorted(range(1, bands), key=lambda k: (k < bands // 2, k))
    moved = {k: xor_swap(values[k], "row", bands, k) for k in order}
    return [moved[k] for k in range(1, bands)]


def added(a, b, *after):
    (total,) = whole_call(add_after, [shaped(a.shape)], [a, b, *after], 0, after=len(after))
    return total


def sum_but_last(part, axis, count):
    step = 1
    while 2 * step < count:
        part = added(part, xor_swap(part, axis, count, step))
        step *= 2
    return part, xor_swap(part, axis, count, step)


def local(features_in, filters_one, filters_two, out_grad):
    channels, band_rows, strip_cols = features_in.shape
    filters, own_cols, pooled_rows = out_grad.shape
    bands = lax.axis_size("row")
    strips = lax.axis_size(COLS)
    band = lax.axis_index("row")
    strip = lax.axis_index(COLS)
    pair = lax.axis_index("pair")
    height, width = band_rows * bands, strip_cols * strips
    total = own_cols * strips

    taps_one = jnp.transpose(filters_one, (1, 2, 0, 3)).reshape(3, 3 * channels, channels)
    back_one = jnp.transpose(filters_one[:, ::-1], (2, 3, 1, 0)).reshape(3 * channels, 3 * channels)
    taps_two = jnp.transpose(filters_two, (1, 2, 0, 3)).reshape(3, 3 * filters, 4 * channels)

    og = jnp.transpose(out_grad, (1, 2, 0))
    edge = REACH - 1
    x = jnp.transpose(features_in, (1, 0, 2))
    even = band % 2 == 0
    to_a, to_b = jnp.where(even, x[-1], x[0]), jnp.where(even, x[0], x[-1])
    head, tail = og[:edge], og[-edge:]
    joined_one, pool, pool_back, order = whole_call(
        functools.partial(constants, total=total),
        [shaped((3 * channels, 3 * channels))] + [shaped((2 * PITCH, 256))] * 2 + [shaped((256, 256))],
        [taps_one],
        10**8,
    )
    head, tail = head.reshape(-1, 128), tail.reshape(-1, 128)
    own_a, own_b = whole_call(
        pack_own, [shaped((channels + head.shape[0], 128))] * 2, [x, head, tail], 10**8
    )
    to_a, to_b, above, below = whole_call(
        functools.partial(pack_borders, bands=bands),
        [shaped((2 * channels + head.shape[0], 128))] * 2 + [shaped((channels, strip_cols))] * 2,
        [even_swap(to_a, "row", bands), odd_swap(to_b, "row", bands), own_a, own_b],
        1,
    )
    side_a, side_b = even_swap(to_a, COLS, strips), odd_swap(to_b, COLS, strips)
    pooled, slope, wide = whole_call(
        functools.partial(layer_one, strips=strips),
        [
            shaped((2, SENT, 4 * channels)),
            shaped((band_rows, channels, 256)),
            shaped((band_rows + 2, channels, 256)),
        ],
        [x, above, below, side_a, side_b, joined_one, pool, order],
        2 * band_rows * 192 * 192 * 256,
    )
    pieces = [pooled] + row_swaps([pooled] * bands, bands)

    even = strip % 2 == 0
    ends = [side[2 * channels :].reshape(og[:edge].shape) for side in (side_a, side_b)]
    ends[1] = jnp.where((strip == 0) | (strip == strips - 1), 0, ends[1])
    before, after = jnp.where(even, ends[1], ends[0]), jnp.where(even, ends[0], ends[1])
    og = jnp.concatenate([before, og, after], 0)
    og = jnp.pad(og, ((1, PITCH - own_cols - 2 * REACH + 1), (0, 0), (0, 0)))
    og = jnp.transpose(og, (1, 0, 2))

    count = pooled_rows * PITCH
    *terms, pooled_map, grad_map = whole_call(
        functools.partial(layer_two, bands=bands),
        [shaped((72, 4 * channels))] * bands
        + [shaped((pooled_rows + 2, PITCH, 4 * channels)), shaped((pooled_rows + 2, PITCH, filters))],
        [og, taps_two] + pieces,
        4 * count * 9 * filters * 4 * channels,
        scratch=[pltpu.VMEM((bands, 72, 4 * channels), BF16)],
    )
    received = [terms[0]] + row_swaps(terms, bands)

    half = 9 * filters // 2
    keep_two, send_two = whole_call(
        filter_two_grads,
        [shaped((half, 4 * channels))] * 2,
        [pooled_map, grad_map],
        2 * count * 9 * filters * 4 * channels,
        scratch=[pltpu.VMEM((2 * half, 4 * channels), BF16)],
    )
    g, up_a, up_b, keep, send = whole_call(
        functools.partial(grad_pre_one, bands=bands),
        [shaped((band_rows, channels, 256))]
        + [shaped((channels, 256))] * 2
        + [shaped((half + TAIL, 256))] * 2,
        received + [slope, wide, pool_back, order, keep_two, send_two],
        2 * 8 * 192 * 192 * 256,
        scratch=[pltpu.VMEM((144, 256), F32)],
    )
    two, one = whole_call(
        add_halves,
        [shaped((half, 256)), shaped((TAIL, 256))],
        [keep, even_swap(send, "pair", 2)],
        0,
    )
    columns = lax.axis_size("col")
    two, two_more = sum_but_last(two, "col", columns)
    one, one_more = sum_but_last(one, "row", bands)
    input_grad, done = whole_call(
        functools.partial(layer_one_back, bands=bands),
        [shaped(features_in.shape), shaped((8, 128), F32)],
        [g, even_swap(up_a, "row", bands), odd_swap(up_b, "row", bands), back_one],
        2 * band_rows * 192 * 192 * 256,
    )
    one, one_more = sum_but_last(added(one, one_more), "col", columns)
    (mine,) = whole_call(
        add_joined,
        [shaped((half + TAIL, 256))],
        [two, two_more, one, one_more, done],
        0,
        after=1,
    )
    grad_one, grad_two = whole_call(
        functools.partial(
            finish,
            scales=(1.0 / math.sqrt(height * width), 1.0 / math.sqrt(pooled_rows * total)),
        ),
        [shaped((3, 3 * channels, channels), F32), shaped((2 * half, 256), F32)],
        [mine, even_swap(mine, "pair", 2)],
        1,
        scratch=[
            pltpu.VMEM((3, 3 * channels, channels), F32),
            pltpu.VMEM((2, half, 256), F32),
            pltpu.VMEM((144, 256), F32),
            pltpu.SemaphoreType.DMA((3,)),
        ],
        out_space=pl.ANY,
    )
    grad_two = jnp.transpose(grad_two.reshape(3, 3, filters, 4 * channels), (2, 0, 1, 3))
    grad_one = jnp.transpose(grad_one.reshape(3, 3, channels, channels), (2, 0, 1, 3))
    return (input_grad, grad_one, grad_two)


def solution(mesh):
    in_specs = (
        P("grp", "row", ("col", "pair")),
        P(),
        P("row", None, None, None),
        P(("grp", "row"), ("col", "pair"), None),
    )
    out_specs = (
        P("grp", "row", ("col", "pair")),
        P("grp", None, None, None),
        P(("grp", "row"), None, None, None),
    )
    return jax.shard_map(local, mesh=mesh, in_specs=in_specs, out_specs=out_specs, check_vma=False)
```

```python
import functools
import math

import jax
import jax.numpy as jnp
from jax import lax
from jax.experimental import pallas as pl
from jax.experimental.pallas import tpu as pltpu
from jax.sharding import PartitionSpec as P

BF16 = jnp.bfloat16
F32 = jnp.float32
COLS = ("col", "pair")
REACH = 3
TAIL = 80
PITCH = 48
SENT = 40


def dot(a, b, contract):
    return lax.dot_general(a, b, ((contract[:1], contract[1:]), ((), ())), preferred_element_type=F32)


def whole_call(body, outs, operands, flops, scratch=(), after=0, out_spaces=None):
    specs = [
        pl.BlockSpec(memory_space=pltpu.VMEM) for _ in range(len(operands) - after)
    ] + [pl.BlockSpec(memory_space=pl.ANY)] * after
    sizes = [math.prod(a.shape) * a.dtype.itemsize for a in tuple(operands) + tuple(outs)]
    moved = sum(sizes) if flops else 0
    return pl.pallas_call(
        body,
        out_shape=outs,
        in_specs=specs,
        out_specs=[pl.BlockSpec(memory_space=space) for space in out_spaces or [pltpu.VMEM] * len(outs)],
        scratch_shapes=list(scratch),
        cost_estimate=pl.CostEstimate(flops=flops, bytes_accessed=moved, transcendentals=0),
        compiler_params=pltpu.CompilerParams(vmem_limit_bytes=40 * 1024 * 1024),
    )(*operands)


def strip_index():
    return lax.axis_index("col") * lax.axis_size("pair") + lax.axis_index("pair")


def shaped(shape, dtype=BF16):
    return jax.ShapeDtypeStruct(shape, dtype)


def roll(values, amount, axis):
    return pltpu.roll(values, amount % values.shape[axis], axis)


def sigmoid(values):
    return 0.5 + 0.5 * jnp.tanh(0.5 * values)


def slope_of(values, sig):
    return sig * (1.0 + values * (1.0 - sig))


def pool_matrix(strip, total, back=False):
    row = lax.broadcasted_iota(jnp.int32, (2 * PITCH, 256), 0)
    lane = lax.broadcasted_iota(jnp.int32, (2 * PITCH, 256), 1)
    half = (row >= PITCH).astype(jnp.int32)
    n = row - half * PITCH
    if back:
        v, most = jnp.where((n == 32) & (half == 1), -1, n), 33
    else:
        v, most = n - REACH, 32 + 2 * REACH
    near = jnp.bitwise_and(lane - 4 * v - 2 * half, 255) < 2
    place = strip * 32 + v
    keep = near & (n < most) & (place >= 0) & (place < total)
    return jnp.where(keep, 0.25, 0.0).astype(BF16)


def order_matrix():
    row = lax.broadcasted_iota(jnp.int32, (256, 256), 0)
    lane = lax.broadcasted_iota(jnp.int32, (256, 256), 1)
    j, i, c = row >> 7, (row >> 6) & 1, row & 63
    return jnp.where(lane == 4 * c + 2 * i + j, 1.0, 0.0).astype(BF16)


def constants(w_ref, joined_ref, pool_ref, back_ref, order_ref, *, total):
    joined_ref[...] = jnp.concatenate([w_ref[0], w_ref[1], w_ref[2]], axis=1)
    pool_ref[...] = pool_matrix(strip_index(), total)
    back_ref[...] = pool_matrix(strip_index(), total, back=True)
    order_ref[...] = order_matrix()


def beside(a_ref, b_ref, place, count):
    even = (place & 1) == 0
    a = a_ref[...].astype(F32)
    b = jnp.where((place > 0) & (place < count - 1), b_ref[...].astype(F32), 0.0)
    return jnp.where(even, b, a).astype(BF16), jnp.where(even, a, b).astype(BF16)


def pack_row(row, r, slot, head, tail):
    turned = roll(row.astype(F32), 16 * r, 1)
    return jnp.where(slot == r, turned, head), jnp.where(slot == (r - 1) % 8, turned, tail)


def pack_own(x_ref, head_ref, tail_ref, a_ref, b_ref):
    even = (strip_index() & 1) == 0
    slot = lax.broadcasted_iota(jnp.int32, (64, 128), 1) >> 4
    head = tail = jnp.zeros((64, 128), F32)
    for r in range(x_ref.shape[0]):
        head, tail = pack_row(x_ref[r], r, slot, head, tail)
    a_ref[:64] = jnp.where(even, tail, head).astype(BF16)
    b_ref[:64] = jnp.where(even, head, tail).astype(BF16)
    first, last = head_ref[...].astype(F32), tail_ref[...].astype(F32)
    a_ref[64:] = jnp.where(even, last, first).astype(BF16)
    b_ref[64:] = jnp.where(even, first, last).astype(BF16)


def pack_borders(up_a_ref, up_b_ref, own_a_ref, own_b_ref, a_ref, b_ref, above_ref, below_ref, *, bands):
    even = (strip_index() & 1) == 0
    above_ref[...], below_ref[...] = beside(up_a_ref, up_b_ref, lax.axis_index("row"), bands)
    slot = lax.broadcasted_iota(jnp.int32, (64, 128), 1) >> 4
    head = tail = jnp.zeros((64, 128), F32)
    for r, ref in enumerate((above_ref, below_ref)):
        head, tail = pack_row(ref[...], r, slot, head, tail)
    a_ref[:64] = jnp.where(even, tail, head).astype(BF16)
    b_ref[:64] = jnp.where(even, head, tail).astype(BF16)
    a_ref[64:] = own_a_ref[...]
    b_ref[64:] = own_b_ref[...]


def layer_one(
    x_ref,
    above_ref,
    below_ref,
    a_ref,
    b_ref,
    w_ref,
    pool_ref,
    order_ref,
    pooled_ref,
    slope_ref,
    wide_ref,
    *,
    strips,
):
    strip = strip_index()
    band_rows = x_ref.shape[0]
    slot = lax.broadcasted_iota(jnp.int32, (128, 128), 1) >> 4
    inner = (strip > 0) & (strip < strips - 1)
    sides = a_ref[:128].astype(F32), jnp.where(inner, b_ref[:128].astype(F32), 0.0)
    from_a = ((slot ^ strip) & 1) == 0
    packed = jnp.where(from_a, *sides), jnp.where(from_a, *sides[::-1])
    for r in range(band_rows):
        wide_ref[1 + r, :, 128:] = roll(packed[r % 2][64:], -16 * r, 1).astype(BF16)
    for r, place in enumerate((0, band_rows + 1)):
        wide_ref[place, :, 128:] = roll(packed[r][:64], -16 * r, 1).astype(BF16)
    wide_ref[0, :, :128] = above_ref[...]
    wide_ref[1 : band_rows + 1, :, :128] = x_ref[...]
    wide_ref[band_rows + 1, :, :128] = below_ref[...]
    weights = w_ref[...]
    rows = slope_ref.shape[0]
    halves, held = [], None
    for h in range(rows):
        y = dot(weights, wide_ref[h : h + 3].reshape(192, 256), (1, 0))
        pre = roll(y[:64], 1, 1) + y[64:128] + roll(y[128:], -1, 1)
        sig = sigmoid(pre)
        slope_ref[h] = slope_of(pre, sig).astype(BF16)
        active = pre * sig
        if h % 2:
            halves.append((held + active).astype(BF16))
        else:
            held = active
    pooled = dot(pool_ref[...], jnp.concatenate(halves, 0), (1, 1))
    stacked = jnp.concatenate(
        [
            jnp.concatenate(
                [pooled[:PITCH, u * 128 : u * 128 + 128], pooled[PITCH:, u * 128 : u * 128 + 128]], 1
            )
            for u in range(2)
        ],
        0,
    ).astype(BF16)
    ordered = dot(stacked, order_ref[...], (1, 0)).astype(BF16)
    for u in range(2):
        pooled_ref[u] = ordered[u * PITCH : u * PITCH + SENT]


def layer_two(og_ref, w_ref, *refs, bands):
    pieces, refs = refs[:bands], refs[bands:]
    terms, refs = refs[:bands], refs[bands:]
    map_ref, grad_ref, pack_ref = refs
    band = lax.axis_index("row")
    rows, _, filters = og_ref.shape
    count = rows * PITCH
    map_ref[0] = jnp.zeros((PITCH, 256), BF16)
    map_ref[rows + 1] = jnp.zeros((PITCH, 256), BF16)
    blank = jnp.zeros((PITCH - SENT, 256), BF16)
    for k in range(bands):
        for t in range(2):
            map_ref[1 + 2 * (band ^ k) + t] = jnp.concatenate([pieces[k][t], blank], 0)
    near = jnp.concatenate([map_ref[i : i + rows].reshape(count, 256) for i in range(3)], 1)
    y = dot(near, jnp.concatenate([w_ref[i] for i in range(3)], 1), (1, 1))
    pre = roll(y[:, :filters], 1, 0) + y[:, filters : 2 * filters] + roll(y[:, 2 * filters :], -1, 0)
    grad = og_ref[...].reshape(count, filters).astype(F32) * slope_of(pre, sigmoid(pre))
    grad = grad.astype(BF16)
    grad_ref[0] = jnp.zeros((PITCH, filters), BF16)
    grad_ref[rows + 1] = jnp.zeros((PITCH, filters), BF16)
    grad_ref[1 : rows + 1] = grad.reshape(rows, PITCH, filters)
    near = jnp.concatenate([grad_ref[2 - i : 2 - i + rows].reshape(count, filters) for i in range(3)], 1)
    weights = [
        jnp.concatenate([w_ref[i, j * filters : (j + 1) * filters] for j in range(3)], 1) for i in range(3)
    ]
    z = dot(near, jnp.concatenate(weights, 0), (1, 0))
    spread = roll(z[:, :256], -1 - REACH, 0) + roll(z[:, 256:512], -REACH, 0) + roll(z[:, 512:], 1 - REACH, 0)
    spread = spread.reshape(rows, PITCH, 256)
    odd = (lax.broadcasted_iota(jnp.int32, (8, 256), 1) & 1) == 1
    row = lax.broadcasted_iota(jnp.int32, (8, 256), 0)
    ends = [jnp.where(odd, spread[u - 1, 47:48], spread[u, 32:33]) for u in range(rows)]
    for p in range(rows // 2):
        shared = jnp.where(row == 0, ends[2 * p], jnp.where(row == 1, ends[2 * p + 1], 0.0))
        pack_ref[p] = jnp.concatenate([spread[2 * p, :32], shared, spread[2 * p + 1, :32]], 0).astype(BF16)
    for k in range(bands):
        terms[k][...] = pack_ref[band ^ k]


def filter_two_grads(map_ref, grad_ref, keep_ref, send_ref, all_ref):
    pair = lax.axis_index("pair")
    rows = map_ref.shape[0] - 2
    filters = grad_ref.shape[2]
    v = lax.broadcasted_iota(jnp.int32, (rows, PITCH, filters), 1)
    own = (v >= REACH) & (v < REACH + 32)
    wide = jnp.where(own, grad_ref[1 : rows + 1].astype(F32), 0.0).reshape(rows * PITCH, filters)
    cat = jnp.concatenate([roll(wide, -1, 0), wide, roll(wide, 1, 0)], 1).astype(BF16)
    taps = 3 * filters
    for i in range(3):
        part = dot(cat, map_ref[i : i + rows].reshape(rows * PITCH, 256), (0, 0))
        all_ref[i * taps : (i + 1) * taps] = part.astype(BF16)
    half = keep_ref.shape[0]
    keep_ref[...] = all_ref[pl.ds(pl.multiple_of(pair * half, 16), half)]
    send_ref[...] = all_ref[pl.ds(pl.multiple_of((1 - pair) * half, 16), half)]


def add_after(a_ref, b_ref, *refs):
    refs[-1][...] = (a_ref[...].astype(F32) + b_ref[...].astype(F32)).astype(BF16)


def add_halves(a_ref, b_ref, two_ref, one_ref):
    half = two_ref.shape[0]
    total = (a_ref[...].astype(F32) + b_ref[...].astype(F32)).astype(BF16)
    two_ref[...] = total[:half]
    one_ref[...] = total[half:]


def grad_pre_one(*refs, bands):
    terms, refs = refs[:bands], refs[bands:]
    slope_ref, wide_ref, pool_ref, order_ref, keep_two_ref, send_two_ref, *refs = refs
    g_ref, a_ref, b_ref, keep_ref, send_ref, part_ref = refs
    pair = lax.axis_index("pair")
    summed = terms[0][...].astype(F32)
    for k in range(1, bands):
        summed = summed + terms[k][...].astype(F32)
    blank = jnp.zeros((8, 256), F32)
    ends = summed[32:40]
    blocks = [summed[:32], ends, blank, summed[40:], roll(ends, -1, 0), blank]
    ordered = dot(jnp.concatenate(blocks, 0).astype(BF16), order_ref[...], (1, 1)).astype(BF16)
    pool = pool_ref[...]
    cats = []
    own = lax.broadcasted_iota(jnp.int32, (64, 256), 1) < 128
    for u in range(2):
        block = ordered[u * PITCH : (u + 1) * PITCH]
        up = dot(jnp.concatenate([block[:, :128], block[:, 128:]], 0), pool, (0, 0))
        for i in range(4):
            h = 4 * u + i
            g = (up[64 * (i // 2) : 64 * (i // 2) + 64] * slope_ref[h].astype(F32)).astype(BF16)
            g_ref[h] = g
            mine = jnp.where(own, g.astype(F32), 0.0)
            cats.append(jnp.concatenate([roll(mine, -1, 1), mine, roll(mine, 1, 1)], 0).astype(BF16))
    around = jnp.concatenate([wide_ref[h : h + 3].reshape(192, 256) for h in range(8)], 1)
    acc = dot(jnp.concatenate(cats, 1), around, (1, 1))
    even = (lax.axis_index("row") & 1) == 0
    first, last = g_ref[0].astype(F32), g_ref[7].astype(F32)
    a_ref[...] = jnp.where(even, last, first).astype(BF16)
    b_ref[...] = jnp.where(even, first, last).astype(BF16)
    part_ref[:96] = jnp.concatenate([acc[:96, :128], acc[96:, :128]], 1)
    part_ref[96:] = jnp.concatenate([acc[48 * q : 48 * q + 48, 128:] for q in range(4)], 1)
    half = keep_two_ref.shape[0]
    blank = jnp.zeros((TAIL - 72, 256), F32)
    for ref, two_ref, place in ((keep_ref, keep_two_ref, pair), (send_ref, send_two_ref, 1 - pair)):
        ref[:half] = two_ref[...]
        mine = part_ref[pl.ds(pl.multiple_of(place * 72, 8), 72)]
        ref[half:] = jnp.concatenate([mine, blank], 0).astype(BF16)


def layer_one_back(g_ref, a_ref, b_ref, w_ref, out_ref, done_ref, *, bands):
    above, below = beside(a_ref, b_ref, lax.axis_index("row"), bands)
    done_ref[...] = jnp.zeros(done_ref.shape, F32)
    lines = [above] + [g_ref[h] for h in range(8)] + [below]
    rows = []
    for h in range(8):
        z = dot(w_ref[...], jnp.concatenate(lines[h : h + 3], 0), (1, 0))
        rows.append((roll(z[:64], -1, 1) + z[64:128] + roll(z[128:], 1, 1))[:, :128])
    out_ref[...] = jnp.swapaxes(jnp.stack(rows, 0), 0, 1).astype(BF16)


def finish_two(mine_ref, other_ref, two_hbm, done_ref, two_ref, sems, *, scale):
    pair, half = lax.axis_index("pair"), mine_ref.shape[0]
    done_ref[...] = jnp.zeros(done_ref.shape, F32)
    copies = []
    for n, (ref, place) in enumerate(((mine_ref, pair), (other_ref, 1 - pair))):
        rows = pl.ds(pl.multiple_of(place * half, 16), half)
        two_ref[n] = ref[...].astype(F32) * scale
        copies.append(pltpu.make_async_copy(two_ref.at[n], two_hbm.at[rows], sems.at[n]))
        copies[-1].start()
    for copy in copies:
        copy.wait()


def finish_one(mine_ref, other_ref, _, out_ref, flat_ref, *, scale):
    pair = lax.axis_index("pair")
    for ref, place in ((mine_ref, pair), (other_ref, 1 - pair)):
        flat_ref[pl.ds(pl.multiple_of(place * 72, 8), 72)] = ref[:72].astype(F32) * scale
    out_ref[0, :96] = flat_ref[:96, :64]
    out_ref[1, :96] = flat_ref[:96, 64:128]
    out_ref[0, 96:] = flat_ref[:96, 128:192]
    out_ref[1, 96:] = flat_ref[:96, 192:]
    for q in range(4):
        out_ref[2, 48 * q : 48 * q + 48] = flat_ref[96:, 64 * q : 64 * q + 64]


def even_swap(values, axis, count):
    return lax.ppermute(values, axis, [(n, n ^ 1) for n in range(count)])


def odd_partner(place):
    return place - 1 if place % 2 == 0 else place + 1


def odd_row_swap(values):
    bands, cores = lax.axis_size("row"), lax.axis_size("pair")
    steps = []
    for n in range(bands):
        for p in range(cores):
            to = (n, p ^ 1) if n in (0, bands - 1) else (odd_partner(n), p)
            steps.append((n * cores + p, to[0] * cores + to[1]))
    return lax.ppermute(values, ("row", "pair"), steps)


def odd_strip_swap(values):
    groups, strips = lax.axis_size("grp"), lax.axis_size(COLS)
    steps = []
    for g in range(groups):
        for n in range(strips):
            to = ((g + 1) % groups, n) if n in (0, strips - 1) else (g, odd_partner(n))
            steps.append((g * strips + n, to[0] * strips + to[1]))
    return lax.ppermute(values, ("grp",) + COLS, steps)


def xor_swap(values, axis, count, k):
    return lax.ppermute(values, axis, [(n, n ^ k) for n in range(count)])


def row_swaps(values, bands):
    order = sorted(range(1, bands), key=lambda k: (k < bands // 2, k))
    moved = {k: xor_swap(values[k], "row", bands, k) for k in order}
    return [moved[k] for k in range(1, bands)]


def added(a, b, *after):
    (total,) = whole_call(add_after, [shaped(a.shape)], [a, b, *after], 0, after=len(after))
    return total


def sum_but_last(part, axis, count):
    step = 1
    while 2 * step < count:
        part = added(part, xor_swap(part, axis, count, step))
        step *= 2
    return part, xor_swap(part, axis, count, step)


def local(features_in, filters_one, filters_two, out_grad):
    channels, band_rows, strip_cols = features_in.shape
    filters, own_cols, pooled_rows = out_grad.shape
    bands = lax.axis_size("row")
    strips = lax.axis_size(COLS)
    band = lax.axis_index("row")
    strip = lax.axis_index(COLS)
    pair = lax.axis_index("pair")
    height, width = band_rows * bands, strip_cols * strips
    total = own_cols * strips

    taps_one = jnp.transpose(filters_one, (1, 2, 0, 3)).reshape(3, 3 * channels, channels)
    back_one = jnp.transpose(filters_one[:, ::-1], (2, 3, 1, 0)).reshape(3 * channels, 3 * channels)
    taps_two = jnp.transpose(filters_two, (1, 2, 0, 3)).reshape(3, 3 * filters, 4 * channels)

    og = jnp.transpose(out_grad, (1, 2, 0))
    edge = REACH - 1
    x = jnp.transpose(features_in, (1, 0, 2))
    even = band % 2 == 0
    to_a, to_b = jnp.where(even, x[-1], x[0]), jnp.where(even, x[0], x[-1])
    head, tail = og[:edge], og[-edge:]
    joined_one, pool, pool_back, order = whole_call(
        functools.partial(constants, total=total),
        [shaped((3 * channels, 3 * channels))] + [shaped((2 * PITCH, 256))] * 2 + [shaped((256, 256))],
        [taps_one],
        10**8,
    )
    head, tail = head.reshape(-1, 128), tail.reshape(-1, 128)
    own_a, own_b = whole_call(
        pack_own, [shaped((channels + head.shape[0], 128))] * 2, [x, head, tail], 10**8
    )
    to_a, to_b, above, below = whole_call(
        functools.partial(pack_borders, bands=bands),
        [shaped((2 * channels + head.shape[0], 128))] * 2 + [shaped((channels, strip_cols))] * 2,
        [even_swap(to_a, "row", bands), odd_row_swap(to_b), own_a, own_b],
        1,
    )
    side_a, side_b = even_swap(to_a, COLS, strips), odd_strip_swap(to_b)
    pooled, slope, wide = whole_call(
        functools.partial(layer_one, strips=strips),
        [
            shaped((2, SENT, 4 * channels)),
            shaped((band_rows, channels, 256)),
            shaped((band_rows + 2, channels, 256)),
        ],
        [x, above, below, side_a, side_b, joined_one, pool, order],
        2 * band_rows * 192 * 192 * 256,
    )
    pieces = [pooled] + row_swaps([pooled] * bands, bands)

    even = strip % 2 == 0
    ends = [side[2 * channels :].reshape(og[:edge].shape) for side in (side_a, side_b)]
    ends[1] = jnp.where((strip == 0) | (strip == strips - 1), 0, ends[1])
    before, after = jnp.where(even, ends[1], ends[0]), jnp.where(even, ends[0], ends[1])
    og = jnp.concatenate([before, og, after], 0)
    og = jnp.pad(og, ((1, PITCH - own_cols - 2 * REACH + 1), (0, 0), (0, 0)))
    og = jnp.transpose(og, (1, 0, 2))

    count = pooled_rows * PITCH
    *terms, pooled_map, grad_map = whole_call(
        functools.partial(layer_two, bands=bands),
        [shaped((72, 4 * channels))] * bands
        + [shaped((pooled_rows + 2, PITCH, 4 * channels)), shaped((pooled_rows + 2, PITCH, filters))],
        [og, taps_two] + pieces,
        4 * count * 9 * filters * 4 * channels,
        scratch=[pltpu.VMEM((bands, 72, 4 * channels), BF16)],
    )
    received = [terms[0]] + row_swaps(terms, bands)

    half = 9 * filters // 2
    keep_two, send_two = whole_call(
        filter_two_grads,
        [shaped((half, 4 * channels))] * 2,
        [pooled_map, grad_map],
        2 * count * 9 * filters * 4 * channels,
        scratch=[pltpu.VMEM((2 * half, 4 * channels), BF16)],
    )
    g, up_a, up_b, keep, send = whole_call(
        functools.partial(grad_pre_one, bands=bands),
        [shaped((band_rows, channels, 256))]
        + [shaped((channels, 256))] * 2
        + [shaped((half + TAIL, 256))] * 2,
        received + [slope, wide, pool_back, order, keep_two, send_two],
        2 * 8 * 192 * 192 * 256,
        scratch=[pltpu.VMEM((144, 256), F32)],
    )
    two, one = whole_call(
        add_halves,
        [shaped((half, 256)), shaped((TAIL, 256))],
        [keep, even_swap(send, "pair", 2)],
        0,
    )
    columns = lax.axis_size("col")
    two, two_more = sum_but_last(two, "col", columns)
    one, one_more = sum_but_last(one, "row", bands)
    input_grad, done = whole_call(
        functools.partial(layer_one_back, bands=bands),
        [shaped(features_in.shape), shaped((8, 128), F32)],
        [g, even_swap(up_a, "row", bands), odd_row_swap(up_b), back_one],
        2 * band_rows * 192 * 192 * 256,
    )
    one = added(one, one_more, done)
    mine_two = added(two, two_more, one)
    grad_two, done = whole_call(
        functools.partial(finish_two, scale=1.0 / math.sqrt(pooled_rows * total)),
        [shaped((2 * half, 256), F32), shaped((8, 128), F32)],
        [mine_two, even_swap(mine_two, "pair", 2)],
        10**8,
        scratch=[pltpu.VMEM((2, half, 256), F32), pltpu.SemaphoreType.DMA((2,))],
        out_spaces=[pl.ANY, pltpu.VMEM],
    )
    mine_one = added(*sum_but_last(one, "col", columns))
    (grad_one,) = whole_call(
        functools.partial(finish_one, scale=1.0 / math.sqrt(height * width)),
        [shaped((3, 3 * channels, channels), F32)],
        [mine_one, even_swap(mine_one, "pair", 2), done],
        1,
        scratch=[pltpu.VMEM((144, 256), F32)],
        after=1,
    )
    grad_two = jnp.transpose(grad_two.reshape(3, 3, filters, 4 * channels), (2, 0, 1, 3))
    grad_one = jnp.transpose(grad_one.reshape(3, 3, channels, channels), (2, 0, 1, 3))
    return (input_grad, grad_one, grad_two)


def solution(mesh):
    in_specs = (
        P("grp", "row", ("col", "pair")),
        P(),
        P("row", None, None, None),
        P(("grp", "row"), ("col", "pair"), None),
    )
    out_specs = (
        P("grp", "row", ("col", "pair")),
        P("grp", None, None, None),
        P(("grp", "row"), None, None, None),
    )
    return jax.shard_map(local, mesh=mesh, in_specs=in_specs, out_specs=out_specs, check_vma=False)
```

```python
import functools
import math

import jax
import jax.numpy as jnp
from jax import lax
from jax.experimental import pallas as pl
from jax.experimental.pallas import tpu as pltpu
from jax.sharding import PartitionSpec as P

BF16 = jnp.bfloat16
F32 = jnp.float32
COLS = ("col", "pair")
REACH = 3
TAIL = 80
PITCH = 48
SENT = 40


def dot(a, b, contract):
    return lax.dot_general(a, b, ((contract[:1], contract[1:]), ((), ())), preferred_element_type=F32)


def whole_call(body, outs, operands, flops, scratch=(), after=0, out_spaces=None):
    specs = [
        pl.BlockSpec(memory_space=pltpu.VMEM) for _ in range(len(operands) - after)
    ] + [pl.BlockSpec(memory_space=pl.ANY)] * after
    sizes = [math.prod(a.shape) * a.dtype.itemsize for a in tuple(operands) + tuple(outs)]
    moved = sum(sizes) if flops else 0
    return pl.pallas_call(
        body,
        out_shape=outs,
        in_specs=specs,
        out_specs=[pl.BlockSpec(memory_space=space) for space in out_spaces or [pltpu.VMEM] * len(outs)],
        scratch_shapes=list(scratch),
        cost_estimate=pl.CostEstimate(flops=flops, bytes_accessed=moved, transcendentals=0),
        compiler_params=pltpu.CompilerParams(vmem_limit_bytes=40 * 1024 * 1024),
    )(*operands)


def strip_index():
    return lax.axis_index("col") * lax.axis_size("pair") + lax.axis_index("pair")


def shaped(shape, dtype=BF16):
    return jax.ShapeDtypeStruct(shape, dtype)


def roll(values, amount, axis):
    return pltpu.roll(values, amount % values.shape[axis], axis)


def sigmoid(values):
    return 0.5 + 0.5 * jnp.tanh(0.5 * values)


def slope_of(values, sig):
    return sig * (1.0 + values * (1.0 - sig))


def pool_matrix(strip, total, back=False):
    row = lax.broadcasted_iota(jnp.int32, (2 * PITCH, 256), 0)
    lane = lax.broadcasted_iota(jnp.int32, (2 * PITCH, 256), 1)
    half = (row >= PITCH).astype(jnp.int32)
    n = row - half * PITCH
    if back:
        v, most = jnp.where((n == 32) & (half == 1), -1, n), 33
    else:
        v, most = n - REACH, 32 + 2 * REACH
    near = jnp.bitwise_and(lane - 4 * v - 2 * half, 255) < 2
    place = strip * 32 + v
    keep = near & (n < most) & (place >= 0) & (place < total)
    return jnp.where(keep, 0.25, 0.0).astype(BF16)


def order_matrix():
    row = lax.broadcasted_iota(jnp.int32, (256, 256), 0)
    lane = lax.broadcasted_iota(jnp.int32, (256, 256), 1)
    j, i, c = row >> 7, (row >> 6) & 1, row & 63
    return jnp.where(lane == 4 * c + 2 * i + j, 1.0, 0.0).astype(BF16)


def constants(w_ref, joined_ref, pool_ref, back_ref, order_ref, *, total):
    joined_ref[...] = jnp.concatenate([w_ref[0], w_ref[1], w_ref[2]], axis=1)
    pool_ref[...] = pool_matrix(strip_index(), total)
    back_ref[...] = pool_matrix(strip_index(), total, back=True)
    order_ref[...] = order_matrix()


def beside(a_ref, b_ref, place, count):
    even = (place & 1) == 0
    a = a_ref[...].astype(F32)
    b = jnp.where((place > 0) & (place < count - 1), b_ref[...].astype(F32), 0.0)
    return jnp.where(even, b, a).astype(BF16), jnp.where(even, a, b).astype(BF16)


def pack_row(row, r, slot, head, tail):
    turned = roll(row.astype(F32), 16 * r, 1)
    return jnp.where(slot == r, turned, head), jnp.where(slot == (r - 1) % 8, turned, tail)


def pack_own(x_ref, head_ref, tail_ref, a_ref, b_ref):
    even = (strip_index() & 1) == 0
    slot = lax.broadcasted_iota(jnp.int32, (64, 128), 1) >> 4
    head = tail = jnp.zeros((64, 128), F32)
    for r in range(x_ref.shape[0]):
        head, tail = pack_row(x_ref[r], r, slot, head, tail)
    a_ref[:64] = jnp.where(even, tail, head).astype(BF16)
    b_ref[:64] = jnp.where(even, head, tail).astype(BF16)
    first, last = head_ref[...].astype(F32), tail_ref[...].astype(F32)
    a_ref[64:] = jnp.where(even, last, first).astype(BF16)
    b_ref[64:] = jnp.where(even, first, last).astype(BF16)


def pack_borders(up_a_ref, up_b_ref, own_a_ref, own_b_ref, a_ref, b_ref, above_ref, below_ref, *, bands):
    even = (strip_index() & 1) == 0
    above_ref[...], below_ref[...] = beside(up_a_ref, up_b_ref, lax.axis_index("row"), bands)
    slot = lax.broadcasted_iota(jnp.int32, (64, 128), 1) >> 4
    head = tail = jnp.zeros((64, 128), F32)
    for r, ref in enumerate((above_ref, below_ref)):
        head, tail = pack_row(ref[...], r, slot, head, tail)
    a_ref[:64] = jnp.where(even, tail, head).astype(BF16)
    b_ref[:64] = jnp.where(even, head, tail).astype(BF16)
    a_ref[64:] = own_a_ref[...]
    b_ref[64:] = own_b_ref[...]


def layer_one(
    x_ref,
    above_ref,
    below_ref,
    a_ref,
    b_ref,
    w_ref,
    pool_ref,
    order_ref,
    pooled_ref,
    slope_ref,
    wide_ref,
    *,
    strips,
):
    strip = strip_index()
    band_rows = x_ref.shape[0]
    slot = lax.broadcasted_iota(jnp.int32, (128, 128), 1) >> 4
    inner = (strip > 0) & (strip < strips - 1)
    sides = a_ref[:128].astype(F32), jnp.where(inner, b_ref[:128].astype(F32), 0.0)
    from_a = ((slot ^ strip) & 1) == 0
    packed = jnp.where(from_a, *sides), jnp.where(from_a, *sides[::-1])
    for r in range(band_rows):
        wide_ref[1 + r, :, 128:] = roll(packed[r % 2][64:], -16 * r, 1).astype(BF16)
    for r, place in enumerate((0, band_rows + 1)):
        wide_ref[place, :, 128:] = roll(packed[r][:64], -16 * r, 1).astype(BF16)
    wide_ref[0, :, :128] = above_ref[...]
    wide_ref[1 : band_rows + 1, :, :128] = x_ref[...]
    wide_ref[band_rows + 1, :, :128] = below_ref[...]
    weights = w_ref[...]
    rows = slope_ref.shape[0]
    halves, held = [], None
    for h in range(rows):
        y = dot(weights, wide_ref[h : h + 3].reshape(192, 256), (1, 0))
        pre = roll(y[:64], 1, 1) + y[64:128] + roll(y[128:], -1, 1)
        sig = sigmoid(pre)
        slope_ref[h] = slope_of(pre, sig).astype(BF16)
        active = pre * sig
        if h % 2:
            halves.append((held + active).astype(BF16))
        else:
            held = active
    pooled = dot(pool_ref[...], jnp.concatenate(halves, 0), (1, 1))
    stacked = jnp.concatenate(
        [
            jnp.concatenate(
                [pooled[:PITCH, u * 128 : u * 128 + 128], pooled[PITCH:, u * 128 : u * 128 + 128]], 1
            )
            for u in range(2)
        ],
        0,
    ).astype(BF16)
    ordered = dot(stacked, order_ref[...], (1, 0)).astype(BF16)
    for u in range(2):
        pooled_ref[u] = ordered[u * PITCH : u * PITCH + SENT]


def layer_two(og_ref, w_ref, *refs, bands):
    pieces, refs = refs[:bands], refs[bands:]
    terms, refs = refs[:bands], refs[bands:]
    map_ref, grad_ref, pack_ref = refs
    band = lax.axis_index("row")
    rows, _, filters = og_ref.shape
    count = rows * PITCH
    map_ref[0] = jnp.zeros((PITCH, 256), BF16)
    map_ref[rows + 1] = jnp.zeros((PITCH, 256), BF16)
    blank = jnp.zeros((PITCH - SENT, 256), BF16)
    for k, piece in zip(row_order(bands), pieces):
        for t in range(2):
            map_ref[1 + 2 * (band ^ k) + t] = jnp.concatenate([piece[t], blank], 0)
    near = jnp.concatenate([map_ref[i : i + rows].reshape(count, 256) for i in range(3)], 1)
    y = dot(near, jnp.concatenate([w_ref[i] for i in range(3)], 1), (1, 1))
    pre = roll(y[:, :filters], 1, 0) + y[:, filters : 2 * filters] + roll(y[:, 2 * filters :], -1, 0)
    grad = og_ref[...].reshape(count, filters).astype(F32) * slope_of(pre, sigmoid(pre))
    grad = grad.astype(BF16)
    grad_ref[0] = jnp.zeros((PITCH, filters), BF16)
    grad_ref[rows + 1] = jnp.zeros((PITCH, filters), BF16)
    grad_ref[1 : rows + 1] = grad.reshape(rows, PITCH, filters)
    near = jnp.concatenate([grad_ref[2 - i : 2 - i + rows].reshape(count, filters) for i in range(3)], 1)
    weights = [
        jnp.concatenate([w_ref[i, j * filters : (j + 1) * filters] for j in range(3)], 1) for i in range(3)
    ]
    z = dot(near, jnp.concatenate(weights, 0), (1, 0))
    spread = roll(z[:, :256], -1 - REACH, 0) + roll(z[:, 256:512], -REACH, 0) + roll(z[:, 512:], 1 - REACH, 0)
    spread = spread.reshape(rows, PITCH, 256)
    odd = (lax.broadcasted_iota(jnp.int32, (8, 256), 1) & 1) == 1
    row = lax.broadcasted_iota(jnp.int32, (8, 256), 0)
    ends = [jnp.where(odd, spread[u - 1, 47:48], spread[u, 32:33]) for u in range(rows)]
    for p in range(rows // 2):
        shared = jnp.where(row == 0, ends[2 * p], jnp.where(row == 1, ends[2 * p + 1], 0.0))
        pack_ref[p] = jnp.concatenate([spread[2 * p, :32], shared, spread[2 * p + 1, :32]], 0).astype(BF16)
    for k in range(bands):
        terms[k][...] = pack_ref[band ^ k]


def filter_two_grads(map_ref, grad_ref, keep_ref, send_ref, all_ref):
    pair = lax.axis_index("pair")
    rows = map_ref.shape[0] - 2
    filters = grad_ref.shape[2]
    v = lax.broadcasted_iota(jnp.int32, (rows, PITCH, filters), 1)
    own = (v >= REACH) & (v < REACH + 32)
    wide = jnp.where(own, grad_ref[1 : rows + 1].astype(F32), 0.0).reshape(rows * PITCH, filters)
    cat = jnp.concatenate([roll(wide, -1, 0), wide, roll(wide, 1, 0)], 1).astype(BF16)
    taps = 3 * filters
    for i in range(3):
        part = dot(cat, map_ref[i : i + rows].reshape(rows * PITCH, 256), (0, 0))
        all_ref[i * taps : (i + 1) * taps] = part.astype(BF16)
    half = keep_ref.shape[0]
    keep_ref[...] = all_ref[pl.ds(pl.multiple_of(pair * half, 16), half)]
    send_ref[...] = all_ref[pl.ds(pl.multiple_of((1 - pair) * half, 16), half)]


def add_after(a_ref, b_ref, *refs):
    refs[-1][...] = (a_ref[...].astype(F32) + b_ref[...].astype(F32)).astype(BF16)


def sum_rows(*refs):
    *refs, _, _, out_ref = refs
    terms = dict(zip(row_order(len(refs)), (ref[...].astype(F32) for ref in refs)))
    terms = [terms[k] for k in range(len(refs))]
    while len(terms) > 1:
        terms = [a + b for a, b in zip(terms[::2], terms[1::2])]
    out_ref[...] = terms[0].astype(BF16)


def add_halves(a_ref, b_ref, two_ref, one_ref):
    half = two_ref.shape[0]
    total = (a_ref[...].astype(F32) + b_ref[...].astype(F32)).astype(BF16)
    two_ref[...] = total[:half]
    one_ref[...] = total[half:]


def grad_pre_one(*refs, bands):
    terms, refs = refs[:bands], refs[bands:]
    slope_ref, wide_ref, pool_ref, order_ref, keep_two_ref, send_two_ref, *refs = refs
    g_ref, a_ref, b_ref, keep_ref, send_ref, part_ref = refs
    pair = lax.axis_index("pair")
    summed = terms[0][...].astype(F32)
    for k in range(1, bands):
        summed = summed + terms[k][...].astype(F32)
    blank = jnp.zeros((8, 256), F32)
    ends = summed[32:40]
    blocks = [summed[:32], ends, blank, summed[40:], roll(ends, -1, 0), blank]
    ordered = dot(jnp.concatenate(blocks, 0).astype(BF16), order_ref[...], (1, 1)).astype(BF16)
    pool = pool_ref[...]
    cats = []
    own = lax.broadcasted_iota(jnp.int32, (64, 256), 1) < 128
    for u in range(2):
        block = ordered[u * PITCH : (u + 1) * PITCH]
        up = dot(jnp.concatenate([block[:, :128], block[:, 128:]], 0), pool, (0, 0))
        for i in range(4):
            h = 4 * u + i
            g = (up[64 * (i // 2) : 64 * (i // 2) + 64] * slope_ref[h].astype(F32)).astype(BF16)
            g_ref[h] = g
            mine = jnp.where(own, g.astype(F32), 0.0)
            cats.append(jnp.concatenate([roll(mine, -1, 1), mine, roll(mine, 1, 1)], 0).astype(BF16))
    around = jnp.concatenate([wide_ref[h : h + 3].reshape(192, 256) for h in range(8)], 1)
    acc = dot(jnp.concatenate(cats, 1), around, (1, 1))
    even = (lax.axis_index("row") & 1) == 0
    first, last = g_ref[0].astype(F32), g_ref[7].astype(F32)
    a_ref[...] = jnp.where(even, last, first).astype(BF16)
    b_ref[...] = jnp.where(even, first, last).astype(BF16)
    part_ref[:96] = jnp.concatenate([acc[:96, :128], acc[96:, :128]], 1)
    part_ref[96:] = jnp.concatenate([acc[48 * q : 48 * q + 48, 128:] for q in range(4)], 1)
    half = keep_two_ref.shape[0]
    blank = jnp.zeros((TAIL - 72, 256), F32)
    for ref, two_ref, place in ((keep_ref, keep_two_ref, pair), (send_ref, send_two_ref, 1 - pair)):
        ref[:half] = two_ref[...]
        mine = part_ref[pl.ds(pl.multiple_of(place * 72, 8), 72)]
        ref[half:] = jnp.concatenate([mine, blank], 0).astype(BF16)


def layer_one_back(g_ref, a_ref, b_ref, w_ref, out_ref, done_ref, *, bands):
    above, below = beside(a_ref, b_ref, lax.axis_index("row"), bands)
    done_ref[...] = jnp.zeros(done_ref.shape, F32)
    lines = [above] + [g_ref[h] for h in range(8)] + [below]
    rows = []
    for h in range(8):
        z = dot(w_ref[...], jnp.concatenate(lines[h : h + 3], 0), (1, 0))
        rows.append((roll(z[:64], -1, 1) + z[64:128] + roll(z[128:], 1, 1))[:, :128])
    out_ref[...] = jnp.swapaxes(jnp.stack(rows, 0), 0, 1).astype(BF16)


def finish_two(mine_ref, other_ref, two_hbm, done_ref, two_ref, sems, *, scale):
    pair, half = lax.axis_index("pair"), mine_ref.shape[0]
    done_ref[...] = jnp.zeros(done_ref.shape, F32)
    copies = []
    for n, (ref, place) in enumerate(((mine_ref, pair), (other_ref, 1 - pair))):
        rows = pl.ds(pl.multiple_of(place * half, 16), half)
        two_ref[n] = ref[...].astype(F32) * scale
        copies.append(pltpu.make_async_copy(two_ref.at[n], two_hbm.at[rows], sems.at[n]))
        copies[-1].start()
    for copy in copies:
        copy.wait()


def finish_one(mine_ref, other_ref, _, out_ref, flat_ref, *, scale):
    pair = lax.axis_index("pair")
    for ref, place in ((mine_ref, pair), (other_ref, 1 - pair)):
        flat_ref[pl.ds(pl.multiple_of(place * 72, 8), 72)] = ref[:72].astype(F32) * scale
    out_ref[0, :96] = flat_ref[:96, :64]
    out_ref[1, :96] = flat_ref[:96, 64:128]
    out_ref[0, 96:] = flat_ref[:96, 128:192]
    out_ref[1, 96:] = flat_ref[:96, 192:]
    for q in range(4):
        out_ref[2, 48 * q : 48 * q + 48] = flat_ref[96:, 64 * q : 64 * q + 64]


def even_swap(values, axis, count):
    return lax.ppermute(values, axis, [(n, n ^ 1) for n in range(count)])


def odd_partner(place):
    return place - 1 if place % 2 == 0 else place + 1


def odd_row_swap(values):
    bands, cores = lax.axis_size("row"), lax.axis_size("pair")
    steps = []
    for n in range(bands):
        for p in range(cores):
            to = (n, p ^ 1) if n in (0, bands - 1) else (odd_partner(n), p)
            steps.append((n * cores + p, to[0] * cores + to[1]))
    return lax.ppermute(values, ("row", "pair"), steps)


def odd_strip_swap(values):
    groups, strips = lax.axis_size("grp"), lax.axis_size(COLS)
    steps = []
    for g in range(groups):
        for n in range(strips):
            to = ((g + 1) % groups, n) if n in (0, strips - 1) else (g, odd_partner(n))
            steps.append((g * strips + n, to[0] * strips + to[1]))
    return lax.ppermute(values, ("grp",) + COLS, steps)


def xor_swap(values, axis, count, k):
    return lax.ppermute(values, axis, [(n, n ^ k) for n in range(count)])


def row_order(bands):
    return [0] + sorted(range(1, bands), key=lambda k: (k < bands // 2, k))


def row_swaps(values, bands):
    order = row_order(bands)
    return [values[0]] + [xor_swap(values[k], "row", bands, k) for k in order[1:]]


def added(a, b, *after):
    (total,) = whole_call(add_after, [shaped(a.shape)], [a, b, *after], 0, after=len(after))
    return total


def sum_but_last(part, axis, count):
    step = 1
    while 2 * step < count:
        part = added(part, xor_swap(part, axis, count, step))
        step *= 2
    return part, xor_swap(part, axis, count, step)


def local(features_in, filters_one, filters_two, out_grad):
    channels, band_rows, strip_cols = features_in.shape
    filters, own_cols, pooled_rows = out_grad.shape
    bands = lax.axis_size("row")
    strips = lax.axis_size(COLS)
    band = lax.axis_index("row")
    strip = lax.axis_index(COLS)
    pair = lax.axis_index("pair")
    height, width = band_rows * bands, strip_cols * strips
    total = own_cols * strips

    taps_one = jnp.transpose(filters_one, (1, 2, 0, 3)).reshape(3, 3 * channels, channels)
    back_one = jnp.transpose(filters_one[:, ::-1], (2, 3, 1, 0)).reshape(3 * channels, 3 * channels)
    taps_two = jnp.transpose(filters_two, (1, 2, 0, 3)).reshape(3, 3 * filters, 4 * channels)

    og = jnp.transpose(out_grad, (1, 2, 0))
    edge = REACH - 1
    x = jnp.transpose(features_in, (1, 0, 2))
    even = band % 2 == 0
    to_a, to_b = jnp.where(even, x[-1], x[0]), jnp.where(even, x[0], x[-1])
    head, tail = og[:edge], og[-edge:]
    joined_one, pool, pool_back, order = whole_call(
        functools.partial(constants, total=total),
        [shaped((3 * channels, 3 * channels))] + [shaped((2 * PITCH, 256))] * 2 + [shaped((256, 256))],
        [taps_one],
        10**8,
    )
    head, tail = head.reshape(-1, 128), tail.reshape(-1, 128)
    own_a, own_b = whole_call(
        pack_own, [shaped((channels + head.shape[0], 128))] * 2, [x, head, tail], 10**8
    )
    to_a, to_b, above, below = whole_call(
        functools.partial(pack_borders, bands=bands),
        [shaped((2 * channels + head.shape[0], 128))] * 2 + [shaped((channels, strip_cols))] * 2,
        [even_swap(to_a, "row", bands), odd_row_swap(to_b), own_a, own_b],
        1,
    )
    side_a, side_b = even_swap(to_a, COLS, strips), odd_strip_swap(to_b)
    pooled, slope, wide = whole_call(
        functools.partial(layer_one, strips=strips),
        [
            shaped((2, SENT, 4 * channels)),
            shaped((band_rows, channels, 256)),
            shaped((band_rows + 2, channels, 256)),
        ],
        [x, above, below, side_a, side_b, joined_one, pool, order],
        2 * band_rows * 192 * 192 * 256,
    )
    pieces = row_swaps([pooled] * bands, bands)

    even = strip % 2 == 0
    ends = [side[2 * channels :].reshape(og[:edge].shape) for side in (side_a, side_b)]
    ends[1] = jnp.where((strip == 0) | (strip == strips - 1), 0, ends[1])
    before, after = jnp.where(even, ends[1], ends[0]), jnp.where(even, ends[0], ends[1])
    og = jnp.concatenate([before, og, after], 0)
    og = jnp.pad(og, ((1, PITCH - own_cols - 2 * REACH + 1), (0, 0), (0, 0)))
    og = jnp.transpose(og, (1, 0, 2))

    count = pooled_rows * PITCH
    *terms, pooled_map, grad_map = whole_call(
        functools.partial(layer_two, bands=bands),
        [shaped((72, 4 * channels))] * bands
        + [shaped((pooled_rows + 2, PITCH, 4 * channels)), shaped((pooled_rows + 2, PITCH, filters))],
        [og, taps_two] + pieces,
        4 * count * 9 * filters * 4 * channels,
        scratch=[pltpu.VMEM((bands, 72, 4 * channels), BF16)],
    )
    received = row_swaps(terms, bands)

    half = 9 * filters // 2
    keep_two, send_two = whole_call(
        filter_two_grads,
        [shaped((half, 4 * channels))] * 2,
        [pooled_map, grad_map],
        2 * count * 9 * filters * 4 * channels,
        scratch=[pltpu.VMEM((2 * half, 4 * channels), BF16)],
    )
    g, up_a, up_b, keep, send = whole_call(
        functools.partial(grad_pre_one, bands=bands),
        [shaped((band_rows, channels, 256))]
        + [shaped((channels, 256))] * 2
        + [shaped((half + TAIL, 256))] * 2,
        received + [slope, wide, pool_back, order, keep_two, send_two],
        2 * 8 * 192 * 192 * 256,
        scratch=[pltpu.VMEM((144, 256), F32)],
    )
    two, one = whole_call(
        add_halves,
        [shaped((half, 256)), shaped((TAIL, 256))],
        [keep, even_swap(send, "pair", 2)],
        0,
    )
    columns = lax.axis_size("col")
    two, two_more = sum_but_last(two, "col", columns)
    ones = row_swaps([one] * bands, bands)
    up_a, up_b = even_swap(up_a, "row", bands), odd_row_swap(up_b)
    (one,) = whole_call(sum_rows, [shaped(one.shape)], ones + [up_a, up_b], 0, after=2)
    input_grad, done = whole_call(
        functools.partial(layer_one_back, bands=bands),
        [shaped(features_in.shape), shaped((8, 128), F32)],
        [g, up_a, up_b, back_one],
        2 * band_rows * 192 * 192 * 256,
    )
    mine_two = added(two, two_more, one)
    grad_two, wrote = whole_call(
        functools.partial(finish_two, scale=1.0 / math.sqrt(pooled_rows * total)),
        [shaped((2 * half, 256), F32), shaped((8, 128), F32)],
        [mine_two, even_swap(mine_two, "pair", 2)],
        10**8,
        scratch=[pltpu.VMEM((2, half, 256), F32), pltpu.SemaphoreType.DMA((2,))],
        out_spaces=[pl.ANY, pltpu.VMEM],
    )
    mine_one = added(*sum_but_last(one, "col", columns), done)
    (grad_one,) = whole_call(
        functools.partial(finish_one, scale=1.0 / math.sqrt(height * width)),
        [shaped((3, 3 * channels, channels), F32)],
        [mine_one, even_swap(mine_one, "pair", 2), wrote],
        1,
        scratch=[pltpu.VMEM((144, 256), F32)],
        after=1,
    )
    grad_two = jnp.transpose(grad_two.reshape(3, 3, filters, 4 * channels), (2, 0, 1, 3))
    grad_one = jnp.transpose(grad_one.reshape(3, 3, channels, channels), (2, 0, 1, 3))
    return (input_grad, grad_one, grad_two)


def solution(mesh):
    in_specs = (
        P("grp", "row", ("col", "pair")),
        P(),
        P("row", None, None, None),
        P(("grp", "row"), ("col", "pair"), None),
    )
    out_specs = (
        P("grp", "row", ("col", "pair")),
        P("grp", None, None, None),
        P(("grp", "row"), None, None, None),
    )
    return jax.shard_map(local, mesh=mesh, in_specs=in_specs, out_specs=out_specs, check_vma=False)
```

```python
import functools
import math

import jax
import jax.numpy as jnp
from jax import lax
from jax.experimental import pallas as pl
from jax.experimental.pallas import tpu as pltpu
from jax.sharding import PartitionSpec as P

BF16 = jnp.bfloat16
F32 = jnp.float32
COLS = ("col", "pair")
REACH = 3
HALF_ONE = 72
PITCH = 48
SENT = 40


def dot(a, b, contract):
    return lax.dot_general(a, b, ((contract[:1], contract[1:]), ((), ())), preferred_element_type=F32)


def whole_call(body, outs, operands, flops, scratch=(), after=0, out_spaces=None):
    specs = [
        pl.BlockSpec(memory_space=pltpu.VMEM) for _ in range(len(operands) - after)
    ] + [pl.BlockSpec(memory_space=pl.ANY)] * after
    sizes = [math.prod(a.shape) * a.dtype.itemsize for a in tuple(operands) + tuple(outs)]
    moved = sum(sizes) if flops else 0
    return pl.pallas_call(
        body,
        out_shape=outs,
        in_specs=specs,
        out_specs=[pl.BlockSpec(memory_space=space) for space in out_spaces or [pltpu.VMEM] * len(outs)],
        scratch_shapes=list(scratch),
        cost_estimate=pl.CostEstimate(flops=flops, bytes_accessed=moved, transcendentals=0),
        compiler_params=pltpu.CompilerParams(vmem_limit_bytes=40 * 1024 * 1024),
    )(*operands)


def strip_index():
    return lax.axis_index("col") * lax.axis_size("pair") + lax.axis_index("pair")


def shaped(shape, dtype=BF16):
    return jax.ShapeDtypeStruct(shape, dtype)


def roll(values, amount, axis):
    return pltpu.roll(values, amount % values.shape[axis], axis)


def sigmoid(values):
    return 0.5 + 0.5 * jnp.tanh(0.5 * values)


def slope_of(values, sig):
    return sig * (1.0 + values * (1.0 - sig))


def pool_matrix(strip, total, back=False):
    row = lax.broadcasted_iota(jnp.int32, (2 * PITCH, 256), 0)
    lane = lax.broadcasted_iota(jnp.int32, (2 * PITCH, 256), 1)
    half = (row >= PITCH).astype(jnp.int32)
    n = row - half * PITCH
    if back:
        v, most = jnp.where((n == 32) & (half == 1), -1, n), 33
    else:
        v, most = n - REACH, 32 + 2 * REACH
    near = jnp.bitwise_and(lane - 4 * v - 2 * half, 255) < 2
    place = strip * 32 + v
    keep = near & (n < most) & (place >= 0) & (place < total)
    return jnp.where(keep, 0.25, 0.0).astype(BF16)


def order_matrix():
    row = lax.broadcasted_iota(jnp.int32, (256, 256), 0)
    lane = lax.broadcasted_iota(jnp.int32, (256, 256), 1)
    j, i, c = row >> 7, (row >> 6) & 1, row & 63
    return jnp.where(lane == 4 * c + 2 * i + j, 1.0, 0.0).astype(BF16)


def constants(w_ref, joined_ref, pool_ref, back_ref, order_ref, *, total):
    joined_ref[...] = jnp.concatenate([w_ref[0], w_ref[1], w_ref[2]], axis=1)
    pool_ref[...] = pool_matrix(strip_index(), total)
    back_ref[...] = pool_matrix(strip_index(), total, back=True)
    order_ref[...] = order_matrix()


def beside(a_ref, b_ref, place, count):
    even = (place & 1) == 0
    a = a_ref[...].astype(F32)
    b = jnp.where((place > 0) & (place < count - 1), b_ref[...].astype(F32), 0.0)
    return jnp.where(even, b, a).astype(BF16), jnp.where(even, a, b).astype(BF16)


def pack_row(row, r, slot, head, tail):
    turned = roll(row.astype(F32), 16 * r, 1)
    return jnp.where(slot == r, turned, head), jnp.where(slot == (r - 1) % 8, turned, tail)


def pack_own(x_ref, head_ref, tail_ref, a_ref, b_ref):
    even = (strip_index() & 1) == 0
    slot = lax.broadcasted_iota(jnp.int32, (64, 128), 1) >> 4
    head = tail = jnp.zeros((64, 128), F32)
    for r in range(x_ref.shape[0]):
        head, tail = pack_row(x_ref[r], r, slot, head, tail)
    a_ref[:64] = jnp.where(even, tail, head).astype(BF16)
    b_ref[:64] = jnp.where(even, head, tail).astype(BF16)
    first, last = head_ref[...].astype(F32), tail_ref[...].astype(F32)
    a_ref[64:] = jnp.where(even, last, first).astype(BF16)
    b_ref[64:] = jnp.where(even, first, last).astype(BF16)


def pack_borders(up_a_ref, up_b_ref, own_a_ref, own_b_ref, a_ref, b_ref, above_ref, below_ref, *, bands):
    even = (strip_index() & 1) == 0
    above_ref[...], below_ref[...] = beside(up_a_ref, up_b_ref, lax.axis_index("row"), bands)
    slot = lax.broadcasted_iota(jnp.int32, (64, 128), 1) >> 4
    head = tail = jnp.zeros((64, 128), F32)
    for r, ref in enumerate((above_ref, below_ref)):
        head, tail = pack_row(ref[...], r, slot, head, tail)
    a_ref[:64] = jnp.where(even, tail, head).astype(BF16)
    b_ref[:64] = jnp.where(even, head, tail).astype(BF16)
    a_ref[64:] = own_a_ref[...]
    b_ref[64:] = own_b_ref[...]


def layer_one(
    x_ref,
    above_ref,
    below_ref,
    a_ref,
    b_ref,
    w_ref,
    pool_ref,
    order_ref,
    pooled_ref,
    slope_ref,
    wide_ref,
    *,
    strips,
):
    strip = strip_index()
    band_rows = x_ref.shape[0]
    slot = lax.broadcasted_iota(jnp.int32, (128, 128), 1) >> 4
    inner = (strip > 0) & (strip < strips - 1)
    sides = a_ref[:128].astype(F32), jnp.where(inner, b_ref[:128].astype(F32), 0.0)
    from_a = ((slot ^ strip) & 1) == 0
    packed = jnp.where(from_a, *sides), jnp.where(from_a, *sides[::-1])
    for r in range(band_rows):
        wide_ref[1 + r, :, 128:] = roll(packed[r % 2][64:], -16 * r, 1).astype(BF16)
    for r, place in enumerate((0, band_rows + 1)):
        wide_ref[place, :, 128:] = roll(packed[r][:64], -16 * r, 1).astype(BF16)
    wide_ref[0, :, :128] = above_ref[...]
    wide_ref[1 : band_rows + 1, :, :128] = x_ref[...]
    wide_ref[band_rows + 1, :, :128] = below_ref[...]
    weights = w_ref[...]
    rows = slope_ref.shape[0]
    halves, held = [], None
    for h in range(rows):
        y = dot(weights, wide_ref[h : h + 3].reshape(192, 256), (1, 0))
        pre = roll(y[:64], 1, 1) + y[64:128] + roll(y[128:], -1, 1)
        sig = sigmoid(pre)
        slope_ref[h] = slope_of(pre, sig).astype(BF16)
        active = pre * sig
        if h % 2:
            halves.append((held + active).astype(BF16))
        else:
            held = active
    pooled = dot(pool_ref[...], jnp.concatenate(halves, 0), (1, 1))
    stacked = jnp.concatenate(
        [
            jnp.concatenate(
                [pooled[:PITCH, u * 128 : u * 128 + 128], pooled[PITCH:, u * 128 : u * 128 + 128]], 1
            )
            for u in range(2)
        ],
        0,
    ).astype(BF16)
    ordered = dot(stacked, order_ref[...], (1, 0)).astype(BF16)
    for u in range(2):
        pooled_ref[u] = ordered[u * PITCH : u * PITCH + SENT]


def layer_two(og_ref, w_ref, *refs, bands):
    pieces, refs = refs[:bands], refs[bands:]
    terms, refs = refs[:bands], refs[bands:]
    map_ref, grad_ref, pack_ref = refs
    band = lax.axis_index("row")
    rows, _, filters = og_ref.shape
    count = rows * PITCH
    map_ref[0] = jnp.zeros((PITCH, 256), BF16)
    map_ref[rows + 1] = jnp.zeros((PITCH, 256), BF16)
    blank = jnp.zeros((PITCH - SENT, 256), BF16)
    for k, piece in zip(row_order(bands, near_first=True), pieces):
        for t in range(2):
            map_ref[1 + 2 * (band ^ k) + t] = jnp.concatenate([piece[t], blank], 0)
    near = jnp.concatenate([map_ref[i : i + rows].reshape(count, 256) for i in range(3)], 1)
    y = dot(near, jnp.concatenate([w_ref[i] for i in range(3)], 1), (1, 1))
    pre = roll(y[:, :filters], 1, 0) + y[:, filters : 2 * filters] + roll(y[:, 2 * filters :], -1, 0)
    grad = og_ref[...].reshape(count, filters).astype(F32) * slope_of(pre, sigmoid(pre))
    grad = grad.astype(BF16)
    grad_ref[0] = jnp.zeros((PITCH, filters), BF16)
    grad_ref[rows + 1] = jnp.zeros((PITCH, filters), BF16)
    grad_ref[1 : rows + 1] = grad.reshape(rows, PITCH, filters)
    near = jnp.concatenate([grad_ref[2 - i : 2 - i + rows].reshape(count, filters) for i in range(3)], 1)
    weights = [
        jnp.concatenate([w_ref[i, j * filters : (j + 1) * filters] for j in range(3)], 1) for i in range(3)
    ]
    z = dot(near, jnp.concatenate(weights, 0), (1, 0))
    spread = roll(z[:, :256], -1 - REACH, 0) + roll(z[:, 256:512], -REACH, 0) + roll(z[:, 512:], 1 - REACH, 0)
    spread = spread.reshape(rows, PITCH, 256)
    odd = (lax.broadcasted_iota(jnp.int32, (8, 256), 1) & 1) == 1
    row = lax.broadcasted_iota(jnp.int32, (8, 256), 0)
    ends = [jnp.where(odd, spread[u - 1, 47:48], spread[u, 32:33]) for u in range(rows)]
    for p in range(rows // 2):
        shared = jnp.where(row == 0, ends[2 * p], jnp.where(row == 1, ends[2 * p + 1], 0.0))
        pack_ref[p] = jnp.concatenate([spread[2 * p, :32], shared, spread[2 * p + 1, :32]], 0).astype(BF16)
    for k in range(bands):
        terms[k][...] = pack_ref[band ^ k]


def filter_two_grads(map_ref, grad_ref, keep_ref, send_ref, all_ref):
    pair = lax.axis_index("pair")
    rows = map_ref.shape[0] - 2
    filters = grad_ref.shape[2]
    v = lax.broadcasted_iota(jnp.int32, (rows, PITCH, filters), 1)
    own = (v >= REACH) & (v < REACH + 32)
    wide = jnp.where(own, grad_ref[1 : rows + 1].astype(F32), 0.0).reshape(rows * PITCH, filters)
    cat = jnp.concatenate([roll(wide, -1, 0), wide, roll(wide, 1, 0)], 1).astype(BF16)
    taps = 3 * filters
    for i in range(3):
        part = dot(cat, map_ref[i : i + rows].reshape(rows * PITCH, 256), (0, 0))
        all_ref[i * taps : (i + 1) * taps] = part.astype(BF16)
    half = keep_ref.shape[0]
    keep_ref[...] = all_ref[pl.ds(pl.multiple_of(pair * half, 16), half)]
    send_ref[...] = all_ref[pl.ds(pl.multiple_of((1 - pair) * half, 16), half)]


def add_after(a_ref, b_ref, *refs):
    refs[-1][...] = (a_ref[...].astype(F32) + b_ref[...].astype(F32)).astype(BF16)


def sum_rows(*refs):
    *refs, a_ref, b_ref, out_ref, passed_a_ref, passed_b_ref = refs
    terms = dict(zip(row_order(len(refs), near_first=True), (ref[...].astype(F32) for ref in refs)))
    terms = [terms[k] for k in range(len(refs))]
    while len(terms) > 1:
        terms = [a + b for a, b in zip(terms[::2], terms[1::2])]
    out_ref[...] = terms[0].astype(BF16)
    passed_a_ref[...] = a_ref[...]
    passed_b_ref[...] = b_ref[...]


def grad_pre_one(*refs, bands):
    terms, refs = refs[:bands], refs[bands:]
    slope_ref, wide_ref, pool_ref, order_ref, g_ref, a_ref, b_ref, keep_ref, send_ref, part_ref = refs
    pair = lax.axis_index("pair")
    summed = terms[0][...].astype(F32)
    for k in range(1, bands):
        summed = summed + terms[k][...].astype(F32)
    blank = jnp.zeros((8, 256), F32)
    ends = summed[32:40]
    blocks = [summed[:32], ends, blank, summed[40:], roll(ends, -1, 0), blank]
    ordered = dot(jnp.concatenate(blocks, 0).astype(BF16), order_ref[...], (1, 1)).astype(BF16)
    pool = pool_ref[...]
    cats = []
    own = lax.broadcasted_iota(jnp.int32, (64, 256), 1) < 128
    for u in range(2):
        block = ordered[u * PITCH : (u + 1) * PITCH]
        up = dot(jnp.concatenate([block[:, :128], block[:, 128:]], 0), pool, (0, 0))
        for i in range(4):
            h = 4 * u + i
            g = (up[64 * (i // 2) : 64 * (i // 2) + 64] * slope_ref[h].astype(F32)).astype(BF16)
            g_ref[h] = g
            mine = jnp.where(own, g.astype(F32), 0.0)
            cats.append(jnp.concatenate([roll(mine, -1, 1), mine, roll(mine, 1, 1)], 0).astype(BF16))
    around = jnp.concatenate([wide_ref[h : h + 3].reshape(192, 256) for h in range(8)], 1)
    acc = dot(jnp.concatenate(cats, 1), around, (1, 1))
    even = (lax.axis_index("row") & 1) == 0
    first, last = g_ref[0].astype(F32), g_ref[7].astype(F32)
    a_ref[...] = jnp.where(even, last, first).astype(BF16)
    b_ref[...] = jnp.where(even, first, last).astype(BF16)
    part_ref[:96] = jnp.concatenate([acc[:96, :128], acc[96:, :128]], 1)
    part_ref[96:] = jnp.concatenate([acc[48 * q : 48 * q + 48, 128:] for q in range(4)], 1)
    for ref, place in ((keep_ref, pair), (send_ref, 1 - pair)):
        ref[...] = part_ref[pl.ds(pl.multiple_of(place * HALF_ONE, 8), HALF_ONE)].astype(BF16)


def layer_one_back(g_ref, a_ref, b_ref, w_ref, out_ref, done_ref, *, bands):
    above, below = beside(a_ref, b_ref, lax.axis_index("row"), bands)
    done_ref[...] = jnp.zeros(done_ref.shape, F32)
    lines = [above] + [g_ref[h] for h in range(8)] + [below]
    rows = []
    for h in range(8):
        z = dot(w_ref[...], jnp.concatenate(lines[h : h + 3], 0), (1, 0))
        rows.append((roll(z[:64], -1, 1) + z[64:128] + roll(z[128:], 1, 1))[:, :128])
    out_ref[...] = jnp.swapaxes(jnp.stack(rows, 0), 0, 1).astype(BF16)


def finish_two(mine_ref, other_ref, two_hbm, done_ref, two_ref, sems, *, scale):
    pair, half = lax.axis_index("pair"), mine_ref.shape[0]
    done_ref[...] = jnp.zeros(done_ref.shape, F32)
    copies = []
    for n, (ref, place) in enumerate(((mine_ref, pair), (other_ref, 1 - pair))):
        rows = pl.ds(pl.multiple_of(place * half, 16), half)
        two_ref[n] = ref[...].astype(F32) * scale
        copies.append(pltpu.make_async_copy(two_ref.at[n], two_hbm.at[rows], sems.at[n]))
        copies[-1].start()
    for copy in copies:
        copy.wait()


def finish_one(mine_ref, other_ref, _, __, out_ref, flat_ref, *, scale):
    pair = lax.axis_index("pair")
    for ref, place in ((mine_ref, pair), (other_ref, 1 - pair)):
        flat_ref[pl.ds(pl.multiple_of(place * HALF_ONE, 8), HALF_ONE)] = ref[...].astype(F32) * scale
    out_ref[0, :96] = flat_ref[:96, :64]
    out_ref[1, :96] = flat_ref[:96, 64:128]
    out_ref[0, 96:] = flat_ref[:96, 128:192]
    out_ref[1, 96:] = flat_ref[:96, 192:]
    for q in range(4):
        out_ref[2, 48 * q : 48 * q + 48] = flat_ref[96:, 64 * q : 64 * q + 64]


def even_swap(values, axis, count):
    return lax.ppermute(values, axis, [(n, n ^ 1) for n in range(count)])


def odd_partner(place):
    return place - 1 if place % 2 == 0 else place + 1


def odd_row_swap(values):
    bands, cores = lax.axis_size("row"), lax.axis_size("pair")
    steps = []
    for n in range(bands):
        for p in range(cores):
            to = (n, p ^ 1) if n in (0, bands - 1) else (odd_partner(n), p)
            steps.append((n * cores + p, to[0] * cores + to[1]))
    return lax.ppermute(values, ("row", "pair"), steps)


def odd_strip_swap(values):
    groups, strips = lax.axis_size("grp"), lax.axis_size(COLS)
    steps = []
    for g in range(groups):
        for n in range(strips):
            to = ((g + 1) % groups, n) if n in (0, strips - 1) else (g, odd_partner(n))
            steps.append((g * strips + n, to[0] * strips + to[1]))
    return lax.ppermute(values, ("grp",) + COLS, steps)


def xor_swap(values, axis, count, k):
    return lax.ppermute(values, axis, [(n, n ^ k) for n in range(count)])


def row_order(bands, near_first=False):
    far_first = sorted(range(1, bands), key=lambda k: (k < bands // 2, k))
    return [0] + (far_first[::-1] if near_first else far_first)


def row_swaps(values, bands, near_first=False):
    order = row_order(bands, near_first)
    return [values[0]] + [xor_swap(values[k], "row", bands, k) for k in order[1:]]


def added(a, b, *after):
    (total,) = whole_call(add_after, [shaped(a.shape)], [a, b, *after], 0, after=len(after))
    return total


def sum_but_last(part, axis, count):
    step = 1
    while 2 * step < count:
        part = added(part, xor_swap(part, axis, count, step))
        step *= 2
    return part, xor_swap(part, axis, count, step)


def local(features_in, filters_one, filters_two, out_grad):
    channels, band_rows, strip_cols = features_in.shape
    filters, own_cols, pooled_rows = out_grad.shape
    bands = lax.axis_size("row")
    strips = lax.axis_size(COLS)
    band = lax.axis_index("row")
    strip = lax.axis_index(COLS)
    pair = lax.axis_index("pair")
    height, width = band_rows * bands, strip_cols * strips
    total = own_cols * strips

    taps_one = jnp.transpose(filters_one, (1, 2, 0, 3)).reshape(3, 3 * channels, channels)
    back_one = jnp.transpose(filters_one[:, ::-1], (2, 3, 1, 0)).reshape(3 * channels, 3 * channels)
    taps_two = jnp.transpose(filters_two, (1, 2, 0, 3)).reshape(3, 3 * filters, 4 * channels)

    og = jnp.transpose(out_grad, (1, 2, 0))
    edge = REACH - 1
    x = jnp.transpose(features_in, (1, 0, 2))
    even = band % 2 == 0
    to_a, to_b = jnp.where(even, x[-1], x[0]), jnp.where(even, x[0], x[-1])
    head, tail = og[:edge], og[-edge:]
    joined_one, pool, pool_back, order = whole_call(
        functools.partial(constants, total=total),
        [shaped((3 * channels, 3 * channels))] + [shaped((2 * PITCH, 256))] * 2 + [shaped((256, 256))],
        [taps_one],
        10**8,
    )
    head, tail = head.reshape(-1, 128), tail.reshape(-1, 128)
    own_a, own_b = whole_call(
        pack_own, [shaped((channels + head.shape[0], 128))] * 2, [x, head, tail], 10**8
    )
    to_a, to_b, above, below = whole_call(
        functools.partial(pack_borders, bands=bands),
        [shaped((2 * channels + head.shape[0], 128))] * 2 + [shaped((channels, strip_cols))] * 2,
        [even_swap(to_a, "row", bands), odd_row_swap(to_b), own_a, own_b],
        1,
    )
    side_a, side_b = even_swap(to_a, COLS, strips), odd_strip_swap(to_b)
    pooled, slope, wide = whole_call(
        functools.partial(layer_one, strips=strips),
        [
            shaped((2, SENT, 4 * channels)),
            shaped((band_rows, channels, 256)),
            shaped((band_rows + 2, channels, 256)),
        ],
        [x, above, below, side_a, side_b, joined_one, pool, order],
        2 * band_rows * 192 * 192 * 256,
    )
    pieces = row_swaps([pooled] * bands, bands, near_first=True)

    even = strip % 2 == 0
    ends = [side[2 * channels :].reshape(og[:edge].shape) for side in (side_a, side_b)]
    ends[1] = jnp.where((strip == 0) | (strip == strips - 1), 0, ends[1])
    before, after = jnp.where(even, ends[1], ends[0]), jnp.where(even, ends[0], ends[1])
    og = jnp.concatenate([before, og, after], 0)
    og = jnp.pad(og, ((1, PITCH - own_cols - 2 * REACH + 1), (0, 0), (0, 0)))
    og = jnp.transpose(og, (1, 0, 2))

    count = pooled_rows * PITCH
    *terms, pooled_map, grad_map = whole_call(
        functools.partial(layer_two, bands=bands),
        [shaped((72, 4 * channels))] * bands
        + [shaped((pooled_rows + 2, PITCH, 4 * channels)), shaped((pooled_rows + 2, PITCH, filters))],
        [og, taps_two] + pieces,
        4 * count * 9 * filters * 4 * channels,
        scratch=[pltpu.VMEM((bands, 72, 4 * channels), BF16)],
    )
    received = row_swaps(terms, bands)

    half = 9 * filters // 2
    keep_two, send_two = whole_call(
        filter_two_grads,
        [shaped((half, 4 * channels))] * 2,
        [pooled_map, grad_map],
        2 * count * 9 * filters * 4 * channels,
        scratch=[pltpu.VMEM((2 * half, 4 * channels), BF16)],
    )
    g, up_a, up_b, keep, send = whole_call(
        functools.partial(grad_pre_one, bands=bands),
        [shaped((band_rows, channels, 256))]
        + [shaped((channels, 256))] * 2
        + [shaped((HALF_ONE, 256))] * 2,
        received + [slope, wide, pool_back, order],
        2 * 8 * 192 * 192 * 256,
        scratch=[pltpu.VMEM((144, 256), F32)],
    )
    one = added(keep, even_swap(send, "pair", 2))
    two = added(keep_two, even_swap(send_two, "pair", 2), keep)
    columns = lax.axis_size("col")
    two, two_more = sum_but_last(two, "col", columns)
    ones = row_swaps([one] * bands, bands, near_first=True)
    one, up_a, up_b = whole_call(
        sum_rows, [shaped(a.shape) for a in (one, up_a, up_b)], ones + [up_a, up_b], 0
    )
    input_grad, done = whole_call(
        functools.partial(layer_one_back, bands=bands),
        [shaped(features_in.shape), shaped((8, 128), F32)],
        [g, even_swap(up_a, "row", bands), odd_row_swap(up_b), back_one],
        2 * band_rows * 192 * 192 * 256,
    )
    mine_two = added(two, two_more, one)
    grad_two, wrote = whole_call(
        functools.partial(finish_two, scale=1.0 / math.sqrt(pooled_rows * total)),
        [shaped((2 * half, 256), F32), shaped((8, 128), F32)],
        [mine_two, even_swap(mine_two, "pair", 2)],
        10**8,
        scratch=[pltpu.VMEM((2, half, 256), F32), pltpu.SemaphoreType.DMA((2,))],
        out_spaces=[pl.ANY, pltpu.VMEM],
    )
    mine_one = added(*sum_but_last(one, "col", columns))
    (grad_one,) = whole_call(
        functools.partial(finish_one, scale=1.0 / math.sqrt(height * width)),
        [shaped((3, 3 * channels, channels), F32)],
        [mine_one, even_swap(mine_one, "pair", 2), wrote, done],
        1,
        scratch=[pltpu.VMEM((144, 256), F32)],
        after=2,
    )
    grad_two = jnp.transpose(grad_two.reshape(3, 3, filters, 4 * channels), (2, 0, 1, 3))
    grad_one = jnp.transpose(grad_one.reshape(3, 3, channels, channels), (2, 0, 1, 3))
    return (input_grad, grad_one, grad_two)


def solution(mesh):
    in_specs = (
        P("grp", "row", ("col", "pair")),
        P(),
        P("row", None, None, None),
        P(("grp", "row"), ("col", "pair"), None),
    )
    out_specs = (
        P("grp", "row", ("col", "pair")),
        P("grp", None, None, None),
        P(("grp", "row"), None, None, None),
    )
    return jax.shard_map(local, mesh=mesh, in_specs=in_specs, out_specs=out_specs, check_vma=False)
```

```python
import functools
import math

import jax
import jax.numpy as jnp
from jax import lax
from jax.experimental import pallas as pl
from jax.experimental.pallas import tpu as pltpu
from jax.sharding import PartitionSpec as P

BF16 = jnp.bfloat16
F32 = jnp.float32
COLS = ("col", "pair")
REACH = 3
HALF_ONE = 72
PITCH = 48
SENT = 40


def dot(a, b, contract):
    return lax.dot_general(a, b, ((contract[:1], contract[1:]), ((), ())), preferred_element_type=F32)


def whole_call(body, outs, operands, flops, scratch=(), after=0, out_spaces=None):
    specs = [
        pl.BlockSpec(memory_space=pltpu.VMEM) for _ in range(len(operands) - after)
    ] + [pl.BlockSpec(memory_space=pl.ANY)] * after
    sizes = [math.prod(a.shape) * a.dtype.itemsize for a in tuple(operands) + tuple(outs)]
    moved = sum(sizes) if flops else 0
    return pl.pallas_call(
        body,
        out_shape=outs,
        in_specs=specs,
        out_specs=[pl.BlockSpec(memory_space=space) for space in out_spaces or [pltpu.VMEM] * len(outs)],
        scratch_shapes=list(scratch),
        cost_estimate=pl.CostEstimate(flops=flops, bytes_accessed=moved, transcendentals=0),
        compiler_params=pltpu.CompilerParams(vmem_limit_bytes=40 * 1024 * 1024),
    )(*operands)


def strip_index():
    return lax.axis_index("col") * lax.axis_size("pair") + lax.axis_index("pair")


def shaped(shape, dtype=BF16):
    return jax.ShapeDtypeStruct(shape, dtype)


def roll(values, amount, axis):
    return pltpu.roll(values, amount % values.shape[axis], axis)


def sigmoid(values):
    return 0.5 + 0.5 * jnp.tanh(0.5 * values)


def slope_of(values, sig):
    return sig * (1.0 + values * (1.0 - sig))


def pool_matrix(strip, total, back=False):
    row = lax.broadcasted_iota(jnp.int32, (2 * PITCH, 256), 0)
    lane = lax.broadcasted_iota(jnp.int32, (2 * PITCH, 256), 1)
    half = (row >= PITCH).astype(jnp.int32)
    n = row - half * PITCH
    if back:
        v, most = jnp.where((n == 32) & (half == 1), -1, n), 33
    else:
        v, most = n - REACH, 32 + 2 * REACH
    near = jnp.bitwise_and(lane - 4 * v - 2 * half, 255) < 2
    place = strip * 32 + v
    keep = near & (n < most) & (place >= 0) & (place < total)
    return jnp.where(keep, 0.25, 0.0).astype(BF16)


def order_matrix():
    row = lax.broadcasted_iota(jnp.int32, (256, 256), 0)
    lane = lax.broadcasted_iota(jnp.int32, (256, 256), 1)
    j, i, c = row >> 7, (row >> 6) & 1, row & 63
    return jnp.where(lane == 4 * c + 2 * i + j, 1.0, 0.0).astype(BF16)


def constants(w_ref, joined_ref, back_w_ref, pool_ref, back_ref, order_ref, *, total):
    turned = [w_ref[2 - i].astype(F32).T for i in range(3)]
    back_w_ref[...] = jnp.concatenate(
        [jnp.concatenate([t[:, 64 * j : 64 * j + 64] for t in turned], 1) for j in range(3)], 0
    ).astype(BF16)
    joined_ref[...] = jnp.concatenate([w_ref[0], w_ref[1], w_ref[2]], axis=1)
    pool_ref[...] = pool_matrix(strip_index(), total)
    back_ref[...] = pool_matrix(strip_index(), total, back=True)
    order_ref[...] = order_matrix()


def beside(a_ref, b_ref, place, count):
    even = (place & 1) == 0
    a = a_ref[...].astype(F32)
    b = jnp.where((place > 0) & (place < count - 1), b_ref[...].astype(F32), 0.0)
    return jnp.where(even, b, a).astype(BF16), jnp.where(even, a, b).astype(BF16)


def pack_row(row, r, slot, head, tail):
    turned = roll(row.astype(F32), 16 * r, 1)
    return jnp.where(slot == r, turned, head), jnp.where(slot == (r - 1) % 8, turned, tail)


def pack_own(x_ref, head_ref, tail_ref, a_ref, b_ref):
    even = (strip_index() & 1) == 0
    slot = lax.broadcasted_iota(jnp.int32, (64, 128), 1) >> 4
    head = tail = jnp.zeros((64, 128), F32)
    for r in range(x_ref.shape[0]):
        head, tail = pack_row(x_ref[r], r, slot, head, tail)
    a_ref[:64] = jnp.where(even, tail, head).astype(BF16)
    b_ref[:64] = jnp.where(even, head, tail).astype(BF16)
    first, last = head_ref[...].astype(F32), tail_ref[...].astype(F32)
    a_ref[64:] = jnp.where(even, last, first).astype(BF16)
    b_ref[64:] = jnp.where(even, first, last).astype(BF16)


def pack_borders(up_a_ref, up_b_ref, own_a_ref, own_b_ref, a_ref, b_ref, above_ref, below_ref, *, bands):
    even = (strip_index() & 1) == 0
    above_ref[...], below_ref[...] = beside(up_a_ref, up_b_ref, lax.axis_index("row"), bands)
    slot = lax.broadcasted_iota(jnp.int32, (64, 128), 1) >> 4
    head = tail = jnp.zeros((64, 128), F32)
    for r, ref in enumerate((above_ref, below_ref)):
        head, tail = pack_row(ref[...], r, slot, head, tail)
    a_ref[:64] = jnp.where(even, tail, head).astype(BF16)
    b_ref[:64] = jnp.where(even, head, tail).astype(BF16)
    a_ref[64:] = own_a_ref[...]
    b_ref[64:] = own_b_ref[...]


def layer_one(
    x_ref,
    above_ref,
    below_ref,
    a_ref,
    b_ref,
    w_ref,
    pool_ref,
    order_ref,
    pooled_ref,
    slope_ref,
    wide_ref,
    *,
    strips,
):
    strip = strip_index()
    band_rows = x_ref.shape[0]
    slot = lax.broadcasted_iota(jnp.int32, (128, 128), 1) >> 4
    inner = (strip > 0) & (strip < strips - 1)
    sides = a_ref[:128].astype(F32), jnp.where(inner, b_ref[:128].astype(F32), 0.0)
    from_a = ((slot ^ strip) & 1) == 0
    packed = jnp.where(from_a, *sides), jnp.where(from_a, *sides[::-1])
    for r in range(band_rows):
        wide_ref[1 + r, :, 128:] = roll(packed[r % 2][64:], -16 * r, 1).astype(BF16)
    for r, place in enumerate((0, band_rows + 1)):
        wide_ref[place, :, 128:] = roll(packed[r][:64], -16 * r, 1).astype(BF16)
    wide_ref[0, :, :128] = above_ref[...]
    wide_ref[1 : band_rows + 1, :, :128] = x_ref[...]
    wide_ref[band_rows + 1, :, :128] = below_ref[...]
    weights = w_ref[...]
    rows = slope_ref.shape[0]
    halves, held = [], None
    for h in range(rows):
        y = dot(weights, wide_ref[h : h + 3].reshape(192, 256), (1, 0))
        pre = roll(y[:64], 1, 1) + y[64:128] + roll(y[128:], -1, 1)
        sig = sigmoid(pre)
        slope_ref[h] = slope_of(pre, sig).astype(BF16)
        active = pre * sig
        if h % 2:
            halves.append((held + active).astype(BF16))
        else:
            held = active
    pooled = dot(pool_ref[...], jnp.concatenate(halves, 0), (1, 1))
    stacked = jnp.concatenate(
        [
            jnp.concatenate(
                [pooled[:PITCH, u * 128 : u * 128 + 128], pooled[PITCH:, u * 128 : u * 128 + 128]], 1
            )
            for u in range(2)
        ],
        0,
    ).astype(BF16)
    ordered = dot(stacked, order_ref[...], (1, 0)).astype(BF16)
    for u in range(2):
        pooled_ref[u] = ordered[u * PITCH : u * PITCH + SENT]


def layer_two(og_ref, w_ref, *refs, bands):
    pieces, refs = refs[:bands], refs[bands:]
    terms, refs = refs[:bands], refs[bands:]
    map_ref, grad_ref, pack_ref = refs
    band = lax.axis_index("row")
    rows, _, filters = og_ref.shape
    count = rows * PITCH
    map_ref[0] = jnp.zeros((PITCH, 256), BF16)
    map_ref[rows + 1] = jnp.zeros((PITCH, 256), BF16)
    blank = jnp.zeros((PITCH - SENT, 256), BF16)
    for k, piece in zip(row_order(bands, near_first=True), pieces):
        for t in range(2):
            map_ref[1 + 2 * (band ^ k) + t] = jnp.concatenate([piece[t], blank], 0)
    near = jnp.concatenate([map_ref[i : i + rows].reshape(count, 256) for i in range(3)], 1)
    y = dot(near, jnp.concatenate([w_ref[i] for i in range(3)], 1), (1, 1))
    pre = roll(y[:, :filters], 1, 0) + y[:, filters : 2 * filters] + roll(y[:, 2 * filters :], -1, 0)
    grad = og_ref[...].reshape(count, filters).astype(F32) * slope_of(pre, sigmoid(pre))
    grad = grad.astype(BF16)
    grad_ref[0] = jnp.zeros((PITCH, filters), BF16)
    grad_ref[rows + 1] = jnp.zeros((PITCH, filters), BF16)
    grad_ref[1 : rows + 1] = grad.reshape(rows, PITCH, filters)
    near = jnp.concatenate([grad_ref[2 - i : 2 - i + rows].reshape(count, filters) for i in range(3)], 1)
    weights = [
        jnp.concatenate([w_ref[i, j * filters : (j + 1) * filters] for j in range(3)], 1) for i in range(3)
    ]
    z = dot(near, jnp.concatenate(weights, 0), (1, 0))
    spread = roll(z[:, :256], -1 - REACH, 0) + roll(z[:, 256:512], -REACH, 0) + roll(z[:, 512:], 1 - REACH, 0)
    spread = spread.reshape(rows, PITCH, 256)
    odd = (lax.broadcasted_iota(jnp.int32, (8, 256), 1) & 1) == 1
    row = lax.broadcasted_iota(jnp.int32, (8, 256), 0)
    ends = [jnp.where(odd, spread[u - 1, 47:48], spread[u, 32:33]) for u in range(rows)]
    for p in range(rows // 2):
        shared = jnp.where(row == 0, ends[2 * p], jnp.where(row == 1, ends[2 * p + 1], 0.0))
        pack_ref[p] = jnp.concatenate([spread[2 * p, :32], shared, spread[2 * p + 1, :32]], 0).astype(BF16)
    for k in range(bands):
        terms[k][...] = pack_ref[band ^ k]


def filter_two_grads(map_ref, grad_ref, keep_ref, send_ref, all_ref):
    pair = lax.axis_index("pair")
    rows = map_ref.shape[0] - 2
    filters = grad_ref.shape[2]
    v = lax.broadcasted_iota(jnp.int32, (rows, PITCH, filters), 1)
    own = (v >= REACH) & (v < REACH + 32)
    wide = jnp.where(own, grad_ref[1 : rows + 1].astype(F32), 0.0).reshape(rows * PITCH, filters)
    cat = jnp.concatenate([roll(wide, -1, 0), wide, roll(wide, 1, 0)], 1).astype(BF16)
    taps = 3 * filters
    for i in range(3):
        part = dot(cat, map_ref[i : i + rows].reshape(rows * PITCH, 256), (0, 0))
        all_ref[i * taps : (i + 1) * taps] = part.astype(BF16)
    half = keep_ref.shape[0]
    keep_ref[...] = all_ref[pl.ds(pl.multiple_of(pair * half, 16), half)]
    send_ref[...] = all_ref[pl.ds(pl.multiple_of((1 - pair) * half, 16), half)]


def add_after(a_ref, b_ref, *refs):
    refs[-1][...] = (a_ref[...].astype(F32) + b_ref[...].astype(F32)).astype(BF16)


def add_halves(a_ref, b_ref, two_ref, one_ref):
    half = two_ref.shape[0]
    total = (a_ref[...].astype(F32) + b_ref[...].astype(F32)).astype(BF16)
    two_ref[...] = total[:half]
    one_ref[...] = total[half:]


def sum_rows(*refs):
    *refs, a_ref, b_ref, out_ref, passed_a_ref, passed_b_ref = refs
    terms = dict(zip(row_order(len(refs), near_first=True), (ref[...].astype(F32) for ref in refs)))
    terms = [terms[k] for k in range(len(refs))]
    while len(terms) > 1:
        terms = [a + b for a, b in zip(terms[::2], terms[1::2])]
    out_ref[...] = terms[0].astype(BF16)
    passed_a_ref[...] = a_ref[...]
    passed_b_ref[...] = b_ref[...]


def grad_pre_one(*refs, bands):
    terms, refs = refs[:bands], refs[bands:]
    slope_ref, wide_ref, pool_ref, order_ref, keep_two_ref, send_two_ref, *refs = refs
    g_ref, a_ref, b_ref, keep_ref, send_ref, part_ref = refs
    pair = lax.axis_index("pair")
    summed = terms[0][...].astype(F32)
    for k in range(1, bands):
        summed = summed + terms[k][...].astype(F32)
    blank = jnp.zeros((8, 256), F32)
    ends = summed[32:40]
    blocks = [summed[:32], ends, blank, summed[40:], roll(ends, -1, 0), blank]
    ordered = dot(jnp.concatenate(blocks, 0).astype(BF16), order_ref[...], (1, 1)).astype(BF16)
    pool = pool_ref[...]
    cats = []
    own = lax.broadcasted_iota(jnp.int32, (64, 256), 1) < 128
    for u in range(2):
        block = ordered[u * PITCH : (u + 1) * PITCH]
        up = dot(jnp.concatenate([block[:, :128], block[:, 128:]], 0), pool, (0, 0))
        for i in range(4):
            h = 4 * u + i
            g = (up[64 * (i // 2) : 64 * (i // 2) + 64] * slope_ref[h].astype(F32)).astype(BF16)
            g_ref[h] = g
            mine = jnp.where(own, g.astype(F32), 0.0)
            cats.append(jnp.concatenate([roll(mine, -1, 1), mine, roll(mine, 1, 1)], 0).astype(BF16))
    around = jnp.concatenate([wide_ref[h : h + 3].reshape(192, 256) for h in range(8)], 1)
    acc = dot(jnp.concatenate(cats, 1), around, (1, 1))
    even = (lax.axis_index("row") & 1) == 0
    first, last = g_ref[0].astype(F32), g_ref[7].astype(F32)
    a_ref[...] = jnp.where(even, last, first).astype(BF16)
    b_ref[...] = jnp.where(even, first, last).astype(BF16)
    part_ref[:96] = jnp.concatenate([acc[:96, :128], acc[96:, :128]], 1)
    part_ref[96:] = jnp.concatenate([acc[48 * q : 48 * q + 48, 128:] for q in range(4)], 1)
    half = keep_two_ref.shape[0]
    for ref, two_ref, place in ((keep_ref, keep_two_ref, pair), (send_ref, send_two_ref, 1 - pair)):
        ref[:half] = two_ref[...]
        ref[half:] = part_ref[pl.ds(pl.multiple_of(place * HALF_ONE, 8), HALF_ONE)].astype(BF16)


def layer_one_back(g_ref, a_ref, b_ref, w_ref, out_ref, done_ref, *, bands):
    above, below = beside(a_ref, b_ref, lax.axis_index("row"), bands)
    done_ref[...] = jnp.zeros(done_ref.shape, F32)
    lines = [above] + [g_ref[h] for h in range(8)] + [below]
    rows = []
    for h in range(8):
        z = dot(w_ref[...], jnp.concatenate(lines[h : h + 3], 0), (1, 0))
        rows.append((roll(z[:64], -1, 1) + z[64:128] + roll(z[128:], 1, 1))[:, :128])
    out_ref[...] = jnp.swapaxes(jnp.stack(rows, 0), 0, 1).astype(BF16)


def finish_two(mine_ref, other_ref, two_hbm, done_ref, two_ref, sems, *, scale):
    pair, half = lax.axis_index("pair"), mine_ref.shape[0]
    done_ref[...] = jnp.zeros(done_ref.shape, F32)
    copies = []
    for n, (ref, place) in enumerate(((mine_ref, pair), (other_ref, 1 - pair))):
        rows = pl.ds(pl.multiple_of(place * half, 16), half)
        two_ref[n] = ref[...].astype(F32) * scale
        copies.append(pltpu.make_async_copy(two_ref.at[n], two_hbm.at[rows], sems.at[n]))
        copies[-1].start()
    for copy in copies:
        copy.wait()


def finish_one(mine_ref, other_ref, _, out_ref, flat_ref, *, scale):
    pair = lax.axis_index("pair")
    for ref, place in ((mine_ref, pair), (other_ref, 1 - pair)):
        flat_ref[pl.ds(pl.multiple_of(place * HALF_ONE, 8), HALF_ONE)] = ref[...].astype(F32) * scale
    out_ref[0, :96] = flat_ref[:96, :64]
    out_ref[1, :96] = flat_ref[:96, 64:128]
    out_ref[0, 96:] = flat_ref[:96, 128:192]
    out_ref[1, 96:] = flat_ref[:96, 192:]
    for q in range(4):
        out_ref[2, 48 * q : 48 * q + 48] = flat_ref[96:, 64 * q : 64 * q + 64]


def even_swap(values, axis, count):
    return lax.ppermute(values, axis, [(n, n ^ 1) for n in range(count)])


def odd_partner(place):
    return place - 1 if place % 2 == 0 else place + 1


def odd_row_swap(values):
    bands, cores = lax.axis_size("row"), lax.axis_size("pair")
    steps = []
    for n in range(bands):
        for p in range(cores):
            to = (n, p ^ 1) if n in (0, bands - 1) else (odd_partner(n), p)
            steps.append((n * cores + p, to[0] * cores + to[1]))
    return lax.ppermute(values, ("row", "pair"), steps)


def odd_strip_swap(values):
    groups, strips = lax.axis_size("grp"), lax.axis_size(COLS)
    steps = []
    for g in range(groups):
        for n in range(strips):
            to = ((g + 1) % groups, n) if n in (0, strips - 1) else (g, odd_partner(n))
            steps.append((g * strips + n, to[0] * strips + to[1]))
    return lax.ppermute(values, ("grp",) + COLS, steps)


def xor_swap(values, axis, count, k):
    return lax.ppermute(values, axis, [(n, n ^ k) for n in range(count)])


def row_order(bands, near_first=False):
    far_first = sorted(range(1, bands), key=lambda k: (k < bands // 2, k))
    return [0] + (far_first[::-1] if near_first else far_first)


def row_swaps(values, bands, near_first=False):
    order = row_order(bands, near_first)
    return [values[0]] + [xor_swap(values[k], "row", bands, k) for k in order[1:]]


def added(a, b, *after):
    (total,) = whole_call(add_after, [shaped(a.shape)], [a, b, *after], 0, after=len(after))
    return total


def sum_but_last(part, axis, count):
    step = 1
    while 2 * step < count:
        part = added(part, xor_swap(part, axis, count, step))
        step *= 2
    return part, xor_swap(part, axis, count, step)


def local(features_in, filters_one, filters_two, out_grad):
    channels, band_rows, strip_cols = features_in.shape
    filters, own_cols, pooled_rows = out_grad.shape
    bands = lax.axis_size("row")
    strips = lax.axis_size(COLS)
    band = lax.axis_index("row")
    strip = lax.axis_index(COLS)
    pair = lax.axis_index("pair")
    height, width = band_rows * bands, strip_cols * strips
    total = own_cols * strips

    taps_one = jnp.transpose(filters_one, (1, 2, 0, 3)).reshape(3, 3 * channels, channels)
    taps_two = jnp.transpose(filters_two, (1, 2, 0, 3)).reshape(3, 3 * filters, 4 * channels)

    og = jnp.transpose(out_grad, (1, 2, 0))
    edge = REACH - 1
    x = jnp.transpose(features_in, (1, 0, 2))
    even = band % 2 == 0
    to_a, to_b = jnp.where(even, x[-1], x[0]), jnp.where(even, x[0], x[-1])
    head, tail = og[:edge], og[-edge:]
    joined_one, back_one, pool, pool_back, order = whole_call(
        functools.partial(constants, total=total),
        [shaped((3 * channels, 3 * channels))] * 2 + [shaped((2 * PITCH, 256))] * 2 + [shaped((256, 256))],
        [taps_one],
        10**8,
    )
    head, tail = head.reshape(-1, 128), tail.reshape(-1, 128)
    own_a, own_b = whole_call(
        pack_own, [shaped((channels + head.shape[0], 128))] * 2, [x, head, tail], 10**8
    )
    to_a, to_b, above, below = whole_call(
        functools.partial(pack_borders, bands=bands),
        [shaped((2 * channels + head.shape[0], 128))] * 2 + [shaped((channels, strip_cols))] * 2,
        [even_swap(to_a, "row", bands), odd_row_swap(to_b), own_a, own_b],
        1,
    )
    side_a, side_b = even_swap(to_a, COLS, strips), odd_strip_swap(to_b)
    pooled, slope, wide = whole_call(
        functools.partial(layer_one, strips=strips),
        [
            shaped((2, SENT, 4 * channels)),
            shaped((band_rows, channels, 256)),
            shaped((band_rows + 2, channels, 256)),
        ],
        [x, above, below, side_a, side_b, joined_one, pool, order],
        2 * band_rows * 192 * 192 * 256,
    )
    pieces = row_swaps([pooled] * bands, bands, near_first=True)

    even = strip % 2 == 0
    ends = [side[2 * channels :].reshape(og[:edge].shape) for side in (side_a, side_b)]
    ends[1] = jnp.where((strip == 0) | (strip == strips - 1), 0, ends[1])
    before, after = jnp.where(even, ends[1], ends[0]), jnp.where(even, ends[0], ends[1])
    og = jnp.concatenate([before, og, after], 0)
    og = jnp.pad(og, ((1, PITCH - own_cols - 2 * REACH + 1), (0, 0), (0, 0)))
    og = jnp.transpose(og, (1, 0, 2))

    count = pooled_rows * PITCH
    *terms, pooled_map, grad_map = whole_call(
        functools.partial(layer_two, bands=bands),
        [shaped((72, 4 * channels))] * bands
        + [shaped((pooled_rows + 2, PITCH, 4 * channels)), shaped((pooled_rows + 2, PITCH, filters))],
        [og, taps_two] + pieces,
        4 * count * 9 * filters * 4 * channels,
        scratch=[pltpu.VMEM((bands, 72, 4 * channels), BF16)],
    )
    received = row_swaps(terms, bands)

    half = 9 * filters // 2
    keep_two, send_two = whole_call(
        filter_two_grads,
        [shaped((half, 4 * channels))] * 2,
        [pooled_map, grad_map],
        2 * count * 9 * filters * 4 * channels,
        scratch=[pltpu.VMEM((2 * half, 4 * channels), BF16)],
    )
    g, up_a, up_b, keep, send = whole_call(
        functools.partial(grad_pre_one, bands=bands),
        [shaped((band_rows, channels, 256))]
        + [shaped((channels, 256))] * 2
        + [shaped((half + HALF_ONE, 256))] * 2,
        received + [slope, wide, pool_back, order, keep_two, send_two],
        2 * 8 * 192 * 192 * 256,
        scratch=[pltpu.VMEM((144, 256), F32)],
    )
    two, one = whole_call(
        add_halves,
        [shaped((half, 256)), shaped((HALF_ONE, 256))],
        [keep, even_swap(send, "pair", 2)],
        0,
    )
    columns = lax.axis_size("col")
    two, two_more = sum_but_last(two, "col", columns)
    ones = row_swaps([one] * bands, bands, near_first=True)
    one, up_a, up_b = whole_call(
        sum_rows, [shaped(a.shape) for a in (one, up_a, up_b)], ones + [up_a, up_b], 0
    )
    input_grad, done = whole_call(
        functools.partial(layer_one_back, bands=bands),
        [shaped(features_in.shape), shaped((8, 128), F32)],
        [g, even_swap(up_a, "row", bands), odd_row_swap(up_b), back_one],
        2 * band_rows * 192 * 192 * 256,
    )
    mine_two = added(two, two_more, one)
    grad_two, wrote = whole_call(
        functools.partial(finish_two, scale=1.0 / math.sqrt(pooled_rows * total)),
        [shaped((2 * half, 256), F32), shaped((8, 128), F32)],
        [mine_two, even_swap(mine_two, "pair", 2)],
        10**8,
        scratch=[pltpu.VMEM((2, half, 256), F32), pltpu.SemaphoreType.DMA((2,))],
        out_spaces=[pl.ANY, pltpu.VMEM],
    )
    mine_one = added(*sum_but_last(one, "col", columns), wrote)
    (grad_one,) = whole_call(
        functools.partial(finish_one, scale=1.0 / math.sqrt(height * width)),
        [shaped((3, 3 * channels, channels), F32)],
        [mine_one, even_swap(mine_one, "pair", 2), done],
        1,
        scratch=[pltpu.VMEM((144, 256), F32)],
        after=1,
    )
    grad_two = jnp.transpose(grad_two.reshape(3, 3, filters, 4 * channels), (2, 0, 1, 3))
    grad_one = jnp.transpose(grad_one.reshape(3, 3, channels, channels), (2, 0, 1, 3))
    return (input_grad, grad_one, grad_two)


def solution(mesh):
    in_specs = (
        P("grp", "row", ("col", "pair")),
        P(),
        P("row", None, None, None),
        P(("grp", "row"), ("col", "pair"), None),
    )
    out_specs = (
        P("grp", "row", ("col", "pair")),
        P("grp", None, None, None),
        P(("grp", "row"), None, None, None),
    )
    return jax.shard_map(local, mesh=mesh, in_specs=in_specs, out_specs=out_specs, check_vma=False)
```

```python
import functools
import math

import jax
import jax.numpy as jnp
from jax import lax
from jax.experimental import pallas as pl
from jax.experimental.pallas import tpu as pltpu
from jax.sharding import PartitionSpec as P

BF16 = jnp.bfloat16
F32 = jnp.float32
COLS = ("col", "pair")
REACH = 3
HALF_ONE = 72
PITCH = 48
SENT = 40


def dot(a, b, contract):
    return lax.dot_general(a, b, ((contract[:1], contract[1:]), ((), ())), preferred_element_type=F32)


def whole_call(body, outs, operands, flops, scratch=(), after=0, out_spaces=None):
    specs = [
        pl.BlockSpec(memory_space=pltpu.VMEM) for _ in range(len(operands) - after)
    ] + [pl.BlockSpec(memory_space=pl.ANY)] * after
    sizes = [math.prod(a.shape) * a.dtype.itemsize for a in tuple(operands) + tuple(outs)]
    moved = sum(sizes) if flops else 0
    return pl.pallas_call(
        body,
        out_shape=outs,
        in_specs=specs,
        out_specs=[pl.BlockSpec(memory_space=space) for space in out_spaces or [pltpu.VMEM] * len(outs)],
        scratch_shapes=list(scratch),
        cost_estimate=pl.CostEstimate(flops=flops, bytes_accessed=moved, transcendentals=0),
        compiler_params=pltpu.CompilerParams(vmem_limit_bytes=40 * 1024 * 1024),
    )(*operands)


def strip_index():
    return lax.axis_index("col") * lax.axis_size("pair") + lax.axis_index("pair")


def shaped(shape, dtype=BF16):
    return jax.ShapeDtypeStruct(shape, dtype)


def roll(values, amount, axis):
    return pltpu.roll(values, amount % values.shape[axis], axis)


def sigmoid(values):
    return 0.5 + 0.5 * jnp.tanh(0.5 * values)


def slope_of(values, sig):
    return sig * (1.0 + values * (1.0 - sig))


def pool_matrix(strip, total, back=False):
    row = lax.broadcasted_iota(jnp.int32, (2 * PITCH, 256), 0)
    lane = lax.broadcasted_iota(jnp.int32, (2 * PITCH, 256), 1)
    half = (row >= PITCH).astype(jnp.int32)
    n = row - half * PITCH
    if back:
        v, most = jnp.where((n == 32) & (half == 1), -1, n), 33
    else:
        v, most = n - REACH, 32 + 2 * REACH
    near = jnp.bitwise_and(lane - 4 * v - 2 * half, 255) < 2
    place = strip * 32 + v
    keep = near & (n < most) & (place >= 0) & (place < total)
    return jnp.where(keep, 0.25, 0.0).astype(BF16)


def order_matrix():
    row = lax.broadcasted_iota(jnp.int32, (256, 256), 0)
    lane = lax.broadcasted_iota(jnp.int32, (256, 256), 1)
    j, i, c = row >> 7, (row >> 6) & 1, row & 63
    return jnp.where(lane == 4 * c + 2 * i + j, 1.0, 0.0).astype(BF16)


def constants(w_ref, joined_ref, back_w_ref, pool_ref, back_ref, order_ref, *, total):
    turned = [w_ref[2 - i].astype(F32).T for i in range(3)]
    back_w_ref[...] = jnp.concatenate(
        [jnp.concatenate([t[:, 64 * j : 64 * j + 64] for t in turned], 1) for j in range(3)], 0
    ).astype(BF16)
    joined_ref[...] = jnp.concatenate([w_ref[0], w_ref[1], w_ref[2]], axis=1)
    pool_ref[...] = pool_matrix(strip_index(), total)
    back_ref[...] = pool_matrix(strip_index(), total, back=True)
    order_ref[...] = order_matrix()


def beside(a_ref, b_ref, place, count):
    even = (place & 1) == 0
    a = a_ref[...].astype(F32)
    b = jnp.where((place > 0) & (place < count - 1), b_ref[...].astype(F32), 0.0)
    return jnp.where(even, b, a).astype(BF16), jnp.where(even, a, b).astype(BF16)


def pack_row(row, r, slot, head, tail):
    turned = roll(row.astype(F32), 16 * r, 1)
    return jnp.where(slot == r, turned, head), jnp.where(slot == (r - 1) % 8, turned, tail)


def pack_own(x_ref, head_ref, tail_ref, a_ref, b_ref):
    even = (strip_index() & 1) == 0
    slot = lax.broadcasted_iota(jnp.int32, (64, 128), 1) >> 4
    head = tail = jnp.zeros((64, 128), F32)
    for r in range(x_ref.shape[0]):
        head, tail = pack_row(x_ref[r], r, slot, head, tail)
    a_ref[:64] = jnp.where(even, tail, head).astype(BF16)
    b_ref[:64] = jnp.where(even, head, tail).astype(BF16)
    first, last = head_ref[...].astype(F32), tail_ref[...].astype(F32)
    a_ref[64:] = jnp.where(even, last, first).astype(BF16)
    b_ref[64:] = jnp.where(even, first, last).astype(BF16)


def pack_borders(up_a_ref, up_b_ref, own_a_ref, own_b_ref, a_ref, b_ref, above_ref, below_ref, *, bands):
    even = (strip_index() & 1) == 0
    above_ref[...], below_ref[...] = beside(up_a_ref, up_b_ref, lax.axis_index("row"), bands)
    slot = lax.broadcasted_iota(jnp.int32, (64, 128), 1) >> 4
    head = tail = jnp.zeros((64, 128), F32)
    for r, ref in enumerate((above_ref, below_ref)):
        head, tail = pack_row(ref[...], r, slot, head, tail)
    a_ref[:64] = jnp.where(even, tail, head).astype(BF16)
    b_ref[:64] = jnp.where(even, head, tail).astype(BF16)
    a_ref[64:] = own_a_ref[...]
    b_ref[64:] = own_b_ref[...]


def layer_one(
    x_ref,
    above_ref,
    below_ref,
    a_ref,
    b_ref,
    w_ref,
    pool_ref,
    order_ref,
    pooled_ref,
    slope_ref,
    wide_ref,
    *,
    strips,
):
    strip = strip_index()
    band_rows = x_ref.shape[0]
    slot = lax.broadcasted_iota(jnp.int32, (128, 128), 1) >> 4
    inner = (strip > 0) & (strip < strips - 1)
    sides = a_ref[:128].astype(F32), jnp.where(inner, b_ref[:128].astype(F32), 0.0)
    from_a = ((slot ^ strip) & 1) == 0
    packed = jnp.where(from_a, *sides), jnp.where(from_a, *sides[::-1])
    for r in range(band_rows):
        wide_ref[1 + r, :, 128:] = roll(packed[r % 2][64:], -16 * r, 1).astype(BF16)
    for r, place in enumerate((0, band_rows + 1)):
        wide_ref[place, :, 128:] = roll(packed[r][:64], -16 * r, 1).astype(BF16)
    wide_ref[0, :, :128] = above_ref[...]
    wide_ref[1 : band_rows + 1, :, :128] = x_ref[...]
    wide_ref[band_rows + 1, :, :128] = below_ref[...]
    weights = w_ref[...]
    rows = slope_ref.shape[0]
    halves, held = [], None
    for h in range(rows):
        y = dot(weights, wide_ref[h : h + 3].reshape(192, 256), (1, 0))
        pre = roll(y[:64], 1, 1) + y[64:128] + roll(y[128:], -1, 1)
        sig = sigmoid(pre)
        slope_ref[h] = slope_of(pre, sig).astype(BF16)
        active = pre * sig
        if h % 2:
            halves.append((held + active).astype(BF16))
        else:
            held = active
    pooled = dot(pool_ref[...], jnp.concatenate(halves, 0), (1, 1))
    stacked = jnp.concatenate(
        [
            jnp.concatenate(
                [pooled[:PITCH, u * 128 : u * 128 + 128], pooled[PITCH:, u * 128 : u * 128 + 128]], 1
            )
            for u in range(2)
        ],
        0,
    ).astype(BF16)
    ordered = dot(stacked, order_ref[...], (1, 0)).astype(BF16)
    for u in range(2):
        pooled_ref[u] = ordered[u * PITCH : u * PITCH + SENT]


def layer_two(og_ref, w_ref, *refs, bands):
    pieces, refs = refs[:bands], refs[bands:]
    terms, refs = refs[:bands], refs[bands:]
    map_ref, grad_ref, pack_ref = refs
    band = lax.axis_index("row")
    rows, _, filters = og_ref.shape
    count = rows * PITCH
    map_ref[0] = jnp.zeros((PITCH, 256), BF16)
    map_ref[rows + 1] = jnp.zeros((PITCH, 256), BF16)
    blank = jnp.zeros((PITCH - SENT, 256), BF16)
    for k, piece in zip(row_order(bands, near_first=True), pieces):
        for t in range(2):
            map_ref[1 + 2 * (band ^ k) + t] = jnp.concatenate([piece[t], blank], 0)
    near = jnp.concatenate([map_ref[i : i + rows].reshape(count, 256) for i in range(3)], 1)
    y = dot(near, jnp.concatenate([w_ref[i] for i in range(3)], 1), (1, 1))
    pre = roll(y[:, :filters], 1, 0) + y[:, filters : 2 * filters] + roll(y[:, 2 * filters :], -1, 0)
    grad = og_ref[...].reshape(count, filters).astype(F32) * slope_of(pre, sigmoid(pre))
    grad = grad.astype(BF16)
    grad_ref[0] = jnp.zeros((PITCH, filters), BF16)
    grad_ref[rows + 1] = jnp.zeros((PITCH, filters), BF16)
    grad_ref[1 : rows + 1] = grad.reshape(rows, PITCH, filters)
    near = jnp.concatenate([grad_ref[2 - i : 2 - i + rows].reshape(count, filters) for i in range(3)], 1)
    weights = [
        jnp.concatenate([w_ref[i, j * filters : (j + 1) * filters] for j in range(3)], 1) for i in range(3)
    ]
    z = dot(near, jnp.concatenate(weights, 0), (1, 0))
    spread = roll(z[:, :256], -1 - REACH, 0) + roll(z[:, 256:512], -REACH, 0) + roll(z[:, 512:], 1 - REACH, 0)
    spread = spread.reshape(rows, PITCH, 256)
    odd = (lax.broadcasted_iota(jnp.int32, (8, 256), 1) & 1) == 1
    row = lax.broadcasted_iota(jnp.int32, (8, 256), 0)
    ends = [jnp.where(odd, spread[u - 1, 47:48], spread[u, 32:33]) for u in range(rows)]
    for p in range(rows // 2):
        shared = jnp.where(row == 0, ends[2 * p], jnp.where(row == 1, ends[2 * p + 1], 0.0))
        pack_ref[p] = jnp.concatenate([spread[2 * p, :32], shared, spread[2 * p + 1, :32]], 0).astype(BF16)
    for k in range(bands):
        terms[k][...] = pack_ref[band ^ k]


def filter_two_grads(map_ref, grad_ref, keep_ref, send_ref, all_ref):
    pair = lax.axis_index("pair")
    rows = map_ref.shape[0] - 2
    filters = grad_ref.shape[2]
    v = lax.broadcasted_iota(jnp.int32, (rows, PITCH, filters), 1)
    own = (v >= REACH) & (v < REACH + 32)
    wide = jnp.where(own, grad_ref[1 : rows + 1].astype(F32), 0.0).reshape(rows * PITCH, filters)
    cat = jnp.concatenate([roll(wide, -1, 0), wide, roll(wide, 1, 0)], 1).astype(BF16)
    taps = 3 * filters
    for i in range(3):
        part = dot(cat, map_ref[i : i + rows].reshape(rows * PITCH, 256), (0, 0))
        all_ref[i * taps : (i + 1) * taps] = part.astype(BF16)
    half = keep_ref.shape[0]
    keep_ref[...] = all_ref[pl.ds(pl.multiple_of(pair * half, 16), half)]
    send_ref[...] = all_ref[pl.ds(pl.multiple_of((1 - pair) * half, 16), half)]


def add_after(a_ref, b_ref, *refs):
    refs[-1][...] = (a_ref[...].astype(F32) + b_ref[...].astype(F32)).astype(BF16)


def add_halves(a_ref, b_ref, two_ref, one_ref):
    half = two_ref.shape[0]
    total = (a_ref[...].astype(F32) + b_ref[...].astype(F32)).astype(BF16)
    two_ref[...] = total[:half]
    one_ref[...] = total[half:]


def add_joined(a_ref, b_ref, c_ref, d_ref, _, __, out_ref):
    half = a_ref.shape[0]
    out_ref[:half] = (a_ref[...].astype(F32) + b_ref[...].astype(F32)).astype(BF16)
    out_ref[half:] = (c_ref[...].astype(F32) + d_ref[...].astype(F32)).astype(BF16)


def sum_rows(*refs):
    *refs, a_ref, b_ref, out_ref, passed_a_ref, passed_b_ref = refs
    terms = dict(zip(row_order(len(refs), near_first=True), (ref[...].astype(F32) for ref in refs)))
    terms = [terms[k] for k in range(len(refs))]
    while len(terms) > 1:
        terms = [a + b for a, b in zip(terms[::2], terms[1::2])]
    out_ref[...] = terms[0].astype(BF16)
    passed_a_ref[...] = a_ref[...]
    passed_b_ref[...] = b_ref[...]


def grad_pre_one(*refs, bands):
    terms, refs = refs[:bands], refs[bands:]
    slope_ref, wide_ref, pool_ref, order_ref, keep_two_ref, send_two_ref, *refs = refs
    g_ref, a_ref, b_ref, keep_ref, send_ref, part_ref = refs
    pair = lax.axis_index("pair")
    summed = terms[0][...].astype(F32)
    for k in range(1, bands):
        summed = summed + terms[k][...].astype(F32)
    blank = jnp.zeros((8, 256), F32)
    ends = summed[32:40]
    blocks = [summed[:32], ends, blank, summed[40:], roll(ends, -1, 0), blank]
    ordered = dot(jnp.concatenate(blocks, 0).astype(BF16), order_ref[...], (1, 1)).astype(BF16)
    pool = pool_ref[...]
    cats = []
    own = lax.broadcasted_iota(jnp.int32, (64, 256), 1) < 128
    for u in range(2):
        block = ordered[u * PITCH : (u + 1) * PITCH]
        up = dot(jnp.concatenate([block[:, :128], block[:, 128:]], 0), pool, (0, 0))
        for i in range(4):
            h = 4 * u + i
            g = (up[64 * (i // 2) : 64 * (i // 2) + 64] * slope_ref[h].astype(F32)).astype(BF16)
            g_ref[h] = g
            mine = jnp.where(own, g.astype(F32), 0.0)
            cats.append(jnp.concatenate([roll(mine, -1, 1), mine, roll(mine, 1, 1)], 0).astype(BF16))
    around = jnp.concatenate([wide_ref[h : h + 3].reshape(192, 256) for h in range(8)], 1)
    acc = dot(jnp.concatenate(cats, 1), around, (1, 1))
    even = (lax.axis_index("row") & 1) == 0
    first, last = g_ref[0].astype(F32), g_ref[7].astype(F32)
    a_ref[...] = jnp.where(even, last, first).astype(BF16)
    b_ref[...] = jnp.where(even, first, last).astype(BF16)
    part_ref[:96] = jnp.concatenate([acc[:96, :128], acc[96:, :128]], 1)
    part_ref[96:] = jnp.concatenate([acc[48 * q : 48 * q + 48, 128:] for q in range(4)], 1)
    half = keep_two_ref.shape[0]
    for ref, two_ref, place in ((keep_ref, keep_two_ref, pair), (send_ref, send_two_ref, 1 - pair)):
        ref[:half] = two_ref[...]
        ref[half:] = part_ref[pl.ds(pl.multiple_of(place * HALF_ONE, 8), HALF_ONE)].astype(BF16)


def layer_one_back(g_ref, a_ref, b_ref, w_ref, out_ref, done_ref, *, bands):
    above, below = beside(a_ref, b_ref, lax.axis_index("row"), bands)
    done_ref[...] = jnp.zeros(done_ref.shape, F32)
    lines = [above] + [g_ref[h] for h in range(8)] + [below]
    rows = []
    for h in range(8):
        z = dot(w_ref[...], jnp.concatenate(lines[h : h + 3], 0), (1, 0))
        rows.append((roll(z[:64], -1, 1) + z[64:128] + roll(z[128:], 1, 1))[:, :128])
    out_ref[...] = jnp.swapaxes(jnp.stack(rows, 0), 0, 1).astype(BF16)


def finish(mine_ref, other_ref, _, one_hbm, two_hbm, one_ref, two_ref, flat_ref, sems, *, scales):
    pair, half = lax.axis_index("pair"), mine_ref.shape[0] - HALF_ONE
    halves = ((mine_ref, pair), (other_ref, 1 - pair))
    copies = []
    for n, (ref, place) in enumerate(halves):
        rows = pl.ds(pl.multiple_of(place * half, 16), half)
        two_ref[n] = ref[:half].astype(F32) * scales[1]
        copies.append(pltpu.make_async_copy(two_ref.at[n], two_hbm.at[rows], sems.at[n]))
        copies[-1].start()
    for ref, place in halves:
        rows = pl.ds(pl.multiple_of(place * HALF_ONE, 8), HALF_ONE)
        flat_ref[rows] = ref[half:].astype(F32) * scales[0]
    one_ref[0, :96] = flat_ref[:96, :64]
    one_ref[1, :96] = flat_ref[:96, 64:128]
    one_ref[0, 96:] = flat_ref[:96, 128:192]
    one_ref[1, 96:] = flat_ref[:96, 192:]
    for q in range(4):
        one_ref[2, 48 * q : 48 * q + 48] = flat_ref[96:, 64 * q : 64 * q + 64]
    copies.append(pltpu.make_async_copy(one_ref, one_hbm, sems.at[2]))
    copies[-1].start()
    for copy in copies:
        copy.wait()


def even_swap(values, axis, count):
    return lax.ppermute(values, axis, [(n, n ^ 1) for n in range(count)])


def odd_partner(place):
    return place - 1 if place % 2 == 0 else place + 1


def odd_row_swap(values):
    bands, cores = lax.axis_size("row"), lax.axis_size("pair")
    steps = []
    for n in range(bands):
        for p in range(cores):
            to = (n, p ^ 1) if n in (0, bands - 1) else (odd_partner(n), p)
            steps.append((n * cores + p, to[0] * cores + to[1]))
    return lax.ppermute(values, ("row", "pair"), steps)


def odd_strip_swap(values):
    groups, strips = lax.axis_size("grp"), lax.axis_size(COLS)
    steps = []
    for g in range(groups):
        for n in range(strips):
            to = ((g + 1) % groups, n) if n in (0, strips - 1) else (g, odd_partner(n))
            steps.append((g * strips + n, to[0] * strips + to[1]))
    return lax.ppermute(values, ("grp",) + COLS, steps)


def xor_swap(values, axis, count, k):
    return lax.ppermute(values, axis, [(n, n ^ k) for n in range(count)])


def row_order(bands, near_first=False):
    far_first = sorted(range(1, bands), key=lambda k: (k < bands // 2, k))
    return [0] + (far_first[::-1] if near_first else far_first)


def row_swaps(values, bands, near_first=False):
    order = row_order(bands, near_first)
    return [values[0]] + [xor_swap(values[k], "row", bands, k) for k in order[1:]]


def added(a, b, *after):
    (total,) = whole_call(add_after, [shaped(a.shape)], [a, b, *after], 0, after=len(after))
    return total


def sum_but_last(part, axis, count):
    step = 1
    while 2 * step < count:
        part = added(part, xor_swap(part, axis, count, step))
        step *= 2
    return part, xor_swap(part, axis, count, step)


def local(features_in, filters_one, filters_two, out_grad):
    channels, band_rows, strip_cols = features_in.shape
    filters, own_cols, pooled_rows = out_grad.shape
    bands = lax.axis_size("row")
    strips = lax.axis_size(COLS)
    band = lax.axis_index("row")
    strip = lax.axis_index(COLS)
    pair = lax.axis_index("pair")
    height, width = band_rows * bands, strip_cols * strips
    total = own_cols * strips

    taps_one = jnp.transpose(filters_one, (1, 2, 0, 3)).reshape(3, 3 * channels, channels)
    taps_two = jnp.transpose(filters_two, (1, 2, 0, 3)).reshape(3, 3 * filters, 4 * channels)

    og = jnp.transpose(out_grad, (1, 2, 0))
    edge = REACH - 1
    x = jnp.transpose(features_in, (1, 0, 2))
    even = band % 2 == 0
    to_a, to_b = jnp.where(even, x[-1], x[0]), jnp.where(even, x[0], x[-1])
    head, tail = og[:edge], og[-edge:]
    joined_one, back_one, pool, pool_back, order = whole_call(
        functools.partial(constants, total=total),
        [shaped((3 * channels, 3 * channels))] * 2 + [shaped((2 * PITCH, 256))] * 2 + [shaped((256, 256))],
        [taps_one],
        10**8,
    )
    head, tail = head.reshape(-1, 128), tail.reshape(-1, 128)
    own_a, own_b = whole_call(
        pack_own, [shaped((channels + head.shape[0], 128))] * 2, [x, head, tail], 10**8
    )
    to_a, to_b, above, below = whole_call(
        functools.partial(pack_borders, bands=bands),
        [shaped((2 * channels + head.shape[0], 128))] * 2 + [shaped((channels, strip_cols))] * 2,
        [even_swap(to_a, "row", bands), odd_row_swap(to_b), own_a, own_b],
        1,
    )
    side_a, side_b = even_swap(to_a, COLS, strips), odd_strip_swap(to_b)
    pooled, slope, wide = whole_call(
        functools.partial(layer_one, strips=strips),
        [
            shaped((2, SENT, 4 * channels)),
            shaped((band_rows, channels, 256)),
            shaped((band_rows + 2, channels, 256)),
        ],
        [x, above, below, side_a, side_b, joined_one, pool, order],
        2 * band_rows * 192 * 192 * 256,
    )
    pieces = row_swaps([pooled] * bands, bands, near_first=True)

    even = strip % 2 == 0
    ends = [side[2 * channels :].reshape(og[:edge].shape) for side in (side_a, side_b)]
    ends[1] = jnp.where((strip == 0) | (strip == strips - 1), 0, ends[1])
    before, after = jnp.where(even, ends[1], ends[0]), jnp.where(even, ends[0], ends[1])
    og = jnp.concatenate([before, og, after], 0)
    og = jnp.pad(og, ((1, PITCH - own_cols - 2 * REACH + 1), (0, 0), (0, 0)))
    og = jnp.transpose(og, (1, 0, 2))

    count = pooled_rows * PITCH
    *terms, pooled_map, grad_map = whole_call(
        functools.partial(layer_two, bands=bands),
        [shaped((72, 4 * channels))] * bands
        + [shaped((pooled_rows + 2, PITCH, 4 * channels)), shaped((pooled_rows + 2, PITCH, filters))],
        [og, taps_two] + pieces,
        4 * count * 9 * filters * 4 * channels,
        scratch=[pltpu.VMEM((bands, 72, 4 * channels), BF16)],
    )
    received = row_swaps(terms, bands)

    half = 9 * filters // 2
    keep_two, send_two = whole_call(
        filter_two_grads,
        [shaped((half, 4 * channels))] * 2,
        [pooled_map, grad_map],
        2 * count * 9 * filters * 4 * channels,
        scratch=[pltpu.VMEM((2 * half, 4 * channels), BF16)],
    )
    g, up_a, up_b, keep, send = whole_call(
        functools.partial(grad_pre_one, bands=bands),
        [shaped((band_rows, channels, 256))]
        + [shaped((channels, 256))] * 2
        + [shaped((half + HALF_ONE, 256))] * 2,
        received + [slope, wide, pool_back, order, keep_two, send_two],
        2 * 8 * 192 * 192 * 256,
        scratch=[pltpu.VMEM((144, 256), F32)],
    )
    two, one = whole_call(
        add_halves,
        [shaped((half, 256)), shaped((HALF_ONE, 256))],
        [keep, even_swap(send, "pair", 2)],
        0,
    )
    columns = lax.axis_size("col")
    two, two_more = sum_but_last(two, "col", columns)
    ones = row_swaps([one] * bands, bands, near_first=True)
    one, up_a, up_b = whole_call(
        sum_rows, [shaped(a.shape) for a in (one, up_a, up_b)], ones + [up_a, up_b], 0
    )
    up_a, up_b = even_swap(up_a, "row", bands), odd_row_swap(up_b)
    input_grad, done = whole_call(
        functools.partial(layer_one_back, bands=bands),
        [shaped(features_in.shape), shaped((8, 128), F32)],
        [g, up_a, up_b, back_one],
        2 * band_rows * 192 * 192 * 256,
    )
    one, one_more = sum_but_last(one, "col", columns)
    (mine,) = whole_call(
        add_joined,
        [shaped((half + HALF_ONE, 256))],
        [two, two_more, one, one_more, up_a, up_b],
        0,
        after=2,
    )
    grad_one, grad_two = whole_call(
        functools.partial(
            finish, scales=(1.0 / math.sqrt(height * width), 1.0 / math.sqrt(pooled_rows * total))
        ),
        [shaped((3, 3 * channels, channels), F32), shaped((2 * half, 256), F32)],
        [mine, even_swap(mine, "pair", 2), done],
        1,
        scratch=[
            pltpu.VMEM((3, 3 * channels, channels), F32),
            pltpu.VMEM((2, half, 256), F32),
            pltpu.VMEM((144, 256), F32),
            pltpu.SemaphoreType.DMA((3,)),
        ],
        after=1,
        out_spaces=[pl.ANY] * 2,
    )
    grad_two = jnp.transpose(grad_two.reshape(3, 3, filters, 4 * channels), (2, 0, 1, 3))
    grad_one = jnp.transpose(grad_one.reshape(3, 3, channels, channels), (2, 0, 1, 3))
    return (input_grad, grad_one, grad_two)


def solution(mesh):
    in_specs = (
        P("grp", "row", ("col", "pair")),
        P(),
        P("row", None, None, None),
        P(("grp", "row"), ("col", "pair"), None),
    )
    out_specs = (
        P("grp", "row", ("col", "pair")),
        P("grp", None, None, None),
        P(("grp", "row"), None, None, None),
    )
    return jax.shard_map(local, mesh=mesh, in_specs=in_specs, out_specs=out_specs, check_vma=False)
```

```python
import functools
import math

import jax
import jax.numpy as jnp
from jax import lax
from jax.experimental import pallas as pl
from jax.experimental.pallas import tpu as pltpu
from jax.sharding import PartitionSpec as P

BF16 = jnp.bfloat16
F32 = jnp.float32
COLS = ("col", "pair")
REACH = 3
HALF_ONE = 72
PITCH = 48
SENT = 40


def dot(a, b, contract):
    return lax.dot_general(a, b, ((contract[:1], contract[1:]), ((), ())), preferred_element_type=F32)


def whole_call(body, outs, operands, flops, scratch=(), after=0, out_spaces=None):
    specs = [
        pl.BlockSpec(memory_space=pltpu.VMEM) for _ in range(len(operands) - after)
    ] + [pl.BlockSpec(memory_space=pl.ANY)] * after
    sizes = [math.prod(a.shape) * a.dtype.itemsize for a in tuple(operands) + tuple(outs)]
    moved = sum(sizes) if flops else 0
    return pl.pallas_call(
        body,
        out_shape=outs,
        in_specs=specs,
        out_specs=[pl.BlockSpec(memory_space=space) for space in out_spaces or [pltpu.VMEM] * len(outs)],
        scratch_shapes=list(scratch),
        cost_estimate=pl.CostEstimate(flops=flops, bytes_accessed=moved, transcendentals=0),
        compiler_params=pltpu.CompilerParams(vmem_limit_bytes=40 * 1024 * 1024),
    )(*operands)


def strip_index():
    return lax.axis_index("col") * lax.axis_size("pair") + lax.axis_index("pair")


def shaped(shape, dtype=BF16):
    return jax.ShapeDtypeStruct(shape, dtype)


def roll(values, amount, axis):
    return pltpu.roll(values, amount % values.shape[axis], axis)


def sigmoid(values):
    return 0.5 + 0.5 * jnp.tanh(0.5 * values)


def slope_of(values, sig):
    return sig * (1.0 + values * (1.0 - sig))


def pool_matrix(strip, total, back=False):
    row = lax.broadcasted_iota(jnp.int32, (2 * PITCH, 256), 0)
    lane = lax.broadcasted_iota(jnp.int32, (2 * PITCH, 256), 1)
    half = (row >= PITCH).astype(jnp.int32)
    n = row - half * PITCH
    if back:
        v, most = jnp.where((n == 32) & (half == 1), -1, n), 33
    else:
        v, most = n - REACH, 32 + 2 * REACH
    near = jnp.bitwise_and(lane - 4 * v - 2 * half, 255) < 2
    place = strip * 32 + v
    keep = near & (n < most) & (place >= 0) & (place < total)
    return jnp.where(keep, 0.25, 0.0).astype(BF16)


def order_matrix():
    row = lax.broadcasted_iota(jnp.int32, (256, 256), 0)
    lane = lax.broadcasted_iota(jnp.int32, (256, 256), 1)
    j, i, c = row >> 7, (row >> 6) & 1, row & 63
    return jnp.where(lane == 4 * c + 2 * i + j, 1.0, 0.0).astype(BF16)


def constants(w_ref, joined_ref, back_w_ref, pool_ref, back_ref, order_ref, *, total):
    turned = [w_ref[2 - i].astype(F32).T for i in range(3)]
    back_w_ref[...] = jnp.concatenate(
        [jnp.concatenate([t[:, 64 * j : 64 * j + 64] for t in turned], 1) for j in range(3)], 0
    ).astype(BF16)
    joined_ref[...] = jnp.concatenate([w_ref[0], w_ref[1], w_ref[2]], axis=1)
    pool_ref[...] = pool_matrix(strip_index(), total)
    back_ref[...] = pool_matrix(strip_index(), total, back=True)
    order_ref[...] = order_matrix()


def beside(a_ref, b_ref, place, count):
    even = (place & 1) == 0
    a = a_ref[...].astype(F32)
    b = jnp.where((place > 0) & (place < count - 1), b_ref[...].astype(F32), 0.0)
    return jnp.where(even, b, a).astype(BF16), jnp.where(even, a, b).astype(BF16)


def pack_row(row, r, slot, head, tail):
    turned = roll(row.astype(F32), 16 * r, 1)
    return jnp.where(slot == r, turned, head), jnp.where(slot == (r - 1) % 8, turned, tail)


def pack_own(x_ref, head_ref, tail_ref, a_ref, b_ref):
    even = (strip_index() & 1) == 0
    slot = lax.broadcasted_iota(jnp.int32, (64, 128), 1) >> 4
    head = tail = jnp.zeros((64, 128), F32)
    for r in range(x_ref.shape[0]):
        head, tail = pack_row(x_ref[r], r, slot, head, tail)
    a_ref[:64] = jnp.where(even, tail, head).astype(BF16)
    b_ref[:64] = jnp.where(even, head, tail).astype(BF16)
    first, last = head_ref[...].astype(F32), tail_ref[...].astype(F32)
    a_ref[64:] = jnp.where(even, last, first).astype(BF16)
    b_ref[64:] = jnp.where(even, first, last).astype(BF16)


def pack_borders(up_a_ref, up_b_ref, own_a_ref, own_b_ref, a_ref, b_ref, above_ref, below_ref, *, bands):
    even = (strip_index() & 1) == 0
    above_ref[...], below_ref[...] = beside(up_a_ref, up_b_ref, lax.axis_index("row"), bands)
    slot = lax.broadcasted_iota(jnp.int32, (64, 128), 1) >> 4
    head = tail = jnp.zeros((64, 128), F32)
    for r, ref in enumerate((above_ref, below_ref)):
        head, tail = pack_row(ref[...], r, slot, head, tail)
    a_ref[:64] = jnp.where(even, tail, head).astype(BF16)
    b_ref[:64] = jnp.where(even, head, tail).astype(BF16)
    a_ref[64:] = own_a_ref[...]
    b_ref[64:] = own_b_ref[...]


def layer_one(
    x_ref,
    above_ref,
    below_ref,
    a_ref,
    b_ref,
    w_ref,
    pool_ref,
    order_ref,
    pooled_ref,
    slope_ref,
    wide_ref,
    *,
    strips,
):
    strip = strip_index()
    band_rows = x_ref.shape[0]
    slot = lax.broadcasted_iota(jnp.int32, (128, 128), 1) >> 4
    inner = (strip > 0) & (strip < strips - 1)
    sides = a_ref[:128].astype(F32), jnp.where(inner, b_ref[:128].astype(F32), 0.0)
    from_a = ((slot ^ strip) & 1) == 0
    packed = jnp.where(from_a, *sides), jnp.where(from_a, *sides[::-1])
    for r in range(band_rows):
        wide_ref[1 + r, :, 128:] = roll(packed[r % 2][64:], -16 * r, 1).astype(BF16)
    for r, place in enumerate((0, band_rows + 1)):
        wide_ref[place, :, 128:] = roll(packed[r][:64], -16 * r, 1).astype(BF16)
    wide_ref[0, :, :128] = above_ref[...]
    wide_ref[1 : band_rows + 1, :, :128] = x_ref[...]
    wide_ref[band_rows + 1, :, :128] = below_ref[...]
    weights = w_ref[...]
    rows = slope_ref.shape[0]
    halves, held = [], None
    for h in range(rows):
        y = dot(weights, wide_ref[h : h + 3].reshape(192, 256), (1, 0))
        pre = roll(y[:64], 1, 1) + y[64:128] + roll(y[128:], -1, 1)
        sig = sigmoid(pre)
        slope_ref[h] = slope_of(pre, sig).astype(BF16)
        active = pre * sig
        if h % 2:
            halves.append((held + active).astype(BF16))
        else:
            held = active
    pooled = dot(pool_ref[...], jnp.concatenate(halves, 0), (1, 1))
    stacked = jnp.concatenate(
        [
            jnp.concatenate(
                [pooled[:PITCH, u * 128 : u * 128 + 128], pooled[PITCH:, u * 128 : u * 128 + 128]], 1
            )
            for u in range(2)
        ],
        0,
    ).astype(BF16)
    ordered = dot(stacked, order_ref[...], (1, 0)).astype(BF16)
    for u in range(2):
        pooled_ref[u] = ordered[u * PITCH : u * PITCH + SENT]


def layer_two(og_ref, w_ref, *refs, bands):
    pieces, refs = refs[:bands], refs[bands:]
    terms, refs = refs[:bands], refs[bands:]
    map_ref, grad_ref, pack_ref = refs
    band = lax.axis_index("row")
    rows, _, filters = og_ref.shape
    count = rows * PITCH
    map_ref[0] = jnp.zeros((PITCH, 256), BF16)
    map_ref[rows + 1] = jnp.zeros((PITCH, 256), BF16)
    blank = jnp.zeros((PITCH - SENT, 256), BF16)
    for k, piece in zip(row_order(bands, near_first=True), pieces):
        for t in range(2):
            map_ref[1 + 2 * (band ^ k) + t] = jnp.concatenate([piece[t], blank], 0)
    near = jnp.concatenate([map_ref[i : i + rows].reshape(count, 256) for i in range(3)], 1)
    y = dot(near, jnp.concatenate([w_ref[i] for i in range(3)], 1), (1, 1))
    pre = roll(y[:, :filters], 1, 0) + y[:, filters : 2 * filters] + roll(y[:, 2 * filters :], -1, 0)
    grad = og_ref[...].reshape(count, filters).astype(F32) * slope_of(pre, sigmoid(pre))
    grad = grad.astype(BF16)
    grad_ref[0] = jnp.zeros((PITCH, filters), BF16)
    grad_ref[rows + 1] = jnp.zeros((PITCH, filters), BF16)
    grad_ref[1 : rows + 1] = grad.reshape(rows, PITCH, filters)
    near = jnp.concatenate([grad_ref[2 - i : 2 - i + rows].reshape(count, filters) for i in range(3)], 1)
    weights = [
        jnp.concatenate([w_ref[i, j * filters : (j + 1) * filters] for j in range(3)], 1) for i in range(3)
    ]
    z = dot(near, jnp.concatenate(weights, 0), (1, 0))
    spread = roll(z[:, :256], -1 - REACH, 0) + roll(z[:, 256:512], -REACH, 0) + roll(z[:, 512:], 1 - REACH, 0)
    spread = spread.reshape(rows, PITCH, 256)
    odd = (lax.broadcasted_iota(jnp.int32, (8, 256), 1) & 1) == 1
    row = lax.broadcasted_iota(jnp.int32, (8, 256), 0)
    ends = [jnp.where(odd, spread[u - 1, 47:48], spread[u, 32:33]) for u in range(rows)]
    for p in range(rows // 2):
        shared = jnp.where(row == 0, ends[2 * p], jnp.where(row == 1, ends[2 * p + 1], 0.0))
        pack_ref[p] = jnp.concatenate([spread[2 * p, :32], shared, spread[2 * p + 1, :32]], 0).astype(BF16)
    for k in range(bands):
        terms[k][...] = pack_ref[band ^ k]


def filter_two_grads(map_ref, grad_ref, keep_ref, send_ref, all_ref):
    pair = lax.axis_index("pair")
    rows = map_ref.shape[0] - 2
    filters = grad_ref.shape[2]
    v = lax.broadcasted_iota(jnp.int32, (rows, PITCH, filters), 1)
    own = (v >= REACH) & (v < REACH + 32)
    wide = jnp.where(own, grad_ref[1 : rows + 1].astype(F32), 0.0).reshape(rows * PITCH, filters)
    cat = jnp.concatenate([roll(wide, -1, 0), wide, roll(wide, 1, 0)], 1).astype(BF16)
    taps = 3 * filters
    for i in range(3):
        part = dot(cat, map_ref[i : i + rows].reshape(rows * PITCH, 256), (0, 0))
        all_ref[i * taps : (i + 1) * taps] = part.astype(BF16)
    half = keep_ref.shape[0]
    keep_ref[...] = all_ref[pl.ds(pl.multiple_of(pair * half, 16), half)]
    send_ref[...] = all_ref[pl.ds(pl.multiple_of((1 - pair) * half, 16), half)]


def add_after(a_ref, b_ref, *refs):
    refs[-1][...] = (a_ref[...].astype(F32) + b_ref[...].astype(F32)).astype(BF16)


def add_halves(a_ref, b_ref, border_ref, two_ref, one_ref, joined_ref):
    half, border = two_ref.shape[0], border_ref.shape[0]
    total = (a_ref[...].astype(F32) + b_ref[...].astype(F32)).astype(BF16)
    two_ref[...] = total[:half]
    one_ref[...] = total[half:]
    joined_ref[:border] = border_ref[...]
    joined_ref[border:] = total[half:]


def add_joined(a_ref, b_ref, c_ref, d_ref, _, out_ref):
    half = a_ref.shape[0]
    out_ref[:half] = (a_ref[...].astype(F32) + b_ref[...].astype(F32)).astype(BF16)
    out_ref[half:] = (c_ref[...].astype(F32) + d_ref[...].astype(F32)).astype(BF16)


def sum_rows(*refs):
    *refs, _, out_ref = refs
    rows = out_ref.shape[0]
    terms = dict(zip(row_order(len(refs), near_first=True), (ref[-rows:].astype(F32) for ref in refs)))
    terms = [terms[k] for k in range(len(refs))]
    while len(terms) > 1:
        terms = [a + b for a, b in zip(terms[::2], terms[1::2])]
    out_ref[...] = terms[0].astype(BF16)


def grad_pre_one(*refs, bands):
    terms, refs = refs[:bands], refs[bands:]
    slope_ref, wide_ref, pool_ref, order_ref, keep_two_ref, send_two_ref, *refs = refs
    g_ref, a_ref, b_ref, keep_ref, send_ref, part_ref = refs
    pair = lax.axis_index("pair")
    summed = terms[0][...].astype(F32)
    for k in range(1, bands):
        summed = summed + terms[k][...].astype(F32)
    blank = jnp.zeros((8, 256), F32)
    ends = summed[32:40]
    blocks = [summed[:32], ends, blank, summed[40:], roll(ends, -1, 0), blank]
    ordered = dot(jnp.concatenate(blocks, 0).astype(BF16), order_ref[...], (1, 1)).astype(BF16)
    pool = pool_ref[...]
    cats = []
    own = lax.broadcasted_iota(jnp.int32, (64, 256), 1) < 128
    for u in range(2):
        block = ordered[u * PITCH : (u + 1) * PITCH]
        up = dot(jnp.concatenate([block[:, :128], block[:, 128:]], 0), pool, (0, 0))
        for i in range(4):
            h = 4 * u + i
            g = (up[64 * (i // 2) : 64 * (i // 2) + 64] * slope_ref[h].astype(F32)).astype(BF16)
            g_ref[h] = g
            mine = jnp.where(own, g.astype(F32), 0.0)
            cats.append(jnp.concatenate([roll(mine, -1, 1), mine, roll(mine, 1, 1)], 0).astype(BF16))
    around = jnp.concatenate([wide_ref[h : h + 3].reshape(192, 256) for h in range(8)], 1)
    acc = dot(jnp.concatenate(cats, 1), around, (1, 1))
    even = (lax.axis_index("row") & 1) == 0
    first, last = g_ref[0].astype(F32), g_ref[7].astype(F32)
    a_ref[...] = jnp.where(even, last, first).astype(BF16)
    b_ref[...] = jnp.where(even, first, last).astype(BF16)
    part_ref[:96] = jnp.concatenate([acc[:96, :128], acc[96:, :128]], 1)
    part_ref[96:] = jnp.concatenate([acc[48 * q : 48 * q + 48, 128:] for q in range(4)], 1)
    half = keep_two_ref.shape[0]
    for ref, two_ref, place in ((keep_ref, keep_two_ref, pair), (send_ref, send_two_ref, 1 - pair)):
        ref[:half] = two_ref[...]
        ref[half:] = part_ref[pl.ds(pl.multiple_of(place * HALF_ONE, 8), HALF_ONE)].astype(BF16)


def layer_one_back(g_ref, a_ref, b_ref, w_ref, out_ref, done_ref, *, bands):
    above, below = beside(a_ref.at[: b_ref.shape[0]], b_ref, lax.axis_index("row"), bands)
    done_ref[...] = jnp.zeros(done_ref.shape, F32)
    lines = [above] + [g_ref[h] for h in range(8)] + [below]
    rows = []
    for h in range(8):
        z = dot(w_ref[...], jnp.concatenate(lines[h : h + 3], 0), (1, 0))
        rows.append((roll(z[:64], -1, 1) + z[64:128] + roll(z[128:], 1, 1))[:, :128])
    out_ref[...] = jnp.swapaxes(jnp.stack(rows, 0), 0, 1).astype(BF16)


def finish(mine_ref, other_ref, one_hbm, two_hbm, one_ref, two_ref, flat_ref, sems, *, scales):
    pair, half = lax.axis_index("pair"), mine_ref.shape[0] - HALF_ONE
    halves = ((mine_ref, pair), (other_ref, 1 - pair))
    copies = []
    for n, (ref, place) in enumerate(halves):
        rows = pl.ds(pl.multiple_of(place * half, 16), half)
        two_ref[n] = ref[:half].astype(F32) * scales[1]
        copies.append(pltpu.make_async_copy(two_ref.at[n], two_hbm.at[rows], sems.at[n]))
        copies[-1].start()
    for ref, place in halves:
        rows = pl.ds(pl.multiple_of(place * HALF_ONE, 8), HALF_ONE)
        flat_ref[rows] = ref[half:].astype(F32) * scales[0]
    one_ref[0, :96] = flat_ref[:96, :64]
    one_ref[1, :96] = flat_ref[:96, 64:128]
    one_ref[0, 96:] = flat_ref[:96, 128:192]
    one_ref[1, 96:] = flat_ref[:96, 192:]
    for q in range(4):
        one_ref[2, 48 * q : 48 * q + 48] = flat_ref[96:, 64 * q : 64 * q + 64]
    copies.append(pltpu.make_async_copy(one_ref, one_hbm, sems.at[2]))
    copies[-1].start()
    for copy in copies:
        copy.wait()


def even_swap(values, axis, count):
    return lax.ppermute(values, axis, [(n, n ^ 1) for n in range(count)])


def odd_partner(place):
    return place - 1 if place % 2 == 0 else place + 1


def odd_row_swap(values):
    bands, cores = lax.axis_size("row"), lax.axis_size("pair")
    steps = []
    for n in range(bands):
        for p in range(cores):
            to = (n, p ^ 1) if n in (0, bands - 1) else (odd_partner(n), p)
            steps.append((n * cores + p, to[0] * cores + to[1]))
    return lax.ppermute(values, ("row", "pair"), steps)


def odd_strip_swap(values):
    groups, strips = lax.axis_size("grp"), lax.axis_size(COLS)
    steps = []
    for g in range(groups):
        for n in range(strips):
            to = ((g + 1) % groups, n) if n in (0, strips - 1) else (g, odd_partner(n))
            steps.append((g * strips + n, to[0] * strips + to[1]))
    return lax.ppermute(values, ("grp",) + COLS, steps)


def xor_swap(values, axis, count, k):
    return lax.ppermute(values, axis, [(n, n ^ k) for n in range(count)])


def row_order(bands, near_first=False):
    far_first = sorted(range(1, bands), key=lambda k: (k < bands // 2, k))
    return [0] + (far_first[::-1] if near_first else far_first)


def row_swaps(values, bands, near_first=False):
    order = row_order(bands, near_first)
    return [values[0]] + [xor_swap(values[k], "row", bands, k) for k in order[1:]]


def added(a, b, *after):
    (total,) = whole_call(add_after, [shaped(a.shape)], [a, b, *after], 0, after=len(after))
    return total


def sum_but_last(part, axis, count):
    step = 1
    while 2 * step < count:
        part = added(part, xor_swap(part, axis, count, step))
        step *= 2
    return part, xor_swap(part, axis, count, step)


def local(features_in, filters_one, filters_two, out_grad):
    channels, band_rows, strip_cols = features_in.shape
    filters, own_cols, pooled_rows = out_grad.shape
    bands = lax.axis_size("row")
    strips = lax.axis_size(COLS)
    band = lax.axis_index("row")
    strip = lax.axis_index(COLS)
    pair = lax.axis_index("pair")
    height, width = band_rows * bands, strip_cols * strips
    total = own_cols * strips

    taps_one = jnp.transpose(filters_one, (1, 2, 0, 3)).reshape(3, 3 * channels, channels)
    taps_two = jnp.transpose(filters_two, (1, 2, 0, 3)).reshape(3, 3 * filters, 4 * channels)

    og = jnp.transpose(out_grad, (1, 2, 0))
    edge = REACH - 1
    x = jnp.transpose(features_in, (1, 0, 2))
    even = band % 2 == 0
    to_a, to_b = jnp.where(even, x[-1], x[0]), jnp.where(even, x[0], x[-1])
    head, tail = og[:edge], og[-edge:]
    joined_one, back_one, pool, pool_back, order = whole_call(
        functools.partial(constants, total=total),
        [shaped((3 * channels, 3 * channels))] * 2 + [shaped((2 * PITCH, 256))] * 2 + [shaped((256, 256))],
        [taps_one],
        10**8,
    )
    head, tail = head.reshape(-1, 128), tail.reshape(-1, 128)
    own_a, own_b = whole_call(
        pack_own, [shaped((channels + head.shape[0], 128))] * 2, [x, head, tail], 10**8
    )
    to_a, to_b, above, below = whole_call(
        functools.partial(pack_borders, bands=bands),
        [shaped((2 * channels + head.shape[0], 128))] * 2 + [shaped((channels, strip_cols))] * 2,
        [even_swap(to_a, "row", bands), odd_row_swap(to_b), own_a, own_b],
        1,
    )
    side_a, side_b = even_swap(to_a, COLS, strips), odd_strip_swap(to_b)
    pooled, slope, wide = whole_call(
        functools.partial(layer_one, strips=strips),
        [
            shaped((2, SENT, 4 * channels)),
            shaped((band_rows, channels, 256)),
            shaped((band_rows + 2, channels, 256)),
        ],
        [x, above, below, side_a, side_b, joined_one, pool, order],
        2 * band_rows * 192 * 192 * 256,
    )
    pieces = row_swaps([pooled] * bands, bands, near_first=True)

    even = strip % 2 == 0
    ends = [side[2 * channels :].reshape(og[:edge].shape) for side in (side_a, side_b)]
    ends[1] = jnp.where((strip == 0) | (strip == strips - 1), 0, ends[1])
    before, after = jnp.where(even, ends[1], ends[0]), jnp.where(even, ends[0], ends[1])
    og = jnp.concatenate([before, og, after], 0)
    og = jnp.pad(og, ((1, PITCH - own_cols - 2 * REACH + 1), (0, 0), (0, 0)))
    og = jnp.transpose(og, (1, 0, 2))

    count = pooled_rows * PITCH
    *terms, pooled_map, grad_map = whole_call(
        functools.partial(layer_two, bands=bands),
        [shaped((72, 4 * channels))] * bands
        + [shaped((pooled_rows + 2, PITCH, 4 * channels)), shaped((pooled_rows + 2, PITCH, filters))],
        [og, taps_two] + pieces,
        4 * count * 9 * filters * 4 * channels,
        scratch=[pltpu.VMEM((bands, 72, 4 * channels), BF16)],
    )
    received = row_swaps(terms, bands)

    half = 9 * filters // 2
    keep_two, send_two = whole_call(
        filter_two_grads,
        [shaped((half, 4 * channels))] * 2,
        [pooled_map, grad_map],
        2 * count * 9 * filters * 4 * channels,
        scratch=[pltpu.VMEM((2 * half, 4 * channels), BF16)],
    )
    g, up_a, up_b, keep, send = whole_call(
        functools.partial(grad_pre_one, bands=bands),
        [shaped((band_rows, channels, 256))]
        + [shaped((channels, 256))] * 2
        + [shaped((half + HALF_ONE, 256))] * 2,
        received + [slope, wide, pool_back, order, keep_two, send_two],
        2 * 8 * 192 * 192 * 256,
        scratch=[pltpu.VMEM((144, 256), F32)],
    )
    two, one, joined = whole_call(
        add_halves,
        [shaped((half, 256)), shaped((HALF_ONE, 256)), shaped((channels + HALF_ONE, 256))],
        [keep, even_swap(send, "pair", 2), up_a],
        0,
    )
    columns = lax.axis_size("col")
    two, two_more = sum_but_last(two, "col", columns)
    ones = row_swaps([one, joined] + [one] * (bands - 2), bands, near_first=True)
    near = ones[row_order(bands, near_first=True).index(1)]
    up_b = odd_row_swap(up_b)
    (one,) = whole_call(sum_rows, [shaped(one.shape)], ones + [up_b], 0, after=1)
    input_grad, done = whole_call(
        functools.partial(layer_one_back, bands=bands),
        [shaped(features_in.shape), shaped((8, 128), F32)],
        [g, near, up_b, back_one],
        2 * band_rows * 192 * 192 * 256,
    )
    one, one_more = sum_but_last(one, "col", columns)
    (mine,) = whole_call(
        add_joined,
        [shaped((half + HALF_ONE, 256))],
        [two, two_more, one, one_more, done],
        0,
        after=1,
    )
    grad_one, grad_two = whole_call(
        functools.partial(
            finish, scales=(1.0 / math.sqrt(height * width), 1.0 / math.sqrt(pooled_rows * total))
        ),
        [shaped((3, 3 * channels, channels), F32), shaped((2 * half, 256), F32)],
        [mine, even_swap(mine, "pair", 2)],
        1,
        scratch=[
            pltpu.VMEM((3, 3 * channels, channels), F32),
            pltpu.VMEM((2, half, 256), F32),
            pltpu.VMEM((144, 256), F32),
            pltpu.SemaphoreType.DMA((3,)),
        ],
        out_spaces=[pl.ANY] * 2,
    )
    grad_two = jnp.transpose(grad_two.reshape(3, 3, filters, 4 * channels), (2, 0, 1, 3))
    grad_one = jnp.transpose(grad_one.reshape(3, 3, channels, channels), (2, 0, 1, 3))
    return (input_grad, grad_one, grad_two)


def solution(mesh):
    in_specs = (
        P("grp", "row", ("col", "pair")),
        P(),
        P("row", None, None, None),
        P(("grp", "row"), ("col", "pair"), None),
    )
    out_specs = (
        P("grp", "row", ("col", "pair")),
        P("grp", None, None, None),
        P(("grp", "row"), None, None, None),
    )
    return jax.shard_map(local, mesh=mesh, in_specs=in_specs, out_specs=out_specs, check_vma=False)
```

```python
import functools
import math

import jax
import jax.numpy as jnp
from jax import lax
from jax.experimental import pallas as pl
from jax.experimental.pallas import tpu as pltpu
from jax.sharding import PartitionSpec as P

BF16 = jnp.bfloat16
F32 = jnp.float32
COLS = ("col", "pair")
REACH = 3
HALF_ONE = 72
PITCH = 48
SENT = 40


def dot(a, b, contract):
    return lax.dot_general(a, b, ((contract[:1], contract[1:]), ((), ())), preferred_element_type=F32)


def whole_call(body, outs, operands, flops, scratch=(), after=0, out_spaces=None):
    specs = [
        pl.BlockSpec(memory_space=pltpu.VMEM) for _ in range(len(operands) - after)
    ] + [pl.BlockSpec(memory_space=pl.ANY)] * after
    sizes = [math.prod(a.shape) * a.dtype.itemsize for a in tuple(operands) + tuple(outs)]
    moved = sum(sizes) if flops else 0
    return pl.pallas_call(
        body,
        out_shape=outs,
        in_specs=specs,
        out_specs=[pl.BlockSpec(memory_space=space) for space in out_spaces or [pltpu.VMEM] * len(outs)],
        scratch_shapes=list(scratch),
        cost_estimate=pl.CostEstimate(flops=flops, bytes_accessed=moved, transcendentals=0),
        compiler_params=pltpu.CompilerParams(vmem_limit_bytes=40 * 1024 * 1024),
    )(*operands)


def strip_index():
    return lax.axis_index("col") * lax.axis_size("pair") + lax.axis_index("pair")


def shaped(shape, dtype=BF16):
    return jax.ShapeDtypeStruct(shape, dtype)


def roll(values, amount, axis):
    return pltpu.roll(values, amount % values.shape[axis], axis)


def sigmoid(values):
    return 0.5 + 0.5 * jnp.tanh(0.5 * values)


def slope_of(values, sig):
    return sig * (1.0 + values * (1.0 - sig))


def pool_matrix(strip, total, back=False):
    row = lax.broadcasted_iota(jnp.int32, (2 * PITCH, 256), 0)
    lane = lax.broadcasted_iota(jnp.int32, (2 * PITCH, 256), 1)
    half = (row >= PITCH).astype(jnp.int32)
    n = row - half * PITCH
    if back:
        v, most = jnp.where((n == 32) & (half == 1), -1, n), 33
    else:
        v, most = n - REACH, 32 + 2 * REACH
    near = jnp.bitwise_and(lane - 4 * v - 2 * half, 255) < 2
    place = strip * 32 + v
    keep = near & (n < most) & (place >= 0) & (place < total)
    return jnp.where(keep, 0.25, 0.0).astype(BF16)


def order_matrix():
    row = lax.broadcasted_iota(jnp.int32, (256, 256), 0)
    lane = lax.broadcasted_iota(jnp.int32, (256, 256), 1)
    j, i, c = row >> 7, (row >> 6) & 1, row & 63
    return jnp.where(lane == 4 * c + 2 * i + j, 1.0, 0.0).astype(BF16)


def constants(w_ref, joined_ref, back_w_ref, pool_ref, back_ref, order_ref, *, total):
    turned = [w_ref[2 - i].astype(F32).T for i in range(3)]
    back_w_ref[...] = jnp.concatenate(
        [jnp.concatenate([t[:, 64 * j : 64 * j + 64] for t in turned], 1) for j in range(3)], 0
    ).astype(BF16)
    joined_ref[...] = jnp.concatenate([w_ref[0], w_ref[1], w_ref[2]], axis=1)
    pool_ref[...] = pool_matrix(strip_index(), total)
    back_ref[...] = pool_matrix(strip_index(), total, back=True)
    order_ref[...] = order_matrix()


def beside(a_ref, b_ref, place, count):
    even = (place & 1) == 0
    a = a_ref[...].astype(F32)
    b = jnp.where((place > 0) & (place < count - 1), b_ref[...].astype(F32), 0.0)
    return jnp.where(even, b, a).astype(BF16), jnp.where(even, a, b).astype(BF16)


def pack_row(row, r, slot, head, tail):
    turned = roll(row.astype(F32), 16 * r, 1)
    return jnp.where(slot == r, turned, head), jnp.where(slot == (r - 1) % 8, turned, tail)


def pack_own(x_ref, head_ref, tail_ref, a_ref, b_ref):
    even = (strip_index() & 1) == 0
    slot = lax.broadcasted_iota(jnp.int32, (64, 128), 1) >> 4
    head = tail = jnp.zeros((64, 128), F32)
    for r in range(x_ref.shape[0]):
        head, tail = pack_row(x_ref[r], r, slot, head, tail)
    a_ref[:64] = jnp.where(even, tail, head).astype(BF16)
    b_ref[:64] = jnp.where(even, head, tail).astype(BF16)
    first, last = head_ref[...].astype(F32), tail_ref[...].astype(F32)
    a_ref[64:] = jnp.where(even, last, first).astype(BF16)
    b_ref[64:] = jnp.where(even, first, last).astype(BF16)


def pack_borders(up_a_ref, up_b_ref, own_a_ref, own_b_ref, a_ref, b_ref, above_ref, below_ref, *, bands):
    even = (strip_index() & 1) == 0
    above_ref[...], below_ref[...] = beside(up_a_ref, up_b_ref, lax.axis_index("row"), bands)
    slot = lax.broadcasted_iota(jnp.int32, (64, 128), 1) >> 4
    head = tail = jnp.zeros((64, 128), F32)
    for r, ref in enumerate((above_ref, below_ref)):
        head, tail = pack_row(ref[...], r, slot, head, tail)
    a_ref[:64] = jnp.where(even, tail, head).astype(BF16)
    b_ref[:64] = jnp.where(even, head, tail).astype(BF16)
    a_ref[64:] = own_a_ref[...]
    b_ref[64:] = own_b_ref[...]


def layer_one(
    x_ref,
    above_ref,
    below_ref,
    a_ref,
    b_ref,
    w_ref,
    pool_ref,
    order_ref,
    pooled_ref,
    slope_ref,
    wide_ref,
    *,
    strips,
):
    strip = strip_index()
    band_rows = x_ref.shape[0]
    slot = lax.broadcasted_iota(jnp.int32, (128, 128), 1) >> 4
    inner = (strip > 0) & (strip < strips - 1)
    sides = a_ref[:128].astype(F32), jnp.where(inner, b_ref[:128].astype(F32), 0.0)
    from_a = ((slot ^ strip) & 1) == 0
    packed = jnp.where(from_a, *sides), jnp.where(from_a, *sides[::-1])
    for r in range(band_rows):
        wide_ref[1 + r, :, 128:] = roll(packed[r % 2][64:], -16 * r, 1).astype(BF16)
    for r, place in enumerate((0, band_rows + 1)):
        wide_ref[place, :, 128:] = roll(packed[r][:64], -16 * r, 1).astype(BF16)
    wide_ref[0, :, :128] = above_ref[...]
    wide_ref[1 : band_rows + 1, :, :128] = x_ref[...]
    wide_ref[band_rows + 1, :, :128] = below_ref[...]
    weights = w_ref[...]
    rows = slope_ref.shape[0]
    halves, held = [], None
    for h in range(rows):
        y = dot(weights, wide_ref[h : h + 3].reshape(192, 256), (1, 0))
        pre = roll(y[:64], 1, 1) + y[64:128] + roll(y[128:], -1, 1)
        sig = sigmoid(pre)
        slope_ref[h] = slope_of(pre, sig).astype(BF16)
        active = pre * sig
        if h % 2:
            halves.append((held + active).astype(BF16))
        else:
            held = active
    pooled = dot(pool_ref[...], jnp.concatenate(halves, 0), (1, 1))
    stacked = jnp.concatenate(
        [
            jnp.concatenate(
                [pooled[:PITCH, u * 128 : u * 128 + 128], pooled[PITCH:, u * 128 : u * 128 + 128]], 1
            )
            for u in range(2)
        ],
        0,
    ).astype(BF16)
    ordered = dot(stacked, order_ref[...], (1, 0)).astype(BF16)
    for u in range(2):
        pooled_ref[u] = ordered[u * PITCH : u * PITCH + SENT]


def layer_two(og_ref, w_ref, *refs, bands):
    pieces, refs = refs[:bands], refs[bands:]
    terms, refs = refs[:bands], refs[bands:]
    map_ref, grad_ref, pack_ref = refs
    band = lax.axis_index("row")
    rows, _, filters = og_ref.shape
    count = rows * PITCH
    map_ref[0] = jnp.zeros((PITCH, 256), BF16)
    map_ref[rows + 1] = jnp.zeros((PITCH, 256), BF16)
    blank = jnp.zeros((PITCH - SENT, 256), BF16)
    for k, piece in zip(row_order(bands, near_first=True), pieces):
        for t in range(2):
            map_ref[1 + 2 * (band ^ k) + t] = jnp.concatenate([piece[t], blank], 0)
    near = jnp.concatenate([map_ref[i : i + rows].reshape(count, 256) for i in range(3)], 1)
    y = dot(near, jnp.concatenate([w_ref[i] for i in range(3)], 1), (1, 1))
    pre = roll(y[:, :filters], 1, 0) + y[:, filters : 2 * filters] + roll(y[:, 2 * filters :], -1, 0)
    grad = og_ref[...].reshape(count, filters).astype(F32) * slope_of(pre, sigmoid(pre))
    grad = grad.astype(BF16)
    grad_ref[0] = jnp.zeros((PITCH, filters), BF16)
    grad_ref[rows + 1] = jnp.zeros((PITCH, filters), BF16)
    grad_ref[1 : rows + 1] = grad.reshape(rows, PITCH, filters)
    near = jnp.concatenate([grad_ref[2 - i : 2 - i + rows].reshape(count, filters) for i in range(3)], 1)
    weights = [
        jnp.concatenate([w_ref[i, j * filters : (j + 1) * filters] for j in range(3)], 1) for i in range(3)
    ]
    z = dot(near, jnp.concatenate(weights, 0), (1, 0))
    spread = roll(z[:, :256], -1 - REACH, 0) + roll(z[:, 256:512], -REACH, 0) + roll(z[:, 512:], 1 - REACH, 0)
    spread = spread.reshape(rows, PITCH, 256)
    odd = (lax.broadcasted_iota(jnp.int32, (8, 256), 1) & 1) == 1
    row = lax.broadcasted_iota(jnp.int32, (8, 256), 0)
    ends = [jnp.where(odd, spread[u - 1, 47:48], spread[u, 32:33]) for u in range(rows)]
    for p in range(rows // 2):
        shared = jnp.where(row == 0, ends[2 * p], jnp.where(row == 1, ends[2 * p + 1], 0.0))
        pack_ref[p] = jnp.concatenate([spread[2 * p, :32], shared, spread[2 * p + 1, :32]], 0).astype(BF16)
    for k in range(bands):
        terms[k][...] = pack_ref[band ^ k]


def filter_two_grads(map_ref, grad_ref, keep_ref, send_ref, all_ref):
    pair = lax.axis_index("pair")
    rows = map_ref.shape[0] - 2
    filters = grad_ref.shape[2]
    v = lax.broadcasted_iota(jnp.int32, (rows, PITCH, filters), 1)
    own = (v >= REACH) & (v < REACH + 32)
    wide = jnp.where(own, grad_ref[1 : rows + 1].astype(F32), 0.0).reshape(rows * PITCH, filters)
    cat = jnp.concatenate([roll(wide, -1, 0), wide, roll(wide, 1, 0)], 1).astype(BF16)
    taps = 3 * filters
    for i in range(3):
        part = dot(cat, map_ref[i : i + rows].reshape(rows * PITCH, 256), (0, 0))
        all_ref[i * taps : (i + 1) * taps] = part.astype(BF16)
    half = keep_ref.shape[0]
    keep_ref[...] = all_ref[pl.ds(pl.multiple_of(pair * half, 16), half)]
    send_ref[...] = all_ref[pl.ds(pl.multiple_of((1 - pair) * half, 16), half)]


def add_after(a_ref, b_ref, *refs):
    refs[-1][...] = (a_ref[...].astype(F32) + b_ref[...].astype(F32)).astype(BF16)


def add_halves(a_ref, b_ref, border_ref, two_ref, one_ref, joined_ref):
    half, border = two_ref.shape[0], border_ref.shape[0]
    total = (a_ref[...].astype(F32) + b_ref[...].astype(F32)).astype(BF16)
    two_ref[...] = total[:half]
    one_ref[...] = total[half:]
    joined_ref[:border] = border_ref[...]
    joined_ref[border:] = total[half:]


def sum_rows(*refs):
    *refs, _, out_ref = refs
    rows = out_ref.shape[0]
    terms = dict(zip(row_order(len(refs), near_first=True), (ref[-rows:].astype(F32) for ref in refs)))
    terms = [terms[k] for k in range(len(refs))]
    while len(terms) > 1:
        terms = [a + b for a, b in zip(terms[::2], terms[1::2])]
    out_ref[...] = terms[0].astype(BF16)


def grad_pre_one(*refs, bands):
    terms, refs = refs[:bands], refs[bands:]
    slope_ref, wide_ref, pool_ref, order_ref, keep_two_ref, send_two_ref, *refs = refs
    g_ref, a_ref, b_ref, keep_ref, send_ref, part_ref = refs
    pair = lax.axis_index("pair")
    summed = terms[0][...].astype(F32)
    for k in range(1, bands):
        summed = summed + terms[k][...].astype(F32)
    blank = jnp.zeros((8, 256), F32)
    ends = summed[32:40]
    blocks = [summed[:32], ends, blank, summed[40:], roll(ends, -1, 0), blank]
    ordered = dot(jnp.concatenate(blocks, 0).astype(BF16), order_ref[...], (1, 1)).astype(BF16)
    pool = pool_ref[...]
    cats = []
    own = lax.broadcasted_iota(jnp.int32, (64, 256), 1) < 128
    for u in range(2):
        block = ordered[u * PITCH : (u + 1) * PITCH]
        up = dot(jnp.concatenate([block[:, :128], block[:, 128:]], 0), pool, (0, 0))
        for i in range(4):
            h = 4 * u + i
            g = (up[64 * (i // 2) : 64 * (i // 2) + 64] * slope_ref[h].astype(F32)).astype(BF16)
            g_ref[h] = g
            mine = jnp.where(own, g.astype(F32), 0.0)
            cats.append(jnp.concatenate([roll(mine, -1, 1), mine, roll(mine, 1, 1)], 0).astype(BF16))
    around = jnp.concatenate([wide_ref[h : h + 3].reshape(192, 256) for h in range(8)], 1)
    acc = dot(jnp.concatenate(cats, 1), around, (1, 1))
    even = (lax.axis_index("row") & 1) == 0
    first, last = g_ref[0].astype(F32), g_ref[7].astype(F32)
    a_ref[...] = jnp.where(even, last, first).astype(BF16)
    b_ref[...] = jnp.where(even, first, last).astype(BF16)
    part_ref[:96] = jnp.concatenate([acc[:96, :128], acc[96:, :128]], 1)
    part_ref[96:] = jnp.concatenate([acc[48 * q : 48 * q + 48, 128:] for q in range(4)], 1)
    half = keep_two_ref.shape[0]
    for ref, two_ref, place in ((keep_ref, keep_two_ref, pair), (send_ref, send_two_ref, 1 - pair)):
        ref[:half] = two_ref[...]
        ref[half:] = part_ref[pl.ds(pl.multiple_of(place * HALF_ONE, 8), HALF_ONE)].astype(BF16)


def layer_one_back(g_ref, a_ref, b_ref, w_ref, out_ref, done_ref, *, bands):
    above, below = beside(a_ref.at[: b_ref.shape[0]], b_ref, lax.axis_index("row"), bands)
    done_ref[...] = jnp.zeros(done_ref.shape, F32)
    lines = [above] + [g_ref[h] for h in range(8)] + [below]
    rows = []
    for h in range(8):
        z = dot(w_ref[...], jnp.concatenate(lines[h : h + 3], 0), (1, 0))
        rows.append((roll(z[:64], -1, 1) + z[64:128] + roll(z[128:], 1, 1))[:, :128])
    out_ref[...] = jnp.swapaxes(jnp.stack(rows, 0), 0, 1).astype(BF16)


def finish_two(mine_ref, other_ref, two_hbm, done_ref, two_ref, sems, *, scale):
    pair, half = lax.axis_index("pair"), mine_ref.shape[0]
    done_ref[...] = jnp.zeros(done_ref.shape, F32)
    copies = []
    for n, (ref, place) in enumerate(((mine_ref, pair), (other_ref, 1 - pair))):
        rows = pl.ds(pl.multiple_of(place * half, 16), half)
        two_ref[n] = ref[...].astype(F32) * scale
        copies.append(pltpu.make_async_copy(two_ref.at[n], two_hbm.at[rows], sems.at[n]))
        copies[-1].start()
    for copy in copies:
        copy.wait()


def finish_one(mine_ref, other_ref, out_ref, flat_ref, *, scale):
    pair = lax.axis_index("pair")
    for ref, place in ((mine_ref, pair), (other_ref, 1 - pair)):
        flat_ref[pl.ds(pl.multiple_of(place * HALF_ONE, 8), HALF_ONE)] = ref[...].astype(F32) * scale
    out_ref[0, :96] = flat_ref[:96, :64]
    out_ref[1, :96] = flat_ref[:96, 64:128]
    out_ref[0, 96:] = flat_ref[:96, 128:192]
    out_ref[1, 96:] = flat_ref[:96, 192:]
    for q in range(4):
        out_ref[2, 48 * q : 48 * q + 48] = flat_ref[96:, 64 * q : 64 * q + 64]


def even_swap(values, axis, count):
    return lax.ppermute(values, axis, [(n, n ^ 1) for n in range(count)])


def odd_partner(place):
    return place - 1 if place % 2 == 0 else place + 1


def odd_row_swap(values):
    bands, cores = lax.axis_size("row"), lax.axis_size("pair")
    steps = []
    for n in range(bands):
        for p in range(cores):
            to = (n, p ^ 1) if n in (0, bands - 1) else (odd_partner(n), p)
            steps.append((n * cores + p, to[0] * cores + to[1]))
    return lax.ppermute(values, ("row", "pair"), steps)


def odd_strip_swap(values):
    groups, strips = lax.axis_size("grp"), lax.axis_size(COLS)
    steps = []
    for g in range(groups):
        for n in range(strips):
            to = ((g + 1) % groups, n) if n in (0, strips - 1) else (g, odd_partner(n))
            steps.append((g * strips + n, to[0] * strips + to[1]))
    return lax.ppermute(values, ("grp",) + COLS, steps)


def xor_swap(values, axis, count, k):
    return lax.ppermute(values, axis, [(n, n ^ k) for n in range(count)])


def row_order(bands, near_first=False):
    far_first = sorted(range(1, bands), key=lambda k: (k < bands // 2, k))
    return [0] + (far_first[::-1] if near_first else far_first)


def row_swaps(values, bands, near_first=False):
    order = row_order(bands, near_first)
    return [values[0]] + [xor_swap(values[k], "row", bands, k) for k in order[1:]]


def added(a, b, *after):
    (total,) = whole_call(add_after, [shaped(a.shape)], [a, b, *after], 0, after=len(after))
    return total


def sum_but_last(part, axis, count):
    step = 1
    while 2 * step < count:
        part = added(part, xor_swap(part, axis, count, step))
        step *= 2
    return part, xor_swap(part, axis, count, step)


def local(features_in, filters_one, filters_two, out_grad):
    channels, band_rows, strip_cols = features_in.shape
    filters, own_cols, pooled_rows = out_grad.shape
    bands = lax.axis_size("row")
    strips = lax.axis_size(COLS)
    band = lax.axis_index("row")
    strip = lax.axis_index(COLS)
    pair = lax.axis_index("pair")
    height, width = band_rows * bands, strip_cols * strips
    total = own_cols * strips

    taps_one = jnp.transpose(filters_one, (1, 2, 0, 3)).reshape(3, 3 * channels, channels)
    taps_two = jnp.transpose(filters_two, (1, 2, 0, 3)).reshape(3, 3 * filters, 4 * channels)

    og = jnp.transpose(out_grad, (1, 2, 0))
    edge = REACH - 1
    x = jnp.transpose(features_in, (1, 0, 2))
    even = band % 2 == 0
    to_a, to_b = jnp.where(even, x[-1], x[0]), jnp.where(even, x[0], x[-1])
    head, tail = og[:edge], og[-edge:]
    joined_one, back_one, pool, pool_back, order = whole_call(
        functools.partial(constants, total=total),
        [shaped((3 * channels, 3 * channels))] * 2 + [shaped((2 * PITCH, 256))] * 2 + [shaped((256, 256))],
        [taps_one],
        10**8,
    )
    head, tail = head.reshape(-1, 128), tail.reshape(-1, 128)
    own_a, own_b = whole_call(
        pack_own, [shaped((channels + head.shape[0], 128))] * 2, [x, head, tail], 10**8
    )
    to_a, to_b, above, below = whole_call(
        functools.partial(pack_borders, bands=bands),
        [shaped((2 * channels + head.shape[0], 128))] * 2 + [shaped((channels, strip_cols))] * 2,
        [even_swap(to_a, "row", bands), odd_row_swap(to_b), own_a, own_b],
        1,
    )
    side_a, side_b = even_swap(to_a, COLS, strips), odd_strip_swap(to_b)
    pooled, slope, wide = whole_call(
        functools.partial(layer_one, strips=strips),
        [
            shaped((2, SENT, 4 * channels)),
            shaped((band_rows, channels, 256)),
            shaped((band_rows + 2, channels, 256)),
        ],
        [x, above, below, side_a, side_b, joined_one, pool, order],
        2 * band_rows * 192 * 192 * 256,
    )
    pieces = row_swaps([pooled] * bands, bands, near_first=True)

    even = strip % 2 == 0
    ends = [side[2 * channels :].reshape(og[:edge].shape) for side in (side_a, side_b)]
    ends[1] = jnp.where((strip == 0) | (strip == strips - 1), 0, ends[1])
    before, after = jnp.where(even, ends[1], ends[0]), jnp.where(even, ends[0], ends[1])
    og = jnp.concatenate([before, og, after], 0)
    og = jnp.pad(og, ((1, PITCH - own_cols - 2 * REACH + 1), (0, 0), (0, 0)))
    og = jnp.transpose(og, (1, 0, 2))

    count = pooled_rows * PITCH
    *terms, pooled_map, grad_map = whole_call(
        functools.partial(layer_two, bands=bands),
        [shaped((72, 4 * channels))] * bands
        + [shaped((pooled_rows + 2, PITCH, 4 * channels)), shaped((pooled_rows + 2, PITCH, filters))],
        [og, taps_two] + pieces,
        4 * count * 9 * filters * 4 * channels,
        scratch=[pltpu.VMEM((bands, 72, 4 * channels), BF16)],
    )
    received = row_swaps(terms, bands)

    half = 9 * filters // 2
    keep_two, send_two = whole_call(
        filter_two_grads,
        [shaped((half, 4 * channels))] * 2,
        [pooled_map, grad_map],
        2 * count * 9 * filters * 4 * channels,
        scratch=[pltpu.VMEM((2 * half, 4 * channels), BF16)],
    )
    g, up_a, up_b, keep, send = whole_call(
        functools.partial(grad_pre_one, bands=bands),
        [shaped((band_rows, channels, 256))]
        + [shaped((channels, 256))] * 2
        + [shaped((half + HALF_ONE, 256))] * 2,
        received + [slope, wide, pool_back, order, keep_two, send_two],
        2 * 8 * 192 * 192 * 256,
        scratch=[pltpu.VMEM((144, 256), F32)],
    )
    two, one, joined = whole_call(
        add_halves,
        [shaped((half, 256)), shaped((HALF_ONE, 256)), shaped((channels + HALF_ONE, 256))],
        [keep, even_swap(send, "pair", 2), up_a],
        0,
    )
    columns = lax.axis_size("col")
    two, two_more = sum_but_last(two, "col", columns)
    ones = row_swaps([one, joined] + [one] * (bands - 2), bands, near_first=True)
    near = ones[row_order(bands, near_first=True).index(1)]
    up_b = odd_row_swap(up_b)
    (one,) = whole_call(sum_rows, [shaped(one.shape)], ones + [up_b], 0, after=1)
    input_grad, done = whole_call(
        functools.partial(layer_one_back, bands=bands),
        [shaped(features_in.shape), shaped((8, 128), F32)],
        [g, near, up_b, back_one],
        2 * band_rows * 192 * 192 * 256,
    )
    mine_two = added(two, two_more, one)
    grad_two, wrote = whole_call(
        functools.partial(finish_two, scale=1.0 / math.sqrt(pooled_rows * total)),
        [shaped((2 * half, 256), F32), shaped((8, 128), F32)],
        [mine_two, even_swap(mine_two, "pair", 2)],
        10**8,
        scratch=[pltpu.VMEM((2, half, 256), F32), pltpu.SemaphoreType.DMA((2,))],
        out_spaces=[pl.ANY, pltpu.VMEM],
    )
    mine_one = added(*sum_but_last(one, "col", columns), wrote, done)
    (grad_one,) = whole_call(
        functools.partial(finish_one, scale=1.0 / math.sqrt(height * width)),
        [shaped((3, 3 * channels, channels), F32)],
        [mine_one, even_swap(mine_one, "pair", 2)],
        1,
        scratch=[pltpu.VMEM((144, 256), F32)],
    )
    grad_two = jnp.transpose(grad_two.reshape(3, 3, filters, 4 * channels), (2, 0, 1, 3))
    grad_one = jnp.transpose(grad_one.reshape(3, 3, channels, channels), (2, 0, 1, 3))
    return (input_grad, grad_one, grad_two)


def solution(mesh):
    in_specs = (
        P("grp", "row", ("col", "pair")),
        P(),
        P("row", None, None, None),
        P(("grp", "row"), ("col", "pair"), None),
    )
    out_specs = (
        P("grp", "row", ("col", "pair")),
        P("grp", None, None, None),
        P(("grp", "row"), None, None, None),
    )
    return jax.shard_map(local, mesh=mesh, in_specs=in_specs, out_specs=out_specs, check_vma=False)
```

```python
import functools
import math

import jax
import jax.numpy as jnp
from jax import lax
from jax.experimental import pallas as pl
from jax.experimental.pallas import tpu as pltpu
from jax.sharding import PartitionSpec as P

BF16 = jnp.bfloat16
F32 = jnp.float32
COLS = ("col", "pair")
REACH = 3
ROWS_ONE = 144
PITCH = 48
SENT = 40


def dot(a, b, contract):
    return lax.dot_general(a, b, ((contract[:1], contract[1:]), ((), ())), preferred_element_type=F32)


def whole_call(body, outs, operands, flops, scratch=(), after=0, out_spaces=None):
    specs = [
        pl.BlockSpec(memory_space=pltpu.VMEM) for _ in range(len(operands) - after)
    ] + [pl.BlockSpec(memory_space=pl.ANY)] * after
    sizes = [math.prod(a.shape) * a.dtype.itemsize for a in tuple(operands) + tuple(outs)]
    moved = sum(sizes) if flops else 0
    return pl.pallas_call(
        body,
        out_shape=outs,
        in_specs=specs,
        out_specs=[pl.BlockSpec(memory_space=space) for space in out_spaces or [pltpu.VMEM] * len(outs)],
        scratch_shapes=list(scratch),
        cost_estimate=pl.CostEstimate(flops=flops, bytes_accessed=moved, transcendentals=0),
        compiler_params=pltpu.CompilerParams(vmem_limit_bytes=40 * 1024 * 1024),
    )(*operands)


def strip_index():
    return lax.axis_index("col") * lax.axis_size("pair") + lax.axis_index("pair")


def shaped(shape, dtype=BF16):
    return jax.ShapeDtypeStruct(shape, dtype)


def roll(values, amount, axis):
    return pltpu.roll(values, amount % values.shape[axis], axis)


def sigmoid(values):
    return 0.5 + 0.5 * jnp.tanh(0.5 * values)


def slope_of(values, sig):
    return sig * (1.0 + values * (1.0 - sig))


def pool_matrix(strip, total, back=False):
    row = lax.broadcasted_iota(jnp.int32, (2 * PITCH, 256), 0)
    lane = lax.broadcasted_iota(jnp.int32, (2 * PITCH, 256), 1)
    half = (row >= PITCH).astype(jnp.int32)
    n = row - half * PITCH
    if back:
        v, most = jnp.where((n == 32) & (half == 1), -1, n), 33
    else:
        v, most = n - REACH, 32 + 2 * REACH
    near = jnp.bitwise_and(lane - 4 * v - 2 * half, 255) < 2
    place = strip * 32 + v
    keep = near & (n < most) & (place >= 0) & (place < total)
    return jnp.where(keep, 0.25, 0.0).astype(BF16)


def order_matrix():
    row = lax.broadcasted_iota(jnp.int32, (256, 256), 0)
    lane = lax.broadcasted_iota(jnp.int32, (256, 256), 1)
    j, i, c = row >> 7, (row >> 6) & 1, row & 63
    return jnp.where(lane == 4 * c + 2 * i + j, 1.0, 0.0).astype(BF16)


def constants(w_ref, joined_ref, back_w_ref, pool_ref, back_ref, order_ref, *, total):
    turned = [w_ref[2 - i].astype(F32).T for i in range(3)]
    back_w_ref[...] = jnp.concatenate(
        [jnp.concatenate([t[:, 64 * j : 64 * j + 64] for t in turned], 1) for j in range(3)], 0
    ).astype(BF16)
    joined_ref[...] = jnp.concatenate([w_ref[0], w_ref[1], w_ref[2]], axis=1)
    pool_ref[...] = pool_matrix(strip_index(), total)
    back_ref[...] = pool_matrix(strip_index(), total, back=True)
    order_ref[...] = order_matrix()


def beside(a_ref, b_ref, place, count):
    even = (place & 1) == 0
    a = a_ref[...].astype(F32)
    b = jnp.where((place > 0) & (place < count - 1), b_ref[...].astype(F32), 0.0)
    return jnp.where(even, b, a).astype(BF16), jnp.where(even, a, b).astype(BF16)


def pack_row(row, r, slot, head, tail):
    turned = roll(row.astype(F32), 16 * r, 1)
    return jnp.where(slot == r, turned, head), jnp.where(slot == (r - 1) % 8, turned, tail)


def pack_own(x_ref, head_ref, tail_ref, a_ref, b_ref):
    even = (strip_index() & 1) == 0
    slot = lax.broadcasted_iota(jnp.int32, (64, 128), 1) >> 4
    head = tail = jnp.zeros((64, 128), F32)
    for r in range(x_ref.shape[0]):
        head, tail = pack_row(x_ref[r], r, slot, head, tail)
    a_ref[:64] = jnp.where(even, tail, head).astype(BF16)
    b_ref[:64] = jnp.where(even, head, tail).astype(BF16)
    first, last = head_ref[...].astype(F32), tail_ref[...].astype(F32)
    a_ref[64:] = jnp.where(even, last, first).astype(BF16)
    b_ref[64:] = jnp.where(even, first, last).astype(BF16)


def pack_borders(up_a_ref, up_b_ref, own_a_ref, own_b_ref, a_ref, b_ref, above_ref, below_ref, *, bands):
    even = (strip_index() & 1) == 0
    above_ref[...], below_ref[...] = beside(up_a_ref, up_b_ref, lax.axis_index("row"), bands)
    slot = lax.broadcasted_iota(jnp.int32, (64, 128), 1) >> 4
    head = tail = jnp.zeros((64, 128), F32)
    for r, ref in enumerate((above_ref, below_ref)):
        head, tail = pack_row(ref[...], r, slot, head, tail)
    a_ref[:64] = jnp.where(even, tail, head).astype(BF16)
    b_ref[:64] = jnp.where(even, head, tail).astype(BF16)
    a_ref[64:] = own_a_ref[...]
    b_ref[64:] = own_b_ref[...]


def layer_one(
    x_ref,
    above_ref,
    below_ref,
    a_ref,
    b_ref,
    w_ref,
    pool_ref,
    order_ref,
    pooled_ref,
    slope_ref,
    wide_ref,
    *,
    strips,
):
    strip = strip_index()
    band_rows = x_ref.shape[0]
    slot = lax.broadcasted_iota(jnp.int32, (128, 128), 1) >> 4
    inner = (strip > 0) & (strip < strips - 1)
    sides = a_ref[:128].astype(F32), jnp.where(inner, b_ref[:128].astype(F32), 0.0)
    from_a = ((slot ^ strip) & 1) == 0
    packed = jnp.where(from_a, *sides), jnp.where(from_a, *sides[::-1])
    for r in range(band_rows):
        wide_ref[1 + r, :, 128:] = roll(packed[r % 2][64:], -16 * r, 1).astype(BF16)
    for r, place in enumerate((0, band_rows + 1)):
        wide_ref[place, :, 128:] = roll(packed[r][:64], -16 * r, 1).astype(BF16)
    wide_ref[0, :, :128] = above_ref[...]
    wide_ref[1 : band_rows + 1, :, :128] = x_ref[...]
    wide_ref[band_rows + 1, :, :128] = below_ref[...]
    weights = w_ref[...]
    rows = slope_ref.shape[0]
    halves, held = [], None
    for h in range(rows):
        y = dot(weights, wide_ref[h : h + 3].reshape(192, 256), (1, 0))
        pre = roll(y[:64], 1, 1) + y[64:128] + roll(y[128:], -1, 1)
        sig = sigmoid(pre)
        slope_ref[h] = slope_of(pre, sig).astype(BF16)
        active = pre * sig
        if h % 2:
            halves.append((held + active).astype(BF16))
        else:
            held = active
    pooled = dot(pool_ref[...], jnp.concatenate(halves, 0), (1, 1))
    stacked = jnp.concatenate(
        [
            jnp.concatenate(
                [pooled[:PITCH, u * 128 : u * 128 + 128], pooled[PITCH:, u * 128 : u * 128 + 128]], 1
            )
            for u in range(2)
        ],
        0,
    ).astype(BF16)
    ordered = dot(stacked, order_ref[...], (1, 0)).astype(BF16)
    for u in range(2):
        pooled_ref[u] = ordered[u * PITCH : u * PITCH + SENT]


def layer_two(og_ref, w_ref, *refs, bands):
    pieces, refs = refs[:bands], refs[bands:]
    terms, refs = refs[:bands], refs[bands:]
    map_ref, grad_ref, pack_ref = refs
    band = lax.axis_index("row")
    rows, _, filters = og_ref.shape
    count = rows * PITCH
    map_ref[0] = jnp.zeros((PITCH, 256), BF16)
    map_ref[rows + 1] = jnp.zeros((PITCH, 256), BF16)
    blank = jnp.zeros((PITCH - SENT, 256), BF16)
    for k, piece in zip(row_order(bands, near_first=True), pieces):
        for t in range(2):
            map_ref[1 + 2 * (band ^ k) + t] = jnp.concatenate([piece[t], blank], 0)
    near = jnp.concatenate([map_ref[i : i + rows].reshape(count, 256) for i in range(3)], 1)
    y = dot(near, jnp.concatenate([w_ref[i] for i in range(3)], 1), (1, 1))
    pre = roll(y[:, :filters], 1, 0) + y[:, filters : 2 * filters] + roll(y[:, 2 * filters :], -1, 0)
    grad = og_ref[...].reshape(count, filters).astype(F32) * slope_of(pre, sigmoid(pre))
    grad = grad.astype(BF16)
    grad_ref[0] = jnp.zeros((PITCH, filters), BF16)
    grad_ref[rows + 1] = jnp.zeros((PITCH, filters), BF16)
    grad_ref[1 : rows + 1] = grad.reshape(rows, PITCH, filters)
    near = jnp.concatenate([grad_ref[2 - i : 2 - i + rows].reshape(count, filters) for i in range(3)], 1)
    weights = [
        jnp.concatenate([w_ref[i, j * filters : (j + 1) * filters] for j in range(3)], 1) for i in range(3)
    ]
    z = dot(near, jnp.concatenate(weights, 0), (1, 0))
    spread = roll(z[:, :256], -1 - REACH, 0) + roll(z[:, 256:512], -REACH, 0) + roll(z[:, 512:], 1 - REACH, 0)
    spread = spread.reshape(rows, PITCH, 256)
    odd = (lax.broadcasted_iota(jnp.int32, (8, 256), 1) & 1) == 1
    row = lax.broadcasted_iota(jnp.int32, (8, 256), 0)
    ends = [jnp.where(odd, spread[u - 1, 47:48], spread[u, 32:33]) for u in range(rows)]
    for p in range(rows // 2):
        shared = jnp.where(row == 0, ends[2 * p], jnp.where(row == 1, ends[2 * p + 1], 0.0))
        pack_ref[p] = jnp.concatenate([spread[2 * p, :32], shared, spread[2 * p + 1, :32]], 0).astype(BF16)
    for k in range(bands):
        terms[k][...] = pack_ref[band ^ k]


def filter_two_grads(map_ref, grad_ref, keep_ref, send_ref, all_ref):
    pair = lax.axis_index("pair")
    rows = map_ref.shape[0] - 2
    filters = grad_ref.shape[2]
    v = lax.broadcasted_iota(jnp.int32, (rows, PITCH, filters), 1)
    own = (v >= REACH) & (v < REACH + 32)
    wide = jnp.where(own, grad_ref[1 : rows + 1].astype(F32), 0.0).reshape(rows * PITCH, filters)
    cat = jnp.concatenate([roll(wide, -1, 0), wide, roll(wide, 1, 0)], 1).astype(BF16)
    taps = 3 * filters
    for i in range(3):
        part = dot(cat, map_ref[i : i + rows].reshape(rows * PITCH, 256), (0, 0))
        all_ref[i * taps : (i + 1) * taps] = part.astype(BF16)
    half = keep_ref.shape[0]
    keep_ref[...] = all_ref[pl.ds(pl.multiple_of(pair * half, 16), half)]
    send_ref[...] = all_ref[pl.ds(pl.multiple_of((1 - pair) * half, 16), half)]


def add_after(a_ref, b_ref, *refs):
    refs[-1][...] = (a_ref[...].astype(F32) + b_ref[...].astype(F32)).astype(BF16)


def add_halves(a_ref, b_ref, two_ref, one_ref):
    half = two_ref.shape[0]
    total = (a_ref[...].astype(F32) + b_ref[...].astype(F32)).astype(BF16)
    two_ref[...] = total[:half]
    one_ref[...] = total[half:]


def add_joined(a_ref, b_ref, c_ref, d_ref, _, out_ref):
    half = a_ref.shape[0]
    out_ref[:half] = (a_ref[...].astype(F32) + b_ref[...].astype(F32)).astype(BF16)
    out_ref[half:] = (c_ref[...].astype(F32) + d_ref[...].astype(F32)).astype(BF16)


def sum_rows(*refs):
    *refs, _, _, out_ref = refs
    terms = dict(zip(row_order(len(refs), near_first=True), (ref[...].astype(F32) for ref in refs)))
    terms = [terms[k] for k in range(len(refs))]
    while len(terms) > 1:
        terms = [a + b for a, b in zip(terms[::2], terms[1::2])]
    out_ref[...] = terms[0].astype(BF16)


def grad_pre_one(*refs, bands):
    terms, refs = refs[:bands], refs[bands:]
    slope_ref, wide_ref, pool_ref, order_ref, keep_two_ref, send_two_ref, *refs = refs
    g_ref, a_ref, b_ref, keep_ref, send_ref, part_ref = refs
    summed = terms[0][...].astype(F32)
    for k in range(1, bands):
        summed = summed + terms[k][...].astype(F32)
    blank = jnp.zeros((8, 256), F32)
    ends = summed[32:40]
    blocks = [summed[:32], ends, blank, summed[40:], roll(ends, -1, 0), blank]
    ordered = dot(jnp.concatenate(blocks, 0).astype(BF16), order_ref[...], (1, 1)).astype(BF16)
    pool = pool_ref[...]
    cats = []
    own = lax.broadcasted_iota(jnp.int32, (64, 256), 1) < 128
    for u in range(2):
        block = ordered[u * PITCH : (u + 1) * PITCH]
        up = dot(jnp.concatenate([block[:, :128], block[:, 128:]], 0), pool, (0, 0))
        for i in range(4):
            h = 4 * u + i
            g = (up[64 * (i // 2) : 64 * (i // 2) + 64] * slope_ref[h].astype(F32)).astype(BF16)
            g_ref[h] = g
            mine = jnp.where(own, g.astype(F32), 0.0)
            cats.append(jnp.concatenate([roll(mine, -1, 1), mine, roll(mine, 1, 1)], 0).astype(BF16))
    around = jnp.concatenate([wide_ref[h : h + 3].reshape(192, 256) for h in range(8)], 1)
    acc = dot(jnp.concatenate(cats, 1), around, (1, 1))
    even = (lax.axis_index("row") & 1) == 0
    first, last = g_ref[0].astype(F32), g_ref[7].astype(F32)
    a_ref[...] = jnp.where(even, last, first).astype(BF16)
    b_ref[...] = jnp.where(even, first, last).astype(BF16)
    part_ref[:96] = jnp.concatenate([acc[:96, :128], acc[96:, :128]], 1)
    part_ref[96:] = jnp.concatenate([acc[48 * q : 48 * q + 48, 128:] for q in range(4)], 1)
    half = keep_two_ref.shape[0]
    for ref, two_ref in ((keep_ref, keep_two_ref), (send_ref, send_two_ref)):
        ref[:half] = two_ref[...]
        ref[half:] = part_ref[...].astype(BF16)


def layer_one_back(g_ref, a_ref, b_ref, w_ref, out_ref, done_ref, *, bands):
    above, below = beside(a_ref, b_ref, lax.axis_index("row"), bands)
    done_ref[...] = jnp.zeros(done_ref.shape, F32)
    lines = [above] + [g_ref[h] for h in range(8)] + [below]
    rows = []
    for h in range(8):
        z = dot(w_ref[...], jnp.concatenate(lines[h : h + 3], 0), (1, 0))
        rows.append((roll(z[:64], -1, 1) + z[64:128] + roll(z[128:], 1, 1))[:, :128])
    out_ref[...] = jnp.swapaxes(jnp.stack(rows, 0), 0, 1).astype(BF16)


def finish(mine_ref, other_ref, one_hbm, two_hbm, one_ref, two_ref, flat_ref, sems, *, scales):
    pair, half = lax.axis_index("pair"), mine_ref.shape[0] - ROWS_ONE
    copies = []
    for n, (ref, place) in enumerate(((mine_ref, pair), (other_ref, 1 - pair))):
        rows = pl.ds(pl.multiple_of(place * half, 16), half)
        two_ref[n] = ref[:half].astype(F32) * scales[1]
        copies.append(pltpu.make_async_copy(two_ref.at[n], two_hbm.at[rows], sems.at[n]))
        copies[-1].start()
    last = pair == lax.axis_size("pair") - 1
    flat_ref[...] = jnp.where(last, mine_ref[half:].astype(F32), other_ref[half:].astype(F32)) * scales[0]
    one_ref[0, :96] = flat_ref[:96, :64]
    one_ref[1, :96] = flat_ref[:96, 64:128]
    one_ref[0, 96:] = flat_ref[:96, 128:192]
    one_ref[1, 96:] = flat_ref[:96, 192:]
    for q in range(4):
        one_ref[2, 48 * q : 48 * q + 48] = flat_ref[96:, 64 * q : 64 * q + 64]
    copies.append(pltpu.make_async_copy(one_ref, one_hbm, sems.at[2]))
    copies[-1].start()
    for copy in copies:
        copy.wait()


def even_swap(values, axis, count):
    return lax.ppermute(values, axis, [(n, n ^ 1) for n in range(count)])


def odd_partner(place):
    return place - 1 if place % 2 == 0 else place + 1


def odd_row_swap(values):
    bands, cores = lax.axis_size("row"), lax.axis_size("pair")
    steps = []
    for n in range(bands):
        for p in range(cores):
            to = (n, p ^ 1) if n in (0, bands - 1) else (odd_partner(n), p)
            steps.append((n * cores + p, to[0] * cores + to[1]))
    return lax.ppermute(values, ("row", "pair"), steps)


def odd_strip_swap(values):
    groups, strips = lax.axis_size("grp"), lax.axis_size(COLS)
    steps = []
    for g in range(groups):
        for n in range(strips):
            to = ((g + 1) % groups, n) if n in (0, strips - 1) else (g, odd_partner(n))
            steps.append((g * strips + n, to[0] * strips + to[1]))
    return lax.ppermute(values, ("grp",) + COLS, steps)


def xor_swap(values, axis, count, k):
    return lax.ppermute(values, axis, [(n, n ^ k) for n in range(count)])


def last_core_swap(values, axis, k):
    groups, count, cores = (lax.axis_size(name) for name in ("grp", axis, "pair"))
    steps = []
    for g in range(groups):
        for n in range(count):
            for p in range(cores):
                to = (g, n ^ k) if p == cores - 1 else ((g + 1) % groups, n)
                steps.append(((g * count + n) * cores + p, (to[0] * count + to[1]) * cores + p))
    return lax.ppermute(values, ("grp", axis, "pair"), steps)


def row_order(bands, near_first=False):
    far_first = sorted(range(1, bands), key=lambda k: (k < bands // 2, k))
    return [0] + (far_first[::-1] if near_first else far_first)


def row_swaps(values, bands, near_first=False):
    order = row_order(bands, near_first)
    return [values[0]] + [xor_swap(values[k], "row", bands, k) for k in order[1:]]


def added(a, b, *after):
    (total,) = whole_call(add_after, [shaped(a.shape)], [a, b, *after], 0, after=len(after))
    return total


def sum_but_last(part, axis, count):
    step = 1
    while 2 * step < count:
        part = added(part, xor_swap(part, axis, count, step))
        step *= 2
    return part, xor_swap(part, axis, count, step)


def local(features_in, filters_one, filters_two, out_grad):
    channels, band_rows, strip_cols = features_in.shape
    filters, own_cols, pooled_rows = out_grad.shape
    bands = lax.axis_size("row")
    strips = lax.axis_size(COLS)
    band = lax.axis_index("row")
    strip = lax.axis_index(COLS)
    pair = lax.axis_index("pair")
    height, width = band_rows * bands, strip_cols * strips
    total = own_cols * strips

    taps_one = jnp.transpose(filters_one, (1, 2, 0, 3)).reshape(3, 3 * channels, channels)
    taps_two = jnp.transpose(filters_two, (1, 2, 0, 3)).reshape(3, 3 * filters, 4 * channels)

    og = jnp.transpose(out_grad, (1, 2, 0))
    edge = REACH - 1
    x = jnp.transpose(features_in, (1, 0, 2))
    even = band % 2 == 0
    to_a, to_b = jnp.where(even, x[-1], x[0]), jnp.where(even, x[0], x[-1])
    head, tail = og[:edge], og[-edge:]
    joined_one, back_one, pool, pool_back, order = whole_call(
        functools.partial(constants, total=total),
        [shaped((3 * channels, 3 * channels))] * 2 + [shaped((2 * PITCH, 256))] * 2 + [shaped((256, 256))],
        [taps_one],
        10**8,
    )
    head, tail = head.reshape(-1, 128), tail.reshape(-1, 128)
    own_a, own_b = whole_call(
        pack_own, [shaped((channels + head.shape[0], 128))] * 2, [x, head, tail], 10**8
    )
    to_a, to_b, above, below = whole_call(
        functools.partial(pack_borders, bands=bands),
        [shaped((2 * channels + head.shape[0], 128))] * 2 + [shaped((channels, strip_cols))] * 2,
        [even_swap(to_a, "row", bands), odd_row_swap(to_b), own_a, own_b],
        1,
    )
    side_a, side_b = even_swap(to_a, COLS, strips), odd_strip_swap(to_b)
    pooled, slope, wide = whole_call(
        functools.partial(layer_one, strips=strips),
        [
            shaped((2, SENT, 4 * channels)),
            shaped((band_rows, channels, 256)),
            shaped((band_rows + 2, channels, 256)),
        ],
        [x, above, below, side_a, side_b, joined_one, pool, order],
        2 * band_rows * 192 * 192 * 256,
    )
    pieces = row_swaps([pooled] * bands, bands, near_first=True)

    even = strip % 2 == 0
    ends = [side[2 * channels :].reshape(og[:edge].shape) for side in (side_a, side_b)]
    ends[1] = jnp.where((strip == 0) | (strip == strips - 1), 0, ends[1])
    before, after = jnp.where(even, ends[1], ends[0]), jnp.where(even, ends[0], ends[1])
    og = jnp.concatenate([before, og, after], 0)
    og = jnp.pad(og, ((1, PITCH - own_cols - 2 * REACH + 1), (0, 0), (0, 0)))
    og = jnp.transpose(og, (1, 0, 2))

    count = pooled_rows * PITCH
    *terms, pooled_map, grad_map = whole_call(
        functools.partial(layer_two, bands=bands),
        [shaped((72, 4 * channels))] * bands
        + [shaped((pooled_rows + 2, PITCH, 4 * channels)), shaped((pooled_rows + 2, PITCH, filters))],
        [og, taps_two] + pieces,
        4 * count * 9 * filters * 4 * channels,
        scratch=[pltpu.VMEM((bands, 72, 4 * channels), BF16)],
    )
    received = row_swaps(terms, bands)

    half = 9 * filters // 2
    keep_two, send_two = whole_call(
        filter_two_grads,
        [shaped((half, 4 * channels))] * 2,
        [pooled_map, grad_map],
        2 * count * 9 * filters * 4 * channels,
        scratch=[pltpu.VMEM((2 * half, 4 * channels), BF16)],
    )
    g, up_a, up_b, keep, send = whole_call(
        functools.partial(grad_pre_one, bands=bands),
        [shaped((band_rows, channels, 256))]
        + [shaped((channels, 256))] * 2
        + [shaped((half + ROWS_ONE, 256))] * 2,
        received + [slope, wide, pool_back, order, keep_two, send_two],
        2 * 8 * 192 * 192 * 256,
        scratch=[pltpu.VMEM((144, 256), F32)],
    )
    two, one = whole_call(
        add_halves,
        [shaped((half, 256)), shaped((ROWS_ONE, 256))],
        [keep, even_swap(send, "pair", 2)],
        0,
    )
    columns = lax.axis_size("col")
    two, two_more = sum_but_last(two, "col", columns)
    ones = [one] + [last_core_swap(one, "row", k) for k in row_order(bands, near_first=True)[1:]]
    up_a, up_b = even_swap(up_a, "row", bands), odd_row_swap(up_b)
    (one,) = whole_call(sum_rows, [shaped(one.shape)], ones + [up_a, up_b], 0, after=2)
    input_grad, done = whole_call(
        functools.partial(layer_one_back, bands=bands),
        [shaped(features_in.shape), shaped((8, 128), F32)],
        [g, up_a, up_b, back_one],
        2 * band_rows * 192 * 192 * 256,
    )
    step = 1
    while 2 * step < columns:
        one = added(one, last_core_swap(one, "col", step))
        step *= 2
    (mine,) = whole_call(
        add_joined,
        [shaped((half + ROWS_ONE, 256))],
        [two, two_more, one, last_core_swap(one, "col", step), done],
        0,
        after=1,
    )
    grad_one, grad_two = whole_call(
        functools.partial(
            finish, scales=(1.0 / math.sqrt(height * width), 1.0 / math.sqrt(pooled_rows * total))
        ),
        [shaped((3, 3 * channels, channels), F32), shaped((2 * half, 256), F32)],
        [mine, even_swap(mine, "pair", 2)],
        1,
        scratch=[
            pltpu.VMEM((3, 3 * channels, channels), F32),
            pltpu.VMEM((2, half, 256), F32),
            pltpu.VMEM((ROWS_ONE, 256), F32),
            pltpu.SemaphoreType.DMA((3,)),
        ],
        out_spaces=[pl.ANY] * 2,
    )
    grad_two = jnp.transpose(grad_two.reshape(3, 3, filters, 4 * channels), (2, 0, 1, 3))
    grad_one = jnp.transpose(grad_one.reshape(3, 3, channels, channels), (2, 0, 1, 3))
    return (input_grad, grad_one, grad_two)


def solution(mesh):
    in_specs = (
        P("grp", "row", ("col", "pair")),
        P(),
        P("row", None, None, None),
        P(("grp", "row"), ("col", "pair"), None),
    )
    out_specs = (
        P("grp", "row", ("col", "pair")),
        P("grp", None, None, None),
        P(("grp", "row"), None, None, None),
    )
    return jax.shard_map(local, mesh=mesh, in_specs=in_specs, out_specs=out_specs, check_vma=False)
```

```python
import functools
import math

import jax
import jax.numpy as jnp
from jax import lax
from jax.experimental import pallas as pl
from jax.experimental.pallas import tpu as pltpu
from jax.sharding import PartitionSpec as P

BF16 = jnp.bfloat16
F32 = jnp.float32
COLS = ("col", "pair")
REACH = 3
ROWS_ONE = 144
PITCH = 48
SENT = 40


def dot(a, b, contract):
    return lax.dot_general(a, b, ((contract[:1], contract[1:]), ((), ())), preferred_element_type=F32)


def whole_call(body, outs, operands, flops, scratch=(), after=0, out_spaces=None):
    specs = [
        pl.BlockSpec(memory_space=pltpu.VMEM) for _ in range(len(operands) - after)
    ] + [pl.BlockSpec(memory_space=pl.ANY)] * after
    sizes = [math.prod(a.shape) * a.dtype.itemsize for a in tuple(operands) + tuple(outs)]
    moved = sum(sizes) if flops else 0
    return pl.pallas_call(
        body,
        out_shape=outs,
        in_specs=specs,
        out_specs=[pl.BlockSpec(memory_space=space) for space in out_spaces or [pltpu.VMEM] * len(outs)],
        scratch_shapes=list(scratch),
        cost_estimate=pl.CostEstimate(flops=flops, bytes_accessed=moved, transcendentals=0),
        compiler_params=pltpu.CompilerParams(vmem_limit_bytes=40 * 1024 * 1024),
    )(*operands)


def strip_index():
    return lax.axis_index("col") * lax.axis_size("pair") + lax.axis_index("pair")


def shaped(shape, dtype=BF16):
    return jax.ShapeDtypeStruct(shape, dtype)


def roll(values, amount, axis):
    return pltpu.roll(values, amount % values.shape[axis], axis)


def sigmoid(values):
    return 0.5 + 0.5 * jnp.tanh(0.5 * values)


def slope_of(values, sig):
    return sig * (1.0 + values * (1.0 - sig))


def pool_matrix(strip, total, back=False):
    row = lax.broadcasted_iota(jnp.int32, (2 * PITCH, 256), 0)
    lane = lax.broadcasted_iota(jnp.int32, (2 * PITCH, 256), 1)
    half = (row >= PITCH).astype(jnp.int32)
    n = row - half * PITCH
    if back:
        v, most = jnp.where((n == 32) & (half == 1), -1, n), 33
    else:
        v, most = n - REACH, 32 + 2 * REACH
    near = jnp.bitwise_and(lane - 4 * v - 2 * half, 255) < 2
    place = strip * 32 + v
    keep = near & (n < most) & (place >= 0) & (place < total)
    return jnp.where(keep, 0.25, 0.0).astype(BF16)


def order_matrix():
    row = lax.broadcasted_iota(jnp.int32, (256, 256), 0)
    lane = lax.broadcasted_iota(jnp.int32, (256, 256), 1)
    j, i, c = row >> 7, (row >> 6) & 1, row & 63
    return jnp.where(lane == 4 * c + 2 * i + j, 1.0, 0.0).astype(BF16)


def constants(w_ref, joined_ref, back_w_ref, pool_ref, back_ref, order_ref, *, total):
    turned = [w_ref[2 - i].astype(F32).T for i in range(3)]
    back_w_ref[...] = jnp.concatenate(
        [jnp.concatenate([t[:, 64 * j : 64 * j + 64] for t in turned], 1) for j in range(3)], 0
    ).astype(BF16)
    joined_ref[...] = jnp.concatenate([w_ref[0], w_ref[1], w_ref[2]], axis=1)
    pool_ref[...] = pool_matrix(strip_index(), total)
    back_ref[...] = pool_matrix(strip_index(), total, back=True)
    order_ref[...] = order_matrix()


def beside(a_ref, b_ref, place, count):
    even = (place & 1) == 0
    a = a_ref[...].astype(F32)
    b = jnp.where((place > 0) & (place < count - 1), b_ref[...].astype(F32), 0.0)
    return jnp.where(even, b, a).astype(BF16), jnp.where(even, a, b).astype(BF16)


def pack_row(row, r, slot, head, tail):
    turned = roll(row.astype(F32), 16 * r, 1)
    return jnp.where(slot == r, turned, head), jnp.where(slot == (r - 1) % 8, turned, tail)


def pack_own(x_ref, head_ref, tail_ref, a_ref, b_ref):
    even = (strip_index() & 1) == 0
    slot = lax.broadcasted_iota(jnp.int32, (64, 128), 1) >> 4
    head = tail = jnp.zeros((64, 128), F32)
    for r in range(x_ref.shape[0]):
        head, tail = pack_row(x_ref[r], r, slot, head, tail)
    a_ref[:64] = jnp.where(even, tail, head).astype(BF16)
    b_ref[:64] = jnp.where(even, head, tail).astype(BF16)
    first, last = head_ref[...].astype(F32), tail_ref[...].astype(F32)
    a_ref[64:] = jnp.where(even, last, first).astype(BF16)
    b_ref[64:] = jnp.where(even, first, last).astype(BF16)


def pack_borders(up_a_ref, up_b_ref, own_a_ref, own_b_ref, a_ref, b_ref, above_ref, below_ref, *, bands):
    even = (strip_index() & 1) == 0
    above_ref[...], below_ref[...] = beside(up_a_ref, up_b_ref, lax.axis_index("row"), bands)
    slot = lax.broadcasted_iota(jnp.int32, (64, 128), 1) >> 4
    head = tail = jnp.zeros((64, 128), F32)
    for r, ref in enumerate((above_ref, below_ref)):
        head, tail = pack_row(ref[...], r, slot, head, tail)
    a_ref[:64] = jnp.where(even, tail, head).astype(BF16)
    b_ref[:64] = jnp.where(even, head, tail).astype(BF16)
    a_ref[64:] = own_a_ref[...]
    b_ref[64:] = own_b_ref[...]


def layer_one(
    x_ref,
    above_ref,
    below_ref,
    a_ref,
    b_ref,
    w_ref,
    pool_ref,
    order_ref,
    pooled_ref,
    slope_ref,
    wide_ref,
    *,
    strips,
):
    strip = strip_index()
    band_rows = x_ref.shape[0]
    slot = lax.broadcasted_iota(jnp.int32, (128, 128), 1) >> 4
    inner = (strip > 0) & (strip < strips - 1)
    sides = a_ref[:128].astype(F32), jnp.where(inner, b_ref[:128].astype(F32), 0.0)
    from_a = ((slot ^ strip) & 1) == 0
    packed = jnp.where(from_a, *sides), jnp.where(from_a, *sides[::-1])
    for r in range(band_rows):
        wide_ref[1 + r, :, 128:] = roll(packed[r % 2][64:], -16 * r, 1).astype(BF16)
    for r, place in enumerate((0, band_rows + 1)):
        wide_ref[place, :, 128:] = roll(packed[r][:64], -16 * r, 1).astype(BF16)
    wide_ref[0, :, :128] = above_ref[...]
    wide_ref[1 : band_rows + 1, :, :128] = x_ref[...]
    wide_ref[band_rows + 1, :, :128] = below_ref[...]
    weights = w_ref[...]
    rows = slope_ref.shape[0]
    halves, held = [], None
    for h in range(rows):
        y = dot(weights, wide_ref[h : h + 3].reshape(192, 256), (1, 0))
        pre = roll(y[:64], 1, 1) + y[64:128] + roll(y[128:], -1, 1)
        sig = sigmoid(pre)
        slope_ref[h] = slope_of(pre, sig).astype(BF16)
        active = pre * sig
        if h % 2:
            halves.append((held + active).astype(BF16))
        else:
            held = active
    pooled = dot(pool_ref[...], jnp.concatenate(halves, 0), (1, 1))
    stacked = jnp.concatenate(
        [
            jnp.concatenate(
                [pooled[:PITCH, u * 128 : u * 128 + 128], pooled[PITCH:, u * 128 : u * 128 + 128]], 1
            )
            for u in range(2)
        ],
        0,
    ).astype(BF16)
    ordered = dot(stacked, order_ref[...], (1, 0)).astype(BF16)
    for u in range(2):
        pooled_ref[u] = ordered[u * PITCH : u * PITCH + SENT]


def layer_two(og_ref, w_ref, *refs, bands):
    pieces, refs = refs[:bands], refs[bands:]
    terms, refs = refs[:bands], refs[bands:]
    map_ref, grad_ref, pack_ref = refs
    band = lax.axis_index("row")
    rows, _, filters = og_ref.shape
    count = rows * PITCH
    map_ref[0] = jnp.zeros((PITCH, 256), BF16)
    map_ref[rows + 1] = jnp.zeros((PITCH, 256), BF16)
    blank = jnp.zeros((PITCH - SENT, 256), BF16)
    for k, piece in zip(row_order(bands, near_first=True), pieces):
        for t in range(2):
            map_ref[1 + 2 * (band ^ k) + t] = jnp.concatenate([piece[t], blank], 0)
    near = jnp.concatenate([map_ref[i : i + rows].reshape(count, 256) for i in range(3)], 1)
    y = dot(near, jnp.concatenate([w_ref[i] for i in range(3)], 1), (1, 1))
    pre = roll(y[:, :filters], 1, 0) + y[:, filters : 2 * filters] + roll(y[:, 2 * filters :], -1, 0)
    grad = og_ref[...].reshape(count, filters).astype(F32) * slope_of(pre, sigmoid(pre))
    grad = grad.astype(BF16)
    grad_ref[0] = jnp.zeros((PITCH, filters), BF16)
    grad_ref[rows + 1] = jnp.zeros((PITCH, filters), BF16)
    grad_ref[1 : rows + 1] = grad.reshape(rows, PITCH, filters)
    near = jnp.concatenate([grad_ref[2 - i : 2 - i + rows].reshape(count, filters) for i in range(3)], 1)
    weights = [
        jnp.concatenate([w_ref[i, j * filters : (j + 1) * filters] for j in range(3)], 1) for i in range(3)
    ]
    z = dot(near, jnp.concatenate(weights, 0), (1, 0))
    spread = roll(z[:, :256], -1 - REACH, 0) + roll(z[:, 256:512], -REACH, 0) + roll(z[:, 512:], 1 - REACH, 0)
    spread = spread.reshape(rows, PITCH, 256)
    odd = (lax.broadcasted_iota(jnp.int32, (8, 256), 1) & 1) == 1
    row = lax.broadcasted_iota(jnp.int32, (8, 256), 0)
    ends = [jnp.where(odd, spread[u - 1, 47:48], spread[u, 32:33]) for u in range(rows)]
    for p in range(rows // 2):
        shared = jnp.where(row == 0, ends[2 * p], jnp.where(row == 1, ends[2 * p + 1], 0.0))
        pack_ref[p] = jnp.concatenate([spread[2 * p, :32], shared, spread[2 * p + 1, :32]], 0).astype(BF16)
    for k in range(bands):
        terms[k][...] = pack_ref[band ^ k]


def filter_two_grads(map_ref, grad_ref, keep_ref, send_ref, all_ref):
    pair = lax.axis_index("pair")
    rows = map_ref.shape[0] - 2
    filters = grad_ref.shape[2]
    v = lax.broadcasted_iota(jnp.int32, (rows, PITCH, filters), 1)
    own = (v >= REACH) & (v < REACH + 32)
    wide = jnp.where(own, grad_ref[1 : rows + 1].astype(F32), 0.0).reshape(rows * PITCH, filters)
    cat = jnp.concatenate([roll(wide, -1, 0), wide, roll(wide, 1, 0)], 1).astype(BF16)
    taps = 3 * filters
    for i in range(3):
        part = dot(cat, map_ref[i : i + rows].reshape(rows * PITCH, 256), (0, 0))
        all_ref[i * taps : (i + 1) * taps] = part.astype(BF16)
    half = keep_ref.shape[0]
    keep_ref[...] = all_ref[pl.ds(pl.multiple_of(pair * half, 16), half)]
    send_ref[...] = all_ref[pl.ds(pl.multiple_of((1 - pair) * half, 16), half)]


def add_after(a_ref, b_ref, *refs):
    refs[-1][...] = (a_ref[...].astype(F32) + b_ref[...].astype(F32)).astype(BF16)


def add_halves(a_ref, b_ref, two_ref, one_ref):
    half = two_ref.shape[0]
    total = (a_ref[...].astype(F32) + b_ref[...].astype(F32)).astype(BF16)
    two_ref[...] = total[:half]
    one_ref[...] = total[half:]


def add_joined(a_ref, b_ref, c_ref, d_ref, _, __, out_ref):
    half = a_ref.shape[0]
    out_ref[:half] = (a_ref[...].astype(F32) + b_ref[...].astype(F32)).astype(BF16)
    out_ref[half:] = (c_ref[...].astype(F32) + d_ref[...].astype(F32)).astype(BF16)


def sum_rows(*refs):
    *refs, a_ref, b_ref, out_ref, passed_a_ref, passed_b_ref = refs
    terms = dict(zip(row_order(len(refs), near_first=True), (ref[...].astype(F32) for ref in refs)))
    terms = [terms[k] for k in range(len(refs))]
    while len(terms) > 1:
        terms = [a + b for a, b in zip(terms[::2], terms[1::2])]
    out_ref[...] = terms[0].astype(BF16)
    passed_a_ref[...] = a_ref[...]
    passed_b_ref[...] = b_ref[...]


def grad_pre_one(*refs, bands):
    terms, refs = refs[:bands], refs[bands:]
    slope_ref, wide_ref, pool_ref, order_ref, keep_two_ref, send_two_ref, *refs = refs
    g_ref, a_ref, b_ref, keep_ref, send_ref, part_ref = refs
    summed = terms[0][...].astype(F32)
    for k in range(1, bands):
        summed = summed + terms[k][...].astype(F32)
    blank = jnp.zeros((8, 256), F32)
    ends = summed[32:40]
    blocks = [summed[:32], ends, blank, summed[40:], roll(ends, -1, 0), blank]
    ordered = dot(jnp.concatenate(blocks, 0).astype(BF16), order_ref[...], (1, 1)).astype(BF16)
    pool = pool_ref[...]
    cats = []
    own = lax.broadcasted_iota(jnp.int32, (64, 256), 1) < 128
    for u in range(2):
        block = ordered[u * PITCH : (u + 1) * PITCH]
        up = dot(jnp.concatenate([block[:, :128], block[:, 128:]], 0), pool, (0, 0))
        for i in range(4):
            h = 4 * u + i
            g = (up[64 * (i // 2) : 64 * (i // 2) + 64] * slope_ref[h].astype(F32)).astype(BF16)
            g_ref[h] = g
            mine = jnp.where(own, g.astype(F32), 0.0)
            cats.append(jnp.concatenate([roll(mine, -1, 1), mine, roll(mine, 1, 1)], 0).astype(BF16))
    around = jnp.concatenate([wide_ref[h : h + 3].reshape(192, 256) for h in range(8)], 1)
    acc = dot(jnp.concatenate(cats, 1), around, (1, 1))
    even = (lax.axis_index("row") & 1) == 0
    first, last = g_ref[0].astype(F32), g_ref[7].astype(F32)
    a_ref[...] = jnp.where(even, last, first).astype(BF16)
    b_ref[...] = jnp.where(even, first, last).astype(BF16)
    part_ref[:96] = jnp.concatenate([acc[:96, :128], acc[96:, :128]], 1)
    part_ref[96:] = jnp.concatenate([acc[48 * q : 48 * q + 48, 128:] for q in range(4)], 1)
    half = keep_two_ref.shape[0]
    for ref, two_ref in ((keep_ref, keep_two_ref), (send_ref, send_two_ref)):
        ref[:half] = two_ref[...]
        ref[half:] = part_ref[...].astype(BF16)


def layer_one_back(g_ref, a_ref, b_ref, w_ref, out_ref, done_ref, *, bands):
    above, below = beside(a_ref, b_ref, lax.axis_index("row"), bands)
    done_ref[...] = jnp.zeros(done_ref.shape, F32)
    lines = [above] + [g_ref[h] for h in range(8)] + [below]
    rows = []
    for h in range(8):
        z = dot(w_ref[...], jnp.concatenate(lines[h : h + 3], 0), (1, 0))
        rows.append((roll(z[:64], -1, 1) + z[64:128] + roll(z[128:], 1, 1))[:, :128])
    out_ref[...] = jnp.swapaxes(jnp.stack(rows, 0), 0, 1).astype(BF16)


def finish(mine_ref, other_ref, _, one_hbm, two_hbm, one_ref, two_ref, flat_ref, sems, *, scales):
    pair, half = lax.axis_index("pair"), mine_ref.shape[0] - ROWS_ONE
    copies = []
    for n, (ref, place) in enumerate(((mine_ref, pair), (other_ref, 1 - pair))):
        rows = pl.ds(pl.multiple_of(place * half, 16), half)
        two_ref[n] = ref[:half].astype(F32) * scales[1]
        copies.append(pltpu.make_async_copy(two_ref.at[n], two_hbm.at[rows], sems.at[n]))
        copies[-1].start()
    last = pair == lax.axis_size("pair") - 1
    flat_ref[...] = jnp.where(last, mine_ref[half:].astype(F32), other_ref[half:].astype(F32)) * scales[0]
    one_ref[0, :96] = flat_ref[:96, :64]
    one_ref[1, :96] = flat_ref[:96, 64:128]
    one_ref[0, 96:] = flat_ref[:96, 128:192]
    one_ref[1, 96:] = flat_ref[:96, 192:]
    for q in range(4):
        one_ref[2, 48 * q : 48 * q + 48] = flat_ref[96:, 64 * q : 64 * q + 64]
    copies.append(pltpu.make_async_copy(one_ref, one_hbm, sems.at[2]))
    copies[-1].start()
    for copy in copies:
        copy.wait()


def even_swap(values, axis, count):
    return lax.ppermute(values, axis, [(n, n ^ 1) for n in range(count)])


def odd_partner(place):
    return place - 1 if place % 2 == 0 else place + 1


def odd_row_swap(values):
    bands, cores = lax.axis_size("row"), lax.axis_size("pair")
    steps = []
    for n in range(bands):
        for p in range(cores):
            to = (n, p ^ 1) if n in (0, bands - 1) else (odd_partner(n), p)
            steps.append((n * cores + p, to[0] * cores + to[1]))
    return lax.ppermute(values, ("row", "pair"), steps)


def odd_strip_swap(values):
    groups, strips = lax.axis_size("grp"), lax.axis_size(COLS)
    steps = []
    for g in range(groups):
        for n in range(strips):
            to = ((g + 1) % groups, n) if n in (0, strips - 1) else (g, odd_partner(n))
            steps.append((g * strips + n, to[0] * strips + to[1]))
    return lax.ppermute(values, ("grp",) + COLS, steps)


def xor_swap(values, axis, count, k):
    return lax.ppermute(values, axis, [(n, n ^ k) for n in range(count)])


def last_core_swap(values, axis, k):
    groups, count, cores = (lax.axis_size(name) for name in ("grp", axis, "pair"))
    steps = []
    for g in range(groups):
        for n in range(count):
            for p in range(cores):
                to = (g, n ^ k) if p == cores - 1 else ((g + 1) % groups, n)
                steps.append(((g * count + n) * cores + p, (to[0] * count + to[1]) * cores + p))
    return lax.ppermute(values, ("grp", axis, "pair"), steps)


def row_order(bands, near_first=False):
    far_first = sorted(range(1, bands), key=lambda k: (k < bands // 2, k))
    return [0] + (far_first[::-1] if near_first else far_first)


def row_swaps(values, bands, near_first=False):
    order = row_order(bands, near_first)
    return [values[0]] + [xor_swap(values[k], "row", bands, k) for k in order[1:]]


def added(a, b, *after):
    (total,) = whole_call(add_after, [shaped(a.shape)], [a, b, *after], 0, after=len(after))
    return total


def sum_but_last(part, axis, count):
    step = 1
    while 2 * step < count:
        part = added(part, xor_swap(part, axis, count, step))
        step *= 2
    return part, xor_swap(part, axis, count, step)


def local(features_in, filters_one, filters_two, out_grad):
    channels, band_rows, strip_cols = features_in.shape
    filters, own_cols, pooled_rows = out_grad.shape
    bands = lax.axis_size("row")
    strips = lax.axis_size(COLS)
    band = lax.axis_index("row")
    strip = lax.axis_index(COLS)
    pair = lax.axis_index("pair")
    height, width = band_rows * bands, strip_cols * strips
    total = own_cols * strips

    taps_one = jnp.transpose(filters_one, (1, 2, 0, 3)).reshape(3, 3 * channels, channels)
    taps_two = jnp.transpose(filters_two, (1, 2, 0, 3)).reshape(3, 3 * filters, 4 * channels)

    og = jnp.transpose(out_grad, (1, 2, 0))
    edge = REACH - 1
    x = jnp.transpose(features_in, (1, 0, 2))
    even = band % 2 == 0
    to_a, to_b = jnp.where(even, x[-1], x[0]), jnp.where(even, x[0], x[-1])
    head, tail = og[:edge], og[-edge:]
    joined_one, back_one, pool, pool_back, order = whole_call(
        functools.partial(constants, total=total),
        [shaped((3 * channels, 3 * channels))] * 2 + [shaped((2 * PITCH, 256))] * 2 + [shaped((256, 256))],
        [taps_one],
        10**8,
    )
    head, tail = head.reshape(-1, 128), tail.reshape(-1, 128)
    own_a, own_b = whole_call(
        pack_own, [shaped((channels + head.shape[0], 128))] * 2, [x, head, tail], 10**8
    )
    to_a, to_b, above, below = whole_call(
        functools.partial(pack_borders, bands=bands),
        [shaped((2 * channels + head.shape[0], 128))] * 2 + [shaped((channels, strip_cols))] * 2,
        [even_swap(to_a, "row", bands), odd_row_swap(to_b), own_a, own_b],
        1,
    )
    side_a, side_b = even_swap(to_a, COLS, strips), odd_strip_swap(to_b)
    pooled, slope, wide = whole_call(
        functools.partial(layer_one, strips=strips),
        [
            shaped((2, SENT, 4 * channels)),
            shaped((band_rows, channels, 256)),
            shaped((band_rows + 2, channels, 256)),
        ],
        [x, above, below, side_a, side_b, joined_one, pool, order],
        2 * band_rows * 192 * 192 * 256,
    )
    pieces = row_swaps([pooled] * bands, bands, near_first=True)

    even = strip % 2 == 0
    ends = [side[2 * channels :].reshape(og[:edge].shape) for side in (side_a, side_b)]
    ends[1] = jnp.where((strip == 0) | (strip == strips - 1), 0, ends[1])
    before, after = jnp.where(even, ends[1], ends[0]), jnp.where(even, ends[0], ends[1])
    og = jnp.concatenate([before, og, after], 0)
    og = jnp.pad(og, ((1, PITCH - own_cols - 2 * REACH + 1), (0, 0), (0, 0)))
    og = jnp.transpose(og, (1, 0, 2))

    count = pooled_rows * PITCH
    *terms, pooled_map, grad_map = whole_call(
        functools.partial(layer_two, bands=bands),
        [shaped((72, 4 * channels))] * bands
        + [shaped((pooled_rows + 2, PITCH, 4 * channels)), shaped((pooled_rows + 2, PITCH, filters))],
        [og, taps_two] + pieces,
        4 * count * 9 * filters * 4 * channels,
        scratch=[pltpu.VMEM((bands, 72, 4 * channels), BF16)],
    )
    received = row_swaps(terms, bands)

    half = 9 * filters // 2
    keep_two, send_two = whole_call(
        filter_two_grads,
        [shaped((half, 4 * channels))] * 2,
        [pooled_map, grad_map],
        2 * count * 9 * filters * 4 * channels,
        scratch=[pltpu.VMEM((2 * half, 4 * channels), BF16)],
    )
    g, up_a, up_b, keep, send = whole_call(
        functools.partial(grad_pre_one, bands=bands),
        [shaped((band_rows, channels, 256))]
        + [shaped((channels, 256))] * 2
        + [shaped((half + ROWS_ONE, 256))] * 2,
        received + [slope, wide, pool_back, order, keep_two, send_two],
        2 * 8 * 192 * 192 * 256,
        scratch=[pltpu.VMEM((144, 256), F32)],
    )
    two, one = whole_call(
        add_halves,
        [shaped((half, 256)), shaped((ROWS_ONE, 256))],
        [keep, even_swap(send, "pair", 2)],
        0,
    )
    columns = lax.axis_size("col")
    two, two_more = sum_but_last(two, "col", columns)
    ones = [one] + [last_core_swap(one, "row", k) for k in row_order(bands, near_first=True)[1:]]
    one, up_a, up_b = whole_call(
        sum_rows, [shaped(a.shape) for a in (one, up_a, up_b)], ones + [up_a, up_b], 0
    )
    up_a, up_b = even_swap(up_a, "row", bands), odd_row_swap(up_b)
    input_grad, done = whole_call(
        functools.partial(layer_one_back, bands=bands),
        [shaped(features_in.shape), shaped((8, 128), F32)],
        [g, up_a, up_b, back_one],
        2 * band_rows * 192 * 192 * 256,
    )
    step = 1
    while 2 * step < columns:
        one = added(one, last_core_swap(one, "col", step))
        step *= 2
    (mine,) = whole_call(
        add_joined,
        [shaped((half + ROWS_ONE, 256))],
        [two, two_more, one, last_core_swap(one, "col", step), up_a, up_b],
        0,
        after=2,
    )
    grad_one, grad_two = whole_call(
        functools.partial(
            finish, scales=(1.0 / math.sqrt(height * width), 1.0 / math.sqrt(pooled_rows * total))
        ),
        [shaped((3, 3 * channels, channels), F32), shaped((2 * half, 256), F32)],
        [mine, even_swap(mine, "pair", 2), done],
        1,
        scratch=[
            pltpu.VMEM((3, 3 * channels, channels), F32),
            pltpu.VMEM((2, half, 256), F32),
            pltpu.VMEM((ROWS_ONE, 256), F32),
            pltpu.SemaphoreType.DMA((3,)),
        ],
        after=1,
        out_spaces=[pl.ANY] * 2,
    )
    grad_two = jnp.transpose(grad_two.reshape(3, 3, filters, 4 * channels), (2, 0, 1, 3))
    grad_one = jnp.transpose(grad_one.reshape(3, 3, channels, channels), (2, 0, 1, 3))
    return (input_grad, grad_one, grad_two)


def solution(mesh):
    in_specs = (
        P("grp", "row", ("col", "pair")),
        P(),
        P("row", None, None, None),
        P(("grp", "row"), ("col", "pair"), None),
    )
    out_specs = (
        P("grp", "row", ("col", "pair")),
        P("grp", None, None, None),
        P(("grp", "row"), None, None, None),
    )
    return jax.shard_map(local, mesh=mesh, in_specs=in_specs, out_specs=out_specs, check_vma=False)
```

```python
import functools
import math

import jax
import jax.numpy as jnp
from jax import lax
from jax.experimental import pallas as pl
from jax.experimental.pallas import tpu as pltpu
from jax.sharding import PartitionSpec as P

BF16 = jnp.bfloat16
F32 = jnp.float32
COLS = ("col", "pair")
REACH = 3
ROWS_ONE = 144
PITCH = 48
SENT = 40


def dot(a, b, contract):
    return lax.dot_general(a, b, ((contract[:1], contract[1:]), ((), ())), preferred_element_type=F32)


def whole_call(body, outs, operands, flops, scratch=(), after=0, out_spaces=None):
    specs = [
        pl.BlockSpec(memory_space=pltpu.VMEM) for _ in range(len(operands) - after)
    ] + [pl.BlockSpec(memory_space=pl.ANY)] * after
    sizes = [math.prod(a.shape) * a.dtype.itemsize for a in tuple(operands) + tuple(outs)]
    moved = sum(sizes) if flops else 0
    return pl.pallas_call(
        body,
        out_shape=outs,
        in_specs=specs,
        out_specs=[pl.BlockSpec(memory_space=space) for space in out_spaces or [pltpu.VMEM] * len(outs)],
        scratch_shapes=list(scratch),
        cost_estimate=pl.CostEstimate(flops=flops, bytes_accessed=moved, transcendentals=0),
        compiler_params=pltpu.CompilerParams(vmem_limit_bytes=40 * 1024 * 1024),
    )(*operands)


def strip_index():
    return lax.axis_index("col") * lax.axis_size("pair") + lax.axis_index("pair")


def shaped(shape, dtype=BF16):
    return jax.ShapeDtypeStruct(shape, dtype)


def roll(values, amount, axis):
    return pltpu.roll(values, amount % values.shape[axis], axis)


def sigmoid(values):
    return 0.5 + 0.5 * jnp.tanh(0.5 * values)


def slope_of(values, sig):
    return sig * (1.0 + values * (1.0 - sig))


def pool_matrix(strip, total, back=False):
    row = lax.broadcasted_iota(jnp.int32, (2 * PITCH, 256), 0)
    lane = lax.broadcasted_iota(jnp.int32, (2 * PITCH, 256), 1)
    half = (row >= PITCH).astype(jnp.int32)
    n = row - half * PITCH
    if back:
        v, most = jnp.where((n == 32) & (half == 1), -1, n), 33
    else:
        v, most = n - REACH, 32 + 2 * REACH
    near = jnp.bitwise_and(lane - 4 * v - 2 * half, 255) < 2
    place = strip * 32 + v
    keep = near & (n < most) & (place >= 0) & (place < total)
    return jnp.where(keep, 0.25, 0.0).astype(BF16)


def order_matrix():
    row = lax.broadcasted_iota(jnp.int32, (256, 256), 0)
    lane = lax.broadcasted_iota(jnp.int32, (256, 256), 1)
    j, i, c = row >> 7, (row >> 6) & 1, row & 63
    return jnp.where(lane == 4 * c + 2 * i + j, 1.0, 0.0).astype(BF16)


def constants(w_ref, joined_ref, back_w_ref, pool_ref, back_ref, order_ref, *, total):
    turned = [w_ref[2 - i].astype(F32).T for i in range(3)]
    back_w_ref[...] = jnp.concatenate(
        [jnp.concatenate([t[:, 64 * j : 64 * j + 64] for t in turned], 1) for j in range(3)], 0
    ).astype(BF16)
    joined_ref[...] = jnp.concatenate([w_ref[0], w_ref[1], w_ref[2]], axis=1)
    pool_ref[...] = pool_matrix(strip_index(), total)
    back_ref[...] = pool_matrix(strip_index(), total, back=True)
    order_ref[...] = order_matrix()


def beside(a_ref, b_ref, place, count):
    even = (place & 1) == 0
    a = a_ref[...].astype(F32)
    b = jnp.where((place > 0) & (place < count - 1), b_ref[...].astype(F32), 0.0)
    return jnp.where(even, b, a).astype(BF16), jnp.where(even, a, b).astype(BF16)


def pack_row(row, r, slot, head, tail):
    turned = roll(row.astype(F32), 16 * r, 1)
    return jnp.where(slot == r, turned, head), jnp.where(slot == (r - 1) % 8, turned, tail)


def pack_own(x_ref, head_ref, tail_ref, a_ref, b_ref):
    even = (strip_index() & 1) == 0
    slot = lax.broadcasted_iota(jnp.int32, (64, 128), 1) >> 4
    head = tail = jnp.zeros((64, 128), F32)
    for r in range(x_ref.shape[0]):
        head, tail = pack_row(x_ref[r], r, slot, head, tail)
    a_ref[:64] = jnp.where(even, tail, head).astype(BF16)
    b_ref[:64] = jnp.where(even, head, tail).astype(BF16)
    first, last = head_ref[...].astype(F32), tail_ref[...].astype(F32)
    a_ref[64:] = jnp.where(even, last, first).astype(BF16)
    b_ref[64:] = jnp.where(even, first, last).astype(BF16)


def pack_borders(up_a_ref, up_b_ref, own_a_ref, own_b_ref, a_ref, b_ref, above_ref, below_ref, *, bands):
    even = (strip_index() & 1) == 0
    above_ref[...], below_ref[...] = beside(up_a_ref, up_b_ref, lax.axis_index("row"), bands)
    slot = lax.broadcasted_iota(jnp.int32, (64, 128), 1) >> 4
    head = tail = jnp.zeros((64, 128), F32)
    for r, ref in enumerate((above_ref, below_ref)):
        head, tail = pack_row(ref[...], r, slot, head, tail)
    a_ref[:64] = jnp.where(even, tail, head).astype(BF16)
    b_ref[:64] = jnp.where(even, head, tail).astype(BF16)
    a_ref[64:] = own_a_ref[...]
    b_ref[64:] = own_b_ref[...]


def layer_one(
    x_ref,
    above_ref,
    below_ref,
    a_ref,
    b_ref,
    w_ref,
    pool_ref,
    order_ref,
    pooled_ref,
    slope_ref,
    wide_ref,
    *,
    strips,
):
    strip = strip_index()
    band_rows = x_ref.shape[0]
    slot = lax.broadcasted_iota(jnp.int32, (128, 128), 1) >> 4
    inner = (strip > 0) & (strip < strips - 1)
    sides = a_ref[:128].astype(F32), jnp.where(inner, b_ref[:128].astype(F32), 0.0)
    from_a = ((slot ^ strip) & 1) == 0
    packed = jnp.where(from_a, *sides), jnp.where(from_a, *sides[::-1])
    for r in range(band_rows):
        wide_ref[1 + r, :, 128:] = roll(packed[r % 2][64:], -16 * r, 1).astype(BF16)
    for r, place in enumerate((0, band_rows + 1)):
        wide_ref[place, :, 128:] = roll(packed[r][:64], -16 * r, 1).astype(BF16)
    wide_ref[0, :, :128] = above_ref[...]
    wide_ref[1 : band_rows + 1, :, :128] = x_ref[...]
    wide_ref[band_rows + 1, :, :128] = below_ref[...]
    weights = w_ref[...]
    rows = slope_ref.shape[0]
    halves, held = [], None
    for h in range(rows):
        y = dot(weights, wide_ref[h : h + 3].reshape(192, 256), (1, 0))
        pre = roll(y[:64], 1, 1) + y[64:128] + roll(y[128:], -1, 1)
        sig = sigmoid(pre)
        slope_ref[h] = slope_of(pre, sig).astype(BF16)
        active = pre * sig
        if h % 2:
            halves.append((held + active).astype(BF16))
        else:
            held = active
    pooled = dot(pool_ref[...], jnp.concatenate(halves, 0), (1, 1))
    stacked = jnp.concatenate(
        [
            jnp.concatenate(
                [pooled[:PITCH, u * 128 : u * 128 + 128], pooled[PITCH:, u * 128 : u * 128 + 128]], 1
            )
            for u in range(2)
        ],
        0,
    ).astype(BF16)
    ordered = dot(stacked, order_ref[...], (1, 0)).astype(BF16)
    for u in range(2):
        pooled_ref[u] = ordered[u * PITCH : u * PITCH + SENT]


def layer_two(og_ref, w_ref, *refs, bands):
    pieces, refs = refs[:bands], refs[bands:]
    terms, refs = refs[:bands], refs[bands:]
    map_ref, grad_ref, pack_ref = refs
    band = lax.axis_index("row")
    rows, _, filters = og_ref.shape
    count = rows * PITCH
    map_ref[0] = jnp.zeros((PITCH, 256), BF16)
    map_ref[rows + 1] = jnp.zeros((PITCH, 256), BF16)
    blank = jnp.zeros((PITCH - SENT, 256), BF16)
    for k, piece in zip(row_order(bands, near_first=True), pieces):
        for t in range(2):
            map_ref[1 + 2 * (band ^ k) + t] = jnp.concatenate([piece[t], blank], 0)
    near = jnp.concatenate([map_ref[i : i + rows].reshape(count, 256) for i in range(3)], 1)
    y = dot(near, jnp.concatenate([w_ref[i] for i in range(3)], 1), (1, 1))
    pre = roll(y[:, :filters], 1, 0) + y[:, filters : 2 * filters] + roll(y[:, 2 * filters :], -1, 0)
    grad = og_ref[...].reshape(count, filters).astype(F32) * slope_of(pre, sigmoid(pre))
    grad = grad.astype(BF16)
    grad_ref[0] = jnp.zeros((PITCH, filters), BF16)
    grad_ref[rows + 1] = jnp.zeros((PITCH, filters), BF16)
    grad_ref[1 : rows + 1] = grad.reshape(rows, PITCH, filters)
    near = jnp.concatenate([grad_ref[2 - i : 2 - i + rows].reshape(count, filters) for i in range(3)], 1)
    weights = [
        jnp.concatenate([w_ref[i, j * filters : (j + 1) * filters] for j in range(3)], 1) for i in range(3)
    ]
    z = dot(near, jnp.concatenate(weights, 0), (1, 0))
    spread = roll(z[:, :256], -1 - REACH, 0) + roll(z[:, 256:512], -REACH, 0) + roll(z[:, 512:], 1 - REACH, 0)
    spread = spread.reshape(rows, PITCH, 256)
    odd = (lax.broadcasted_iota(jnp.int32, (8, 256), 1) & 1) == 1
    row = lax.broadcasted_iota(jnp.int32, (8, 256), 0)
    ends = [jnp.where(odd, spread[u - 1, 47:48], spread[u, 32:33]) for u in range(rows)]
    for p in range(rows // 2):
        shared = jnp.where(row == 0, ends[2 * p], jnp.where(row == 1, ends[2 * p + 1], 0.0))
        pack_ref[p] = jnp.concatenate([spread[2 * p, :32], shared, spread[2 * p + 1, :32]], 0).astype(BF16)
    for k in range(bands):
        terms[k][...] = pack_ref[band ^ k]


def filter_two_grads(map_ref, grad_ref, keep_ref, send_ref, all_ref):
    pair = lax.axis_index("pair")
    rows = map_ref.shape[0] - 2
    filters = grad_ref.shape[2]
    v = lax.broadcasted_iota(jnp.int32, (rows, PITCH, filters), 1)
    own = (v >= REACH) & (v < REACH + 32)
    wide = jnp.where(own, grad_ref[1 : rows + 1].astype(F32), 0.0).reshape(rows * PITCH, filters)
    cat = jnp.concatenate([roll(wide, -1, 0), wide, roll(wide, 1, 0)], 1).astype(BF16)
    taps = 3 * filters
    for i in range(3):
        part = dot(cat, map_ref[i : i + rows].reshape(rows * PITCH, 256), (0, 0))
        all_ref[i * taps : (i + 1) * taps] = part.astype(BF16)
    half = keep_ref.shape[0]
    keep_ref[...] = all_ref[pl.ds(pl.multiple_of(pair * half, 16), half)]
    send_ref[...] = all_ref[pl.ds(pl.multiple_of((1 - pair) * half, 16), half)]


def add_after(a_ref, b_ref, *refs):
    refs[-1][...] = (a_ref[...].astype(F32) + b_ref[...].astype(F32)).astype(BF16)


def add_halves(a_ref, b_ref, two_ref, one_ref):
    half = two_ref.shape[0]
    total = (a_ref[...].astype(F32) + b_ref[...].astype(F32)).astype(BF16)
    two_ref[...] = total[:half]
    one_ref[...] = total[half:]


def grad_pre_one(*refs, bands):
    terms, refs = refs[:bands], refs[bands:]
    slope_ref, wide_ref, pool_ref, order_ref, keep_two_ref, send_two_ref, *refs = refs
    g_ref, a_ref, b_ref, keep_ref, send_ref, part_ref = refs
    summed = terms[0][...].astype(F32)
    for k in range(1, bands):
        summed = summed + terms[k][...].astype(F32)
    blank = jnp.zeros((8, 256), F32)
    ends = summed[32:40]
    blocks = [summed[:32], ends, blank, summed[40:], roll(ends, -1, 0), blank]
    ordered = dot(jnp.concatenate(blocks, 0).astype(BF16), order_ref[...], (1, 1)).astype(BF16)
    pool = pool_ref[...]
    cats = []
    own = lax.broadcasted_iota(jnp.int32, (64, 256), 1) < 128
    for u in range(2):
        block = ordered[u * PITCH : (u + 1) * PITCH]
        up = dot(jnp.concatenate([block[:, :128], block[:, 128:]], 0), pool, (0, 0))
        for i in range(4):
            h = 4 * u + i
            g = (up[64 * (i // 2) : 64 * (i // 2) + 64] * slope_ref[h].astype(F32)).astype(BF16)
            g_ref[h] = g
            mine = jnp.where(own, g.astype(F32), 0.0)
            cats.append(jnp.concatenate([roll(mine, -1, 1), mine, roll(mine, 1, 1)], 0).astype(BF16))
    around = jnp.concatenate([wide_ref[h : h + 3].reshape(192, 256) for h in range(8)], 1)
    acc = dot(jnp.concatenate(cats, 1), around, (1, 1))
    even = (lax.axis_index("row") & 1) == 0
    first, last = g_ref[0].astype(F32), g_ref[7].astype(F32)
    a_ref[...] = jnp.where(even, last, first).astype(BF16)
    b_ref[...] = jnp.where(even, first, last).astype(BF16)
    part_ref[:96] = jnp.concatenate([acc[:96, :128], acc[96:, :128]], 1)
    part_ref[96:] = jnp.concatenate([acc[48 * q : 48 * q + 48, 128:] for q in range(4)], 1)
    half = keep_two_ref.shape[0]
    for ref, two_ref in ((keep_ref, keep_two_ref), (send_ref, send_two_ref)):
        ref[:half] = two_ref[...]
        ref[half:] = part_ref[...].astype(BF16)


def layer_one_back(g_ref, a_ref, b_ref, w_ref, out_ref, done_ref, *, bands):
    above, below = beside(a_ref, b_ref, lax.axis_index("row"), bands)
    done_ref[...] = jnp.zeros(done_ref.shape, F32)
    lines = [above] + [g_ref[h] for h in range(8)] + [below]
    rows = []
    for h in range(8):
        z = dot(w_ref[...], jnp.concatenate(lines[h : h + 3], 0), (1, 0))
        rows.append((roll(z[:64], -1, 1) + z[64:128] + roll(z[128:], 1, 1))[:, :128])
    out_ref[...] = jnp.swapaxes(jnp.stack(rows, 0), 0, 1).astype(BF16)


def finish_two(mine_ref, other_ref, two_hbm, done_ref, two_ref, sems, *, scale):
    pair, half = lax.axis_index("pair"), mine_ref.shape[0]
    done_ref[...] = jnp.zeros(done_ref.shape, F32)
    copies = []
    for n, (ref, place) in enumerate(((mine_ref, pair), (other_ref, 1 - pair))):
        rows = pl.ds(pl.multiple_of(place * half, 16), half)
        two_ref[n] = ref[...].astype(F32) * scale
        copies.append(pltpu.make_async_copy(two_ref.at[n], two_hbm.at[rows], sems.at[n]))
        copies[-1].start()
    for copy in copies:
        copy.wait()


def finish_one(mine_ref, other_ref, out_ref, flat_ref, *, scale):
    last = lax.axis_index("pair") == lax.axis_size("pair") - 1
    flat_ref[...] = jnp.where(last, mine_ref[...].astype(F32), other_ref[...].astype(F32)) * scale
    out_ref[0, :96] = flat_ref[:96, :64]
    out_ref[1, :96] = flat_ref[:96, 64:128]
    out_ref[0, 96:] = flat_ref[:96, 128:192]
    out_ref[1, 96:] = flat_ref[:96, 192:]
    for q in range(4):
        out_ref[2, 48 * q : 48 * q + 48] = flat_ref[96:, 64 * q : 64 * q + 64]


def even_swap(values, axis, count):
    return lax.ppermute(values, axis, [(n, n ^ 1) for n in range(count)])


def odd_partner(place):
    return place - 1 if place % 2 == 0 else place + 1


def odd_row_swap(values):
    bands, cores = lax.axis_size("row"), lax.axis_size("pair")
    steps = []
    for n in range(bands):
        for p in range(cores):
            to = (n, p ^ 1) if n in (0, bands - 1) else (odd_partner(n), p)
            steps.append((n * cores + p, to[0] * cores + to[1]))
    return lax.ppermute(values, ("row", "pair"), steps)


def odd_strip_swap(values):
    groups, strips = lax.axis_size("grp"), lax.axis_size(COLS)
    steps = []
    for g in range(groups):
        for n in range(strips):
            to = ((g + 1) % groups, n) if n in (0, strips - 1) else (g, odd_partner(n))
            steps.append((g * strips + n, to[0] * strips + to[1]))
    return lax.ppermute(values, ("grp",) + COLS, steps)


def xor_swap(values, axis, count, k):
    return lax.ppermute(values, axis, [(n, n ^ k) for n in range(count)])


def last_core_swap(values, axis, k):
    groups, count, cores = (lax.axis_size(name) for name in ("grp", axis, "pair"))
    steps = []
    for g in range(groups):
        for n in range(count):
            for p in range(cores):
                to = (g, n ^ k) if p == cores - 1 else ((g + 1) % groups, n)
                steps.append(((g * count + n) * cores + p, (to[0] * count + to[1]) * cores + p))
    return lax.ppermute(values, ("grp", axis, "pair"), steps)


def row_order(bands, near_first=False):
    far_first = sorted(range(1, bands), key=lambda k: (k < bands // 2, k))
    return [0] + (far_first[::-1] if near_first else far_first)


def row_swaps(values, bands, near_first=False):
    order = row_order(bands, near_first)
    return [values[0]] + [xor_swap(values[k], "row", bands, k) for k in order[1:]]


def added(a, b, *after):
    (total,) = whole_call(add_after, [shaped(a.shape)], [a, b, *after], 0, after=len(after))
    return total


def sum_but_last(part, axis, count):
    step = 1
    while 2 * step < count:
        part = added(part, xor_swap(part, axis, count, step))
        step *= 2
    return part, xor_swap(part, axis, count, step)


def local(features_in, filters_one, filters_two, out_grad):
    channels, band_rows, strip_cols = features_in.shape
    filters, own_cols, pooled_rows = out_grad.shape
    bands = lax.axis_size("row")
    strips = lax.axis_size(COLS)
    band = lax.axis_index("row")
    strip = lax.axis_index(COLS)
    pair = lax.axis_index("pair")
    height, width = band_rows * bands, strip_cols * strips
    total = own_cols * strips

    taps_one = jnp.transpose(filters_one, (1, 2, 0, 3)).reshape(3, 3 * channels, channels)
    taps_two = jnp.transpose(filters_two, (1, 2, 0, 3)).reshape(3, 3 * filters, 4 * channels)

    og = jnp.transpose(out_grad, (1, 2, 0))
    edge = REACH - 1
    x = jnp.transpose(features_in, (1, 0, 2))
    even = band % 2 == 0
    to_a, to_b = jnp.where(even, x[-1], x[0]), jnp.where(even, x[0], x[-1])
    head, tail = og[:edge], og[-edge:]
    joined_one, back_one, pool, pool_back, order = whole_call(
        functools.partial(constants, total=total),
        [shaped((3 * channels, 3 * channels))] * 2 + [shaped((2 * PITCH, 256))] * 2 + [shaped((256, 256))],
        [taps_one],
        10**8,
    )
    head, tail = head.reshape(-1, 128), tail.reshape(-1, 128)
    own_a, own_b = whole_call(
        pack_own, [shaped((channels + head.shape[0], 128))] * 2, [x, head, tail], 10**8
    )
    to_a, to_b, above, below = whole_call(
        functools.partial(pack_borders, bands=bands),
        [shaped((2 * channels + head.shape[0], 128))] * 2 + [shaped((channels, strip_cols))] * 2,
        [even_swap(to_a, "row", bands), odd_row_swap(to_b), own_a, own_b],
        1,
    )
    side_a, side_b = even_swap(to_a, COLS, strips), odd_strip_swap(to_b)
    pooled, slope, wide = whole_call(
        functools.partial(layer_one, strips=strips),
        [
            shaped((2, SENT, 4 * channels)),
            shaped((band_rows, channels, 256)),
            shaped((band_rows + 2, channels, 256)),
        ],
        [x, above, below, side_a, side_b, joined_one, pool, order],
        2 * band_rows * 192 * 192 * 256,
    )
    pieces = row_swaps([pooled] * bands, bands, near_first=True)

    even = strip % 2 == 0
    ends = [side[2 * channels :].reshape(og[:edge].shape) for side in (side_a, side_b)]
    ends[1] = jnp.where((strip == 0) | (strip == strips - 1), 0, ends[1])
    before, after = jnp.where(even, ends[1], ends[0]), jnp.where(even, ends[0], ends[1])
    og = jnp.concatenate([before, og, after], 0)
    og = jnp.pad(og, ((1, PITCH - own_cols - 2 * REACH + 1), (0, 0), (0, 0)))
    og = jnp.transpose(og, (1, 0, 2))

    count = pooled_rows * PITCH
    *terms, pooled_map, grad_map = whole_call(
        functools.partial(layer_two, bands=bands),
        [shaped((72, 4 * channels))] * bands
        + [shaped((pooled_rows + 2, PITCH, 4 * channels)), shaped((pooled_rows + 2, PITCH, filters))],
        [og, taps_two] + pieces,
        4 * count * 9 * filters * 4 * channels,
        scratch=[pltpu.VMEM((bands, 72, 4 * channels), BF16)],
    )
    received = row_swaps(terms, bands)

    half = 9 * filters // 2
    keep_two, send_two = whole_call(
        filter_two_grads,
        [shaped((half, 4 * channels))] * 2,
        [pooled_map, grad_map],
        2 * count * 9 * filters * 4 * channels,
        scratch=[pltpu.VMEM((2 * half, 4 * channels), BF16)],
    )
    g, up_a, up_b, keep, send = whole_call(
        functools.partial(grad_pre_one, bands=bands),
        [shaped((band_rows, channels, 256))]
        + [shaped((channels, 256))] * 2
        + [shaped((half + ROWS_ONE, 256))] * 2,
        received + [slope, wide, pool_back, order, keep_two, send_two],
        2 * 8 * 192 * 192 * 256,
        scratch=[pltpu.VMEM((144, 256), F32)],
    )
    two, one = whole_call(
        add_halves,
        [shaped((half, 256)), shaped((ROWS_ONE, 256))],
        [keep, even_swap(send, "pair", 2)],
        0,
    )
    columns = lax.axis_size("col")
    two, two_more = sum_but_last(two, "col", columns)
    up_a, up_b = even_swap(up_a, "row", bands), odd_row_swap(up_b)
    step = 1
    while step < bands:
        one = added(one, last_core_swap(one, "row", step), *((up_a, up_b) if step == 1 else ()))
        step *= 2
    input_grad, done = whole_call(
        functools.partial(layer_one_back, bands=bands),
        [shaped(features_in.shape), shaped((8, 128), F32)],
        [g, up_a, up_b, back_one],
        2 * band_rows * 192 * 192 * 256,
    )
    mine_two = added(two, two_more, one)
    grad_two, wrote = whole_call(
        functools.partial(finish_two, scale=1.0 / math.sqrt(pooled_rows * total)),
        [shaped((2 * half, 256), F32), shaped((8, 128), F32)],
        [mine_two, even_swap(mine_two, "pair", 2)],
        10**8,
        scratch=[pltpu.VMEM((2, half, 256), F32), pltpu.SemaphoreType.DMA((2,))],
        out_spaces=[pl.ANY, pltpu.VMEM],
    )
    step = 1
    while step < columns:
        last = 2 * step >= columns
        one = added(one, last_core_swap(one, "col", step), *((wrote, done) if last else ()))
        step *= 2
    (grad_one,) = whole_call(
        functools.partial(finish_one, scale=1.0 / math.sqrt(height * width)),
        [shaped((3, 3 * channels, channels), F32)],
        [one, even_swap(one, "pair", 2)],
        1,
        scratch=[pltpu.VMEM((ROWS_ONE, 256), F32)],
    )
    grad_two = jnp.transpose(grad_two.reshape(3, 3, filters, 4 * channels), (2, 0, 1, 3))
    grad_one = jnp.transpose(grad_one.reshape(3, 3, channels, channels), (2, 0, 1, 3))
    return (input_grad, grad_one, grad_two)


def solution(mesh):
    in_specs = (
        P("grp", "row", ("col", "pair")),
        P(),
        P("row", None, None, None),
        P(("grp", "row"), ("col", "pair"), None),
    )
    out_specs = (
        P("grp", "row", ("col", "pair")),
        P("grp", None, None, None),
        P(("grp", "row"), None, None, None),
    )
    return jax.shard_map(local, mesh=mesh, in_specs=in_specs, out_specs=out_specs, check_vma=False)
```

```python
import functools
import math

import jax
import jax.numpy as jnp
from jax import lax
from jax.experimental import pallas as pl
from jax.experimental.pallas import tpu as pltpu
from jax.sharding import PartitionSpec as P

BF16 = jnp.bfloat16
F32 = jnp.float32
COLS = ("col", "pair")
REACH = 3
HALF_ONE = 72
PITCH = 48
SENT = 40


def dot(a, b, contract):
    return lax.dot_general(a, b, ((contract[:1], contract[1:]), ((), ())), preferred_element_type=F32)


def whole_call(body, outs, operands, flops, scratch=(), after=0, out_spaces=None):
    specs = [
        pl.BlockSpec(memory_space=pltpu.VMEM) for _ in range(len(operands) - after)
    ] + [pl.BlockSpec(memory_space=pl.ANY)] * after
    sizes = [math.prod(a.shape) * a.dtype.itemsize for a in tuple(operands) + tuple(outs)]
    moved = sum(sizes) if flops else 0
    return pl.pallas_call(
        body,
        out_shape=outs,
        in_specs=specs,
        out_specs=[pl.BlockSpec(memory_space=space) for space in out_spaces or [pltpu.VMEM] * len(outs)],
        scratch_shapes=list(scratch),
        cost_estimate=pl.CostEstimate(flops=flops, bytes_accessed=moved, transcendentals=0),
        compiler_params=pltpu.CompilerParams(vmem_limit_bytes=40 * 1024 * 1024),
    )(*operands)


def strip_index():
    return lax.axis_index("col") * lax.axis_size("pair") + lax.axis_index("pair")


def shaped(shape, dtype=BF16):
    return jax.ShapeDtypeStruct(shape, dtype)


def roll(values, amount, axis):
    return pltpu.roll(values, amount % values.shape[axis], axis)


def sigmoid(values):
    return 0.5 + 0.5 * jnp.tanh(0.5 * values)


def slope_of(values, sig):
    return sig * (1.0 + values * (1.0 - sig))


def pool_matrix(strip, total, back=False):
    row = lax.broadcasted_iota(jnp.int32, (2 * PITCH, 256), 0)
    lane = lax.broadcasted_iota(jnp.int32, (2 * PITCH, 256), 1)
    half = (row >= PITCH).astype(jnp.int32)
    n = row - half * PITCH
    if back:
        v, most = jnp.where((n == 32) & (half == 1), -1, n), 33
    else:
        v, most = n - REACH, 32 + 2 * REACH
    near = jnp.bitwise_and(lane - 4 * v - 2 * half, 255) < 2
    place = strip * 32 + v
    keep = near & (n < most) & (place >= 0) & (place < total)
    return jnp.where(keep, 0.25, 0.0).astype(BF16)


def order_matrix():
    row = lax.broadcasted_iota(jnp.int32, (256, 256), 0)
    lane = lax.broadcasted_iota(jnp.int32, (256, 256), 1)
    j, i, c = row >> 7, (row >> 6) & 1, row & 63
    return jnp.where(lane == 4 * c + 2 * i + j, 1.0, 0.0).astype(BF16)


def constants(w_ref, joined_ref, back_w_ref, pool_ref, back_ref, order_ref, *, total):
    turned = [w_ref[2 - i].astype(F32).T for i in range(3)]
    back_w_ref[...] = jnp.concatenate(
        [jnp.concatenate([t[:, 64 * j : 64 * j + 64] for t in turned], 1) for j in range(3)], 0
    ).astype(BF16)
    joined_ref[...] = jnp.concatenate([w_ref[0], w_ref[1], w_ref[2]], axis=1)
    pool_ref[...] = pool_matrix(strip_index(), total)
    back_ref[...] = pool_matrix(strip_index(), total, back=True)
    order_ref[...] = order_matrix()


def beside(a_ref, b_ref, place, count):
    even = (place & 1) == 0
    a = a_ref[...].astype(F32)
    b = jnp.where((place > 0) & (place < count - 1), b_ref[...].astype(F32), 0.0)
    return jnp.where(even, b, a).astype(BF16), jnp.where(even, a, b).astype(BF16)


def pack_row(row, r, slot, head, tail):
    turned = roll(row.astype(F32), 16 * r, 1)
    return jnp.where(slot == r, turned, head), jnp.where(slot == (r - 1) % 8, turned, tail)


def pack_own(x_ref, head_ref, tail_ref, a_ref, b_ref):
    even = (strip_index() & 1) == 0
    slot = lax.broadcasted_iota(jnp.int32, (64, 128), 1) >> 4
    head = tail = jnp.zeros((64, 128), F32)
    for r in range(x_ref.shape[0]):
        head, tail = pack_row(x_ref[r], r, slot, head, tail)
    a_ref[:64] = jnp.where(even, tail, head).astype(BF16)
    b_ref[:64] = jnp.where(even, head, tail).astype(BF16)
    first, last = head_ref[...].astype(F32), tail_ref[...].astype(F32)
    a_ref[64:] = jnp.where(even, last, first).astype(BF16)
    b_ref[64:] = jnp.where(even, first, last).astype(BF16)


def pack_borders(up_a_ref, up_b_ref, own_a_ref, own_b_ref, a_ref, b_ref, above_ref, below_ref, *, bands):
    even = (strip_index() & 1) == 0
    above_ref[...], below_ref[...] = beside(up_a_ref, up_b_ref, lax.axis_index("row"), bands)
    slot = lax.broadcasted_iota(jnp.int32, (64, 128), 1) >> 4
    head = tail = jnp.zeros((64, 128), F32)
    for r, ref in enumerate((above_ref, below_ref)):
        head, tail = pack_row(ref[...], r, slot, head, tail)
    a_ref[:64] = jnp.where(even, tail, head).astype(BF16)
    b_ref[:64] = jnp.where(even, head, tail).astype(BF16)
    a_ref[64:] = own_a_ref[...]
    b_ref[64:] = own_b_ref[...]


def layer_one(
    x_ref,
    above_ref,
    below_ref,
    a_ref,
    b_ref,
    w_ref,
    pool_ref,
    order_ref,
    pooled_ref,
    slope_ref,
    wide_ref,
    *,
    strips,
):
    strip = strip_index()
    band_rows = x_ref.shape[0]
    slot = lax.broadcasted_iota(jnp.int32, (128, 128), 1) >> 4
    inner = (strip > 0) & (strip < strips - 1)
    sides = a_ref[:128].astype(F32), jnp.where(inner, b_ref[:128].astype(F32), 0.0)
    from_a = ((slot ^ strip) & 1) == 0
    packed = jnp.where(from_a, *sides), jnp.where(from_a, *sides[::-1])
    for r in range(band_rows):
        wide_ref[1 + r, :, 128:] = roll(packed[r % 2][64:], -16 * r, 1).astype(BF16)
    for r, place in enumerate((0, band_rows + 1)):
        wide_ref[place, :, 128:] = roll(packed[r][:64], -16 * r, 1).astype(BF16)
    wide_ref[0, :, :128] = above_ref[...]
    wide_ref[1 : band_rows + 1, :, :128] = x_ref[...]
    wide_ref[band_rows + 1, :, :128] = below_ref[...]
    weights = w_ref[...]
    rows = slope_ref.shape[0]
    halves, held = [], None
    for h in range(rows):
        y = dot(weights, wide_ref[h : h + 3].reshape(192, 256), (1, 0))
        pre = roll(y[:64], 1, 1) + y[64:128] + roll(y[128:], -1, 1)
        sig = sigmoid(pre)
        slope_ref[h] = slope_of(pre, sig).astype(BF16)
        active = pre * sig
        if h % 2:
            halves.append((held + active).astype(BF16))
        else:
            held = active
    pooled = dot(pool_ref[...], jnp.concatenate(halves, 0), (1, 1))
    stacked = jnp.concatenate(
        [
            jnp.concatenate(
                [pooled[:PITCH, u * 128 : u * 128 + 128], pooled[PITCH:, u * 128 : u * 128 + 128]], 1
            )
            for u in range(2)
        ],
        0,
    ).astype(BF16)
    ordered = dot(stacked, order_ref[...], (1, 0)).astype(BF16)
    for u in range(2):
        pooled_ref[u] = ordered[u * PITCH : u * PITCH + SENT]


def layer_two(og_ref, w_ref, *refs, bands):
    pieces, refs = refs[:bands], refs[bands:]
    terms, refs = refs[:bands], refs[bands:]
    map_ref, grad_ref, pack_ref = refs
    band = lax.axis_index("row")
    rows, _, filters = og_ref.shape
    count = rows * PITCH
    map_ref[0] = jnp.zeros((PITCH, 256), BF16)
    map_ref[rows + 1] = jnp.zeros((PITCH, 256), BF16)
    blank = jnp.zeros((PITCH - SENT, 256), BF16)
    for k, piece in zip(row_order(bands, near_first=True), pieces):
        for t in range(2):
            map_ref[1 + 2 * (band ^ k) + t] = jnp.concatenate([piece[t], blank], 0)
    near = jnp.concatenate([map_ref[i : i + rows].reshape(count, 256) for i in range(3)], 1)
    y = dot(near, jnp.concatenate([w_ref[i] for i in range(3)], 1), (1, 1))
    pre = roll(y[:, :filters], 1, 0) + y[:, filters : 2 * filters] + roll(y[:, 2 * filters :], -1, 0)
    grad = og_ref[...].reshape(count, filters).astype(F32) * slope_of(pre, sigmoid(pre))
    grad = grad.astype(BF16)
    grad_ref[0] = jnp.zeros((PITCH, filters), BF16)
    grad_ref[rows + 1] = jnp.zeros((PITCH, filters), BF16)
    grad_ref[1 : rows + 1] = grad.reshape(rows, PITCH, filters)
    near = jnp.concatenate([grad_ref[2 - i : 2 - i + rows].reshape(count, filters) for i in range(3)], 1)
    weights = [
        jnp.concatenate([w_ref[i, j * filters : (j + 1) * filters] for j in range(3)], 1) for i in range(3)
    ]
    z = dot(near, jnp.concatenate(weights, 0), (1, 0))
    spread = roll(z[:, :256], -1 - REACH, 0) + roll(z[:, 256:512], -REACH, 0) + roll(z[:, 512:], 1 - REACH, 0)
    spread = spread.reshape(rows, PITCH, 256)
    odd = (lax.broadcasted_iota(jnp.int32, (8, 256), 1) & 1) == 1
    row = lax.broadcasted_iota(jnp.int32, (8, 256), 0)
    ends = [jnp.where(odd, spread[u - 1, 47:48], spread[u, 32:33]) for u in range(rows)]
    for p in range(rows // 2):
        shared = jnp.where(row == 0, ends[2 * p], jnp.where(row == 1, ends[2 * p + 1], 0.0))
        pack_ref[p] = jnp.concatenate([spread[2 * p, :32], shared, spread[2 * p + 1, :32]], 0).astype(BF16)
    for k in range(bands):
        terms[k][...] = pack_ref[band ^ k]


def filter_two_grads(map_ref, grad_ref, keep_ref, send_ref, all_ref):
    pair = lax.axis_index("pair")
    rows = map_ref.shape[0] - 2
    filters = grad_ref.shape[2]
    v = lax.broadcasted_iota(jnp.int32, (rows, PITCH, filters), 1)
    own = (v >= REACH) & (v < REACH + 32)
    wide = jnp.where(own, grad_ref[1 : rows + 1].astype(F32), 0.0).reshape(rows * PITCH, filters)
    cat = jnp.concatenate([roll(wide, -1, 0), wide, roll(wide, 1, 0)], 1).astype(BF16)
    taps = 3 * filters
    for i in range(3):
        part = dot(cat, map_ref[i : i + rows].reshape(rows * PITCH, 256), (0, 0))
        all_ref[i * taps : (i + 1) * taps] = part.astype(BF16)
    half = keep_ref.shape[0]
    keep_ref[...] = all_ref[pl.ds(pl.multiple_of(pair * half, 16), half)]
    send_ref[...] = all_ref[pl.ds(pl.multiple_of((1 - pair) * half, 16), half)]


def add_after(a_ref, b_ref, *refs):
    refs[-1][...] = (a_ref[...].astype(F32) + b_ref[...].astype(F32)).astype(BF16)


def add_halves(a_ref, b_ref, border_ref, two_ref, one_ref, joined_ref):
    half, border = two_ref.shape[0], border_ref.shape[0]
    total = (a_ref[...].astype(F32) + b_ref[...].astype(F32)).astype(BF16)
    two_ref[...] = total[:half]
    one_ref[...] = total[half:]
    joined_ref[:border] = border_ref[...]
    joined_ref[border:] = total[half:]


def sum_rows(*refs):
    *refs, _, out_ref = refs
    rows = out_ref.shape[0]
    terms = dict(zip(row_order(len(refs), near_first=True), (ref[-rows:].astype(F32) for ref in refs)))
    terms = [terms[k] for k in range(len(refs))]
    while len(terms) > 1:
        terms = [a + b for a, b in zip(terms[::2], terms[1::2])]
    out_ref[...] = terms[0].astype(BF16)


def grad_pre_one(*refs, bands):
    terms, refs = refs[:bands], refs[bands:]
    slope_ref, wide_ref, pool_ref, order_ref, keep_two_ref, send_two_ref, *refs = refs
    g_ref, a_ref, b_ref, keep_ref, send_ref, part_ref = refs
    pair = lax.axis_index("pair")
    summed = terms[0][...].astype(F32)
    for k in range(1, bands):
        summed = summed + terms[k][...].astype(F32)
    blank = jnp.zeros((8, 256), F32)
    ends = summed[32:40]
    blocks = [summed[:32], ends, blank, summed[40:], roll(ends, -1, 0), blank]
    ordered = dot(jnp.concatenate(blocks, 0).astype(BF16), order_ref[...], (1, 1)).astype(BF16)
    pool = pool_ref[...]
    cats = []
    own = lax.broadcasted_iota(jnp.int32, (64, 256), 1) < 128
    for u in range(2):
        block = ordered[u * PITCH : (u + 1) * PITCH]
        up = dot(jnp.concatenate([block[:, :128], block[:, 128:]], 0), pool, (0, 0))
        for i in range(4):
            h = 4 * u + i
            g = (up[64 * (i // 2) : 64 * (i // 2) + 64] * slope_ref[h].astype(F32)).astype(BF16)
            g_ref[h] = g
            mine = jnp.where(own, g.astype(F32), 0.0)
            cats.append(jnp.concatenate([roll(mine, -1, 1), mine, roll(mine, 1, 1)], 0).astype(BF16))
    around = jnp.concatenate([wide_ref[h : h + 3].reshape(192, 256) for h in range(8)], 1)
    acc = dot(jnp.concatenate(cats, 1), around, (1, 1))
    even = (lax.axis_index("row") & 1) == 0
    first, last = g_ref[0].astype(F32), g_ref[7].astype(F32)
    a_ref[...] = jnp.where(even, last, first).astype(BF16)
    b_ref[...] = jnp.where(even, first, last).astype(BF16)
    part_ref[:96] = jnp.concatenate([acc[:96, :128], acc[96:, :128]], 1)
    part_ref[96:] = jnp.concatenate([acc[48 * q : 48 * q + 48, 128:] for q in range(4)], 1)
    half = keep_two_ref.shape[0]
    for ref, two_ref, place in ((keep_ref, keep_two_ref, pair), (send_ref, send_two_ref, 1 - pair)):
        ref[:half] = two_ref[...]
        ref[half:] = part_ref[pl.ds(pl.multiple_of(place * HALF_ONE, 8), HALF_ONE)].astype(BF16)


def layer_one_back(g_ref, a_ref, b_ref, w_ref, out_ref, done_ref, *, bands):
    above, below = beside(a_ref.at[: b_ref.shape[0]], b_ref, lax.axis_index("row"), bands)
    done_ref[...] = jnp.zeros(done_ref.shape, F32)
    lines = [above] + [g_ref[h] for h in range(8)] + [below]
    rows = []
    for h in range(8):
        z = dot(w_ref[...], jnp.concatenate(lines[h : h + 3], 0), (1, 0))
        rows.append((roll(z[:64], -1, 1) + z[64:128] + roll(z[128:], 1, 1))[:, :128])
    out_ref[...] = jnp.swapaxes(jnp.stack(rows, 0), 0, 1).astype(BF16)


def finish_two(mine_ref, other_ref, two_hbm, done_ref, two_ref, sems, *, scale):
    pair, half = lax.axis_index("pair"), mine_ref.shape[0]
    done_ref[...] = jnp.zeros(done_ref.shape, F32)
    copies = []
    for n, (ref, place) in enumerate(((mine_ref, pair), (other_ref, 1 - pair))):
        rows = pl.ds(pl.multiple_of(place * half, 16), half)
        two_ref[n] = ref[...].astype(F32) * scale
        copies.append(pltpu.make_async_copy(two_ref.at[n], two_hbm.at[rows], sems.at[n]))
        copies[-1].start()
    for copy in copies:
        copy.wait()


def finish_one(mine_ref, other_ref, out_ref, flat_ref, *, scale):
    pair = lax.axis_index("pair")
    for ref, place in ((mine_ref, pair), (other_ref, 1 - pair)):
        flat_ref[pl.ds(pl.multiple_of(place * HALF_ONE, 8), HALF_ONE)] = ref[...].astype(F32) * scale
    out_ref[0, :96] = flat_ref[:96, :64]
    out_ref[1, :96] = flat_ref[:96, 64:128]
    out_ref[0, 96:] = flat_ref[:96, 128:192]
    out_ref[1, 96:] = flat_ref[:96, 192:]
    for q in range(4):
        out_ref[2, 48 * q : 48 * q + 48] = flat_ref[96:, 64 * q : 64 * q + 64]


def even_swap(values, axis, count):
    return lax.ppermute(values, axis, [(n, n ^ 1) for n in range(count)])


def odd_partner(place):
    return place - 1 if place % 2 == 0 else place + 1


def odd_row_swap(values):
    bands, cores = lax.axis_size("row"), lax.axis_size("pair")
    steps = []
    for n in range(bands):
        for p in range(cores):
            to = (n, p ^ 1) if n in (0, bands - 1) else (odd_partner(n), p)
            steps.append((n * cores + p, to[0] * cores + to[1]))
    return lax.ppermute(values, ("row", "pair"), steps)


def odd_strip_swap(values):
    groups, strips = lax.axis_size("grp"), lax.axis_size(COLS)
    steps = []
    for g in range(groups):
        for n in range(strips):
            to = ((g + 1) % groups, n) if n in (0, strips - 1) else (g, odd_partner(n))
            steps.append((g * strips + n, to[0] * strips + to[1]))
    return lax.ppermute(values, ("grp",) + COLS, steps)


def xor_swap(values, axis, count, k):
    return lax.ppermute(values, axis, [(n, n ^ k) for n in range(count)])


def row_order(bands, near_first=False):
    far_first = sorted(range(1, bands), key=lambda k: (k < bands // 2, k))
    return [0] + (far_first[::-1] if near_first else far_first)


def row_swaps(values, bands, near_first=False):
    order = row_order(bands, near_first)
    return [values[0]] + [xor_swap(values[k], "row", bands, k) for k in order[1:]]


def added(a, b, *after):
    (total,) = whole_call(add_after, [shaped(a.shape)], [a, b, *after], 0, after=len(after))
    return total


def sum_but_last(part, axis, count):
    step = 1
    while 2 * step < count:
        part = added(part, xor_swap(part, axis, count, step))
        step *= 2
    return part, xor_swap(part, axis, count, step)


def local(features_in, filters_one, filters_two, out_grad):
    channels, band_rows, strip_cols = features_in.shape
    filters, own_cols, pooled_rows = out_grad.shape
    bands = lax.axis_size("row")
    strips = lax.axis_size(COLS)
    band = lax.axis_index("row")
    strip = lax.axis_index(COLS)
    pair = lax.axis_index("pair")
    height, width = band_rows * bands, strip_cols * strips
    total = own_cols * strips

    taps_one = jnp.transpose(filters_one, (1, 2, 0, 3)).reshape(3, 3 * channels, channels)
    taps_two = jnp.transpose(filters_two, (1, 2, 0, 3)).reshape(3, 3 * filters, 4 * channels)

    edge = REACH - 1
    even = band % 2 == 0
    first, last = features_in[:, 0], features_in[:, -1]
    to_a, to_b = jnp.where(even, last, first), jnp.where(even, first, last)
    head, tail = (jnp.transpose(e, (1, 2, 0)) for e in (out_grad[:, :edge], out_grad[:, -edge:]))
    whole_in, whole_grad = lax.optimization_barrier((features_in, out_grad))
    x = jnp.transpose(whole_in, (1, 0, 2))
    og = jnp.transpose(whole_grad, (1, 2, 0))
    joined_one, back_one, pool, pool_back, order = whole_call(
        functools.partial(constants, total=total),
        [shaped((3 * channels, 3 * channels))] * 2 + [shaped((2 * PITCH, 256))] * 2 + [shaped((256, 256))],
        [taps_one],
        10**8,
    )
    head, tail = head.reshape(-1, 128), tail.reshape(-1, 128)
    own_a, own_b = whole_call(
        pack_own, [shaped((channels + head.shape[0], 128))] * 2, [x, head, tail], 10**8
    )
    to_a, to_b, above, below = whole_call(
        functools.partial(pack_borders, bands=bands),
        [shaped((2 * channels + head.shape[0], 128))] * 2 + [shaped((channels, strip_cols))] * 2,
        [even_swap(to_a, "row", bands), odd_row_swap(to_b), own_a, own_b],
        1,
    )
    side_a, side_b = even_swap(to_a, COLS, strips), odd_strip_swap(to_b)
    pooled, slope, wide = whole_call(
        functools.partial(layer_one, strips=strips),
        [
            shaped((2, SENT, 4 * channels)),
            shaped((band_rows, channels, 256)),
            shaped((band_rows + 2, channels, 256)),
        ],
        [x, above, below, side_a, side_b, joined_one, pool, order],
        2 * band_rows * 192 * 192 * 256,
    )
    pieces = row_swaps([pooled] * bands, bands, near_first=True)

    even = strip % 2 == 0
    ends = [side[2 * channels :].reshape(og[:edge].shape) for side in (side_a, side_b)]
    ends[1] = jnp.where((strip == 0) | (strip == strips - 1), 0, ends[1])
    before, after = jnp.where(even, ends[1], ends[0]), jnp.where(even, ends[0], ends[1])
    og = jnp.concatenate([before, og, after], 0)
    og = jnp.pad(og, ((1, PITCH - own_cols - 2 * REACH + 1), (0, 0), (0, 0)))
    og = jnp.transpose(og, (1, 0, 2))

    count = pooled_rows * PITCH
    *terms, pooled_map, grad_map = whole_call(
        functools.partial(layer_two, bands=bands),
        [shaped((72, 4 * channels))] * bands
        + [shaped((pooled_rows + 2, PITCH, 4 * channels)), shaped((pooled_rows + 2, PITCH, filters))],
        [og, taps_two] + pieces,
        4 * count * 9 * filters * 4 * channels,
        scratch=[pltpu.VMEM((bands, 72, 4 * channels), BF16)],
    )
    received = row_swaps(terms, bands)

    half = 9 * filters // 2
    keep_two, send_two = whole_call(
        filter_two_grads,
        [shaped((half, 4 * channels))] * 2,
        [pooled_map, grad_map],
        2 * count * 9 * filters * 4 * channels,
        scratch=[pltpu.VMEM((2 * half, 4 * channels), BF16)],
    )
    g, up_a, up_b, keep, send = whole_call(
        functools.partial(grad_pre_one, bands=bands),
        [shaped((band_rows, channels, 256))]
        + [shaped((channels, 256))] * 2
        + [shaped((half + HALF_ONE, 256))] * 2,
        received + [slope, wide, pool_back, order, keep_two, send_two],
        2 * 8 * 192 * 192 * 256,
        scratch=[pltpu.VMEM((144, 256), F32)],
    )
    two, one, joined = whole_call(
        add_halves,
        [shaped((half, 256)), shaped((HALF_ONE, 256)), shaped((channels + HALF_ONE, 256))],
        [keep, even_swap(send, "pair", 2), up_a],
        0,
    )
    columns = lax.axis_size("col")
    two, two_more = sum_but_last(two, "col", columns)
    ones = row_swaps([one, joined] + [one] * (bands - 2), bands, near_first=True)
    near = ones[row_order(bands, near_first=True).index(1)]
    up_b = odd_row_swap(up_b)
    (one,) = whole_call(sum_rows, [shaped(one.shape)], ones + [up_b], 0, after=1)
    input_grad, done = whole_call(
        functools.partial(layer_one_back, bands=bands),
        [shaped(features_in.shape), shaped((8, 128), F32)],
        [g, near, up_b, back_one],
        2 * band_rows * 192 * 192 * 256,
    )
    mine_two = added(two, two_more, one)
    grad_two, wrote = whole_call(
        functools.partial(finish_two, scale=1.0 / math.sqrt(pooled_rows * total)),
        [shaped((2 * half, 256), F32), shaped((8, 128), F32)],
        [mine_two, even_swap(mine_two, "pair", 2)],
        10**8,
        scratch=[pltpu.VMEM((2, half, 256), F32), pltpu.SemaphoreType.DMA((2,))],
        out_spaces=[pl.ANY, pltpu.VMEM],
    )
    mine_one = added(*sum_but_last(one, "col", columns), wrote, done)
    (grad_one,) = whole_call(
        functools.partial(finish_one, scale=1.0 / math.sqrt(height * width)),
        [shaped((3, 3 * channels, channels), F32)],
        [mine_one, even_swap(mine_one, "pair", 2)],
        1,
        scratch=[pltpu.VMEM((144, 256), F32)],
    )
    grad_two = jnp.transpose(grad_two.reshape(3, 3, filters, 4 * channels), (2, 0, 1, 3))
    grad_one = jnp.transpose(grad_one.reshape(3, 3, channels, channels), (2, 0, 1, 3))
    return (input_grad, grad_one, grad_two)


def solution(mesh):
    in_specs = (
        P("grp", "row", ("col", "pair")),
        P(),
        P("row", None, None, None),
        P(("grp", "row"), ("col", "pair"), None),
    )
    out_specs = (
        P("grp", "row", ("col", "pair")),
        P("grp", None, None, None),
        P(("grp", "row"), None, None, None),
    )
    return jax.shard_map(local, mesh=mesh, in_specs=in_specs, out_specs=out_specs, check_vma=False)
```

```python
import functools
import math

import jax
import jax.numpy as jnp
from jax import lax
from jax.experimental import pallas as pl
from jax.experimental.pallas import tpu as pltpu
from jax.sharding import PartitionSpec as P

BF16 = jnp.bfloat16
F32 = jnp.float32
COLS = ("col", "pair")
REACH = 3
HALF_ONE = 72
PITCH = 48
SENT = 40


def dot(a, b, contract):
    return lax.dot_general(a, b, ((contract[:1], contract[1:]), ((), ())), preferred_element_type=F32)


def whole_call(body, outs, operands, flops, scratch=(), after=0, out_spaces=None):
    specs = [
        pl.BlockSpec(memory_space=pltpu.VMEM) for _ in range(len(operands) - after)
    ] + [pl.BlockSpec(memory_space=pl.ANY)] * after
    sizes = [math.prod(a.shape) * a.dtype.itemsize for a in tuple(operands) + tuple(outs)]
    moved = sum(sizes) if flops else 0
    return pl.pallas_call(
        body,
        out_shape=outs,
        in_specs=specs,
        out_specs=[pl.BlockSpec(memory_space=space) for space in out_spaces or [pltpu.VMEM] * len(outs)],
        scratch_shapes=list(scratch),
        cost_estimate=pl.CostEstimate(flops=flops, bytes_accessed=moved, transcendentals=0),
        compiler_params=pltpu.CompilerParams(vmem_limit_bytes=40 * 1024 * 1024),
    )(*operands)


def strip_index():
    return lax.axis_index("col") * lax.axis_size("pair") + lax.axis_index("pair")


def shaped(shape, dtype=BF16):
    return jax.ShapeDtypeStruct(shape, dtype)


def roll(values, amount, axis):
    return pltpu.roll(values, amount % values.shape[axis], axis)


def sigmoid(values):
    return 0.5 + 0.5 * jnp.tanh(0.5 * values)


def slope_of(values, sig):
    return sig * (1.0 + values * (1.0 - sig))


def pool_matrix(strip, total, back=False):
    row = lax.broadcasted_iota(jnp.int32, (2 * PITCH, 256), 0)
    lane = lax.broadcasted_iota(jnp.int32, (2 * PITCH, 256), 1)
    half = (row >= PITCH).astype(jnp.int32)
    n = row - half * PITCH
    if back:
        v, most = jnp.where((n == 32) & (half == 1), -1, n), 33
    else:
        v, most = n - REACH, 32 + 2 * REACH
    near = jnp.bitwise_and(lane - 4 * v - 2 * half, 255) < 2
    place = strip * 32 + v
    keep = near & (n < most) & (place >= 0) & (place < total)
    return jnp.where(keep, 0.25, 0.0).astype(BF16)


def order_matrix():
    row = lax.broadcasted_iota(jnp.int32, (256, 256), 0)
    lane = lax.broadcasted_iota(jnp.int32, (256, 256), 1)
    j, i, c = row >> 7, (row >> 6) & 1, row & 63
    return jnp.where(lane == 4 * c + 2 * i + j, 1.0, 0.0).astype(BF16)


def constants(w_ref, joined_ref, back_w_ref, pool_ref, back_ref, order_ref, *, total):
    turned = [w_ref[2 - i].astype(F32).T for i in range(3)]
    back_w_ref[...] = jnp.concatenate(
        [jnp.concatenate([t[:, 64 * j : 64 * j + 64] for t in turned], 1) for j in range(3)], 0
    ).astype(BF16)
    joined_ref[...] = jnp.concatenate([w_ref[0], w_ref[1], w_ref[2]], axis=1)
    pool_ref[...] = pool_matrix(strip_index(), total)
    back_ref[...] = pool_matrix(strip_index(), total, back=True)
    order_ref[...] = order_matrix()


def beside(a_ref, b_ref, place, count):
    even = (place & 1) == 0
    a = a_ref[...].astype(F32)
    b = jnp.where((place > 0) & (place < count - 1), b_ref[...].astype(F32), 0.0)
    return jnp.where(even, b, a).astype(BF16), jnp.where(even, a, b).astype(BF16)


def pack_row(row, r, slot, head, tail):
    turned = roll(row.astype(F32), 16 * r, 1)
    return jnp.where(slot == r, turned, head), jnp.where(slot == (r - 1) % 8, turned, tail)


def pack_own(x_ref, head_ref, tail_ref, a_ref, b_ref):
    even = (strip_index() & 1) == 0
    slot = lax.broadcasted_iota(jnp.int32, (64, 128), 1) >> 4
    head = tail = jnp.zeros((64, 128), F32)
    for r in range(x_ref.shape[0]):
        head, tail = pack_row(x_ref[r], r, slot, head, tail)
    a_ref[:64] = jnp.where(even, tail, head).astype(BF16)
    b_ref[:64] = jnp.where(even, head, tail).astype(BF16)
    first, last = head_ref[...].astype(F32), tail_ref[...].astype(F32)
    a_ref[64:] = jnp.where(even, last, first).astype(BF16)
    b_ref[64:] = jnp.where(even, first, last).astype(BF16)


def pack_borders(up_a_ref, up_b_ref, own_a_ref, own_b_ref, a_ref, b_ref, above_ref, below_ref, *, bands):
    even = (strip_index() & 1) == 0
    above_ref[...], below_ref[...] = beside(up_a_ref, up_b_ref, lax.axis_index("row"), bands)
    slot = lax.broadcasted_iota(jnp.int32, (64, 128), 1) >> 4
    head = tail = jnp.zeros((64, 128), F32)
    for r, ref in enumerate((above_ref, below_ref)):
        head, tail = pack_row(ref[...], r, slot, head, tail)
    a_ref[:64] = jnp.where(even, tail, head).astype(BF16)
    b_ref[:64] = jnp.where(even, head, tail).astype(BF16)
    a_ref[64:] = own_a_ref[...]
    b_ref[64:] = own_b_ref[...]


def layer_one(
    x_ref,
    above_ref,
    below_ref,
    a_ref,
    b_ref,
    w_ref,
    pool_ref,
    order_ref,
    pooled_ref,
    slope_ref,
    wide_ref,
    *,
    strips,
):
    strip = strip_index()
    band_rows = x_ref.shape[0]
    slot = lax.broadcasted_iota(jnp.int32, (128, 128), 1) >> 4
    inner = (strip > 0) & (strip < strips - 1)
    sides = a_ref[:128].astype(F32), jnp.where(inner, b_ref[:128].astype(F32), 0.0)
    from_a = ((slot ^ strip) & 1) == 0
    packed = jnp.where(from_a, *sides), jnp.where(from_a, *sides[::-1])
    for r in range(band_rows):
        wide_ref[1 + r, :, 128:] = roll(packed[r % 2][64:], -16 * r, 1).astype(BF16)
    for r, place in enumerate((0, band_rows + 1)):
        wide_ref[place, :, 128:] = roll(packed[r][:64], -16 * r, 1).astype(BF16)
    wide_ref[0, :, :128] = above_ref[...]
    wide_ref[1 : band_rows + 1, :, :128] = x_ref[...]
    wide_ref[band_rows + 1, :, :128] = below_ref[...]
    weights = w_ref[...]
    rows = slope_ref.shape[0]
    halves, held = [], None
    for h in range(rows):
        y = dot(weights, wide_ref[h : h + 3].reshape(192, 256), (1, 0))
        pre = roll(y[:64], 1, 1) + y[64:128] + roll(y[128:], -1, 1)
        sig = sigmoid(pre)
        slope_ref[h] = slope_of(pre, sig).astype(BF16)
        active = pre * sig
        if h % 2:
            halves.append((held + active).astype(BF16))
        else:
            held = active
    pooled = dot(pool_ref[...], jnp.concatenate(halves, 0), (1, 1))
    stacked = jnp.concatenate(
        [
            jnp.concatenate(
                [pooled[:PITCH, u * 128 : u * 128 + 128], pooled[PITCH:, u * 128 : u * 128 + 128]], 1
            )
            for u in range(2)
        ],
        0,
    ).astype(BF16)
    ordered = dot(stacked, order_ref[...], (1, 0)).astype(BF16)
    for u in range(2):
        pooled_ref[u] = ordered[u * PITCH : u * PITCH + SENT]


def layer_two(og_ref, w_ref, *refs, bands):
    pieces, refs = refs[:bands], refs[bands:]
    terms, refs = refs[:bands], refs[bands:]
    map_ref, grad_ref, pack_ref = refs
    band = lax.axis_index("row")
    rows, _, filters = og_ref.shape
    count = rows * PITCH
    map_ref[0] = jnp.zeros((PITCH, 256), BF16)
    map_ref[rows + 1] = jnp.zeros((PITCH, 256), BF16)
    blank = jnp.zeros((PITCH - SENT, 256), BF16)
    for k, piece in zip(row_order(bands, near_first=True), pieces):
        for t in range(2):
            map_ref[1 + 2 * (band ^ k) + t] = jnp.concatenate([piece[t], blank], 0)
    near = jnp.concatenate([map_ref[i : i + rows].reshape(count, 256) for i in range(3)], 1)
    y = dot(near, jnp.concatenate([w_ref[i] for i in range(3)], 1), (1, 1))
    pre = roll(y[:, :filters], 1, 0) + y[:, filters : 2 * filters] + roll(y[:, 2 * filters :], -1, 0)
    grad = og_ref[...].reshape(count, filters).astype(F32) * slope_of(pre, sigmoid(pre))
    grad = grad.astype(BF16)
    grad_ref[0] = jnp.zeros((PITCH, filters), BF16)
    grad_ref[rows + 1] = jnp.zeros((PITCH, filters), BF16)
    grad_ref[1 : rows + 1] = grad.reshape(rows, PITCH, filters)
    near = jnp.concatenate([grad_ref[2 - i : 2 - i + rows].reshape(count, filters) for i in range(3)], 1)
    weights = [
        jnp.concatenate([w_ref[i, j * filters : (j + 1) * filters] for j in range(3)], 1) for i in range(3)
    ]
    z = dot(near, jnp.concatenate(weights, 0), (1, 0))
    spread = roll(z[:, :256], -1 - REACH, 0) + roll(z[:, 256:512], -REACH, 0) + roll(z[:, 512:], 1 - REACH, 0)
    spread = spread.reshape(rows, PITCH, 256)
    odd = (lax.broadcasted_iota(jnp.int32, (8, 256), 1) & 1) == 1
    row = lax.broadcasted_iota(jnp.int32, (8, 256), 0)
    ends = [jnp.where(odd, spread[u - 1, 47:48], spread[u, 32:33]) for u in range(rows)]
    for p in range(rows // 2):
        shared = jnp.where(row == 0, ends[2 * p], jnp.where(row == 1, ends[2 * p + 1], 0.0))
        pack_ref[p] = jnp.concatenate([spread[2 * p, :32], shared, spread[2 * p + 1, :32]], 0).astype(BF16)
    for k in range(bands):
        terms[k][...] = pack_ref[band ^ k]


def filter_two_grads(map_ref, grad_ref, keep_ref, send_ref, all_ref):
    pair = lax.axis_index("pair")
    rows = map_ref.shape[0] - 2
    filters = grad_ref.shape[2]
    v = lax.broadcasted_iota(jnp.int32, (rows, PITCH, filters), 1)
    own = (v >= REACH) & (v < REACH + 32)
    wide = jnp.where(own, grad_ref[1 : rows + 1].astype(F32), 0.0).reshape(rows * PITCH, filters)
    cat = jnp.concatenate([roll(wide, -1, 0), wide, roll(wide, 1, 0)], 1).astype(BF16)
    taps = 3 * filters
    for i in range(3):
        part = dot(cat, map_ref[i : i + rows].reshape(rows * PITCH, 256), (0, 0))
        all_ref[i * taps : (i + 1) * taps] = part.astype(BF16)
    half = keep_ref.shape[0]
    keep_ref[...] = all_ref[pl.ds(pl.multiple_of(pair * half, 16), half)]
    send_ref[...] = all_ref[pl.ds(pl.multiple_of((1 - pair) * half, 16), half)]


def add_after(a_ref, b_ref, *refs):
    refs[-1][...] = (a_ref[...].astype(F32) + b_ref[...].astype(F32)).astype(BF16)


def add_halves(a_ref, b_ref, border_ref, two_ref, one_ref, joined_ref):
    half, border = two_ref.shape[0], border_ref.shape[0]
    total = (a_ref[...].astype(F32) + b_ref[...].astype(F32)).astype(BF16)
    two_ref[...] = total[:half]
    one_ref[...] = total[half:]
    joined_ref[:border] = border_ref[...]
    joined_ref[border:] = total[half:]


def sum_rows(*refs):
    *refs, _, out_ref = refs
    rows = out_ref.shape[0]
    terms = dict(zip(row_order(len(refs), near_first=True), (ref[-rows:].astype(F32) for ref in refs)))
    terms = [terms[k] for k in range(len(refs))]
    while len(terms) > 1:
        terms = [a + b for a, b in zip(terms[::2], terms[1::2])]
    out_ref[...] = terms[0].astype(BF16)


def grad_pre_one(*refs, bands):
    terms, refs = refs[:bands], refs[bands:]
    slope_ref, wide_ref, pool_ref, order_ref, keep_two_ref, send_two_ref, *refs = refs
    g_ref, a_ref, b_ref, keep_ref, send_ref, part_ref = refs
    pair = lax.axis_index("pair")
    summed = terms[0][...].astype(F32)
    for k in range(1, bands):
        summed = summed + terms[k][...].astype(F32)
    blank = jnp.zeros((8, 256), F32)
    ends = summed[32:40]
    blocks = [summed[:32], ends, blank, summed[40:], roll(ends, -1, 0), blank]
    ordered = dot(jnp.concatenate(blocks, 0).astype(BF16), order_ref[...], (1, 1)).astype(BF16)
    pool = pool_ref[...]
    cats = []
    own = lax.broadcasted_iota(jnp.int32, (64, 256), 1) < 128
    for u in range(2):
        block = ordered[u * PITCH : (u + 1) * PITCH]
        up = dot(jnp.concatenate([block[:, :128], block[:, 128:]], 0), pool, (0, 0))
        for i in range(4):
            h = 4 * u + i
            g = (up[64 * (i // 2) : 64 * (i // 2) + 64] * slope_ref[h].astype(F32)).astype(BF16)
            g_ref[h] = g
            mine = jnp.where(own, g.astype(F32), 0.0)
            cats.append(jnp.concatenate([roll(mine, -1, 1), mine, roll(mine, 1, 1)], 0).astype(BF16))
    around = jnp.concatenate([wide_ref[h : h + 3].reshape(192, 256) for h in range(8)], 1)
    acc = dot(jnp.concatenate(cats, 1), around, (1, 1))
    even = (lax.axis_index("row") & 1) == 0
    first, last = g_ref[0].astype(F32), g_ref[7].astype(F32)
    a_ref[...] = jnp.where(even, last, first).astype(BF16)
    b_ref[...] = jnp.where(even, first, last).astype(BF16)
    part_ref[:96] = jnp.concatenate([acc[:96, :128], acc[96:, :128]], 1)
    part_ref[96:] = jnp.concatenate([acc[48 * q : 48 * q + 48, 128:] for q in range(4)], 1)
    half = keep_two_ref.shape[0]
    for ref, two_ref, place in ((keep_ref, keep_two_ref, pair), (send_ref, send_two_ref, 1 - pair)):
        ref[:half] = two_ref[...]
        ref[half:] = part_ref[pl.ds(pl.multiple_of(place * HALF_ONE, 8), HALF_ONE)].astype(BF16)


def layer_one_back(g_ref, a_ref, b_ref, w_ref, out_ref, done_ref, *, bands):
    above, below = beside(a_ref.at[: b_ref.shape[0]], b_ref, lax.axis_index("row"), bands)
    done_ref[...] = jnp.zeros(done_ref.shape, F32)
    lines = [above] + [g_ref[h] for h in range(8)] + [below]
    rows = []
    for h in range(8):
        z = dot(w_ref[...], jnp.concatenate(lines[h : h + 3], 0), (1, 0))
        rows.append((roll(z[:64], -1, 1) + z[64:128] + roll(z[128:], 1, 1))[:, :128])
    out_ref[...] = jnp.swapaxes(jnp.stack(rows, 0), 0, 1).astype(BF16)


def finish_two(mine_ref, other_ref, two_hbm, done_ref, two_ref, sems, *, scale):
    pair, half = lax.axis_index("pair"), mine_ref.shape[0]
    done_ref[...] = jnp.zeros(done_ref.shape, F32)
    copies = []
    for n, (ref, place) in enumerate(((mine_ref, pair), (other_ref, 1 - pair))):
        rows = pl.ds(pl.multiple_of(place * half, 16), half)
        two_ref[n] = ref[...].astype(F32) * scale
        copies.append(pltpu.make_async_copy(two_ref.at[n], two_hbm.at[rows], sems.at[n]))
        copies[-1].start()
    for copy in copies:
        copy.wait()


def finish_one(mine_ref, other_ref, out_ref, flat_ref, *, scale):
    pair = lax.axis_index("pair")
    for ref, place in ((mine_ref, pair), (other_ref, 1 - pair)):
        flat_ref[pl.ds(pl.multiple_of(place * HALF_ONE, 8), HALF_ONE)] = ref[...].astype(F32) * scale
    out_ref[0, :96] = flat_ref[:96, :64]
    out_ref[1, :96] = flat_ref[:96, 64:128]
    out_ref[0, 96:] = flat_ref[:96, 128:192]
    out_ref[1, 96:] = flat_ref[:96, 192:]
    for q in range(4):
        out_ref[2, 48 * q : 48 * q + 48] = flat_ref[96:, 64 * q : 64 * q + 64]


def even_swap(values, axis, count):
    return lax.ppermute(values, axis, [(n, n ^ 1) for n in range(count)])


def odd_partner(place):
    return place - 1 if place % 2 == 0 else place + 1


def odd_row_swap(values):
    bands, cores = lax.axis_size("row"), lax.axis_size("pair")
    steps = []
    for n in range(bands):
        for p in range(cores):
            to = (n, p ^ 1) if n in (0, bands - 1) else (odd_partner(n), p)
            steps.append((n * cores + p, to[0] * cores + to[1]))
    return lax.ppermute(values, ("row", "pair"), steps)


def odd_strip_swap(values):
    groups, strips = lax.axis_size("grp"), lax.axis_size(COLS)
    steps = []
    for g in range(groups):
        for n in range(strips):
            to = ((g + 1) % groups, n) if n in (0, strips - 1) else (g, odd_partner(n))
            steps.append((g * strips + n, to[0] * strips + to[1]))
    return lax.ppermute(values, ("grp",) + COLS, steps)


def xor_swap(values, axis, count, k):
    return lax.ppermute(values, axis, [(n, n ^ k) for n in range(count)])


def row_order(bands, near_first=False):
    far_first = list(range(bands - 1, 0, -1))
    return [0] + (far_first[::-1] if near_first else far_first)


def row_swaps(values, bands, near_first=False):
    order = row_order(bands, near_first)
    return [values[0]] + [xor_swap(values[k], "row", bands, k) for k in order[1:]]


def added(a, b, *after):
    (total,) = whole_call(add_after, [shaped(a.shape)], [a, b, *after], 0, after=len(after))
    return total


def sum_but_last(part, axis, count):
    step = 1
    while 2 * step < count:
        part = added(part, xor_swap(part, axis, count, step))
        step *= 2
    return part, xor_swap(part, axis, count, step)


def local(features_in, filters_one, filters_two, out_grad):
    channels, band_rows, strip_cols = features_in.shape
    filters, own_cols, pooled_rows = out_grad.shape
    bands = lax.axis_size("row")
    strips = lax.axis_size(COLS)
    band = lax.axis_index("row")
    strip = lax.axis_index(COLS)
    pair = lax.axis_index("pair")
    height, width = band_rows * bands, strip_cols * strips
    total = own_cols * strips

    taps_one = jnp.transpose(filters_one, (1, 2, 0, 3)).reshape(3, 3 * channels, channels)
    taps_two = jnp.transpose(filters_two, (1, 2, 0, 3)).reshape(3, 3 * filters, 4 * channels)

    og = jnp.transpose(out_grad, (1, 2, 0))
    edge = REACH - 1
    x = jnp.transpose(features_in, (1, 0, 2))
    even = band % 2 == 0
    to_a, to_b = jnp.where(even, x[-1], x[0]), jnp.where(even, x[0], x[-1])
    head, tail = og[:edge], og[-edge:]
    joined_one, back_one, pool, pool_back, order = whole_call(
        functools.partial(constants, total=total),
        [shaped((3 * channels, 3 * channels))] * 2 + [shaped((2 * PITCH, 256))] * 2 + [shaped((256, 256))],
        [taps_one],
        10**8,
    )
    head, tail = head.reshape(-1, 128), tail.reshape(-1, 128)
    own_a, own_b = whole_call(
        pack_own, [shaped((channels + head.shape[0], 128))] * 2, [x, head, tail], 10**8
    )
    to_a, to_b, above, below = whole_call(
        functools.partial(pack_borders, bands=bands),
        [shaped((2 * channels + head.shape[0], 128))] * 2 + [shaped((channels, strip_cols))] * 2,
        [even_swap(to_a, "row", bands), odd_row_swap(to_b), own_a, own_b],
        1,
    )
    side_a, side_b = even_swap(to_a, COLS, strips), odd_strip_swap(to_b)
    pooled, slope, wide = whole_call(
        functools.partial(layer_one, strips=strips),
        [
            shaped((2, SENT, 4 * channels)),
            shaped((band_rows, channels, 256)),
            shaped((band_rows + 2, channels, 256)),
        ],
        [x, above, below, side_a, side_b, joined_one, pool, order],
        2 * band_rows * 192 * 192 * 256,
    )
    pieces = row_swaps([pooled] * bands, bands, near_first=True)

    even = strip % 2 == 0
    ends = [side[2 * channels :].reshape(og[:edge].shape) for side in (side_a, side_b)]
    ends[1] = jnp.where((strip == 0) | (strip == strips - 1), 0, ends[1])
    before, after = jnp.where(even, ends[1], ends[0]), jnp.where(even, ends[0], ends[1])
    og = jnp.concatenate([before, og, after], 0)
    og = jnp.pad(og, ((1, PITCH - own_cols - 2 * REACH + 1), (0, 0), (0, 0)))
    og = jnp.transpose(og, (1, 0, 2))

    count = pooled_rows * PITCH
    *terms, pooled_map, grad_map = whole_call(
        functools.partial(layer_two, bands=bands),
        [shaped((72, 4 * channels))] * bands
        + [shaped((pooled_rows + 2, PITCH, 4 * channels)), shaped((pooled_rows + 2, PITCH, filters))],
        [og, taps_two] + pieces,
        4 * count * 9 * filters * 4 * channels,
        scratch=[pltpu.VMEM((bands, 72, 4 * channels), BF16)],
    )
    received = row_swaps(terms, bands)

    half = 9 * filters // 2
    keep_two, send_two = whole_call(
        filter_two_grads,
        [shaped((half, 4 * channels))] * 2,
        [pooled_map, grad_map],
        2 * count * 9 * filters * 4 * channels,
        scratch=[pltpu.VMEM((2 * half, 4 * channels), BF16)],
    )
    g, up_a, up_b, keep, send = whole_call(
        functools.partial(grad_pre_one, bands=bands),
        [shaped((band_rows, channels, 256))]
        + [shaped((channels, 256))] * 2
        + [shaped((half + HALF_ONE, 256))] * 2,
        received + [slope, wide, pool_back, order, keep_two, send_two],
        2 * 8 * 192 * 192 * 256,
        scratch=[pltpu.VMEM((144, 256), F32)],
    )
    two, one, joined = whole_call(
        add_halves,
        [shaped((half, 256)), shaped((HALF_ONE, 256)), shaped((channels + HALF_ONE, 256))],
        [keep, even_swap(send, "pair", 2), up_a],
        0,
    )
    columns = lax.axis_size("col")
    two, two_more = sum_but_last(two, "col", columns)
    ones = row_swaps([one, joined] + [one] * (bands - 2), bands, near_first=True)
    near = ones[row_order(bands, near_first=True).index(1)]
    up_b = odd_row_swap(up_b)
    (one,) = whole_call(sum_rows, [shaped(one.shape)], ones + [up_b], 0, after=1)
    input_grad, done = whole_call(
        functools.partial(layer_one_back, bands=bands),
        [shaped(features_in.shape), shaped((8, 128), F32)],
        [g, near, up_b, back_one],
        2 * band_rows * 192 * 192 * 256,
    )
    mine_two = added(two, two_more, one)
    grad_two, wrote = whole_call(
        functools.partial(finish_two, scale=1.0 / math.sqrt(pooled_rows * total)),
        [shaped((2 * half, 256), F32), shaped((8, 128), F32)],
        [mine_two, even_swap(mine_two, "pair", 2)],
        10**8,
        scratch=[pltpu.VMEM((2, half, 256), F32), pltpu.SemaphoreType.DMA((2,))],
        out_spaces=[pl.ANY, pltpu.VMEM],
    )
    mine_one = added(*sum_but_last(one, "col", columns), wrote, done)
    (grad_one,) = whole_call(
        functools.partial(finish_one, scale=1.0 / math.sqrt(height * width)),
        [shaped((3, 3 * channels, channels), F32)],
        [mine_one, even_swap(mine_one, "pair", 2)],
        1,
        scratch=[pltpu.VMEM((144, 256), F32)],
    )
    grad_two = jnp.transpose(grad_two.reshape(3, 3, filters, 4 * channels), (2, 0, 1, 3))
    grad_one = jnp.transpose(grad_one.reshape(3, 3, channels, channels), (2, 0, 1, 3))
    return (input_grad, grad_one, grad_two)


def solution(mesh):
    in_specs = (
        P("grp", "row", ("col", "pair")),
        P(),
        P("row", None, None, None),
        P(("grp", "row"), ("col", "pair"), None),
    )
    out_specs = (
        P("grp", "row", ("col", "pair")),
        P("grp", None, None, None),
        P(("grp", "row"), None, None, None),
    )
    return jax.shard_map(local, mesh=mesh, in_specs=in_specs, out_specs=out_specs, check_vma=False)
```

```python
import functools
import math

import jax
import jax.numpy as jnp
from jax import lax
from jax.experimental import pallas as pl
from jax.experimental.pallas import tpu as pltpu
from jax.sharding import PartitionSpec as P

BF16 = jnp.bfloat16
F32 = jnp.float32
COLS = ("col", "pair")
REACH = 3
HALF_ONE = 72
PITCH = 48
SENT = 40


def dot(a, b, contract):
    return lax.dot_general(a, b, ((contract[:1], contract[1:]), ((), ())), preferred_element_type=F32)


def whole_call(body, outs, operands, flops, scratch=(), after=0, out_spaces=None):
    specs = [
        pl.BlockSpec(memory_space=pltpu.VMEM) for _ in range(len(operands) - after)
    ] + [pl.BlockSpec(memory_space=pl.ANY)] * after
    sizes = [math.prod(a.shape) * a.dtype.itemsize for a in tuple(operands) + tuple(outs)]
    moved = sum(sizes) if flops else 0
    return pl.pallas_call(
        body,
        out_shape=outs,
        in_specs=specs,
        out_specs=[pl.BlockSpec(memory_space=space) for space in out_spaces or [pltpu.VMEM] * len(outs)],
        scratch_shapes=list(scratch),
        cost_estimate=pl.CostEstimate(flops=flops, bytes_accessed=moved, transcendentals=0),
        compiler_params=pltpu.CompilerParams(vmem_limit_bytes=40 * 1024 * 1024),
    )(*operands)


def strip_index():
    return lax.axis_index("col") * lax.axis_size("pair") + lax.axis_index("pair")


def shaped(shape, dtype=BF16):
    return jax.ShapeDtypeStruct(shape, dtype)


def roll(values, amount, axis):
    return pltpu.roll(values, amount % values.shape[axis], axis)


def sigmoid(values):
    return 0.5 + 0.5 * jnp.tanh(0.5 * values)


def slope_of(values, sig):
    return sig * (1.0 + values * (1.0 - sig))


def pool_matrix(strip, total, back=False):
    row = lax.broadcasted_iota(jnp.int32, (2 * PITCH, 256), 0)
    lane = lax.broadcasted_iota(jnp.int32, (2 * PITCH, 256), 1)
    half = (row >= PITCH).astype(jnp.int32)
    n = row - half * PITCH
    if back:
        v, most = jnp.where((n == 32) & (half == 1), -1, n), 33
    else:
        v, most = n - REACH, 32 + 2 * REACH
    near = jnp.bitwise_and(lane - 4 * v - 2 * half, 255) < 2
    place = strip * 32 + v
    keep = near & (n < most) & (place >= 0) & (place < total)
    return jnp.where(keep, 0.25, 0.0).astype(BF16)


def order_matrix():
    row = lax.broadcasted_iota(jnp.int32, (256, 256), 0)
    lane = lax.broadcasted_iota(jnp.int32, (256, 256), 1)
    j, i, c = row >> 7, (row >> 6) & 1, row & 63
    return jnp.where(lane == 4 * c + 2 * i + j, 1.0, 0.0).astype(BF16)


def constants(w_ref, joined_ref, back_w_ref, pool_ref, back_ref, order_ref, *, total):
    turned = [w_ref[2 - i].astype(F32).T for i in range(3)]
    back_w_ref[...] = jnp.concatenate(
        [jnp.concatenate([t[:, 64 * j : 64 * j + 64] for t in turned], 1) for j in range(3)], 0
    ).astype(BF16)
    joined_ref[...] = jnp.concatenate([w_ref[0], w_ref[1], w_ref[2]], axis=1)
    pool_ref[...] = pool_matrix(strip_index(), total)
    back_ref[...] = pool_matrix(strip_index(), total, back=True)
    order_ref[...] = order_matrix()


def beside(a_ref, b_ref, place, count):
    even = (place & 1) == 0
    a = a_ref[...].astype(F32)
    b = jnp.where((place > 0) & (place < count - 1), b_ref[...].astype(F32), 0.0)
    return jnp.where(even, b, a).astype(BF16), jnp.where(even, a, b).astype(BF16)


def pack_row(row, r, slot, head, tail):
    turned = roll(row.astype(F32), 16 * r, 1)
    return jnp.where(slot == r, turned, head), jnp.where(slot == (r - 1) % 8, turned, tail)


def pack_own(x_ref, head_ref, tail_ref, a_ref, b_ref):
    even = (strip_index() & 1) == 0
    slot = lax.broadcasted_iota(jnp.int32, (64, 128), 1) >> 4
    head = tail = jnp.zeros((64, 128), F32)
    for r in range(x_ref.shape[0]):
        head, tail = pack_row(x_ref[r], r, slot, head, tail)
    a_ref[:64] = jnp.where(even, tail, head).astype(BF16)
    b_ref[:64] = jnp.where(even, head, tail).astype(BF16)
    first, last = head_ref[...].astype(F32), tail_ref[...].astype(F32)
    a_ref[64:] = jnp.where(even, last, first).astype(BF16)
    b_ref[64:] = jnp.where(even, first, last).astype(BF16)


def pack_borders(up_a_ref, up_b_ref, own_a_ref, own_b_ref, a_ref, b_ref, above_ref, below_ref, *, bands):
    even = (strip_index() & 1) == 0
    above_ref[...], below_ref[...] = beside(up_a_ref, up_b_ref, lax.axis_index("row"), bands)
    slot = lax.broadcasted_iota(jnp.int32, (64, 128), 1) >> 4
    head = tail = jnp.zeros((64, 128), F32)
    for r, ref in enumerate((above_ref, below_ref)):
        head, tail = pack_row(ref[...], r, slot, head, tail)
    a_ref[:64] = jnp.where(even, tail, head).astype(BF16)
    b_ref[:64] = jnp.where(even, head, tail).astype(BF16)
    a_ref[64:] = own_a_ref[...]
    b_ref[64:] = own_b_ref[...]


def layer_one(
    x_ref,
    above_ref,
    below_ref,
    a_ref,
    b_ref,
    w_ref,
    pool_ref,
    order_ref,
    pooled_ref,
    slope_ref,
    wide_ref,
    *,
    strips,
):
    strip = strip_index()
    band_rows = x_ref.shape[0]
    slot = lax.broadcasted_iota(jnp.int32, (128, 128), 1) >> 4
    inner = (strip > 0) & (strip < strips - 1)
    sides = a_ref[:128].astype(F32), jnp.where(inner, b_ref[:128].astype(F32), 0.0)
    from_a = ((slot ^ strip) & 1) == 0
    packed = jnp.where(from_a, *sides), jnp.where(from_a, *sides[::-1])
    for r in range(band_rows):
        wide_ref[1 + r, :, 128:] = roll(packed[r % 2][64:], -16 * r, 1).astype(BF16)
    for r, place in enumerate((0, band_rows + 1)):
        wide_ref[place, :, 128:] = roll(packed[r][:64], -16 * r, 1).astype(BF16)
    wide_ref[0, :, :128] = above_ref[...]
    wide_ref[1 : band_rows + 1, :, :128] = x_ref[...]
    wide_ref[band_rows + 1, :, :128] = below_ref[...]
    weights = w_ref[...]
    rows = slope_ref.shape[0]
    halves, held = [], None
    for h in range(rows):
        y = dot(weights, wide_ref[h : h + 3].reshape(192, 256), (1, 0))
        pre = roll(y[:64], 1, 1) + y[64:128] + roll(y[128:], -1, 1)
        sig = sigmoid(pre)
        slope_ref[h] = slope_of(pre, sig).astype(BF16)
        active = pre * sig
        if h % 2:
            halves.append((held + active).astype(BF16))
        else:
            held = active
    pooled = dot(pool_ref[...], jnp.concatenate(halves, 0), (1, 1))
    stacked = jnp.concatenate(
        [
            jnp.concatenate(
                [pooled[:PITCH, u * 128 : u * 128 + 128], pooled[PITCH:, u * 128 : u * 128 + 128]], 1
            )
            for u in range(2)
        ],
        0,
    ).astype(BF16)
    ordered = dot(stacked, order_ref[...], (1, 0)).astype(BF16)
    for u in range(2):
        pooled_ref[u] = ordered[u * PITCH : u * PITCH + SENT]


def layer_two(og_ref, w_ref, *refs, bands):
    pieces, refs = refs[:bands], refs[bands:]
    terms, refs = refs[:bands], refs[bands:]
    map_ref, grad_ref, pack_ref = refs
    band = lax.axis_index("row")
    rows, _, filters = og_ref.shape
    count = rows * PITCH
    map_ref[0] = jnp.zeros((PITCH, 256), BF16)
    map_ref[rows + 1] = jnp.zeros((PITCH, 256), BF16)
    blank = jnp.zeros((PITCH - SENT, 256), BF16)
    for k, piece in zip(row_order(bands, near_first=True), pieces):
        for t in range(2):
            map_ref[1 + 2 * (band ^ k) + t] = jnp.concatenate([piece[t], blank], 0)
    near = jnp.concatenate([map_ref[i : i + rows].reshape(count, 256) for i in range(3)], 1)
    y = dot(near, jnp.concatenate([w_ref[i] for i in range(3)], 1), (1, 1))
    pre = roll(y[:, :filters], 1, 0) + y[:, filters : 2 * filters] + roll(y[:, 2 * filters :], -1, 0)
    grad = og_ref[...].reshape(count, filters).astype(F32) * slope_of(pre, sigmoid(pre))
    grad = grad.astype(BF16)
    grad_ref[0] = jnp.zeros((PITCH, filters), BF16)
    grad_ref[rows + 1] = jnp.zeros((PITCH, filters), BF16)
    grad_ref[1 : rows + 1] = grad.reshape(rows, PITCH, filters)
    near = jnp.concatenate([grad_ref[2 - i : 2 - i + rows].reshape(count, filters) for i in range(3)], 1)
    weights = [
        jnp.concatenate([w_ref[i, j * filters : (j + 1) * filters] for j in range(3)], 1) for i in range(3)
    ]
    z = dot(near, jnp.concatenate(weights, 0), (1, 0))
    spread = roll(z[:, :256], -1 - REACH, 0) + roll(z[:, 256:512], -REACH, 0) + roll(z[:, 512:], 1 - REACH, 0)
    spread = spread.reshape(rows, PITCH, 256)
    odd = (lax.broadcasted_iota(jnp.int32, (8, 256), 1) & 1) == 1
    row = lax.broadcasted_iota(jnp.int32, (8, 256), 0)
    ends = [jnp.where(odd, spread[u - 1, 47:48], spread[u, 32:33]) for u in range(rows)]
    for p in range(rows // 2):
        shared = jnp.where(row == 0, ends[2 * p], jnp.where(row == 1, ends[2 * p + 1], 0.0))
        pack_ref[p] = jnp.concatenate([spread[2 * p, :32], shared, spread[2 * p + 1, :32]], 0).astype(BF16)
    for k in range(bands):
        terms[k][...] = pack_ref[band ^ k]


def filter_two_grads(map_ref, grad_ref, keep_ref, send_ref, all_ref):
    pair = lax.axis_index("pair")
    rows = map_ref.shape[0] - 2
    filters = grad_ref.shape[2]
    v = lax.broadcasted_iota(jnp.int32, (rows, PITCH, filters), 1)
    own = (v >= REACH) & (v < REACH + 32)
    wide = jnp.where(own, grad_ref[1 : rows + 1].astype(F32), 0.0).reshape(rows * PITCH, filters)
    cat = jnp.concatenate([roll(wide, -1, 0), wide, roll(wide, 1, 0)], 1).astype(BF16)
    taps = 3 * filters
    for i in range(3):
        part = dot(cat, map_ref[i : i + rows].reshape(rows * PITCH, 256), (0, 0))
        all_ref[i * taps : (i + 1) * taps] = part.astype(BF16)
    half = keep_ref.shape[0]
    keep_ref[...] = all_ref[pl.ds(pl.multiple_of(pair * half, 16), half)]
    send_ref[...] = all_ref[pl.ds(pl.multiple_of((1 - pair) * half, 16), half)]


def add_after(a_ref, b_ref, *refs):
    refs[-1][...] = (a_ref[...].astype(F32) + b_ref[...].astype(F32)).astype(BF16)


def add_halves(a_ref, b_ref, border_ref, two_ref, one_ref, joined_ref):
    half, border = two_ref.shape[0], border_ref.shape[0]
    total = (a_ref[...].astype(F32) + b_ref[...].astype(F32)).astype(BF16)
    two_ref[...] = total[:half]
    one_ref[...] = total[half:]
    joined_ref[:border] = border_ref[...]
    joined_ref[border:] = total[half:]


def add_near(a_ref, near_ref, _, out_ref):
    out_ref[...] = (a_ref[...].astype(F32) + near_ref[-a_ref.shape[0] :].astype(F32)).astype(BF16)


def grad_pre_one(*refs, bands):
    terms, refs = refs[:bands], refs[bands:]
    slope_ref, wide_ref, pool_ref, order_ref, keep_two_ref, send_two_ref, *refs = refs
    g_ref, a_ref, b_ref, keep_ref, send_ref, part_ref = refs
    pair = lax.axis_index("pair")
    summed = terms[0][...].astype(F32)
    for k in range(1, bands):
        summed = summed + terms[k][...].astype(F32)
    blank = jnp.zeros((8, 256), F32)
    ends = summed[32:40]
    blocks = [summed[:32], ends, blank, summed[40:], roll(ends, -1, 0), blank]
    ordered = dot(jnp.concatenate(blocks, 0).astype(BF16), order_ref[...], (1, 1)).astype(BF16)
    pool = pool_ref[...]
    cats = []
    own = lax.broadcasted_iota(jnp.int32, (64, 256), 1) < 128
    for u in range(2):
        block = ordered[u * PITCH : (u + 1) * PITCH]
        up = dot(jnp.concatenate([block[:, :128], block[:, 128:]], 0), pool, (0, 0))
        for i in range(4):
            h = 4 * u + i
            g = (up[64 * (i // 2) : 64 * (i // 2) + 64] * slope_ref[h].astype(F32)).astype(BF16)
            g_ref[h] = g
            mine = jnp.where(own, g.astype(F32), 0.0)
            cats.append(jnp.concatenate([roll(mine, -1, 1), mine, roll(mine, 1, 1)], 0).astype(BF16))
    around = jnp.concatenate([wide_ref[h : h + 3].reshape(192, 256) for h in range(8)], 1)
    acc = dot(jnp.concatenate(cats, 1), around, (1, 1))
    even = (lax.axis_index("row") & 1) == 0
    first, last = g_ref[0].astype(F32), g_ref[7].astype(F32)
    a_ref[...] = jnp.where(even, last, first).astype(BF16)
    b_ref[...] = jnp.where(even, first, last).astype(BF16)
    part_ref[:96] = jnp.concatenate([acc[:96, :128], acc[96:, :128]], 1)
    part_ref[96:] = jnp.concatenate([acc[48 * q : 48 * q + 48, 128:] for q in range(4)], 1)
    half = keep_two_ref.shape[0]
    for ref, two_ref, place in ((keep_ref, keep_two_ref, pair), (send_ref, send_two_ref, 1 - pair)):
        ref[:half] = two_ref[...]
        ref[half:] = part_ref[pl.ds(pl.multiple_of(place * HALF_ONE, 8), HALF_ONE)].astype(BF16)


def layer_one_back(g_ref, a_ref, b_ref, w_ref, out_ref, done_ref, *, bands):
    above, below = beside(a_ref.at[: b_ref.shape[0]], b_ref, lax.axis_index("row"), bands)
    done_ref[...] = jnp.zeros(done_ref.shape, F32)
    lines = [above] + [g_ref[h] for h in range(8)] + [below]
    rows = []
    for h in range(8):
        z = dot(w_ref[...], jnp.concatenate(lines[h : h + 3], 0), (1, 0))
        rows.append((roll(z[:64], -1, 1) + z[64:128] + roll(z[128:], 1, 1))[:, :128])
    out_ref[...] = jnp.swapaxes(jnp.stack(rows, 0), 0, 1).astype(BF16)


def finish_two(mine_ref, other_ref, two_hbm, done_ref, two_ref, sems, *, scale):
    pair, half = lax.axis_index("pair"), mine_ref.shape[0]
    done_ref[...] = jnp.zeros(done_ref.shape, F32)
    copies = []
    for n, (ref, place) in enumerate(((mine_ref, pair), (other_ref, 1 - pair))):
        rows = pl.ds(pl.multiple_of(place * half, 16), half)
        two_ref[n] = ref[...].astype(F32) * scale
        copies.append(pltpu.make_async_copy(two_ref.at[n], two_hbm.at[rows], sems.at[n]))
        copies[-1].start()
    for copy in copies:
        copy.wait()


def finish_one(mine_ref, other_ref, out_ref, flat_ref, *, scale):
    pair = lax.axis_index("pair")
    for ref, place in ((mine_ref, pair), (other_ref, 1 - pair)):
        flat_ref[pl.ds(pl.multiple_of(place * HALF_ONE, 8), HALF_ONE)] = ref[...].astype(F32) * scale
    out_ref[0, :96] = flat_ref[:96, :64]
    out_ref[1, :96] = flat_ref[:96, 64:128]
    out_ref[0, 96:] = flat_ref[:96, 128:192]
    out_ref[1, 96:] = flat_ref[:96, 192:]
    for q in range(4):
        out_ref[2, 48 * q : 48 * q + 48] = flat_ref[96:, 64 * q : 64 * q + 64]


def even_swap(values, axis, count):
    return lax.ppermute(values, axis, [(n, n ^ 1) for n in range(count)])


def odd_partner(place):
    return place - 1 if place % 2 == 0 else place + 1


def odd_row_swap(values):
    bands, cores = lax.axis_size("row"), lax.axis_size("pair")
    steps = []
    for n in range(bands):
        for p in range(cores):
            to = (n, p ^ 1) if n in (0, bands - 1) else (odd_partner(n), p)
            steps.append((n * cores + p, to[0] * cores + to[1]))
    return lax.ppermute(values, ("row", "pair"), steps)


def odd_strip_swap(values):
    groups, strips = lax.axis_size("grp"), lax.axis_size(COLS)
    steps = []
    for g in range(groups):
        for n in range(strips):
            to = ((g + 1) % groups, n) if n in (0, strips - 1) else (g, odd_partner(n))
            steps.append((g * strips + n, to[0] * strips + to[1]))
    return lax.ppermute(values, ("grp",) + COLS, steps)


def xor_swap(values, axis, count, k):
    return lax.ppermute(values, axis, [(n, n ^ k) for n in range(count)])


def row_order(bands, near_first=False):
    far_first = list(range(bands - 1, 0, -1))
    return [0] + (far_first[::-1] if near_first else far_first)


def row_swaps(values, bands, near_first=False):
    order = row_order(bands, near_first)
    return [values[0]] + [xor_swap(values[k], "row", bands, k) for k in order[1:]]


def added(a, b, *after):
    (total,) = whole_call(add_after, [shaped(a.shape)], [a, b, *after], 0, after=len(after))
    return total


def sum_but_last(part, axis, count):
    step = 1
    while 2 * step < count:
        part = added(part, xor_swap(part, axis, count, step))
        step *= 2
    return part, xor_swap(part, axis, count, step)


def local(features_in, filters_one, filters_two, out_grad):
    channels, band_rows, strip_cols = features_in.shape
    filters, own_cols, pooled_rows = out_grad.shape
    bands = lax.axis_size("row")
    strips = lax.axis_size(COLS)
    band = lax.axis_index("row")
    strip = lax.axis_index(COLS)
    pair = lax.axis_index("pair")
    height, width = band_rows * bands, strip_cols * strips
    total = own_cols * strips

    taps_one = jnp.transpose(filters_one, (1, 2, 0, 3)).reshape(3, 3 * channels, channels)
    taps_two = jnp.transpose(filters_two, (1, 2, 0, 3)).reshape(3, 3 * filters, 4 * channels)

    og = jnp.transpose(out_grad, (1, 2, 0))
    edge = REACH - 1
    x = jnp.transpose(features_in, (1, 0, 2))
    even = band % 2 == 0
    to_a, to_b = jnp.where(even, x[-1], x[0]), jnp.where(even, x[0], x[-1])
    head, tail = og[:edge], og[-edge:]
    joined_one, back_one, pool, pool_back, order = whole_call(
        functools.partial(constants, total=total),
        [shaped((3 * channels, 3 * channels))] * 2 + [shaped((2 * PITCH, 256))] * 2 + [shaped((256, 256))],
        [taps_one],
        10**8,
    )
    head, tail = head.reshape(-1, 128), tail.reshape(-1, 128)
    own_a, own_b = whole_call(
        pack_own, [shaped((channels + head.shape[0], 128))] * 2, [x, head, tail], 10**8
    )
    to_a, to_b, above, below = whole_call(
        functools.partial(pack_borders, bands=bands),
        [shaped((2 * channels + head.shape[0], 128))] * 2 + [shaped((channels, strip_cols))] * 2,
        [even_swap(to_a, "row", bands), odd_row_swap(to_b), own_a, own_b],
        1,
    )
    side_a, side_b = even_swap(to_a, COLS, strips), odd_strip_swap(to_b)
    pooled, slope, wide = whole_call(
        functools.partial(layer_one, strips=strips),
        [
            shaped((2, SENT, 4 * channels)),
            shaped((band_rows, channels, 256)),
            shaped((band_rows + 2, channels, 256)),
        ],
        [x, above, below, side_a, side_b, joined_one, pool, order],
        2 * band_rows * 192 * 192 * 256,
    )
    pieces = row_swaps([pooled] * bands, bands, near_first=True)

    even = strip % 2 == 0
    ends = [side[2 * channels :].reshape(og[:edge].shape) for side in (side_a, side_b)]
    ends[1] = jnp.where((strip == 0) | (strip == strips - 1), 0, ends[1])
    before, after = jnp.where(even, ends[1], ends[0]), jnp.where(even, ends[0], ends[1])
    og = jnp.concatenate([before, og, after], 0)
    og = jnp.pad(og, ((1, PITCH - own_cols - 2 * REACH + 1), (0, 0), (0, 0)))
    og = jnp.transpose(og, (1, 0, 2))

    count = pooled_rows * PITCH
    *terms, pooled_map, grad_map = whole_call(
        functools.partial(layer_two, bands=bands),
        [shaped((72, 4 * channels))] * bands
        + [shaped((pooled_rows + 2, PITCH, 4 * channels)), shaped((pooled_rows + 2, PITCH, filters))],
        [og, taps_two] + pieces,
        4 * count * 9 * filters * 4 * channels,
        scratch=[pltpu.VMEM((bands, 72, 4 * channels), BF16)],
    )
    received = row_swaps(terms, bands)

    half = 9 * filters // 2
    keep_two, send_two = whole_call(
        filter_two_grads,
        [shaped((half, 4 * channels))] * 2,
        [pooled_map, grad_map],
        2 * count * 9 * filters * 4 * channels,
        scratch=[pltpu.VMEM((2 * half, 4 * channels), BF16)],
    )
    g, up_a, up_b, keep, send = whole_call(
        functools.partial(grad_pre_one, bands=bands),
        [shaped((band_rows, channels, 256))]
        + [shaped((channels, 256))] * 2
        + [shaped((half + HALF_ONE, 256))] * 2,
        received + [slope, wide, pool_back, order, keep_two, send_two],
        2 * 8 * 192 * 192 * 256,
        scratch=[pltpu.VMEM((144, 256), F32)],
    )
    two, one, joined = whole_call(
        add_halves,
        [shaped((half, 256)), shaped((HALF_ONE, 256)), shaped((channels + HALF_ONE, 256))],
        [keep, even_swap(send, "pair", 2), up_a],
        0,
    )
    columns = lax.axis_size("col")
    two, two_more = sum_but_last(two, "col", columns)
    near, up_b = xor_swap(joined, "row", bands, 1), odd_row_swap(up_b)
    (one,) = whole_call(add_near, [shaped(one.shape)], [one, near, up_b], 0, after=1)
    step = 2
    while step < bands:
        one = added(one, xor_swap(one, "row", bands, step))
        step *= 2
    input_grad, done = whole_call(
        functools.partial(layer_one_back, bands=bands),
        [shaped(features_in.shape), shaped((8, 128), F32)],
        [g, near, up_b, back_one],
        2 * band_rows * 192 * 192 * 256,
    )
    mine_two = added(two, two_more, one)
    grad_two, wrote = whole_call(
        functools.partial(finish_two, scale=1.0 / math.sqrt(pooled_rows * total)),
        [shaped((2 * half, 256), F32), shaped((8, 128), F32)],
        [mine_two, even_swap(mine_two, "pair", 2)],
        10**8,
        scratch=[pltpu.VMEM((2, half, 256), F32), pltpu.SemaphoreType.DMA((2,))],
        out_spaces=[pl.ANY, pltpu.VMEM],
    )
    mine_one = added(*sum_but_last(one, "col", columns), wrote, done)
    (grad_one,) = whole_call(
        functools.partial(finish_one, scale=1.0 / math.sqrt(height * width)),
        [shaped((3, 3 * channels, channels), F32)],
        [mine_one, even_swap(mine_one, "pair", 2)],
        1,
        scratch=[pltpu.VMEM((144, 256), F32)],
    )
    grad_two = jnp.transpose(grad_two.reshape(3, 3, filters, 4 * channels), (2, 0, 1, 3))
    grad_one = jnp.transpose(grad_one.reshape(3, 3, channels, channels), (2, 0, 1, 3))
    return (input_grad, grad_one, grad_two)


def solution(mesh):
    in_specs = (
        P("grp", "row", ("col", "pair")),
        P(),
        P("row", None, None, None),
        P(("grp", "row"), ("col", "pair"), None),
    )
    out_specs = (
        P("grp", "row", ("col", "pair")),
        P("grp", None, None, None),
        P(("grp", "row"), None, None, None),
    )
    return jax.shard_map(local, mesh=mesh, in_specs=in_specs, out_specs=out_specs, check_vma=False)
```

```python
import functools
import math

import jax
import jax.numpy as jnp
from jax import lax
from jax.experimental import pallas as pl
from jax.experimental.pallas import tpu as pltpu
from jax.sharding import PartitionSpec as P

BF16 = jnp.bfloat16
F32 = jnp.float32
COLS = ("col", "pair")
REACH = 3
HALF_ONE = 72
PITCH = 48
SENT = 40


def dot(a, b, contract):
    return lax.dot_general(a, b, ((contract[:1], contract[1:]), ((), ())), preferred_element_type=F32)


def whole_call(body, outs, operands, flops, scratch=(), after=0, out_spaces=None):
    specs = [
        pl.BlockSpec(memory_space=pltpu.VMEM) for _ in range(len(operands) - after)
    ] + [pl.BlockSpec(memory_space=pl.ANY)] * after
    sizes = [math.prod(a.shape) * a.dtype.itemsize for a in tuple(operands) + tuple(outs)]
    moved = sum(sizes) if flops else 0
    return pl.pallas_call(
        body,
        out_shape=outs,
        in_specs=specs,
        out_specs=[pl.BlockSpec(memory_space=space) for space in out_spaces or [pltpu.VMEM] * len(outs)],
        scratch_shapes=list(scratch),
        cost_estimate=pl.CostEstimate(flops=flops, bytes_accessed=moved, transcendentals=0),
        compiler_params=pltpu.CompilerParams(vmem_limit_bytes=40 * 1024 * 1024),
    )(*operands)


def strip_index():
    return lax.axis_index("col") * lax.axis_size("pair") + lax.axis_index("pair")


def shaped(shape, dtype=BF16):
    return jax.ShapeDtypeStruct(shape, dtype)


def roll(values, amount, axis):
    return pltpu.roll(values, amount % values.shape[axis], axis)


def sigmoid(values):
    return 0.5 + 0.5 * jnp.tanh(0.5 * values)


def slope_of(values, sig):
    return sig * (1.0 + values * (1.0 - sig))


def pool_matrix(strip, total, back=False):
    row = lax.broadcasted_iota(jnp.int32, (2 * PITCH, 256), 0)
    lane = lax.broadcasted_iota(jnp.int32, (2 * PITCH, 256), 1)
    half = (row >= PITCH).astype(jnp.int32)
    n = row - half * PITCH
    if back:
        v, most = jnp.where((n == 32) & (half == 1), -1, n), 33
    else:
        v, most = n - REACH, 32 + 2 * REACH
    near = jnp.bitwise_and(lane - 4 * v - 2 * half, 255) < 2
    place = strip * 32 + v
    keep = near & (n < most) & (place >= 0) & (place < total)
    return jnp.where(keep, 0.25, 0.0).astype(BF16)


def order_matrix():
    row = lax.broadcasted_iota(jnp.int32, (256, 256), 0)
    lane = lax.broadcasted_iota(jnp.int32, (256, 256), 1)
    j, i, c = row >> 7, (row >> 6) & 1, row & 63
    return jnp.where(lane == 4 * c + 2 * i + j, 1.0, 0.0).astype(BF16)


def constants(w_ref, joined_ref, back_w_ref, pool_ref, back_ref, order_ref, *, total):
    turned = [w_ref[2 - i].astype(F32).T for i in range(3)]
    back_w_ref[...] = jnp.concatenate(
        [jnp.concatenate([t[:, 64 * j : 64 * j + 64] for t in turned], 1) for j in range(3)], 0
    ).astype(BF16)
    joined_ref[...] = jnp.concatenate([w_ref[0], w_ref[1], w_ref[2]], axis=1)
    pool_ref[...] = pool_matrix(strip_index(), total)
    back_ref[...] = pool_matrix(strip_index(), total, back=True)
    order_ref[...] = order_matrix()


def beside(a_ref, b_ref, place, count):
    even = (place & 1) == 0
    a = a_ref[...].astype(F32)
    b = jnp.where((place > 0) & (place < count - 1), b_ref[...].astype(F32), 0.0)
    return jnp.where(even, b, a).astype(BF16), jnp.where(even, a, b).astype(BF16)


def pack_row(row, r, slot, head, tail):
    turned = roll(row.astype(F32), 16 * r, 1)
    return jnp.where(slot == r, turned, head), jnp.where(slot == (r - 1) % 8, turned, tail)


def pack_own(x_ref, head_ref, tail_ref, a_ref, b_ref):
    even = (strip_index() & 1) == 0
    slot = lax.broadcasted_iota(jnp.int32, (64, 128), 1) >> 4
    head = tail = jnp.zeros((64, 128), F32)
    for r in range(x_ref.shape[0]):
        head, tail = pack_row(x_ref[r], r, slot, head, tail)
    a_ref[:64] = jnp.where(even, tail, head).astype(BF16)
    b_ref[:64] = jnp.where(even, head, tail).astype(BF16)
    first, last = head_ref[...].astype(F32), tail_ref[...].astype(F32)
    a_ref[64:] = jnp.where(even, last, first).astype(BF16)
    b_ref[64:] = jnp.where(even, first, last).astype(BF16)


def pack_borders(up_a_ref, up_b_ref, own_a_ref, own_b_ref, a_ref, b_ref, above_ref, below_ref, *, bands):
    even = (strip_index() & 1) == 0
    above_ref[...], below_ref[...] = beside(up_a_ref, up_b_ref, lax.axis_index("row"), bands)
    slot = lax.broadcasted_iota(jnp.int32, (64, 128), 1) >> 4
    head = tail = jnp.zeros((64, 128), F32)
    for r, ref in enumerate((above_ref, below_ref)):
        head, tail = pack_row(ref[...], r, slot, head, tail)
    a_ref[:64] = jnp.where(even, tail, head).astype(BF16)
    b_ref[:64] = jnp.where(even, head, tail).astype(BF16)
    a_ref[64:] = own_a_ref[...]
    b_ref[64:] = own_b_ref[...]


def layer_one(
    x_ref,
    above_ref,
    below_ref,
    a_ref,
    b_ref,
    w_ref,
    pool_ref,
    order_ref,
    pooled_ref,
    slope_ref,
    wide_ref,
    *,
    strips,
):
    strip = strip_index()
    band_rows = x_ref.shape[0]
    slot = lax.broadcasted_iota(jnp.int32, (128, 128), 1) >> 4
    inner = (strip > 0) & (strip < strips - 1)
    sides = a_ref[:128].astype(F32), jnp.where(inner, b_ref[:128].astype(F32), 0.0)
    from_a = ((slot ^ strip) & 1) == 0
    packed = jnp.where(from_a, *sides), jnp.where(from_a, *sides[::-1])
    for r in range(band_rows):
        wide_ref[1 + r, :, 128:] = roll(packed[r % 2][64:], -16 * r, 1).astype(BF16)
    for r, place in enumerate((0, band_rows + 1)):
        wide_ref[place, :, 128:] = roll(packed[r][:64], -16 * r, 1).astype(BF16)
    wide_ref[0, :, :128] = above_ref[...]
    wide_ref[1 : band_rows + 1, :, :128] = x_ref[...]
    wide_ref[band_rows + 1, :, :128] = below_ref[...]
    weights = w_ref[...]
    rows = slope_ref.shape[0]
    halves, held = [], None
    for h in range(rows):
        y = dot(weights, wide_ref[h : h + 3].reshape(192, 256), (1, 0))
        pre = roll(y[:64], 1, 1) + y[64:128] + roll(y[128:], -1, 1)
        sig = sigmoid(pre)
        slope_ref[h] = slope_of(pre, sig).astype(BF16)
        active = pre * sig
        if h % 2:
            halves.append((held + active).astype(BF16))
        else:
            held = active
    pooled = dot(pool_ref[...], jnp.concatenate(halves, 0), (1, 1))
    stacked = jnp.concatenate(
        [
            jnp.concatenate(
                [pooled[:PITCH, u * 128 : u * 128 + 128], pooled[PITCH:, u * 128 : u * 128 + 128]], 1
            )
            for u in range(2)
        ],
        0,
    ).astype(BF16)
    ordered = dot(stacked, order_ref[...], (1, 0)).astype(BF16)
    for u in range(2):
        pooled_ref[u] = ordered[u * PITCH : u * PITCH + SENT]


def layer_two(og_ref, w_ref, *refs, bands):
    pieces, refs = refs[:bands], refs[bands:]
    terms, refs = refs[:bands], refs[bands:]
    map_ref, grad_ref, pack_ref = refs
    band = lax.axis_index("row")
    rows, _, filters = og_ref.shape
    count = rows * PITCH
    map_ref[0] = jnp.zeros((PITCH, 256), BF16)
    map_ref[rows + 1] = jnp.zeros((PITCH, 256), BF16)
    blank = jnp.zeros((PITCH - SENT, 256), BF16)
    for k, piece in zip(row_order(bands, near_first=True), pieces):
        for t in range(2):
            map_ref[1 + 2 * (band ^ k) + t] = jnp.concatenate([piece[t], blank], 0)
    near = jnp.concatenate([map_ref[i : i + rows].reshape(count, 256) for i in range(3)], 1)
    y = dot(near, jnp.concatenate([w_ref[i] for i in range(3)], 1), (1, 1))
    pre = roll(y[:, :filters], 1, 0) + y[:, filters : 2 * filters] + roll(y[:, 2 * filters :], -1, 0)
    grad = og_ref[...].reshape(count, filters).astype(F32) * slope_of(pre, sigmoid(pre))
    grad = grad.astype(BF16)
    grad_ref[0] = jnp.zeros((PITCH, filters), BF16)
    grad_ref[rows + 1] = jnp.zeros((PITCH, filters), BF16)
    grad_ref[1 : rows + 1] = grad.reshape(rows, PITCH, filters)
    near = jnp.concatenate([grad_ref[2 - i : 2 - i + rows].reshape(count, filters) for i in range(3)], 1)
    weights = [
        jnp.concatenate([w_ref[i, j * filters : (j + 1) * filters] for j in range(3)], 1) for i in range(3)
    ]
    z = dot(near, jnp.concatenate(weights, 0), (1, 0))
    spread = roll(z[:, :256], -1 - REACH, 0) + roll(z[:, 256:512], -REACH, 0) + roll(z[:, 512:], 1 - REACH, 0)
    spread = spread.reshape(rows, PITCH, 256)
    odd = (lax.broadcasted_iota(jnp.int32, (8, 256), 1) & 1) == 1
    row = lax.broadcasted_iota(jnp.int32, (8, 256), 0)
    ends = [jnp.where(odd, spread[u - 1, 47:48], spread[u, 32:33]) for u in range(rows)]
    for p in range(rows // 2):
        shared = jnp.where(row == 0, ends[2 * p], jnp.where(row == 1, ends[2 * p + 1], 0.0))
        pack_ref[p] = jnp.concatenate([spread[2 * p, :32], shared, spread[2 * p + 1, :32]], 0).astype(BF16)
    for k in range(bands):
        terms[k][...] = pack_ref[band ^ k]


def filter_two_grads(map_ref, grad_ref, keep_ref, send_ref, all_ref):
    pair = lax.axis_index("pair")
    rows = map_ref.shape[0] - 2
    filters = grad_ref.shape[2]
    v = lax.broadcasted_iota(jnp.int32, (rows, PITCH, filters), 1)
    own = (v >= REACH) & (v < REACH + 32)
    wide = jnp.where(own, grad_ref[1 : rows + 1].astype(F32), 0.0).reshape(rows * PITCH, filters)
    cat = jnp.concatenate([roll(wide, -1, 0), wide, roll(wide, 1, 0)], 1).astype(BF16)
    taps = 3 * filters
    for i in range(3):
        part = dot(cat, map_ref[i : i + rows].reshape(rows * PITCH, 256), (0, 0))
        all_ref[i * taps : (i + 1) * taps] = part.astype(BF16)
    half = keep_ref.shape[0]
    keep_ref[...] = all_ref[pl.ds(pl.multiple_of(pair * half, 16), half)]
    send_ref[...] = all_ref[pl.ds(pl.multiple_of((1 - pair) * half, 16), half)]


def add_after(a_ref, b_ref, *refs):
    refs[-1][...] = (a_ref[...].astype(F32) + b_ref[...].astype(F32)).astype(BF16)


def add_halves(a_ref, b_ref, border_ref, two_ref, one_ref, joined_ref):
    half, border = two_ref.shape[0], border_ref.shape[0]
    total = (a_ref[...].astype(F32) + b_ref[...].astype(F32)).astype(BF16)
    two_ref[...] = total[:half]
    one_ref[...] = total[half:]
    joined_ref[:border] = border_ref[...]
    joined_ref[border:] = total[half:]


def sum_rows(*refs):
    *refs, _, out_ref = refs
    rows = out_ref.shape[0]
    terms = dict(zip(row_order(len(refs), near_first=True), (ref[-rows:].astype(F32) for ref in refs)))
    terms = [terms[k] for k in range(len(refs))]
    while len(terms) > 1:
        terms = [a + b for a, b in zip(terms[::2], terms[1::2])]
    out_ref[...] = terms[0].astype(BF16)


def grad_pre_one(*refs, bands):
    terms, refs = refs[:bands], refs[bands:]
    slope_ref, wide_ref, pool_ref, order_ref, keep_two_ref, send_two_ref, *refs = refs
    g_ref, a_ref, b_ref, keep_ref, send_ref, part_ref = refs
    pair = lax.axis_index("pair")
    summed = terms[0][...].astype(F32)
    for k in range(1, bands):
        summed = summed + terms[k][...].astype(F32)
    blank = jnp.zeros((8, 256), F32)
    ends = summed[32:40]
    blocks = [summed[:32], ends, blank, summed[40:], roll(ends, -1, 0), blank]
    ordered = dot(jnp.concatenate(blocks, 0).astype(BF16), order_ref[...], (1, 1)).astype(BF16)
    pool = pool_ref[...]
    cats = []
    own = lax.broadcasted_iota(jnp.int32, (64, 256), 1) < 128
    for u in range(2):
        block = ordered[u * PITCH : (u + 1) * PITCH]
        up = dot(jnp.concatenate([block[:, :128], block[:, 128:]], 0), pool, (0, 0))
        for i in range(4):
            h = 4 * u + i
            g = (up[64 * (i // 2) : 64 * (i // 2) + 64] * slope_ref[h].astype(F32)).astype(BF16)
            g_ref[h] = g
            mine = jnp.where(own, g.astype(F32), 0.0)
            cats.append(jnp.concatenate([roll(mine, -1, 1), mine, roll(mine, 1, 1)], 0).astype(BF16))
    around = jnp.concatenate([wide_ref[h : h + 3].reshape(192, 256) for h in range(8)], 1)
    acc = dot(jnp.concatenate(cats, 1), around, (1, 1))
    even = (lax.axis_index("row") & 1) == 0
    first, last = g_ref[0].astype(F32), g_ref[7].astype(F32)
    a_ref[...] = jnp.where(even, last, first).astype(BF16)
    b_ref[...] = jnp.where(even, first, last).astype(BF16)
    part_ref[:96] = jnp.concatenate([acc[:96, :128], acc[96:, :128]], 1)
    part_ref[96:] = jnp.concatenate([acc[48 * q : 48 * q + 48, 128:] for q in range(4)], 1)
    half = keep_two_ref.shape[0]
    for ref, two_ref, place in ((keep_ref, keep_two_ref, pair), (send_ref, send_two_ref, 1 - pair)):
        ref[:half] = two_ref[...]
        ref[half:] = part_ref[pl.ds(pl.multiple_of(place * HALF_ONE, 8), HALF_ONE)].astype(BF16)


def layer_one_back(g_ref, a_ref, b_ref, w_ref, out_ref, done_ref, *, bands):
    above, below = beside(a_ref.at[: b_ref.shape[0]], b_ref, lax.axis_index("row"), bands)
    done_ref[...] = jnp.zeros(done_ref.shape, F32)
    lines = [above] + [g_ref[h] for h in range(8)] + [below]
    rows = []
    for h in range(8):
        z = dot(w_ref[...], jnp.concatenate(lines[h : h + 3], 0), (1, 0))
        rows.append((roll(z[:64], -1, 1) + z[64:128] + roll(z[128:], 1, 1))[:, :128])
    out_ref[...] = jnp.swapaxes(jnp.stack(rows, 0), 0, 1).astype(BF16)


def finish_two(mine_ref, other_ref, two_hbm, done_ref, two_ref, sems, *, scale):
    pair, half = lax.axis_index("pair"), mine_ref.shape[0]
    done_ref[...] = jnp.zeros(done_ref.shape, F32)
    copies = []
    for n, (ref, place) in enumerate(((mine_ref, pair), (other_ref, 1 - pair))):
        rows = pl.ds(pl.multiple_of(place * half, 16), half)
        two_ref[n] = ref[...].astype(F32) * scale
        copies.append(pltpu.make_async_copy(two_ref.at[n], two_hbm.at[rows], sems.at[n]))
        copies[-1].start()
    for copy in copies:
        copy.wait()


def finish_one(mine_ref, across_ref, beside_ref, corner_ref, _, __, out_ref, flat_ref, *, scale):
    pair = lax.axis_index("pair")
    for refs, place in (((mine_ref, across_ref), pair), ((beside_ref, corner_ref), 1 - pair)):
        total = refs[0][...].astype(F32) + refs[1][...].astype(F32)
        flat_ref[pl.ds(pl.multiple_of(place * HALF_ONE, 8), HALF_ONE)] = total * scale
    out_ref[0, :96] = flat_ref[:96, :64]
    out_ref[1, :96] = flat_ref[:96, 64:128]
    out_ref[0, 96:] = flat_ref[:96, 128:192]
    out_ref[1, 96:] = flat_ref[:96, 192:]
    for q in range(4):
        out_ref[2, 48 * q : 48 * q + 48] = flat_ref[96:, 64 * q : 64 * q + 64]


def even_swap(values, axis, count):
    return lax.ppermute(values, axis, [(n, n ^ 1) for n in range(count)])


def odd_partner(place):
    return place - 1 if place % 2 == 0 else place + 1


def odd_row_swap(values):
    bands, cores = lax.axis_size("row"), lax.axis_size("pair")
    steps = []
    for n in range(bands):
        for p in range(cores):
            to = (n, p ^ 1) if n in (0, bands - 1) else (odd_partner(n), p)
            steps.append((n * cores + p, to[0] * cores + to[1]))
    return lax.ppermute(values, ("row", "pair"), steps)


def odd_strip_swap(values):
    groups, strips = lax.axis_size("grp"), lax.axis_size(COLS)
    steps = []
    for g in range(groups):
        for n in range(strips):
            to = ((g + 1) % groups, n) if n in (0, strips - 1) else (g, odd_partner(n))
            steps.append((g * strips + n, to[0] * strips + to[1]))
    return lax.ppermute(values, ("grp",) + COLS, steps)


def xor_swap(values, axis, count, k):
    return lax.ppermute(values, axis, [(n, n ^ k) for n in range(count)])


def corner_swap(values, k):
    columns, cores = lax.axis_size("col"), lax.axis_size("pair")
    steps = [(c * cores + p, (c ^ k) * cores + (p ^ 1)) for c in range(columns) for p in range(cores)]
    return lax.ppermute(values, COLS, steps)


def row_order(bands, near_first=False):
    far_first = list(range(bands - 1, 0, -1))
    return [0] + (far_first[::-1] if near_first else far_first)


def row_swaps(values, bands, near_first=False):
    order = row_order(bands, near_first)
    return [values[0]] + [xor_swap(values[k], "row", bands, k) for k in order[1:]]


def added(a, b, *after):
    (total,) = whole_call(add_after, [shaped(a.shape)], [a, b, *after], 0, after=len(after))
    return total


def sum_but_last(part, axis, count):
    step = 1
    while 2 * step < count:
        part = added(part, xor_swap(part, axis, count, step))
        step *= 2
    return part, xor_swap(part, axis, count, step)


def local(features_in, filters_one, filters_two, out_grad):
    channels, band_rows, strip_cols = features_in.shape
    filters, own_cols, pooled_rows = out_grad.shape
    bands = lax.axis_size("row")
    strips = lax.axis_size(COLS)
    band = lax.axis_index("row")
    strip = lax.axis_index(COLS)
    pair = lax.axis_index("pair")
    height, width = band_rows * bands, strip_cols * strips
    total = own_cols * strips

    taps_one = jnp.transpose(filters_one, (1, 2, 0, 3)).reshape(3, 3 * channels, channels)
    taps_two = jnp.transpose(filters_two, (1, 2, 0, 3)).reshape(3, 3 * filters, 4 * channels)

    og = jnp.transpose(out_grad, (1, 2, 0))
    edge = REACH - 1
    x = jnp.transpose(features_in, (1, 0, 2))
    even = band % 2 == 0
    to_a, to_b = jnp.where(even, x[-1], x[0]), jnp.where(even, x[0], x[-1])
    head, tail = og[:edge], og[-edge:]
    joined_one, back_one, pool, pool_back, order = whole_call(
        functools.partial(constants, total=total),
        [shaped((3 * channels, 3 * channels))] * 2 + [shaped((2 * PITCH, 256))] * 2 + [shaped((256, 256))],
        [taps_one],
        10**8,
    )
    head, tail = head.reshape(-1, 128), tail.reshape(-1, 128)
    own_a, own_b = whole_call(
        pack_own, [shaped((channels + head.shape[0], 128))] * 2, [x, head, tail], 10**8
    )
    to_a, to_b, above, below = whole_call(
        functools.partial(pack_borders, bands=bands),
        [shaped((2 * channels + head.shape[0], 128))] * 2 + [shaped((channels, strip_cols))] * 2,
        [even_swap(to_a, "row", bands), odd_row_swap(to_b), own_a, own_b],
        1,
    )
    side_a, side_b = even_swap(to_a, COLS, strips), odd_strip_swap(to_b)
    pooled, slope, wide = whole_call(
        functools.partial(layer_one, strips=strips),
        [
            shaped((2, SENT, 4 * channels)),
            shaped((band_rows, channels, 256)),
            shaped((band_rows + 2, channels, 256)),
        ],
        [x, above, below, side_a, side_b, joined_one, pool, order],
        2 * band_rows * 192 * 192 * 256,
    )
    pieces = row_swaps([pooled] * bands, bands, near_first=True)

    even = strip % 2 == 0
    ends = [side[2 * channels :].reshape(og[:edge].shape) for side in (side_a, side_b)]
    ends[1] = jnp.where((strip == 0) | (strip == strips - 1), 0, ends[1])
    before, after = jnp.where(even, ends[1], ends[0]), jnp.where(even, ends[0], ends[1])
    og = jnp.concatenate([before, og, after], 0)
    og = jnp.pad(og, ((1, PITCH - own_cols - 2 * REACH + 1), (0, 0), (0, 0)))
    og = jnp.transpose(og, (1, 0, 2))

    count = pooled_rows * PITCH
    *terms, pooled_map, grad_map = whole_call(
        functools.partial(layer_two, bands=bands),
        [shaped((72, 4 * channels))] * bands
        + [shaped((pooled_rows + 2, PITCH, 4 * channels)), shaped((pooled_rows + 2, PITCH, filters))],
        [og, taps_two] + pieces,
        4 * count * 9 * filters * 4 * channels,
        scratch=[pltpu.VMEM((bands, 72, 4 * channels), BF16)],
    )
    received = row_swaps(terms, bands)

    half = 9 * filters // 2
    keep_two, send_two = whole_call(
        filter_two_grads,
        [shaped((half, 4 * channels))] * 2,
        [pooled_map, grad_map],
        2 * count * 9 * filters * 4 * channels,
        scratch=[pltpu.VMEM((2 * half, 4 * channels), BF16)],
    )
    g, up_a, up_b, keep, send = whole_call(
        functools.partial(grad_pre_one, bands=bands),
        [shaped((band_rows, channels, 256))]
        + [shaped((channels, 256))] * 2
        + [shaped((half + HALF_ONE, 256))] * 2,
        received + [slope, wide, pool_back, order, keep_two, send_two],
        2 * 8 * 192 * 192 * 256,
        scratch=[pltpu.VMEM((144, 256), F32)],
    )
    two, one, joined = whole_call(
        add_halves,
        [shaped((half, 256)), shaped((HALF_ONE, 256)), shaped((channels + HALF_ONE, 256))],
        [keep, even_swap(send, "pair", 2), up_a],
        0,
    )
    columns = lax.axis_size("col")
    two, two_more = sum_but_last(two, "col", columns)
    ones = row_swaps([one, joined] + [one] * (bands - 2), bands, near_first=True)
    near = ones[row_order(bands, near_first=True).index(1)]
    up_b = odd_row_swap(up_b)
    (one,) = whole_call(sum_rows, [shaped(one.shape)], ones + [up_b], 0, after=1)
    input_grad, done = whole_call(
        functools.partial(layer_one_back, bands=bands),
        [shaped(features_in.shape), shaped((8, 128), F32)],
        [g, near, up_b, back_one],
        2 * band_rows * 192 * 192 * 256,
    )
    mine_two = added(two, two_more, one)
    grad_two, wrote = whole_call(
        functools.partial(finish_two, scale=1.0 / math.sqrt(pooled_rows * total)),
        [shaped((2 * half, 256), F32), shaped((8, 128), F32)],
        [mine_two, even_swap(mine_two, "pair", 2)],
        10**8,
        scratch=[pltpu.VMEM((2, half, 256), F32), pltpu.SemaphoreType.DMA((2,))],
        out_spaces=[pl.ANY, pltpu.VMEM],
    )
    one, across = sum_but_last(one, "col", columns)
    beside_one = even_swap(one, "pair", 2)
    corner = corner_swap(one, columns // 2)
    (grad_one,) = whole_call(
        functools.partial(finish_one, scale=1.0 / math.sqrt(height * width)),
        [shaped((3, 3 * channels, channels), F32)],
        [one, across, beside_one, corner, wrote, done],
        1,
        scratch=[pltpu.VMEM((144, 256), F32)],
        after=2,
    )
    grad_two = jnp.transpose(grad_two.reshape(3, 3, filters, 4 * channels), (2, 0, 1, 3))
    grad_one = jnp.transpose(grad_one.reshape(3, 3, channels, channels), (2, 0, 1, 3))
    return (input_grad, grad_one, grad_two)


def solution(mesh):
    in_specs = (
        P("grp", "row", ("col", "pair")),
        P(),
        P("row", None, None, None),
        P(("grp", "row"), ("col", "pair"), None),
    )
    out_specs = (
        P("grp", "row", ("col", "pair")),
        P("grp", None, None, None),
        P(("grp", "row"), None, None, None),
    )
    return jax.shard_map(local, mesh=mesh, in_specs=in_specs, out_specs=out_specs, check_vma=False)
```

```python
import functools
import math

import jax
import jax.numpy as jnp
from jax import lax
from jax.experimental import pallas as pl
from jax.experimental.pallas import tpu as pltpu
from jax.sharding import PartitionSpec as P

BF16 = jnp.bfloat16
F32 = jnp.float32
COLS = ("col", "pair")
REACH = 3
HALF_ONE = 72
PITCH = 48
SENT = 40


def dot(a, b, contract):
    return lax.dot_general(a, b, ((contract[:1], contract[1:]), ((), ())), preferred_element_type=F32)


def whole_call(body, outs, operands, flops, scratch=(), after=0, out_spaces=None):
    specs = [
        pl.BlockSpec(memory_space=pltpu.VMEM) for _ in range(len(operands) - after)
    ] + [pl.BlockSpec(memory_space=pl.ANY)] * after
    sizes = [math.prod(a.shape) * a.dtype.itemsize for a in tuple(operands) + tuple(outs)]
    moved = sum(sizes) if flops else 0
    return pl.pallas_call(
        body,
        out_shape=outs,
        in_specs=specs,
        out_specs=[pl.BlockSpec(memory_space=space) for space in out_spaces or [pltpu.VMEM] * len(outs)],
        scratch_shapes=list(scratch),
        cost_estimate=pl.CostEstimate(flops=flops, bytes_accessed=moved, transcendentals=0),
        compiler_params=pltpu.CompilerParams(vmem_limit_bytes=40 * 1024 * 1024),
    )(*operands)


def strip_index():
    return lax.axis_index("col") * lax.axis_size("pair") + lax.axis_index("pair")


def shaped(shape, dtype=BF16):
    return jax.ShapeDtypeStruct(shape, dtype)


def roll(values, amount, axis):
    return pltpu.roll(values, amount % values.shape[axis], axis)


def sigmoid(values):
    return 0.5 + 0.5 * jnp.tanh(0.5 * values)


def slope_of(values, sig):
    return sig * (1.0 + values * (1.0 - sig))


def pool_matrix(strip, total, back=False):
    row = lax.broadcasted_iota(jnp.int32, (2 * PITCH, 256), 0)
    lane = lax.broadcasted_iota(jnp.int32, (2 * PITCH, 256), 1)
    half = (row >= PITCH).astype(jnp.int32)
    n = row - half * PITCH
    if back:
        v, most = jnp.where((n == 32) & (half == 1), -1, n), 33
    else:
        v, most = n - REACH, 32 + 2 * REACH
    near = jnp.bitwise_and(lane - 4 * v - 2 * half, 255) < 2
    place = strip * 32 + v
    keep = near & (n < most) & (place >= 0) & (place < total)
    return jnp.where(keep, 0.25, 0.0).astype(BF16)


def order_matrix():
    row = lax.broadcasted_iota(jnp.int32, (256, 256), 0)
    lane = lax.broadcasted_iota(jnp.int32, (256, 256), 1)
    j, i, c = row >> 7, (row >> 6) & 1, row & 63
    return jnp.where(lane == 4 * c + 2 * i + j, 1.0, 0.0).astype(BF16)


def constants(w_ref, joined_ref, back_w_ref, pool_ref, back_ref, order_ref, *, total):
    turned = [w_ref[2 - i].astype(F32).T for i in range(3)]
    back_w_ref[...] = jnp.concatenate(
        [jnp.concatenate([t[:, 64 * j : 64 * j + 64] for t in turned], 1) for j in range(3)], 0
    ).astype(BF16)
    joined_ref[...] = jnp.concatenate([w_ref[0], w_ref[1], w_ref[2]], axis=1)
    pool_ref[...] = pool_matrix(strip_index(), total)
    back_ref[...] = pool_matrix(strip_index(), total, back=True)
    order_ref[...] = order_matrix()


def beside(a_ref, b_ref, place, count):
    even = (place & 1) == 0
    a = a_ref[...].astype(F32)
    b = jnp.where((place > 0) & (place < count - 1), b_ref[...].astype(F32), 0.0)
    return jnp.where(even, b, a).astype(BF16), jnp.where(even, a, b).astype(BF16)


def pack_row(row, r, slot, head, tail):
    turned = roll(row.astype(F32), 16 * r, 1)
    return jnp.where(slot == r, turned, head), jnp.where(slot == (r - 1) % 8, turned, tail)


def pack_own(x_ref, head_ref, tail_ref, a_ref, b_ref):
    even = (strip_index() & 1) == 0
    slot = lax.broadcasted_iota(jnp.int32, (64, 128), 1) >> 4
    head = tail = jnp.zeros((64, 128), F32)
    for r in range(x_ref.shape[0]):
        head, tail = pack_row(x_ref[r], r, slot, head, tail)
    a_ref[:64] = jnp.where(even, tail, head).astype(BF16)
    b_ref[:64] = jnp.where(even, head, tail).astype(BF16)
    first, last = head_ref[...].astype(F32), tail_ref[...].astype(F32)
    a_ref[64:] = jnp.where(even, last, first).astype(BF16)
    b_ref[64:] = jnp.where(even, first, last).astype(BF16)


def pack_borders(up_a_ref, up_b_ref, own_a_ref, own_b_ref, a_ref, b_ref, above_ref, below_ref, *, bands):
    even = (strip_index() & 1) == 0
    above_ref[...], below_ref[...] = beside(up_a_ref, up_b_ref, lax.axis_index("row"), bands)
    slot = lax.broadcasted_iota(jnp.int32, (64, 128), 1) >> 4
    head = tail = jnp.zeros((64, 128), F32)
    for r, ref in enumerate((above_ref, below_ref)):
        head, tail = pack_row(ref[...], r, slot, head, tail)
    a_ref[:64] = jnp.where(even, tail, head).astype(BF16)
    b_ref[:64] = jnp.where(even, head, tail).astype(BF16)
    a_ref[64:] = own_a_ref[...]
    b_ref[64:] = own_b_ref[...]


def layer_one(
    x_ref,
    above_ref,
    below_ref,
    a_ref,
    b_ref,
    w_ref,
    pool_ref,
    order_ref,
    pooled_ref,
    slope_ref,
    wide_ref,
    *,
    strips,
):
    strip = strip_index()
    band_rows = x_ref.shape[0]
    slot = lax.broadcasted_iota(jnp.int32, (128, 128), 1) >> 4
    inner = (strip > 0) & (strip < strips - 1)
    sides = a_ref[:128].astype(F32), jnp.where(inner, b_ref[:128].astype(F32), 0.0)
    from_a = ((slot ^ strip) & 1) == 0
    packed = jnp.where(from_a, *sides), jnp.where(from_a, *sides[::-1])
    for r in range(band_rows):
        wide_ref[1 + r, :, 128:] = roll(packed[r % 2][64:], -16 * r, 1).astype(BF16)
    for r, place in enumerate((0, band_rows + 1)):
        wide_ref[place, :, 128:] = roll(packed[r][:64], -16 * r, 1).astype(BF16)
    wide_ref[0, :, :128] = above_ref[...]
    wide_ref[1 : band_rows + 1, :, :128] = x_ref[...]
    wide_ref[band_rows + 1, :, :128] = below_ref[...]
    weights = w_ref[...]
    rows = slope_ref.shape[0]
    halves, held = [], None
    for h in range(rows):
        y = dot(weights, wide_ref[h : h + 3].reshape(192, 256), (1, 0))
        pre = roll(y[:64], 1, 1) + y[64:128] + roll(y[128:], -1, 1)
        sig = sigmoid(pre)
        slope_ref[h] = slope_of(pre, sig).astype(BF16)
        active = pre * sig
        if h % 2:
            halves.append((held + active).astype(BF16))
        else:
            held = active
    pooled = dot(pool_ref[...], jnp.concatenate(halves, 0), (1, 1))
    stacked = jnp.concatenate(
        [
            jnp.concatenate(
                [pooled[:PITCH, u * 128 : u * 128 + 128], pooled[PITCH:, u * 128 : u * 128 + 128]], 1
            )
            for u in range(2)
        ],
        0,
    ).astype(BF16)
    ordered = dot(stacked, order_ref[...], (1, 0)).astype(BF16)
    for u in range(2):
        pooled_ref[u] = ordered[u * PITCH : u * PITCH + SENT]


def layer_two(og_ref, w_ref, *refs, bands):
    pieces, refs = refs[:bands], refs[bands:]
    terms, refs = refs[:bands], refs[bands:]
    map_ref, grad_ref, pack_ref = refs
    band = lax.axis_index("row")
    rows, _, filters = og_ref.shape
    count = rows * PITCH
    map_ref[0] = jnp.zeros((PITCH, 256), BF16)
    map_ref[rows + 1] = jnp.zeros((PITCH, 256), BF16)
    blank = jnp.zeros((PITCH - SENT, 256), BF16)
    for k, piece in zip(row_order(bands, near_first=True), pieces):
        for t in range(2):
            map_ref[1 + 2 * (band ^ k) + t] = jnp.concatenate([piece[t], blank], 0)
    near = jnp.concatenate([map_ref[i : i + rows].reshape(count, 256) for i in range(3)], 1)
    y = dot(near, jnp.concatenate([w_ref[i] for i in range(3)], 1), (1, 1))
    pre = roll(y[:, :filters], 1, 0) + y[:, filters : 2 * filters] + roll(y[:, 2 * filters :], -1, 0)
    grad = og_ref[...].reshape(count, filters).astype(F32) * slope_of(pre, sigmoid(pre))
    grad = grad.astype(BF16)
    grad_ref[0] = jnp.zeros((PITCH, filters), BF16)
    grad_ref[rows + 1] = jnp.zeros((PITCH, filters), BF16)
    grad_ref[1 : rows + 1] = grad.reshape(rows, PITCH, filters)
    near = jnp.concatenate([grad_ref[2 - i : 2 - i + rows].reshape(count, filters) for i in range(3)], 1)
    weights = [
        jnp.concatenate([w_ref[i, j * filters : (j + 1) * filters] for j in range(3)], 1) for i in range(3)
    ]
    z = dot(near, jnp.concatenate(weights, 0), (1, 0))
    spread = roll(z[:, :256], -1 - REACH, 0) + roll(z[:, 256:512], -REACH, 0) + roll(z[:, 512:], 1 - REACH, 0)
    spread = spread.reshape(rows, PITCH, 256)
    odd = (lax.broadcasted_iota(jnp.int32, (8, 256), 1) & 1) == 1
    row = lax.broadcasted_iota(jnp.int32, (8, 256), 0)
    ends = [jnp.where(odd, spread[u - 1, 47:48], spread[u, 32:33]) for u in range(rows)]
    for p in range(rows // 2):
        shared = jnp.where(row == 0, ends[2 * p], jnp.where(row == 1, ends[2 * p + 1], 0.0))
        pack_ref[p] = jnp.concatenate([spread[2 * p, :32], shared, spread[2 * p + 1, :32]], 0).astype(BF16)
    for k in range(bands):
        terms[k][...] = pack_ref[band ^ k]


def filter_two_grads(map_ref, grad_ref, keep_ref, send_ref, all_ref):
    pair = lax.axis_index("pair")
    rows = map_ref.shape[0] - 2
    filters = grad_ref.shape[2]
    v = lax.broadcasted_iota(jnp.int32, (rows, PITCH, filters), 1)
    own = (v >= REACH) & (v < REACH + 32)
    wide = jnp.where(own, grad_ref[1 : rows + 1].astype(F32), 0.0).reshape(rows * PITCH, filters)
    cat = jnp.concatenate([roll(wide, -1, 0), wide, roll(wide, 1, 0)], 1).astype(BF16)
    taps = 3 * filters
    for i in range(3):
        part = dot(cat, map_ref[i : i + rows].reshape(rows * PITCH, 256), (0, 0))
        all_ref[i * taps : (i + 1) * taps] = part.astype(BF16)
    half = keep_ref.shape[0]
    keep_ref[...] = all_ref[pl.ds(pl.multiple_of(pair * half, 16), half)]
    send_ref[...] = all_ref[pl.ds(pl.multiple_of((1 - pair) * half, 16), half)]


def add_after(a_ref, b_ref, *refs):
    refs[-1][...] = (a_ref[...].astype(F32) + b_ref[...].astype(F32)).astype(BF16)


def add_halves(a_ref, b_ref, border_ref, two_ref, one_ref, joined_ref):
    half, border = two_ref.shape[0], border_ref.shape[0]
    total = (a_ref[...].astype(F32) + b_ref[...].astype(F32)).astype(BF16)
    two_ref[...] = total[:half]
    one_ref[...] = total[half:]
    joined_ref[:border] = border_ref[...]
    joined_ref[border:] = total[half:]


def sum_rows(*refs):
    *refs, _, out_ref = refs
    rows = out_ref.shape[0]
    terms = dict(zip(row_order(len(refs), near_first=True, by_half=True), (ref[-rows:].astype(F32) for ref in refs)))
    terms = [terms[k] for k in range(len(refs))]
    while len(terms) > 1:
        terms = [a + b for a, b in zip(terms[::2], terms[1::2])]
    out_ref[...] = terms[0].astype(BF16)


def grad_pre_one(*refs, bands):
    terms, refs = refs[:bands], refs[bands:]
    slope_ref, wide_ref, pool_ref, order_ref, keep_two_ref, send_two_ref, *refs = refs
    g_ref, a_ref, b_ref, keep_ref, send_ref, part_ref = refs
    pair = lax.axis_index("pair")
    summed = terms[0][...].astype(F32)
    for k in range(1, bands):
        summed = summed + terms[k][...].astype(F32)
    blank = jnp.zeros((8, 256), F32)
    ends = summed[32:40]
    blocks = [summed[:32], ends, blank, summed[40:], roll(ends, -1, 0), blank]
    ordered = dot(jnp.concatenate(blocks, 0).astype(BF16), order_ref[...], (1, 1)).astype(BF16)
    pool = pool_ref[...]
    cats = []
    own = lax.broadcasted_iota(jnp.int32, (64, 256), 1) < 128
    for u in range(2):
        block = ordered[u * PITCH : (u + 1) * PITCH]
        up = dot(jnp.concatenate([block[:, :128], block[:, 128:]], 0), pool, (0, 0))
        for i in range(4):
            h = 4 * u + i
            g = (up[64 * (i // 2) : 64 * (i // 2) + 64] * slope_ref[h].astype(F32)).astype(BF16)
            g_ref[h] = g
            mine = jnp.where(own, g.astype(F32), 0.0)
            cats.append(jnp.concatenate([roll(mine, -1, 1), mine, roll(mine, 1, 1)], 0).astype(BF16))
    around = jnp.concatenate([wide_ref[h : h + 3].reshape(192, 256) for h in range(8)], 1)
    acc = dot(jnp.concatenate(cats, 1), around, (1, 1))
    even = (lax.axis_index("row") & 1) == 0
    first, last = g_ref[0].astype(F32), g_ref[7].astype(F32)
    a_ref[...] = jnp.where(even, last, first).astype(BF16)
    b_ref[...] = jnp.where(even, first, last).astype(BF16)
    part_ref[:96] = jnp.concatenate([acc[:96, :128], acc[96:, :128]], 1)
    part_ref[96:] = jnp.concatenate([acc[48 * q : 48 * q + 48, 128:] for q in range(4)], 1)
    half = keep_two_ref.shape[0]
    for ref, two_ref, place in ((keep_ref, keep_two_ref, pair), (send_ref, send_two_ref, 1 - pair)):
        ref[:half] = two_ref[...]
        ref[half:] = part_ref[pl.ds(pl.multiple_of(place * HALF_ONE, 8), HALF_ONE)].astype(BF16)


def layer_one_back(g_ref, a_ref, b_ref, w_ref, out_ref, done_ref, *, bands):
    above, below = beside(a_ref.at[: b_ref.shape[0]], b_ref, lax.axis_index("row"), bands)
    done_ref[...] = jnp.zeros(done_ref.shape, F32)
    lines = [above] + [g_ref[h] for h in range(8)] + [below]
    rows = []
    for h in range(8):
        z = dot(w_ref[...], jnp.concatenate(lines[h : h + 3], 0), (1, 0))
        rows.append((roll(z[:64], -1, 1) + z[64:128] + roll(z[128:], 1, 1))[:, :128])
    out_ref[...] = jnp.swapaxes(jnp.stack(rows, 0), 0, 1).astype(BF16)


def finish_two(mine_ref, other_ref, two_hbm, done_ref, two_ref, sems, *, scale):
    pair, half = lax.axis_index("pair"), mine_ref.shape[0]
    done_ref[...] = jnp.zeros(done_ref.shape, F32)
    copies = []
    for n, (ref, place) in enumerate(((mine_ref, pair), (other_ref, 1 - pair))):
        rows = pl.ds(pl.multiple_of(place * half, 16), half)
        two_ref[n] = ref[...].astype(F32) * scale
        copies.append(pltpu.make_async_copy(two_ref.at[n], two_hbm.at[rows], sems.at[n]))
        copies[-1].start()
    for copy in copies:
        copy.wait()


def finish_one(mine_ref, corner_ref, beside_ref, across_ref, _, __, out_ref, flat_ref, *, scale):
    pair = lax.axis_index("pair")
    for refs, place in (((mine_ref, across_ref), pair), ((beside_ref, corner_ref), 1 - pair)):
        total = refs[0][...].astype(F32) + refs[1][...].astype(F32)
        flat_ref[pl.ds(pl.multiple_of(place * HALF_ONE, 8), HALF_ONE)] = total * scale
    out_ref[0, :96] = flat_ref[:96, :64]
    out_ref[1, :96] = flat_ref[:96, 64:128]
    out_ref[0, 96:] = flat_ref[:96, 128:192]
    out_ref[1, 96:] = flat_ref[:96, 192:]
    for q in range(4):
        out_ref[2, 48 * q : 48 * q + 48] = flat_ref[96:, 64 * q : 64 * q + 64]


def even_swap(values, axis, count):
    return lax.ppermute(values, axis, [(n, n ^ 1) for n in range(count)])


def odd_partner(place):
    return place - 1 if place % 2 == 0 else place + 1


def odd_row_swap(values):
    bands, cores = lax.axis_size("row"), lax.axis_size("pair")
    steps = []
    for n in range(bands):
        for p in range(cores):
            to = (n, p ^ 1) if n in (0, bands - 1) else (odd_partner(n), p)
            steps.append((n * cores + p, to[0] * cores + to[1]))
    return lax.ppermute(values, ("row", "pair"), steps)


def odd_strip_swap(values):
    groups, strips = lax.axis_size("grp"), lax.axis_size(COLS)
    steps = []
    for g in range(groups):
        for n in range(strips):
            to = ((g + 1) % groups, n) if n in (0, strips - 1) else (g, odd_partner(n))
            steps.append((g * strips + n, to[0] * strips + to[1]))
    return lax.ppermute(values, ("grp",) + COLS, steps)


def xor_swap(values, axis, count, k):
    return lax.ppermute(values, axis, [(n, n ^ k) for n in range(count)])


def corner_swap(values, k):
    columns, cores = lax.axis_size("col"), lax.axis_size("pair")
    steps = [(c * cores + p, (c ^ k) * cores + (p ^ 1)) for c in range(columns) for p in range(cores)]
    return lax.ppermute(values, COLS, steps)


def row_order(bands, near_first=False, by_half=False):
    far_first = sorted(range(1, bands), key=lambda k: (k < bands // 2, k if by_half else -k))
    return [0] + (far_first[::-1] if near_first else far_first)


def row_swaps(values, bands, near_first=False, by_half=False):
    order = row_order(bands, near_first, by_half)
    return [values[0]] + [xor_swap(values[k], "row", bands, k) for k in order[1:]]


def added(a, b, *after):
    (total,) = whole_call(add_after, [shaped(a.shape)], [a, b, *after], 0, after=len(after))
    return total


def sum_but_last(part, axis, count):
    step = 1
    while 2 * step < count:
        part = added(part, xor_swap(part, axis, count, step))
        step *= 2
    return part, xor_swap(part, axis, count, step)


def local(features_in, filters_one, filters_two, out_grad):
    channels, band_rows, strip_cols = features_in.shape
    filters, own_cols, pooled_rows = out_grad.shape
    bands = lax.axis_size("row")
    strips = lax.axis_size(COLS)
    band = lax.axis_index("row")
    strip = lax.axis_index(COLS)
    pair = lax.axis_index("pair")
    height, width = band_rows * bands, strip_cols * strips
    total = own_cols * strips

    taps_one = jnp.transpose(filters_one, (1, 2, 0, 3)).reshape(3, 3 * channels, channels)
    taps_two = jnp.transpose(filters_two, (1, 2, 0, 3)).reshape(3, 3 * filters, 4 * channels)

    og = jnp.transpose(out_grad, (1, 2, 0))
    edge = REACH - 1
    x = jnp.transpose(features_in, (1, 0, 2))
    even = band % 2 == 0
    to_a, to_b = jnp.where(even, x[-1], x[0]), jnp.where(even, x[0], x[-1])
    head, tail = og[:edge], og[-edge:]
    joined_one, back_one, pool, pool_back, order = whole_call(
        functools.partial(constants, total=total),
        [shaped((3 * channels, 3 * channels))] * 2 + [shaped((2 * PITCH, 256))] * 2 + [shaped((256, 256))],
        [taps_one],
        10**8,
    )
    head, tail = head.reshape(-1, 128), tail.reshape(-1, 128)
    own_a, own_b = whole_call(
        pack_own, [shaped((channels + head.shape[0], 128))] * 2, [x, head, tail], 10**8
    )
    to_a, to_b, above, below = whole_call(
        functools.partial(pack_borders, bands=bands),
        [shaped((2 * channels + head.shape[0], 128))] * 2 + [shaped((channels, strip_cols))] * 2,
        [even_swap(to_a, "row", bands), odd_row_swap(to_b), own_a, own_b],
        1,
    )
    side_a, side_b = even_swap(to_a, COLS, strips), odd_strip_swap(to_b)
    pooled, slope, wide = whole_call(
        functools.partial(layer_one, strips=strips),
        [
            shaped((2, SENT, 4 * channels)),
            shaped((band_rows, channels, 256)),
            shaped((band_rows + 2, channels, 256)),
        ],
        [x, above, below, side_a, side_b, joined_one, pool, order],
        2 * band_rows * 192 * 192 * 256,
    )
    pieces = row_swaps([pooled] * bands, bands, near_first=True)

    even = strip % 2 == 0
    ends = [side[2 * channels :].reshape(og[:edge].shape) for side in (side_a, side_b)]
    ends[1] = jnp.where((strip == 0) | (strip == strips - 1), 0, ends[1])
    before, after = jnp.where(even, ends[1], ends[0]), jnp.where(even, ends[0], ends[1])
    og = jnp.concatenate([before, og, after], 0)
    og = jnp.pad(og, ((1, PITCH - own_cols - 2 * REACH + 1), (0, 0), (0, 0)))
    og = jnp.transpose(og, (1, 0, 2))

    count = pooled_rows * PITCH
    *terms, pooled_map, grad_map = whole_call(
        functools.partial(layer_two, bands=bands),
        [shaped((72, 4 * channels))] * bands
        + [shaped((pooled_rows + 2, PITCH, 4 * channels)), shaped((pooled_rows + 2, PITCH, filters))],
        [og, taps_two] + pieces,
        4 * count * 9 * filters * 4 * channels,
        scratch=[pltpu.VMEM((bands, 72, 4 * channels), BF16)],
    )
    received = row_swaps(terms, bands)

    half = 9 * filters // 2
    keep_two, send_two = whole_call(
        filter_two_grads,
        [shaped((half, 4 * channels))] * 2,
        [pooled_map, grad_map],
        2 * count * 9 * filters * 4 * channels,
        scratch=[pltpu.VMEM((2 * half, 4 * channels), BF16)],
    )
    g, up_a, up_b, keep, send = whole_call(
        functools.partial(grad_pre_one, bands=bands),
        [shaped((band_rows, channels, 256))]
        + [shaped((channels, 256))] * 2
        + [shaped((half + HALF_ONE, 256))] * 2,
        received + [slope, wide, pool_back, order, keep_two, send_two],
        2 * 8 * 192 * 192 * 256,
        scratch=[pltpu.VMEM((144, 256), F32)],
    )
    two, one, joined = whole_call(
        add_halves,
        [shaped((half, 256)), shaped((HALF_ONE, 256)), shaped((channels + HALF_ONE, 256))],
        [keep, even_swap(send, "pair", 2), up_a],
        0,
    )
    columns = lax.axis_size("col")
    two, two_more = sum_but_last(two, "col", columns)
    ones = row_swaps([one, joined] + [one] * (bands - 2), bands, near_first=True, by_half=True)
    near = ones[row_order(bands, near_first=True, by_half=True).index(1)]
    up_b = odd_row_swap(up_b)
    (one,) = whole_call(sum_rows, [shaped(one.shape)], ones + [up_b], 0, after=1)
    input_grad, done = whole_call(
        functools.partial(layer_one_back, bands=bands),
        [shaped(features_in.shape), shaped((8, 128), F32)],
        [g, near, up_b, back_one],
        2 * band_rows * 192 * 192 * 256,
    )
    mine_two = added(two, two_more, one)
    grad_two, wrote = whole_call(
        functools.partial(finish_two, scale=1.0 / math.sqrt(pooled_rows * total)),
        [shaped((2 * half, 256), F32), shaped((8, 128), F32)],
        [mine_two, even_swap(mine_two, "pair", 2)],
        10**8,
        scratch=[pltpu.VMEM((2, half, 256), F32), pltpu.SemaphoreType.DMA((2,))],
        out_spaces=[pl.ANY, pltpu.VMEM],
    )
    one, across = sum_but_last(one, "col", columns)
    beside_one = even_swap(one, "pair", 2)
    corner = corner_swap(one, columns // 2)
    (grad_one,) = whole_call(
        functools.partial(finish_one, scale=1.0 / math.sqrt(height * width)),
        [shaped((3, 3 * channels, channels), F32)],
        [one, corner, beside_one, across, wrote, done],
        1,
        scratch=[pltpu.VMEM((144, 256), F32)],
        after=2,
    )
    grad_two = jnp.transpose(grad_two.reshape(3, 3, filters, 4 * channels), (2, 0, 1, 3))
    grad_one = jnp.transpose(grad_one.reshape(3, 3, channels, channels), (2, 0, 1, 3))
    return (input_grad, grad_one, grad_two)


def solution(mesh):
    in_specs = (
        P("grp", "row", ("col", "pair")),
        P(),
        P("row", None, None, None),
        P(("grp", "row"), ("col", "pair"), None),
    )
    out_specs = (
        P("grp", "row", ("col", "pair")),
        P("grp", None, None, None),
        P(("grp", "row"), None, None, None),
    )
    return jax.shard_map(local, mesh=mesh, in_specs=in_specs, out_specs=out_specs, check_vma=False)
```

```python
import functools
import math

import jax
import jax.numpy as jnp
from jax import lax
from jax.experimental import pallas as pl
from jax.experimental.pallas import tpu as pltpu
from jax.sharding import PartitionSpec as P

BF16 = jnp.bfloat16
F32 = jnp.float32
COLS = ("col", "pair")
REACH = 3
HALF_ONE = 72
PITCH = 48
SENT = 40


def dot(a, b, contract):
    return lax.dot_general(a, b, ((contract[:1], contract[1:]), ((), ())), preferred_element_type=F32)


def whole_call(body, outs, operands, flops, scratch=(), after=0, out_spaces=None):
    specs = [
        pl.BlockSpec(memory_space=pltpu.VMEM) for _ in range(len(operands) - after)
    ] + [pl.BlockSpec(memory_space=pl.ANY)] * after
    sizes = [math.prod(a.shape) * a.dtype.itemsize for a in tuple(operands) + tuple(outs)]
    moved = sum(sizes) if flops else 0
    return pl.pallas_call(
        body,
        out_shape=outs,
        in_specs=specs,
        out_specs=[pl.BlockSpec(memory_space=space) for space in out_spaces or [pltpu.VMEM] * len(outs)],
        scratch_shapes=list(scratch),
        cost_estimate=pl.CostEstimate(flops=flops, bytes_accessed=moved, transcendentals=0),
        compiler_params=pltpu.CompilerParams(vmem_limit_bytes=40 * 1024 * 1024),
    )(*operands)


def strip_index():
    return lax.axis_index("col") * lax.axis_size("pair") + lax.axis_index("pair")


def shaped(shape, dtype=BF16):
    return jax.ShapeDtypeStruct(shape, dtype)


def roll(values, amount, axis):
    return pltpu.roll(values, amount % values.shape[axis], axis)


def sigmoid(values):
    return 0.5 + 0.5 * jnp.tanh(0.5 * values)


def slope_of(values, sig):
    return sig * (1.0 + values * (1.0 - sig))


def pool_matrix(strip, total, back=False):
    row = lax.broadcasted_iota(jnp.int32, (2 * PITCH, 256), 0)
    lane = lax.broadcasted_iota(jnp.int32, (2 * PITCH, 256), 1)
    half = (row >= PITCH).astype(jnp.int32)
    n = row - half * PITCH
    if back:
        v, most = jnp.where((n == 32) & (half == 1), -1, n), 33
    else:
        v, most = n - REACH, 32 + 2 * REACH
    near = jnp.bitwise_and(lane - 4 * v - 2 * half, 255) < 2
    place = strip * 32 + v
    keep = near & (n < most) & (place >= 0) & (place < total)
    return jnp.where(keep, 0.25, 0.0).astype(BF16)


def order_matrix():
    row = lax.broadcasted_iota(jnp.int32, (256, 256), 0)
    lane = lax.broadcasted_iota(jnp.int32, (256, 256), 1)
    j, i, c = row >> 7, (row >> 6) & 1, row & 63
    return jnp.where(lane == 4 * c + 2 * i + j, 1.0, 0.0).astype(BF16)


def constants(w_ref, joined_ref, back_w_ref, pool_ref, back_ref, order_ref, *, total):
    turned = [w_ref[2 - i].astype(F32).T for i in range(3)]
    back_w_ref[...] = jnp.concatenate(
        [jnp.concatenate([t[:, 64 * j : 64 * j + 64] for t in turned], 1) for j in range(3)], 0
    ).astype(BF16)
    joined_ref[...] = jnp.concatenate([w_ref[0], w_ref[1], w_ref[2]], axis=1)
    pool_ref[...] = pool_matrix(strip_index(), total)
    back_ref[...] = pool_matrix(strip_index(), total, back=True)
    order_ref[...] = order_matrix()


def beside(a_ref, b_ref, place, count):
    even = (place & 1) == 0
    a = a_ref[...].astype(F32)
    b = jnp.where((place > 0) & (place < count - 1), b_ref[...].astype(F32), 0.0)
    return jnp.where(even, b, a).astype(BF16), jnp.where(even, a, b).astype(BF16)


def pack_row(row, r, slot, head, tail):
    turned = roll(row.astype(F32), 16 * r, 1)
    return jnp.where(slot == r, turned, head), jnp.where(slot == (r - 1) % 8, turned, tail)


def pack_own(x_ref, head_ref, tail_ref, a_ref, b_ref):
    even = (strip_index() & 1) == 0
    slot = lax.broadcasted_iota(jnp.int32, (64, 128), 1) >> 4
    head = tail = jnp.zeros((64, 128), F32)
    for r in range(x_ref.shape[0]):
        head, tail = pack_row(x_ref[r], r, slot, head, tail)
    a_ref[:64] = jnp.where(even, tail, head).astype(BF16)
    b_ref[:64] = jnp.where(even, head, tail).astype(BF16)
    first, last = head_ref[...].astype(F32), tail_ref[...].astype(F32)
    a_ref[64:] = jnp.where(even, last, first).astype(BF16)
    b_ref[64:] = jnp.where(even, first, last).astype(BF16)


def pack_borders(up_b_ref, up_a_ref, own_a_ref, own_b_ref, a_ref, b_ref, above_ref, below_ref, *, bands):
    even = (strip_index() & 1) == 0
    above_ref[...], below_ref[...] = beside(up_a_ref, up_b_ref, lax.axis_index("row"), bands)
    slot = lax.broadcasted_iota(jnp.int32, (64, 128), 1) >> 4
    head = tail = jnp.zeros((64, 128), F32)
    for r, ref in enumerate((above_ref, below_ref)):
        head, tail = pack_row(ref[...], r, slot, head, tail)
    a_ref[:64] = jnp.where(even, tail, head).astype(BF16)
    b_ref[:64] = jnp.where(even, head, tail).astype(BF16)
    a_ref[64:] = own_a_ref[...]
    b_ref[64:] = own_b_ref[...]


def layer_one(
    x_ref,
    above_ref,
    below_ref,
    a_ref,
    b_ref,
    w_ref,
    pool_ref,
    order_ref,
    pooled_ref,
    slope_ref,
    wide_ref,
    *,
    strips,
):
    strip = strip_index()
    band_rows = x_ref.shape[0]
    slot = lax.broadcasted_iota(jnp.int32, (128, 128), 1) >> 4
    inner = (strip > 0) & (strip < strips - 1)
    sides = a_ref[:128].astype(F32), jnp.where(inner, b_ref[:128].astype(F32), 0.0)
    from_a = ((slot ^ strip) & 1) == 0
    packed = jnp.where(from_a, *sides), jnp.where(from_a, *sides[::-1])
    for r in range(band_rows):
        wide_ref[1 + r, :, 128:] = roll(packed[r % 2][64:], -16 * r, 1).astype(BF16)
    for r, place in enumerate((0, band_rows + 1)):
        wide_ref[place, :, 128:] = roll(packed[r][:64], -16 * r, 1).astype(BF16)
    wide_ref[0, :, :128] = above_ref[...]
    wide_ref[1 : band_rows + 1, :, :128] = x_ref[...]
    wide_ref[band_rows + 1, :, :128] = below_ref[...]
    weights = w_ref[...]
    rows = slope_ref.shape[0]
    halves, held = [], None
    for h in range(rows):
        y = dot(weights, wide_ref[h : h + 3].reshape(192, 256), (1, 0))
        pre = roll(y[:64], 1, 1) + y[64:128] + roll(y[128:], -1, 1)
        sig = sigmoid(pre)
        slope_ref[h] = slope_of(pre, sig).astype(BF16)
        active = pre * sig
        if h % 2:
            halves.append((held + active).astype(BF16))
        else:
            held = active
    pooled = dot(pool_ref[...], jnp.concatenate(halves, 0), (1, 1))
    stacked = jnp.concatenate(
        [
            jnp.concatenate(
                [pooled[:PITCH, u * 128 : u * 128 + 128], pooled[PITCH:, u * 128 : u * 128 + 128]], 1
            )
            for u in range(2)
        ],
        0,
    ).astype(BF16)
    ordered = dot(stacked, order_ref[...], (1, 0)).astype(BF16)
    for u in range(2):
        pooled_ref[u] = ordered[u * PITCH : u * PITCH + SENT]


def layer_two(og_ref, w_ref, *refs, bands):
    pieces, refs = refs[:bands], refs[bands:]
    terms, refs = refs[:bands], refs[bands:]
    map_ref, grad_ref, pack_ref = refs
    band = lax.axis_index("row")
    rows, _, filters = og_ref.shape
    count = rows * PITCH
    map_ref[0] = jnp.zeros((PITCH, 256), BF16)
    map_ref[rows + 1] = jnp.zeros((PITCH, 256), BF16)
    blank = jnp.zeros((PITCH - SENT, 256), BF16)
    for k, piece in zip(row_order(bands, near_first=True), pieces):
        for t in range(2):
            map_ref[1 + 2 * (band ^ k) + t] = jnp.concatenate([piece[t], blank], 0)
    near = jnp.concatenate([map_ref[i : i + rows].reshape(count, 256) for i in range(3)], 1)
    y = dot(near, jnp.concatenate([w_ref[i] for i in range(3)], 1), (1, 1))
    pre = roll(y[:, :filters], 1, 0) + y[:, filters : 2 * filters] + roll(y[:, 2 * filters :], -1, 0)
    grad = og_ref[...].reshape(count, filters).astype(F32) * slope_of(pre, sigmoid(pre))
    grad = grad.astype(BF16)
    grad_ref[0] = jnp.zeros((PITCH, filters), BF16)
    grad_ref[rows + 1] = jnp.zeros((PITCH, filters), BF16)
    grad_ref[1 : rows + 1] = grad.reshape(rows, PITCH, filters)
    near = jnp.concatenate([grad_ref[2 - i : 2 - i + rows].reshape(count, filters) for i in range(3)], 1)
    weights = [
        jnp.concatenate([w_ref[i, j * filters : (j + 1) * filters] for j in range(3)], 1) for i in range(3)
    ]
    z = dot(near, jnp.concatenate(weights, 0), (1, 0))
    spread = roll(z[:, :256], -1 - REACH, 0) + roll(z[:, 256:512], -REACH, 0) + roll(z[:, 512:], 1 - REACH, 0)
    spread = spread.reshape(rows, PITCH, 256)
    odd = (lax.broadcasted_iota(jnp.int32, (8, 256), 1) & 1) == 1
    row = lax.broadcasted_iota(jnp.int32, (8, 256), 0)
    ends = [jnp.where(odd, spread[u - 1, 47:48], spread[u, 32:33]) for u in range(rows)]
    for p in range(rows // 2):
        shared = jnp.where(row == 0, ends[2 * p], jnp.where(row == 1, ends[2 * p + 1], 0.0))
        pack_ref[p] = jnp.concatenate([spread[2 * p, :32], shared, spread[2 * p + 1, :32]], 0).astype(BF16)
    for k in range(bands):
        terms[k][...] = pack_ref[band ^ k]


def filter_two_grads(map_ref, grad_ref, keep_ref, send_ref, all_ref):
    pair = lax.axis_index("pair")
    rows = map_ref.shape[0] - 2
    filters = grad_ref.shape[2]
    v = lax.broadcasted_iota(jnp.int32, (rows, PITCH, filters), 1)
    own = (v >= REACH) & (v < REACH + 32)
    wide = jnp.where(own, grad_ref[1 : rows + 1].astype(F32), 0.0).reshape(rows * PITCH, filters)
    cat = jnp.concatenate([roll(wide, -1, 0), wide, roll(wide, 1, 0)], 1).astype(BF16)
    taps = 3 * filters
    for i in range(3):
        part = dot(cat, map_ref[i : i + rows].reshape(rows * PITCH, 256), (0, 0))
        all_ref[i * taps : (i + 1) * taps] = part.astype(BF16)
    half = keep_ref.shape[0]
    keep_ref[...] = all_ref[pl.ds(pl.multiple_of(pair * half, 16), half)]
    send_ref[...] = all_ref[pl.ds(pl.multiple_of((1 - pair) * half, 16), half)]


def add_after(a_ref, b_ref, *refs):
    refs[-1][...] = (a_ref[...].astype(F32) + b_ref[...].astype(F32)).astype(BF16)


def add_halves(a_ref, b_ref, border_ref, two_ref, one_ref, joined_ref):
    half, border = two_ref.shape[0], border_ref.shape[0]
    total = (a_ref[...].astype(F32) + b_ref[...].astype(F32)).astype(BF16)
    two_ref[...] = total[:half]
    one_ref[...] = total[half:]
    joined_ref[:border] = border_ref[...]
    joined_ref[border:] = total[half:]


def sum_rows(*refs):
    *refs, _, out_ref = refs
    rows = out_ref.shape[0]
    terms = dict(zip(row_order(len(refs), near_first=True, by_half=True), (ref[-rows:].astype(F32) for ref in refs)))
    terms = [terms[k] for k in range(len(refs))]
    while len(terms) > 1:
        terms = [a + b for a, b in zip(terms[::2], terms[1::2])]
    out_ref[...] = terms[0].astype(BF16)


def grad_pre_one(*refs, bands):
    terms, refs = refs[:bands], refs[bands:]
    slope_ref, wide_ref, pool_ref, order_ref, keep_two_ref, send_two_ref, *refs = refs
    g_ref, a_ref, b_ref, keep_ref, send_ref, part_ref = refs
    pair = lax.axis_index("pair")
    summed = terms[0][...].astype(F32)
    for k in range(1, bands):
        summed = summed + terms[k][...].astype(F32)
    blank = jnp.zeros((8, 256), F32)
    ends = summed[32:40]
    blocks = [summed[:32], ends, blank, summed[40:], roll(ends, -1, 0), blank]
    ordered = dot(jnp.concatenate(blocks, 0).astype(BF16), order_ref[...], (1, 1)).astype(BF16)
    pool = pool_ref[...]
    cats = []
    own = lax.broadcasted_iota(jnp.int32, (64, 256), 1) < 128
    for u in range(2):
        block = ordered[u * PITCH : (u + 1) * PITCH]
        up = dot(jnp.concatenate([block[:, :128], block[:, 128:]], 0), pool, (0, 0))
        for i in range(4):
            h = 4 * u + i
            g = (up[64 * (i // 2) : 64 * (i // 2) + 64] * slope_ref[h].astype(F32)).astype(BF16)
            g_ref[h] = g
            mine = jnp.where(own, g.astype(F32), 0.0)
            cats.append(jnp.concatenate([roll(mine, -1, 1), mine, roll(mine, 1, 1)], 0).astype(BF16))
    around = jnp.concatenate([wide_ref[h : h + 3].reshape(192, 256) for h in range(8)], 1)
    acc = dot(jnp.concatenate(cats, 1), around, (1, 1))
    even = (lax.axis_index("row") & 1) == 0
    first, last = g_ref[0].astype(F32), g_ref[7].astype(F32)
    a_ref[...] = jnp.where(even, last, first).astype(BF16)
    b_ref[...] = jnp.where(even, first, last).astype(BF16)
    part_ref[:96] = jnp.concatenate([acc[:96, :128], acc[96:, :128]], 1)
    part_ref[96:] = jnp.concatenate([acc[48 * q : 48 * q + 48, 128:] for q in range(4)], 1)
    half = keep_two_ref.shape[0]
    for ref, two_ref, place in ((keep_ref, keep_two_ref, pair), (send_ref, send_two_ref, 1 - pair)):
        ref[:half] = two_ref[...]
        ref[half:] = part_ref[pl.ds(pl.multiple_of(place * HALF_ONE, 8), HALF_ONE)].astype(BF16)


def layer_one_back(g_ref, a_ref, b_ref, w_ref, out_ref, done_ref, *, bands):
    above, below = beside(a_ref.at[: b_ref.shape[0]], b_ref, lax.axis_index("row"), bands)
    done_ref[...] = jnp.zeros(done_ref.shape, F32)
    lines = [above] + [g_ref[h] for h in range(8)] + [below]
    rows = []
    for h in range(8):
        z = dot(w_ref[...], jnp.concatenate(lines[h : h + 3], 0), (1, 0))
        rows.append((roll(z[:64], -1, 1) + z[64:128] + roll(z[128:], 1, 1))[:, :128])
    out_ref[...] = jnp.swapaxes(jnp.stack(rows, 0), 0, 1).astype(BF16)


def finish_two(mine_ref, other_ref, two_hbm, done_ref, two_ref, sems, *, scale):
    pair, half = lax.axis_index("pair"), mine_ref.shape[0]
    done_ref[...] = jnp.zeros(done_ref.shape, F32)
    copies = []
    for n, (ref, place) in enumerate(((mine_ref, pair), (other_ref, 1 - pair))):
        rows = pl.ds(pl.multiple_of(place * half, 16), half)
        two_ref[n] = ref[...].astype(F32) * scale
        copies.append(pltpu.make_async_copy(two_ref.at[n], two_hbm.at[rows], sems.at[n]))
        copies[-1].start()
    for copy in copies:
        copy.wait()


def finish_one(mine_ref, beside_ref, corner_ref, across_ref, _, __, out_ref, flat_ref, *, scale):
    pair = lax.axis_index("pair")
    for refs, place in (((mine_ref, across_ref), pair), ((beside_ref, corner_ref), 1 - pair)):
        total = refs[0][...].astype(F32) + refs[1][...].astype(F32)
        flat_ref[pl.ds(pl.multiple_of(place * HALF_ONE, 8), HALF_ONE)] = total * scale
    out_ref[0, :96] = flat_ref[:96, :64]
    out_ref[1, :96] = flat_ref[:96, 64:128]
    out_ref[0, 96:] = flat_ref[:96, 128:192]
    out_ref[1, 96:] = flat_ref[:96, 192:]
    for q in range(4):
        out_ref[2, 48 * q : 48 * q + 48] = flat_ref[96:, 64 * q : 64 * q + 64]


def even_swap(values, axis, count):
    return lax.ppermute(values, axis, [(n, n ^ 1) for n in range(count)])


def odd_partner(place):
    return place - 1 if place % 2 == 0 else place + 1


def odd_row_swap(values):
    bands, cores = lax.axis_size("row"), lax.axis_size("pair")
    steps = []
    for n in range(bands):
        for p in range(cores):
            to = (n, p ^ 1) if n in (0, bands - 1) else (odd_partner(n), p)
            steps.append((n * cores + p, to[0] * cores + to[1]))
    return lax.ppermute(values, ("row", "pair"), steps)


def odd_strip_swap(values):
    groups, strips = lax.axis_size("grp"), lax.axis_size(COLS)
    steps = []
    for g in range(groups):
        for n in range(strips):
            to = ((g + 1) % groups, n) if n in (0, strips - 1) else (g, odd_partner(n))
            steps.append((g * strips + n, to[0] * strips + to[1]))
    return lax.ppermute(values, ("grp",) + COLS, steps)


def xor_swap(values, axis, count, k):
    return lax.ppermute(values, axis, [(n, n ^ k) for n in range(count)])


def corner_swap(values, k):
    columns, cores = lax.axis_size("col"), lax.axis_size("pair")
    steps = [(c * cores + p, (c ^ k) * cores + (p ^ 1)) for c in range(columns) for p in range(cores)]
    return lax.ppermute(values, COLS, steps)


def row_order(bands, near_first=False, by_half=False):
    far_first = sorted(range(1, bands), key=lambda k: (k < bands // 2, k if by_half else -k))
    return [0] + (far_first[::-1] if near_first else far_first)


def row_swaps(values, bands, near_first=False, by_half=False):
    order = row_order(bands, near_first, by_half)
    return [values[0]] + [xor_swap(values[k], "row", bands, k) for k in order[1:]]


def added(a, b, *after):
    (total,) = whole_call(add_after, [shaped(a.shape)], [a, b, *after], 0, after=len(after))
    return total


def sum_but_last(part, axis, count):
    step = 1
    while 2 * step < count:
        part = added(part, xor_swap(part, axis, count, step))
        step *= 2
    return part, xor_swap(part, axis, count, step)


def local(features_in, filters_one, filters_two, out_grad):
    channels, band_rows, strip_cols = features_in.shape
    filters, own_cols, pooled_rows = out_grad.shape
    bands = lax.axis_size("row")
    strips = lax.axis_size(COLS)
    band = lax.axis_index("row")
    strip = lax.axis_index(COLS)
    pair = lax.axis_index("pair")
    height, width = band_rows * bands, strip_cols * strips
    total = own_cols * strips

    taps_one = jnp.transpose(filters_one, (1, 2, 0, 3)).reshape(3, 3 * channels, channels)
    taps_two = jnp.transpose(filters_two, (1, 2, 0, 3)).reshape(3, 3 * filters, 4 * channels)

    og = jnp.transpose(out_grad, (1, 2, 0))
    edge = REACH - 1
    x = jnp.transpose(features_in, (1, 0, 2))
    even = band % 2 == 0
    to_a, to_b = jnp.where(even, x[-1], x[0]), jnp.where(even, x[0], x[-1])
    head, tail = og[:edge], og[-edge:]
    joined_one, back_one, pool, pool_back, order = whole_call(
        functools.partial(constants, total=total),
        [shaped((3 * channels, 3 * channels))] * 2 + [shaped((2 * PITCH, 256))] * 2 + [shaped((256, 256))],
        [taps_one],
        10**8,
    )
    head, tail = head.reshape(-1, 128), tail.reshape(-1, 128)
    own_a, own_b = whole_call(
        pack_own, [shaped((channels + head.shape[0], 128))] * 2, [x, head, tail], 10**8
    )
    to_a, to_b, above, below = whole_call(
        functools.partial(pack_borders, bands=bands),
        [shaped((2 * channels + head.shape[0], 128))] * 2 + [shaped((channels, strip_cols))] * 2,
        [odd_row_swap(to_b), even_swap(to_a, "row", bands), own_a, own_b],
        1,
    )
    side_a, side_b = even_swap(to_a, COLS, strips), odd_strip_swap(to_b)
    pooled, slope, wide = whole_call(
        functools.partial(layer_one, strips=strips),
        [
            shaped((2, SENT, 4 * channels)),
            shaped((band_rows, channels, 256)),
            shaped((band_rows + 2, channels, 256)),
        ],
        [x, above, below, side_a, side_b, joined_one, pool, order],
        2 * band_rows * 192 * 192 * 256,
    )
    pieces = row_swaps([pooled] * bands, bands, near_first=True)

    even = strip % 2 == 0
    ends = [side[2 * channels :].reshape(og[:edge].shape) for side in (side_a, side_b)]
    ends[1] = jnp.where((strip == 0) | (strip == strips - 1), 0, ends[1])
    before, after = jnp.where(even, ends[1], ends[0]), jnp.where(even, ends[0], ends[1])
    og = jnp.concatenate([before, og, after], 0)
    og = jnp.pad(og, ((1, PITCH - own_cols - 2 * REACH + 1), (0, 0), (0, 0)))
    og = jnp.transpose(og, (1, 0, 2))

    count = pooled_rows * PITCH
    *terms, pooled_map, grad_map = whole_call(
        functools.partial(layer_two, bands=bands),
        [shaped((72, 4 * channels))] * bands
        + [shaped((pooled_rows + 2, PITCH, 4 * channels)), shaped((pooled_rows + 2, PITCH, filters))],
        [og, taps_two] + pieces,
        4 * count * 9 * filters * 4 * channels,
        scratch=[pltpu.VMEM((bands, 72, 4 * channels), BF16)],
    )
    received = row_swaps(terms, bands)

    half = 9 * filters // 2
    keep_two, send_two = whole_call(
        filter_two_grads,
        [shaped((half, 4 * channels))] * 2,
        [pooled_map, grad_map],
        2 * count * 9 * filters * 4 * channels,
        scratch=[pltpu.VMEM((2 * half, 4 * channels), BF16)],
    )
    g, up_a, up_b, keep, send = whole_call(
        functools.partial(grad_pre_one, bands=bands),
        [shaped((band_rows, channels, 256))]
        + [shaped((channels, 256))] * 2
        + [shaped((half + HALF_ONE, 256))] * 2,
        received + [slope, wide, pool_back, order, keep_two, send_two],
        2 * 8 * 192 * 192 * 256,
        scratch=[pltpu.VMEM((144, 256), F32)],
    )
    two, one, joined = whole_call(
        add_halves,
        [shaped((half, 256)), shaped((HALF_ONE, 256)), shaped((channels + HALF_ONE, 256))],
        [keep, even_swap(send, "pair", 2), up_a],
        0,
    )
    columns = lax.axis_size("col")
    two, two_more = sum_but_last(two, "col", columns)
    ones = row_swaps([one, joined] + [one] * (bands - 2), bands, near_first=True, by_half=True)
    near = ones[row_order(bands, near_first=True, by_half=True).index(1)]
    up_b = odd_row_swap(up_b)
    (one,) = whole_call(sum_rows, [shaped(one.shape)], ones + [up_b], 0, after=1)
    input_grad, done = whole_call(
        functools.partial(layer_one_back, bands=bands),
        [shaped(features_in.shape), shaped((8, 128), F32)],
        [g, near, up_b, back_one],
        2 * band_rows * 192 * 192 * 256,
    )
    mine_two = added(two, two_more, one)
    grad_two, wrote = whole_call(
        functools.partial(finish_two, scale=1.0 / math.sqrt(pooled_rows * total)),
        [shaped((2 * half, 256), F32), shaped((8, 128), F32)],
        [mine_two, even_swap(mine_two, "pair", 2)],
        10**8,
        scratch=[pltpu.VMEM((2, half, 256), F32), pltpu.SemaphoreType.DMA((2,))],
        out_spaces=[pl.ANY, pltpu.VMEM],
    )
    one, across = sum_but_last(one, "col", columns)
    beside_one = even_swap(one, "pair", 2)
    corner = corner_swap(one, columns // 2)
    (grad_one,) = whole_call(
        functools.partial(finish_one, scale=1.0 / math.sqrt(height * width)),
        [shaped((3, 3 * channels, channels), F32)],
        [one, beside_one, corner, across, wrote, done],
        1,
        scratch=[pltpu.VMEM((144, 256), F32)],
        after=2,
    )
    grad_two = jnp.transpose(grad_two.reshape(3, 3, filters, 4 * channels), (2, 0, 1, 3))
    grad_one = jnp.transpose(grad_one.reshape(3, 3, channels, channels), (2, 0, 1, 3))
    return (input_grad, grad_one, grad_two)


def solution(mesh):
    in_specs = (
        P("grp", "row", ("col", "pair")),
        P(),
        P("row", None, None, None),
        P(("grp", "row"), ("col", "pair"), None),
    )
    out_specs = (
        P("grp", "row", ("col", "pair")),
        P("grp", None, None, None),
        P(("grp", "row"), None, None, None),
    )
    return jax.shard_map(local, mesh=mesh, in_specs=in_specs, out_specs=out_specs, check_vma=False)
```

```python
import functools
import math

import jax
import jax.numpy as jnp
from jax import lax
from jax.experimental import pallas as pl
from jax.experimental.pallas import tpu as pltpu
from jax.sharding import PartitionSpec as P

BF16 = jnp.bfloat16
F32 = jnp.float32
COLS = ("col", "pair")
REACH = 3
HALF_ONE = 72
PITCH = 48
SENT = 40


def dot(a, b, contract):
    return lax.dot_general(a, b, ((contract[:1], contract[1:]), ((), ())), preferred_element_type=F32)


def whole_call(body, outs, operands, flops, scratch=(), after=0, out_spaces=None):
    specs = [
        pl.BlockSpec(memory_space=pltpu.VMEM) for _ in range(len(operands) - after)
    ] + [pl.BlockSpec(memory_space=pl.ANY)] * after
    sizes = [math.prod(a.shape) * a.dtype.itemsize for a in tuple(operands) + tuple(outs)]
    moved = sum(sizes) if flops else 0
    return pl.pallas_call(
        body,
        out_shape=outs,
        in_specs=specs,
        out_specs=[pl.BlockSpec(memory_space=space) for space in out_spaces or [pltpu.VMEM] * len(outs)],
        scratch_shapes=list(scratch),
        cost_estimate=pl.CostEstimate(flops=flops, bytes_accessed=moved, transcendentals=0),
        compiler_params=pltpu.CompilerParams(vmem_limit_bytes=40 * 1024 * 1024),
    )(*operands)


def strip_index():
    return lax.axis_index("col") * lax.axis_size("pair") + lax.axis_index("pair")


def shaped(shape, dtype=BF16):
    return jax.ShapeDtypeStruct(shape, dtype)


def roll(values, amount, axis):
    return pltpu.roll(values, amount % values.shape[axis], axis)


def sigmoid(values):
    return 0.5 + 0.5 * jnp.tanh(0.5 * values)


def slope_of(values, sig):
    return sig * (1.0 + values * (1.0 - sig))


def pool_matrix(strip, total, back=False):
    row = lax.broadcasted_iota(jnp.int32, (2 * PITCH, 256), 0)
    lane = lax.broadcasted_iota(jnp.int32, (2 * PITCH, 256), 1)
    half = (row >= PITCH).astype(jnp.int32)
    n = row - half * PITCH
    if back:
        v, most = jnp.where((n == 32) & (half == 1), -1, n), 33
    else:
        v, most = n - REACH, 32 + 2 * REACH
    near = jnp.bitwise_and(lane - 4 * v - 2 * half, 255) < 2
    place = strip * 32 + v
    keep = near & (n < most) & (place >= 0) & (place < total)
    return jnp.where(keep, 0.25, 0.0).astype(BF16)


def order_matrix():
    row = lax.broadcasted_iota(jnp.int32, (256, 256), 0)
    lane = lax.broadcasted_iota(jnp.int32, (256, 256), 1)
    j, i, c = row >> 7, (row >> 6) & 1, row & 63
    return jnp.where(lane == 4 * c + 2 * i + j, 1.0, 0.0).astype(BF16)


def constants(w_ref, joined_ref, back_w_ref, pool_ref, back_ref, order_ref, *, total):
    turned = [w_ref[2 - i].astype(F32).T for i in range(3)]
    back_w_ref[...] = jnp.concatenate(
        [jnp.concatenate([t[:, 64 * j : 64 * j + 64] for t in turned], 1) for j in range(3)], 0
    ).astype(BF16)
    joined_ref[...] = jnp.concatenate([w_ref[0], w_ref[1], w_ref[2]], axis=1)
    pool_ref[...] = pool_matrix(strip_index(), total)
    back_ref[...] = pool_matrix(strip_index(), total, back=True)
    order_ref[...] = order_matrix()


def beside(a_ref, b_ref, place, count):
    even = (place & 1) == 0
    a = a_ref[...].astype(F32)
    b = jnp.where((place > 0) & (place < count - 1), b_ref[...].astype(F32), 0.0)
    return jnp.where(even, b, a).astype(BF16), jnp.where(even, a, b).astype(BF16)


def pack_row(row, r, slot, head, tail):
    turned = roll(row.astype(F32), 16 * r, 1)
    return jnp.where(slot == r, turned, head), jnp.where(slot == (r - 1) % 8, turned, tail)


def pack_own(x_ref, head_ref, tail_ref, a_ref, b_ref):
    even = (strip_index() & 1) == 0
    slot = lax.broadcasted_iota(jnp.int32, (64, 128), 1) >> 4
    head = tail = jnp.zeros((64, 128), F32)
    for r in range(x_ref.shape[0]):
        head, tail = pack_row(x_ref[r], r, slot, head, tail)
    a_ref[:64] = jnp.where(even, tail, head).astype(BF16)
    b_ref[:64] = jnp.where(even, head, tail).astype(BF16)
    first, last = head_ref[...].astype(F32), tail_ref[...].astype(F32)
    a_ref[64:] = jnp.where(even, last, first).astype(BF16)
    b_ref[64:] = jnp.where(even, first, last).astype(BF16)


def pack_borders(up_b_ref, up_a_ref, own_a_ref, own_b_ref, a_ref, b_ref, above_ref, below_ref, *, bands):
    even = (strip_index() & 1) == 0
    above_ref[...], below_ref[...] = beside(up_a_ref, up_b_ref, lax.axis_index("row"), bands)
    slot = lax.broadcasted_iota(jnp.int32, (64, 128), 1) >> 4
    head = tail = jnp.zeros((64, 128), F32)
    for r, ref in enumerate((above_ref, below_ref)):
        head, tail = pack_row(ref[...], r, slot, head, tail)
    a_ref[:64] = jnp.where(even, tail, head).astype(BF16)
    b_ref[:64] = jnp.where(even, head, tail).astype(BF16)
    a_ref[64:] = own_a_ref[...]
    b_ref[64:] = own_b_ref[...]


def layer_one(
    x_ref,
    above_ref,
    below_ref,
    a_ref,
    b_ref,
    w_ref,
    pool_ref,
    order_ref,
    pooled_ref,
    slope_ref,
    wide_ref,
    *,
    strips,
):
    strip = strip_index()
    band_rows = x_ref.shape[0]
    slot = lax.broadcasted_iota(jnp.int32, (128, 128), 1) >> 4
    inner = (strip > 0) & (strip < strips - 1)
    sides = a_ref[:128].astype(F32), jnp.where(inner, b_ref[:128].astype(F32), 0.0)
    from_a = ((slot ^ strip) & 1) == 0
    packed = jnp.where(from_a, *sides), jnp.where(from_a, *sides[::-1])
    for r in range(band_rows):
        wide_ref[1 + r, :, 128:] = roll(packed[r % 2][64:], -16 * r, 1).astype(BF16)
    for r, place in enumerate((0, band_rows + 1)):
        wide_ref[place, :, 128:] = roll(packed[r][:64], -16 * r, 1).astype(BF16)
    wide_ref[0, :, :128] = above_ref[...]
    wide_ref[1 : band_rows + 1, :, :128] = x_ref[...]
    wide_ref[band_rows + 1, :, :128] = below_ref[...]
    weights = w_ref[...]
    rows = slope_ref.shape[0]
    halves, held = [], None
    for h in range(rows):
        y = dot(weights, wide_ref[h : h + 3].reshape(192, 256), (1, 0))
        pre = roll(y[:64], 1, 1) + y[64:128] + roll(y[128:], -1, 1)
        sig = sigmoid(pre)
        slope_ref[h] = slope_of(pre, sig).astype(BF16)
        active = pre * sig
        if h % 2:
            halves.append((held + active).astype(BF16))
        else:
            held = active
    pooled = dot(pool_ref[...], jnp.concatenate(halves, 0), (1, 1))
    stacked = jnp.concatenate(
        [
            jnp.concatenate(
                [pooled[:PITCH, u * 128 : u * 128 + 128], pooled[PITCH:, u * 128 : u * 128 + 128]], 1
            )
            for u in range(2)
        ],
        0,
    ).astype(BF16)
    ordered = dot(stacked, order_ref[...], (1, 0)).astype(BF16)
    for u in range(2):
        pooled_ref[u] = ordered[u * PITCH : u * PITCH + SENT]


def layer_two(og_ref, w_ref, *refs, bands):
    pieces, refs = refs[:bands], refs[bands:]
    terms, refs = refs[:bands], refs[bands:]
    map_ref, grad_ref, pack_ref = refs
    band = lax.axis_index("row")
    rows, _, filters = og_ref.shape
    count = rows * PITCH
    map_ref[0] = jnp.zeros((PITCH, 256), BF16)
    map_ref[rows + 1] = jnp.zeros((PITCH, 256), BF16)
    blank = jnp.zeros((PITCH - SENT, 256), BF16)
    for k, piece in zip(row_order(bands, near_first=True), pieces):
        for t in range(2):
            map_ref[1 + 2 * (band ^ k) + t] = jnp.concatenate([piece[t], blank], 0)
    near = jnp.concatenate([map_ref[i : i + rows].reshape(count, 256) for i in range(3)], 1)
    y = dot(near, jnp.concatenate([w_ref[i] for i in range(3)], 1), (1, 1))
    pre = roll(y[:, :filters], 1, 0) + y[:, filters : 2 * filters] + roll(y[:, 2 * filters :], -1, 0)
    grad = og_ref[...].reshape(count, filters).astype(F32) * slope_of(pre, sigmoid(pre))
    grad = grad.astype(BF16)
    grad_ref[0] = jnp.zeros((PITCH, filters), BF16)
    grad_ref[rows + 1] = jnp.zeros((PITCH, filters), BF16)
    grad_ref[1 : rows + 1] = grad.reshape(rows, PITCH, filters)
    near = jnp.concatenate([grad_ref[2 - i : 2 - i + rows].reshape(count, filters) for i in range(3)], 1)
    weights = [
        jnp.concatenate([w_ref[i, j * filters : (j + 1) * filters] for j in range(3)], 1) for i in range(3)
    ]
    z = dot(near, jnp.concatenate(weights, 0), (1, 0))
    spread = roll(z[:, :256], -1 - REACH, 0) + roll(z[:, 256:512], -REACH, 0) + roll(z[:, 512:], 1 - REACH, 0)
    spread = spread.reshape(rows, PITCH, 256)
    odd = (lax.broadcasted_iota(jnp.int32, (8, 256), 1) & 1) == 1
    row = lax.broadcasted_iota(jnp.int32, (8, 256), 0)
    ends = [jnp.where(odd, spread[u - 1, 47:48], spread[u, 32:33]) for u in range(rows)]
    for p in range(rows // 2):
        shared = jnp.where(row == 0, ends[2 * p], jnp.where(row == 1, ends[2 * p + 1], 0.0))
        pack_ref[p] = jnp.concatenate([spread[2 * p, :32], shared, spread[2 * p + 1, :32]], 0).astype(BF16)
    for k in range(bands):
        terms[k][...] = pack_ref[band ^ k]


def filter_two_grads(map_ref, grad_ref, keep_ref, send_ref, all_ref):
    pair = lax.axis_index("pair")
    rows = map_ref.shape[0] - 2
    filters = grad_ref.shape[2]
    v = lax.broadcasted_iota(jnp.int32, (rows, PITCH, filters), 1)
    own = (v >= REACH) & (v < REACH + 32)
    wide = jnp.where(own, grad_ref[1 : rows + 1].astype(F32), 0.0).reshape(rows * PITCH, filters)
    cat = jnp.concatenate([roll(wide, -1, 0), wide, roll(wide, 1, 0)], 1).astype(BF16)
    taps = 3 * filters
    for i in range(3):
        part = dot(cat, map_ref[i : i + rows].reshape(rows * PITCH, 256), (0, 0))
        all_ref[i * taps : (i + 1) * taps] = part.astype(BF16)
    half = keep_ref.shape[0]
    keep_ref[...] = all_ref[pl.ds(pl.multiple_of(pair * half, 16), half)]
    send_ref[...] = all_ref[pl.ds(pl.multiple_of((1 - pair) * half, 16), half)]


def add_after(a_ref, b_ref, *refs):
    refs[-1][...] = (a_ref[...].astype(F32) + b_ref[...].astype(F32)).astype(BF16)


def add_halves(a_ref, b_ref, border_ref, two_ref, one_ref, joined_ref):
    half, border = two_ref.shape[0], border_ref.shape[0]
    total = (a_ref[...].astype(F32) + b_ref[...].astype(F32)).astype(BF16)
    two_ref[...] = total[:half]
    one_ref[...] = total[half:]
    joined_ref[:border] = border_ref[...]
    joined_ref[border:] = total[half:]


def sum_rows(*refs):
    *refs, _, out_ref = refs
    rows = out_ref.shape[0]
    terms = dict(zip(row_order(len(refs), near_first=True, by_half=True), (ref[-rows:].astype(F32) for ref in refs)))
    terms = [terms[k] for k in range(len(refs))]
    while len(terms) > 1:
        terms = [a + b for a, b in zip(terms[::2], terms[1::2])]
    out_ref[...] = terms[0].astype(BF16)


def grad_pre_one(*refs, bands):
    terms, refs = refs[:bands], refs[bands:]
    slope_ref, wide_ref, pool_ref, order_ref, keep_two_ref, send_two_ref, *refs = refs
    g_ref, a_ref, b_ref, keep_ref, send_ref, part_ref = refs
    pair = lax.axis_index("pair")
    summed = terms[0][...].astype(F32)
    for k in range(1, bands):
        summed = summed + terms[k][...].astype(F32)
    blank = jnp.zeros((8, 256), F32)
    ends = summed[32:40]
    blocks = [summed[:32], ends, blank, summed[40:], roll(ends, -1, 0), blank]
    ordered = dot(jnp.concatenate(blocks, 0).astype(BF16), order_ref[...], (1, 1)).astype(BF16)
    pool = pool_ref[...]
    cats = []
    own = lax.broadcasted_iota(jnp.int32, (64, 256), 1) < 128
    for u in range(2):
        block = ordered[u * PITCH : (u + 1) * PITCH]
        up = dot(jnp.concatenate([block[:, :128], block[:, 128:]], 0), pool, (0, 0))
        for i in range(4):
            h = 4 * u + i
            g = (up[64 * (i // 2) : 64 * (i // 2) + 64] * slope_ref[h].astype(F32)).astype(BF16)
            g_ref[h] = g
            mine = jnp.where(own, g.astype(F32), 0.0)
            cats.append(jnp.concatenate([roll(mine, -1, 1), mine, roll(mine, 1, 1)], 0).astype(BF16))
    around = jnp.concatenate([wide_ref[h : h + 3].reshape(192, 256) for h in range(8)], 1)
    acc = dot(jnp.concatenate(cats, 1), around, (1, 1))
    even = (lax.axis_index("row") & 1) == 0
    first, last = g_ref[0].astype(F32), g_ref[7].astype(F32)
    a_ref[...] = jnp.where(even, last, first).astype(BF16)
    b_ref[...] = jnp.where(even, first, last).astype(BF16)
    part_ref[:96] = jnp.concatenate([acc[:96, :128], acc[96:, :128]], 1)
    part_ref[96:] = jnp.concatenate([acc[48 * q : 48 * q + 48, 128:] for q in range(4)], 1)
    half = keep_two_ref.shape[0]
    for ref, two_ref, place in ((keep_ref, keep_two_ref, pair), (send_ref, send_two_ref, 1 - pair)):
        ref[:half] = two_ref[...]
        ref[half:] = part_ref[pl.ds(pl.multiple_of(place * HALF_ONE, 8), HALF_ONE)].astype(BF16)


def last_outputs(
    g_ref, a_ref, b_ref, w_ref, mine_ref, other_ref, out_ref, two_hbm, done_ref, two_ref, sems, *, bands, scale
):
    pair, half = lax.axis_index("pair"), mine_ref.shape[0]
    copies = []
    for n, (ref, place) in enumerate(((mine_ref, pair), (other_ref, 1 - pair))):
        target = pl.ds(pl.multiple_of(place * half, 16), half)
        two_ref[n] = ref[...].astype(F32) * scale
        copies.append(pltpu.make_async_copy(two_ref.at[n], two_hbm.at[target], sems.at[n]))
        copies[-1].start()
    above, below = beside(a_ref.at[: b_ref.shape[0]], b_ref, lax.axis_index("row"), bands)
    done_ref[...] = jnp.zeros(done_ref.shape, F32)
    lines = [above] + [g_ref[h] for h in range(8)] + [below]
    rows = []
    for h in range(8):
        z = dot(w_ref[...], jnp.concatenate(lines[h : h + 3], 0), (1, 0))
        rows.append((roll(z[:64], -1, 1) + z[64:128] + roll(z[128:], 1, 1))[:, :128])
    out_ref[...] = jnp.swapaxes(jnp.stack(rows, 0), 0, 1).astype(BF16)
    for copy in copies:
        copy.wait()


def finish_one(mine_ref, beside_ref, corner_ref, across_ref, _, out_ref, flat_ref, *, scale):
    pair = lax.axis_index("pair")
    for refs, place in (((mine_ref, across_ref), pair), ((beside_ref, corner_ref), 1 - pair)):
        total = refs[0][...].astype(F32) + refs[1][...].astype(F32)
        flat_ref[pl.ds(pl.multiple_of(place * HALF_ONE, 8), HALF_ONE)] = total * scale
    out_ref[0, :96] = flat_ref[:96, :64]
    out_ref[1, :96] = flat_ref[:96, 64:128]
    out_ref[0, 96:] = flat_ref[:96, 128:192]
    out_ref[1, 96:] = flat_ref[:96, 192:]
    for q in range(4):
        out_ref[2, 48 * q : 48 * q + 48] = flat_ref[96:, 64 * q : 64 * q + 64]


def even_swap(values, axis, count):
    return lax.ppermute(values, axis, [(n, n ^ 1) for n in range(count)])


def odd_partner(place):
    return place - 1 if place % 2 == 0 else place + 1


def odd_row_swap(values):
    bands, cores = lax.axis_size("row"), lax.axis_size("pair")
    steps = []
    for n in range(bands):
        for p in range(cores):
            to = (n, p ^ 1) if n in (0, bands - 1) else (odd_partner(n), p)
            steps.append((n * cores + p, to[0] * cores + to[1]))
    return lax.ppermute(values, ("row", "pair"), steps)


def odd_strip_swap(values):
    groups, strips = lax.axis_size("grp"), lax.axis_size(COLS)
    steps = []
    for g in range(groups):
        for n in range(strips):
            to = ((g + 1) % groups, n) if n in (0, strips - 1) else (g, odd_partner(n))
            steps.append((g * strips + n, to[0] * strips + to[1]))
    return lax.ppermute(values, ("grp",) + COLS, steps)


def xor_swap(values, axis, count, k):
    return lax.ppermute(values, axis, [(n, n ^ k) for n in range(count)])


def corner_swap(values, k):
    columns, cores = lax.axis_size("col"), lax.axis_size("pair")
    steps = [(c * cores + p, (c ^ k) * cores + (p ^ 1)) for c in range(columns) for p in range(cores)]
    return lax.ppermute(values, COLS, steps)


def row_order(bands, near_first=False, by_half=False):
    far_first = sorted(range(1, bands), key=lambda k: (k < bands // 2, k if by_half else -k))
    return [0] + (far_first[::-1] if near_first else far_first)


def row_swaps(values, bands, near_first=False, by_half=False):
    order = row_order(bands, near_first, by_half)
    return [values[0]] + [xor_swap(values[k], "row", bands, k) for k in order[1:]]


def added(a, b, *after):
    (total,) = whole_call(add_after, [shaped(a.shape)], [a, b, *after], 0, after=len(after))
    return total


def sum_but_last(part, axis, count):
    step = 1
    while 2 * step < count:
        part = added(part, xor_swap(part, axis, count, step))
        step *= 2
    return part, xor_swap(part, axis, count, step)


def local(features_in, filters_one, filters_two, out_grad):
    channels, band_rows, strip_cols = features_in.shape
    filters, own_cols, pooled_rows = out_grad.shape
    bands = lax.axis_size("row")
    strips = lax.axis_size(COLS)
    band = lax.axis_index("row")
    strip = lax.axis_index(COLS)
    pair = lax.axis_index("pair")
    height, width = band_rows * bands, strip_cols * strips
    total = own_cols * strips

    taps_one = jnp.transpose(filters_one, (1, 2, 0, 3)).reshape(3, 3 * channels, channels)
    taps_two = jnp.transpose(filters_two, (1, 2, 0, 3)).reshape(3, 3 * filters, 4 * channels)

    og = jnp.transpose(out_grad, (1, 2, 0))
    edge = REACH - 1
    x = jnp.transpose(features_in, (1, 0, 2))
    even = band % 2 == 0
    to_a, to_b = jnp.where(even, x[-1], x[0]), jnp.where(even, x[0], x[-1])
    head, tail = og[:edge], og[-edge:]
    joined_one, back_one, pool, pool_back, order = whole_call(
        functools.partial(constants, total=total),
        [shaped((3 * channels, 3 * channels))] * 2 + [shaped((2 * PITCH, 256))] * 2 + [shaped((256, 256))],
        [taps_one],
        10**8,
    )
    head, tail = head.reshape(-1, 128), tail.reshape(-1, 128)
    own_a, own_b = whole_call(
        pack_own, [shaped((channels + head.shape[0], 128))] * 2, [x, head, tail], 10**8
    )
    to_a, to_b, above, below = whole_call(
        functools.partial(pack_borders, bands=bands),
        [shaped((2 * channels + head.shape[0], 128))] * 2 + [shaped((channels, strip_cols))] * 2,
        [odd_row_swap(to_b), even_swap(to_a, "row", bands), own_a, own_b],
        1,
    )
    side_a, side_b = even_swap(to_a, COLS, strips), odd_strip_swap(to_b)
    pooled, slope, wide = whole_call(
        functools.partial(layer_one, strips=strips),
        [
            shaped((2, SENT, 4 * channels)),
            shaped((band_rows, channels, 256)),
            shaped((band_rows + 2, channels, 256)),
        ],
        [x, above, below, side_a, side_b, joined_one, pool, order],
        2 * band_rows * 192 * 192 * 256,
    )
    pieces = row_swaps([pooled] * bands, bands, near_first=True)

    even = strip % 2 == 0
    ends = [side[2 * channels :].reshape(og[:edge].shape) for side in (side_a, side_b)]
    ends[1] = jnp.where((strip == 0) | (strip == strips - 1), 0, ends[1])
    before, after = jnp.where(even, ends[1], ends[0]), jnp.where(even, ends[0], ends[1])
    og = jnp.concatenate([before, og, after], 0)
    og = jnp.pad(og, ((1, PITCH - own_cols - 2 * REACH + 1), (0, 0), (0, 0)))
    og = jnp.transpose(og, (1, 0, 2))

    count = pooled_rows * PITCH
    *terms, pooled_map, grad_map = whole_call(
        functools.partial(layer_two, bands=bands),
        [shaped((72, 4 * channels))] * bands
        + [shaped((pooled_rows + 2, PITCH, 4 * channels)), shaped((pooled_rows + 2, PITCH, filters))],
        [og, taps_two] + pieces,
        4 * count * 9 * filters * 4 * channels,
        scratch=[pltpu.VMEM((bands, 72, 4 * channels), BF16)],
    )
    received = row_swaps(terms, bands)

    half = 9 * filters // 2
    keep_two, send_two = whole_call(
        filter_two_grads,
        [shaped((half, 4 * channels))] * 2,
        [pooled_map, grad_map],
        2 * count * 9 * filters * 4 * channels,
        scratch=[pltpu.VMEM((2 * half, 4 * channels), BF16)],
    )
    g, up_a, up_b, keep, send = whole_call(
        functools.partial(grad_pre_one, bands=bands),
        [shaped((band_rows, channels, 256))]
        + [shaped((channels, 256))] * 2
        + [shaped((half + HALF_ONE, 256))] * 2,
        received + [slope, wide, pool_back, order, keep_two, send_two],
        2 * 8 * 192 * 192 * 256,
        scratch=[pltpu.VMEM((144, 256), F32)],
    )
    two, one, joined = whole_call(
        add_halves,
        [shaped((half, 256)), shaped((HALF_ONE, 256)), shaped((channels + HALF_ONE, 256))],
        [keep, even_swap(send, "pair", 2), up_a],
        0,
    )
    columns = lax.axis_size("col")
    two, two_more = sum_but_last(two, "col", columns)
    ones = row_swaps([one, joined] + [one] * (bands - 2), bands, near_first=True, by_half=True)
    near = ones[row_order(bands, near_first=True, by_half=True).index(1)]
    up_b = odd_row_swap(up_b)
    (one,) = whole_call(sum_rows, [shaped(one.shape)], ones + [up_b], 0, after=1)
    mine_two = added(two, two_more, one)
    input_grad, grad_two, done = whole_call(
        functools.partial(last_outputs, bands=bands, scale=1.0 / math.sqrt(pooled_rows * total)),
        [shaped(features_in.shape), shaped((2 * half, 256), F32), shaped((8, 128), F32)],
        [g, near, up_b, back_one, mine_two, even_swap(mine_two, "pair", 2)],
        2 * band_rows * 192 * 192 * 256,
        scratch=[pltpu.VMEM((2, half, 256), F32), pltpu.SemaphoreType.DMA((2,))],
        out_spaces=[pltpu.VMEM, pl.ANY, pltpu.VMEM],
    )
    one, across = sum_but_last(one, "col", columns)
    beside_one = even_swap(one, "pair", 2)
    corner = corner_swap(one, columns // 2)
    (grad_one,) = whole_call(
        functools.partial(finish_one, scale=1.0 / math.sqrt(height * width)),
        [shaped((3, 3 * channels, channels), F32)],
        [one, beside_one, corner, across, done],
        1,
        scratch=[pltpu.VMEM((144, 256), F32)],
        after=1,
    )
    grad_two = jnp.transpose(grad_two.reshape(3, 3, filters, 4 * channels), (2, 0, 1, 3))
    grad_one = jnp.transpose(grad_one.reshape(3, 3, channels, channels), (2, 0, 1, 3))
    return (input_grad, grad_one, grad_two)


def solution(mesh):
    in_specs = (
        P("grp", "row", ("col", "pair")),
        P(),
        P("row", None, None, None),
        P(("grp", "row"), ("col", "pair"), None),
    )
    out_specs = (
        P("grp", "row", ("col", "pair")),
        P("grp", None, None, None),
        P(("grp", "row"), None, None, None),
    )
    return jax.shard_map(local, mesh=mesh, in_specs=in_specs, out_specs=out_specs, check_vma=False)
```

```python
import functools
import math

import jax
import jax.numpy as jnp
from jax import lax
from jax.experimental import pallas as pl
from jax.experimental.pallas import tpu as pltpu
from jax.sharding import PartitionSpec as P

BF16 = jnp.bfloat16
F32 = jnp.float32
COLS = ("col", "pair")
REACH = 3
HALF_ONE = 72
PITCH = 48
SENT = 40


def dot(a, b, contract):
    return lax.dot_general(a, b, ((contract[:1], contract[1:]), ((), ())), preferred_element_type=F32)


def whole_call(body, outs, operands, flops, scratch=(), after=0, out_spaces=None):
    specs = [
        pl.BlockSpec(memory_space=pltpu.VMEM) for _ in range(len(operands) - after)
    ] + [pl.BlockSpec(memory_space=pl.ANY)] * after
    sizes = [math.prod(a.shape) * a.dtype.itemsize for a in tuple(operands) + tuple(outs)]
    moved = sum(sizes) if flops else 0
    return pl.pallas_call(
        body,
        out_shape=outs,
        in_specs=specs,
        out_specs=[pl.BlockSpec(memory_space=space) for space in out_spaces or [pltpu.VMEM] * len(outs)],
        scratch_shapes=list(scratch),
        cost_estimate=pl.CostEstimate(flops=flops, bytes_accessed=moved, transcendentals=0),
        compiler_params=pltpu.CompilerParams(vmem_limit_bytes=40 * 1024 * 1024),
    )(*operands)


def strip_index():
    return lax.axis_index("col") * lax.axis_size("pair") + lax.axis_index("pair")


def shaped(shape, dtype=BF16):
    return jax.ShapeDtypeStruct(shape, dtype)


def roll(values, amount, axis):
    return pltpu.roll(values, amount % values.shape[axis], axis)


def sigmoid(values):
    return 0.5 + 0.5 * jnp.tanh(0.5 * values)


def slope_of(values, sig):
    return sig * (1.0 + values * (1.0 - sig))


def pool_matrix(strip, total, back=False):
    row = lax.broadcasted_iota(jnp.int32, (2 * PITCH, 256), 0)
    lane = lax.broadcasted_iota(jnp.int32, (2 * PITCH, 256), 1)
    half = (row >= PITCH).astype(jnp.int32)
    n = row - half * PITCH
    if back:
        v, most = jnp.where((n == 32) & (half == 1), -1, n), 33
    else:
        v, most = n - REACH, 32 + 2 * REACH
    near = jnp.bitwise_and(lane - 4 * v - 2 * half, 255) < 2
    place = strip * 32 + v
    keep = near & (n < most) & (place >= 0) & (place < total)
    return jnp.where(keep, 0.25, 0.0).astype(BF16)


def order_matrix():
    row = lax.broadcasted_iota(jnp.int32, (256, 256), 0)
    lane = lax.broadcasted_iota(jnp.int32, (256, 256), 1)
    j, i, c = row >> 7, (row >> 6) & 1, row & 63
    return jnp.where(lane == 4 * c + 2 * i + j, 1.0, 0.0).astype(BF16)


def constants(w_ref, joined_ref, back_w_ref, pool_ref, back_ref, order_ref, *, total):
    turned = [w_ref[2 - i].astype(F32).T for i in range(3)]
    back_w_ref[...] = jnp.concatenate(
        [jnp.concatenate([t[:, 64 * j : 64 * j + 64] for t in turned], 1) for j in range(3)], 0
    ).astype(BF16)
    joined_ref[...] = jnp.concatenate([w_ref[0], w_ref[1], w_ref[2]], axis=1)
    pool_ref[...] = pool_matrix(strip_index(), total)
    back_ref[...] = pool_matrix(strip_index(), total, back=True)
    order_ref[...] = order_matrix()


def beside(a_ref, b_ref, place, count):
    even = (place & 1) == 0
    a = a_ref[...].astype(F32)
    b = jnp.where((place > 0) & (place < count - 1), b_ref[...].astype(F32), 0.0)
    return jnp.where(even, b, a).astype(BF16), jnp.where(even, a, b).astype(BF16)


def pack_row(row, r, slot, head, tail):
    turned = roll(row.astype(F32), 16 * r, 1)
    return jnp.where(slot == r, turned, head), jnp.where(slot == (r - 1) % 8, turned, tail)


def pack_own(x_ref, head_ref, tail_ref, a_ref, b_ref):
    even = (strip_index() & 1) == 0
    slot = lax.broadcasted_iota(jnp.int32, (64, 128), 1) >> 4
    head = tail = jnp.zeros((64, 128), F32)
    for r in range(x_ref.shape[0]):
        head, tail = pack_row(x_ref[r], r, slot, head, tail)
    a_ref[:64] = jnp.where(even, tail, head).astype(BF16)
    b_ref[:64] = jnp.where(even, head, tail).astype(BF16)
    first, last = head_ref[...].astype(F32), tail_ref[...].astype(F32)
    a_ref[64:] = jnp.where(even, last, first).astype(BF16)
    b_ref[64:] = jnp.where(even, first, last).astype(BF16)


def pack_borders(up_b_ref, up_a_ref, own_a_ref, own_b_ref, a_ref, b_ref, above_ref, below_ref, *, bands):
    even = (strip_index() & 1) == 0
    above_ref[...], below_ref[...] = beside(up_a_ref, up_b_ref, lax.axis_index("row"), bands)
    slot = lax.broadcasted_iota(jnp.int32, (64, 128), 1) >> 4
    head = tail = jnp.zeros((64, 128), F32)
    for r, ref in enumerate((above_ref, below_ref)):
        head, tail = pack_row(ref[...], r, slot, head, tail)
    a_ref[:64] = jnp.where(even, tail, head).astype(BF16)
    b_ref[:64] = jnp.where(even, head, tail).astype(BF16)
    a_ref[64:] = own_a_ref[...]
    b_ref[64:] = own_b_ref[...]


def layer_one(
    x_ref,
    above_ref,
    below_ref,
    a_ref,
    b_ref,
    w_ref,
    pool_ref,
    order_ref,
    pooled_ref,
    slope_ref,
    wide_ref,
    *,
    strips,
):
    strip = strip_index()
    band_rows = x_ref.shape[0]
    slot = lax.broadcasted_iota(jnp.int32, (128, 128), 1) >> 4
    inner = (strip > 0) & (strip < strips - 1)
    sides = a_ref[:128].astype(F32), jnp.where(inner, b_ref[:128].astype(F32), 0.0)
    from_a = ((slot ^ strip) & 1) == 0
    packed = jnp.where(from_a, *sides), jnp.where(from_a, *sides[::-1])
    for r in range(band_rows):
        wide_ref[1 + r, :, 128:] = roll(packed[r % 2][64:], -16 * r, 1).astype(BF16)
    for r, place in enumerate((0, band_rows + 1)):
        wide_ref[place, :, 128:] = roll(packed[r][:64], -16 * r, 1).astype(BF16)
    wide_ref[0, :, :128] = above_ref[...]
    wide_ref[1 : band_rows + 1, :, :128] = x_ref[...]
    wide_ref[band_rows + 1, :, :128] = below_ref[...]
    weights = w_ref[...]
    rows = slope_ref.shape[0]
    halves, held = [], None
    for h in range(rows):
        y = dot(weights, wide_ref[h : h + 3].reshape(192, 256), (1, 0))
        pre = roll(y[:64], 1, 1) + y[64:128] + roll(y[128:], -1, 1)
        sig = sigmoid(pre)
        slope_ref[h] = slope_of(pre, sig).astype(BF16)
        active = pre * sig
        if h % 2:
            halves.append((held + active).astype(BF16))
        else:
            held = active
    pooled = dot(pool_ref[...], jnp.concatenate(halves, 0), (1, 1))
    stacked = jnp.concatenate(
        [
            jnp.concatenate(
                [pooled[:PITCH, u * 128 : u * 128 + 128], pooled[PITCH:, u * 128 : u * 128 + 128]], 1
            )
            for u in range(2)
        ],
        0,
    ).astype(BF16)
    ordered = dot(stacked, order_ref[...], (1, 0)).astype(BF16)
    for u in range(2):
        pooled_ref[u] = ordered[u * PITCH : u * PITCH + SENT]


def layer_two(og_ref, w_ref, *refs, bands):
    pieces, refs = refs[:bands], refs[bands:]
    terms, refs = refs[:bands], refs[bands:]
    map_ref, grad_ref, pack_ref = refs
    band = lax.axis_index("row")
    rows, _, filters = og_ref.shape
    count = rows * PITCH
    map_ref[0] = jnp.zeros((PITCH, 256), BF16)
    map_ref[rows + 1] = jnp.zeros((PITCH, 256), BF16)
    blank = jnp.zeros((PITCH - SENT, 256), BF16)
    for k, piece in zip(row_order(bands, near_first=True), pieces):
        for t in range(2):
            map_ref[1 + 2 * (band ^ k) + t] = jnp.concatenate([piece[t], blank], 0)
    near = jnp.concatenate([map_ref[i : i + rows].reshape(count, 256) for i in range(3)], 1)
    y = dot(near, jnp.concatenate([w_ref[i] for i in range(3)], 1), (1, 1))
    pre = roll(y[:, :filters], 1, 0) + y[:, filters : 2 * filters] + roll(y[:, 2 * filters :], -1, 0)
    grad = og_ref[...].reshape(count, filters).astype(F32) * slope_of(pre, sigmoid(pre))
    grad = grad.astype(BF16)
    grad_ref[0] = jnp.zeros((PITCH, filters), BF16)
    grad_ref[rows + 1] = jnp.zeros((PITCH, filters), BF16)
    grad_ref[1 : rows + 1] = grad.reshape(rows, PITCH, filters)
    near = jnp.concatenate([grad_ref[2 - i : 2 - i + rows].reshape(count, filters) for i in range(3)], 1)
    weights = [
        jnp.concatenate([w_ref[i, j * filters : (j + 1) * filters] for j in range(3)], 1) for i in range(3)
    ]
    z = dot(near, jnp.concatenate(weights, 0), (1, 0))
    spread = roll(z[:, :256], -1 - REACH, 0) + roll(z[:, 256:512], -REACH, 0) + roll(z[:, 512:], 1 - REACH, 0)
    spread = spread.reshape(rows, PITCH, 256)
    odd = (lax.broadcasted_iota(jnp.int32, (8, 256), 1) & 1) == 1
    row = lax.broadcasted_iota(jnp.int32, (8, 256), 0)
    ends = [jnp.where(odd, spread[u - 1, 47:48], spread[u, 32:33]) for u in range(rows)]
    for p in range(rows // 2):
        shared = jnp.where(row == 0, ends[2 * p], jnp.where(row == 1, ends[2 * p + 1], 0.0))
        pack_ref[p] = jnp.concatenate([spread[2 * p, :32], shared, spread[2 * p + 1, :32]], 0).astype(BF16)
    for k in range(bands):
        terms[k][...] = pack_ref[band ^ k]


def filter_two_grads(map_ref, grad_ref, keep_ref, send_ref, all_ref):
    pair = lax.axis_index("pair")
    rows = map_ref.shape[0] - 2
    filters = grad_ref.shape[2]
    v = lax.broadcasted_iota(jnp.int32, (rows, PITCH, filters), 1)
    own = (v >= REACH) & (v < REACH + 32)
    wide = jnp.where(own, grad_ref[1 : rows + 1].astype(F32), 0.0).reshape(rows * PITCH, filters)
    cat = jnp.concatenate([roll(wide, -1, 0), wide, roll(wide, 1, 0)], 1).astype(BF16)
    taps = 3 * filters
    for i in range(3):
        part = dot(cat, map_ref[i : i + rows].reshape(rows * PITCH, 256), (0, 0))
        all_ref[i * taps : (i + 1) * taps] = part.astype(BF16)
    half = keep_ref.shape[0]
    keep_ref[...] = all_ref[pl.ds(pl.multiple_of(pair * half, 16), half)]
    send_ref[...] = all_ref[pl.ds(pl.multiple_of((1 - pair) * half, 16), half)]


def add_after(a_ref, b_ref, *refs):
    refs[-1][...] = (a_ref[...].astype(F32) + b_ref[...].astype(F32)).astype(BF16)


def add_halves(a_ref, b_ref, border_ref, two_ref, one_ref, joined_ref):
    half, border = two_ref.shape[0], border_ref.shape[0]
    total = (a_ref[...].astype(F32) + b_ref[...].astype(F32)).astype(BF16)
    two_ref[...] = total[:half]
    one_ref[...] = total[half:]
    joined_ref[:border] = border_ref[...]
    joined_ref[border:] = total[half:]


def sum_rows(*refs):
    *refs, _, out_ref = refs
    rows = out_ref.shape[0]
    terms = dict(zip(row_order(len(refs), near_first=True, by_half=True), (ref[-rows:].astype(F32) for ref in refs)))
    terms = [terms[k] for k in range(len(refs))]
    while len(terms) > 1:
        terms = [a + b for a, b in zip(terms[::2], terms[1::2])]
    out_ref[...] = terms[0].astype(BF16)


def grad_pre_one(*refs, bands):
    terms, refs = refs[:bands], refs[bands:]
    slope_ref, wide_ref, pool_ref, order_ref, keep_two_ref, send_two_ref, *refs = refs
    g_ref, a_ref, b_ref, keep_ref, send_ref, part_ref = refs
    pair = lax.axis_index("pair")
    summed = terms[0][...].astype(F32)
    for k in range(1, bands):
        summed = summed + terms[k][...].astype(F32)
    blank = jnp.zeros((8, 256), F32)
    ends = summed[32:40]
    blocks = [summed[:32], ends, blank, summed[40:], roll(ends, -1, 0), blank]
    ordered = dot(jnp.concatenate(blocks, 0).astype(BF16), order_ref[...], (1, 1)).astype(BF16)
    pool = pool_ref[...]
    cats = []
    own = lax.broadcasted_iota(jnp.int32, (64, 256), 1) < 128
    for u in range(2):
        block = ordered[u * PITCH : (u + 1) * PITCH]
        up = dot(jnp.concatenate([block[:, :128], block[:, 128:]], 0), pool, (0, 0))
        for i in range(4):
            h = 4 * u + i
            g = (up[64 * (i // 2) : 64 * (i // 2) + 64] * slope_ref[h].astype(F32)).astype(BF16)
            g_ref[h] = g
            mine = jnp.where(own, g.astype(F32), 0.0)
            cats.append(jnp.concatenate([roll(mine, -1, 1), mine, roll(mine, 1, 1)], 0).astype(BF16))
    around = jnp.concatenate([wide_ref[h : h + 3].reshape(192, 256) for h in range(8)], 1)
    acc = dot(jnp.concatenate(cats, 1), around, (1, 1))
    even = (lax.axis_index("row") & 1) == 0
    first, last = g_ref[0].astype(F32), g_ref[7].astype(F32)
    a_ref[...] = jnp.where(even, last, first).astype(BF16)
    b_ref[...] = jnp.where(even, first, last).astype(BF16)
    part_ref[:96] = jnp.concatenate([acc[:96, :128], acc[96:, :128]], 1)
    part_ref[96:] = jnp.concatenate([acc[48 * q : 48 * q + 48, 128:] for q in range(4)], 1)
    half = keep_two_ref.shape[0]
    for ref, two_ref, place in ((keep_ref, keep_two_ref, pair), (send_ref, send_two_ref, 1 - pair)):
        ref[:half] = two_ref[...]
        ref[half:] = part_ref[pl.ds(pl.multiple_of(place * HALF_ONE, 8), HALF_ONE)].astype(BF16)


def layer_one_back(g_ref, a_ref, b_ref, w_ref, out_ref, done_ref, *, bands):
    above, below = beside(a_ref.at[: b_ref.shape[0]], b_ref, lax.axis_index("row"), bands)
    done_ref[...] = jnp.zeros(done_ref.shape, F32)
    lines = [above] + [g_ref[h] for h in range(8)] + [below]
    rows = []
    for h in range(8):
        z = dot(w_ref[...], jnp.concatenate(lines[h : h + 3], 0), (1, 0))
        rows.append((roll(z[:64], -1, 1) + z[64:128] + roll(z[128:], 1, 1))[:, :128])
    out_ref[...] = jnp.swapaxes(jnp.stack(rows, 0), 0, 1).astype(BF16)


def finish_two(mine_ref, other_ref, two_hbm, done_ref, two_ref, sems, *, scale):
    pair, half = lax.axis_index("pair"), mine_ref.shape[0]
    done_ref[...] = jnp.zeros(done_ref.shape, F32)
    copies = []
    for n, (ref, place) in enumerate(((mine_ref, pair), (other_ref, 1 - pair))):
        rows = pl.ds(pl.multiple_of(place * half, 16), half)
        two_ref[n] = ref[...].astype(F32) * scale
        copies.append(pltpu.make_async_copy(two_ref.at[n], two_hbm.at[rows], sems.at[n]))
        copies[-1].start()
    for copy in copies:
        copy.wait()


def finish_one(mine_ref, beside_ref, corner_ref, across_ref, _, __, out_ref, flat_ref, *, scale):
    pair = lax.axis_index("pair")
    for refs, place in (((mine_ref, across_ref), pair), ((beside_ref, corner_ref), 1 - pair)):
        total = refs[0][...].astype(F32) + refs[1][...].astype(F32)
        flat_ref[pl.ds(pl.multiple_of(place * HALF_ONE, 8), HALF_ONE)] = total * scale
    out_ref[0, :96] = flat_ref[:96, :64]
    out_ref[1, :96] = flat_ref[:96, 64:128]
    out_ref[0, 96:] = flat_ref[:96, 128:192]
    out_ref[1, 96:] = flat_ref[:96, 192:]
    for q in range(4):
        out_ref[2, 48 * q : 48 * q + 48] = flat_ref[96:, 64 * q : 64 * q + 64]


def even_swap(values, axis, count):
    return lax.ppermute(values, axis, [(n, n ^ 1) for n in range(count)])


def odd_partner(place):
    return place - 1 if place % 2 == 0 else place + 1


def odd_row_swap(values):
    bands, cores = lax.axis_size("row"), lax.axis_size("pair")
    steps = []
    for n in range(bands):
        for p in range(cores):
            to = (n, p ^ 1) if n in (0, bands - 1) else (odd_partner(n), p)
            steps.append((n * cores + p, to[0] * cores + to[1]))
    return lax.ppermute(values, ("row", "pair"), steps)


def odd_strip_swap(values):
    groups, strips = lax.axis_size("grp"), lax.axis_size(COLS)
    steps = []
    for g in range(groups):
        for n in range(strips):
            to = ((g + 1) % groups, n) if n in (0, strips - 1) else (g, odd_partner(n))
            steps.append((g * strips + n, to[0] * strips + to[1]))
    return lax.ppermute(values, ("grp",) + COLS, steps)


def xor_swap(values, axis, count, k):
    return lax.ppermute(values, axis, [(n, n ^ k) for n in range(count)])


def corner_swap(values, k):
    columns, cores = lax.axis_size("col"), lax.axis_size("pair")
    steps = [(c * cores + p, (c ^ k) * cores + (p ^ 1)) for c in range(columns) for p in range(cores)]
    return lax.ppermute(values, COLS, steps)


def row_order(bands, near_first=False, by_half=False):
    far_first = sorted(range(1, bands), key=lambda k: (k < bands // 2, k if by_half else -k))
    return [0] + (far_first[::-1] if near_first else far_first)


def row_swaps(values, bands, near_first=False, by_half=False):
    order = row_order(bands, near_first, by_half)
    return [values[0]] + [xor_swap(values[k], "row", bands, k) for k in order[1:]]


def added(a, b, *after):
    (total,) = whole_call(add_after, [shaped(a.shape)], [a, b, *after], 0, after=len(after))
    return total


def sum_but_last(part, axis, count):
    step = 1
    while 2 * step < count:
        part = added(part, xor_swap(part, axis, count, step))
        step *= 2
    return part, xor_swap(part, axis, count, step)


def local(features_in, filters_one, filters_two, out_grad):
    channels, band_rows, strip_cols = features_in.shape
    filters, own_cols, pooled_rows = out_grad.shape
    bands = lax.axis_size("row")
    strips = lax.axis_size(COLS)
    band = lax.axis_index("row")
    strip = lax.axis_index(COLS)
    pair = lax.axis_index("pair")
    height, width = band_rows * bands, strip_cols * strips
    total = own_cols * strips

    taps_one = jnp.transpose(filters_one, (1, 2, 0, 3)).reshape(3, 3 * channels, channels)
    taps_two = jnp.transpose(filters_two, (1, 2, 0, 3)).reshape(3, 3 * filters, 4 * channels)

    og = jnp.transpose(out_grad, (1, 2, 0))
    edge = REACH - 1
    x = jnp.transpose(features_in, (1, 0, 2))
    even = band % 2 == 0
    to_a, to_b = jnp.where(even, x[-1], x[0]), jnp.where(even, x[0], x[-1])
    head, tail = og[:edge], og[-edge:]
    joined_one, back_one, pool, pool_back, order = whole_call(
        functools.partial(constants, total=total),
        [shaped((3 * channels, 3 * channels))] * 2 + [shaped((2 * PITCH, 256))] * 2 + [shaped((256, 256))],
        [taps_one],
        10**8,
    )
    head, tail = head.reshape(-1, 128), tail.reshape(-1, 128)
    own_a, own_b = whole_call(
        pack_own, [shaped((channels + head.shape[0], 128))] * 2, [x, head, tail], 10**8
    )
    to_a, to_b, above, below = whole_call(
        functools.partial(pack_borders, bands=bands),
        [shaped((2 * channels + head.shape[0], 128))] * 2 + [shaped((channels, strip_cols))] * 2,
        [odd_row_swap(to_b), even_swap(to_a, "row", bands), own_a, own_b],
        1,
    )
    side_a, side_b = even_swap(to_a, COLS, strips), odd_strip_swap(to_b)
    pooled, slope, wide = whole_call(
        functools.partial(layer_one, strips=strips),
        [
            shaped((2, SENT, 4 * channels)),
            shaped((band_rows, channels, 256)),
            shaped((band_rows + 2, channels, 256)),
        ],
        [x, above, below, side_a, side_b, joined_one, pool, order],
        2 * band_rows * 192 * 192 * 256,
    )
    pieces = row_swaps([pooled] * bands, bands, near_first=True)

    even = strip % 2 == 0
    ends = [side[2 * channels :].reshape(og[:edge].shape) for side in (side_a, side_b)]
    ends[1] = jnp.where((strip == 0) | (strip == strips - 1), 0, ends[1])
    before, after = jnp.where(even, ends[1], ends[0]), jnp.where(even, ends[0], ends[1])
    og = jnp.concatenate([before, og, after], 0)
    og = jnp.pad(og, ((1, PITCH - own_cols - 2 * REACH + 1), (0, 0), (0, 0)))
    og = jnp.transpose(og, (1, 0, 2))

    count = pooled_rows * PITCH
    *terms, pooled_map, grad_map = whole_call(
        functools.partial(layer_two, bands=bands),
        [shaped((72, 4 * channels))] * bands
        + [shaped((pooled_rows + 2, PITCH, 4 * channels)), shaped((pooled_rows + 2, PITCH, filters))],
        [og, taps_two] + pieces,
        4 * count * 9 * filters * 4 * channels,
        scratch=[pltpu.VMEM((bands, 72, 4 * channels), BF16)],
    )
    received = row_swaps(terms, bands, by_half=True)

    half = 9 * filters // 2
    keep_two, send_two = whole_call(
        filter_two_grads,
        [shaped((half, 4 * channels))] * 2,
        [pooled_map, grad_map],
        2 * count * 9 * filters * 4 * channels,
        scratch=[pltpu.VMEM((2 * half, 4 * channels), BF16)],
    )
    g, up_a, up_b, keep, send = whole_call(
        functools.partial(grad_pre_one, bands=bands),
        [shaped((band_rows, channels, 256))]
        + [shaped((channels, 256))] * 2
        + [shaped((half + HALF_ONE, 256))] * 2,
        received + [slope, wide, pool_back, order, keep_two, send_two],
        2 * 8 * 192 * 192 * 256,
        scratch=[pltpu.VMEM((144, 256), F32)],
    )
    two, one, joined = whole_call(
        add_halves,
        [shaped((half, 256)), shaped((HALF_ONE, 256)), shaped((channels + HALF_ONE, 256))],
        [keep, even_swap(send, "pair", 2), up_a],
        0,
    )
    columns = lax.axis_size("col")
    two, two_more = sum_but_last(two, "col", columns)
    ones = row_swaps([one, joined] + [one] * (bands - 2), bands, near_first=True, by_half=True)
    near = ones[row_order(bands, near_first=True, by_half=True).index(1)]
    up_b = odd_row_swap(up_b)
    (one,) = whole_call(sum_rows, [shaped(one.shape)], ones + [up_b], 0, after=1)
    input_grad, done = whole_call(
        functools.partial(layer_one_back, bands=bands),
        [shaped(features_in.shape), shaped((8, 128), F32)],
        [g, near, up_b, back_one],
        2 * band_rows * 192 * 192 * 256,
    )
    mine_two = added(two, two_more, one)
    grad_two, wrote = whole_call(
        functools.partial(finish_two, scale=1.0 / math.sqrt(pooled_rows * total)),
        [shaped((2 * half, 256), F32), shaped((8, 128), F32)],
        [mine_two, even_swap(mine_two, "pair", 2)],
        10**8,
        scratch=[pltpu.VMEM((2, half, 256), F32), pltpu.SemaphoreType.DMA((2,))],
        out_spaces=[pl.ANY, pltpu.VMEM],
    )
    one, across = sum_but_last(one, "col", columns)
    beside_one = even_swap(one, "pair", 2)
    corner = corner_swap(one, columns // 2)
    (grad_one,) = whole_call(
        functools.partial(finish_one, scale=1.0 / math.sqrt(height * width)),
        [shaped((3, 3 * channels, channels), F32)],
        [one, beside_one, corner, across, wrote, done],
        1,
        scratch=[pltpu.VMEM((144, 256), F32)],
        after=2,
    )
    grad_two = jnp.transpose(grad_two.reshape(3, 3, filters, 4 * channels), (2, 0, 1, 3))
    grad_one = jnp.transpose(grad_one.reshape(3, 3, channels, channels), (2, 0, 1, 3))
    return (input_grad, grad_one, grad_two)


def solution(mesh):
    in_specs = (
        P("grp", "row", ("col", "pair")),
        P(),
        P("row", None, None, None),
        P(("grp", "row"), ("col", "pair"), None),
    )
    out_specs = (
        P("grp", "row", ("col", "pair")),
        P("grp", None, None, None),
        P(("grp", "row"), None, None, None),
    )
    return jax.shard_map(local, mesh=mesh, in_specs=in_specs, out_specs=out_specs, check_vma=False)
```

```python
import functools
import math

import jax
import jax.numpy as jnp
from jax import lax
from jax.experimental import pallas as pl
from jax.experimental.pallas import tpu as pltpu
from jax.sharding import PartitionSpec as P

BF16 = jnp.bfloat16
F32 = jnp.float32
COLS = ("col", "pair")
REACH = 3
HALF_ONE = 72
PITCH = 48
SENT = 40


def dot(a, b, contract):
    return lax.dot_general(a, b, ((contract[:1], contract[1:]), ((), ())), preferred_element_type=F32)


def whole_call(body, outs, operands, flops, scratch=(), after=0, out_spaces=None):
    specs = [
        pl.BlockSpec(memory_space=pltpu.VMEM) for _ in range(len(operands) - after)
    ] + [pl.BlockSpec(memory_space=pl.ANY)] * after
    sizes = [math.prod(a.shape) * a.dtype.itemsize for a in tuple(operands) + tuple(outs)]
    moved = sum(sizes) if flops else 0
    return pl.pallas_call(
        body,
        out_shape=outs,
        in_specs=specs,
        out_specs=[pl.BlockSpec(memory_space=space) for space in out_spaces or [pltpu.VMEM] * len(outs)],
        scratch_shapes=list(scratch),
        cost_estimate=pl.CostEstimate(flops=flops, bytes_accessed=moved, transcendentals=0),
        compiler_params=pltpu.CompilerParams(vmem_limit_bytes=40 * 1024 * 1024),
    )(*operands)


def strip_index():
    return lax.axis_index("col") * lax.axis_size("pair") + lax.axis_index("pair")


def shaped(shape, dtype=BF16):
    return jax.ShapeDtypeStruct(shape, dtype)


def roll(values, amount, axis):
    return pltpu.roll(values, amount % values.shape[axis], axis)


def sigmoid(values):
    return 0.5 + 0.5 * jnp.tanh(0.5 * values)


def slope_of(values, sig):
    return sig * (1.0 + values * (1.0 - sig))


def pool_matrix(strip, total, back=False):
    row = lax.broadcasted_iota(jnp.int32, (2 * PITCH, 256), 0)
    lane = lax.broadcasted_iota(jnp.int32, (2 * PITCH, 256), 1)
    half = (row >= PITCH).astype(jnp.int32)
    n = row - half * PITCH
    if back:
        v, most = jnp.where((n == 32) & (half == 1), -1, n), 33
    else:
        v, most = n - REACH, 32 + 2 * REACH
    near = jnp.bitwise_and(lane - 4 * v - 2 * half, 255) < 2
    place = strip * 32 + v
    keep = near & (n < most) & (place >= 0) & (place < total)
    return jnp.where(keep, 0.25, 0.0).astype(BF16)


def order_matrix():
    row = lax.broadcasted_iota(jnp.int32, (256, 256), 0)
    lane = lax.broadcasted_iota(jnp.int32, (256, 256), 1)
    j, i, c = row >> 7, (row >> 6) & 1, row & 63
    return jnp.where(lane == 4 * c + 2 * i + j, 1.0, 0.0).astype(BF16)


def constants(w_ref, joined_ref, back_w_ref, pool_ref, back_ref, order_ref, *, total):
    turned = [w_ref[2 - i].astype(F32).T for i in range(3)]
    back_w_ref[...] = jnp.concatenate(
        [jnp.concatenate([t[:, 64 * j : 64 * j + 64] for t in turned], 1) for j in range(3)], 0
    ).astype(BF16)
    joined_ref[...] = jnp.concatenate([w_ref[0], w_ref[1], w_ref[2]], axis=1)
    pool_ref[...] = pool_matrix(strip_index(), total)
    back_ref[...] = pool_matrix(strip_index(), total, back=True)
    order_ref[...] = order_matrix()


def beside(a_ref, b_ref, place, count):
    even = (place & 1) == 0
    a = a_ref[...].astype(F32)
    b = jnp.where((place > 0) & (place < count - 1), b_ref[...].astype(F32), 0.0)
    return jnp.where(even, b, a).astype(BF16), jnp.where(even, a, b).astype(BF16)


def pack_row(row, r, slot, head, tail):
    turned = roll(row.astype(F32), 16 * r, 1)
    return jnp.where(slot == r, turned, head), jnp.where(slot == (r - 1) % 8, turned, tail)


def pack_own(x_ref, head_ref, tail_ref, a_ref, b_ref):
    even = (strip_index() & 1) == 0
    slot = lax.broadcasted_iota(jnp.int32, (64, 128), 1) >> 4
    head = tail = jnp.zeros((64, 128), F32)
    for r in range(x_ref.shape[0]):
        head, tail = pack_row(x_ref[r], r, slot, head, tail)
    a_ref[:64] = jnp.where(even, tail, head).astype(BF16)
    b_ref[:64] = jnp.where(even, head, tail).astype(BF16)
    first, last = head_ref[...].astype(F32), tail_ref[...].astype(F32)
    a_ref[64:] = jnp.where(even, last, first).astype(BF16)
    b_ref[64:] = jnp.where(even, first, last).astype(BF16)


def pack_borders(up_b_ref, up_a_ref, own_a_ref, own_b_ref, a_ref, b_ref, above_ref, below_ref, *, bands):
    even = (strip_index() & 1) == 0
    above_ref[...], below_ref[...] = beside(up_a_ref, up_b_ref, lax.axis_index("row"), bands)
    slot = lax.broadcasted_iota(jnp.int32, (64, 128), 1) >> 4
    head = tail = jnp.zeros((64, 128), F32)
    for r, ref in enumerate((above_ref, below_ref)):
        head, tail = pack_row(ref[...], r, slot, head, tail)
    a_ref[:64] = jnp.where(even, tail, head).astype(BF16)
    b_ref[:64] = jnp.where(even, head, tail).astype(BF16)
    a_ref[64:] = own_a_ref[...]
    b_ref[64:] = own_b_ref[...]


def layer_one(
    x_ref,
    above_ref,
    below_ref,
    a_ref,
    b_ref,
    w_ref,
    pool_ref,
    order_ref,
    pooled_ref,
    slope_ref,
    wide_ref,
    *,
    strips,
):
    strip = strip_index()
    band_rows = x_ref.shape[0]
    slot = lax.broadcasted_iota(jnp.int32, (128, 128), 1) >> 4
    inner = (strip > 0) & (strip < strips - 1)
    sides = a_ref[:128].astype(F32), jnp.where(inner, b_ref[:128].astype(F32), 0.0)
    from_a = ((slot ^ strip) & 1) == 0
    packed = jnp.where(from_a, *sides), jnp.where(from_a, *sides[::-1])
    for r in range(band_rows):
        wide_ref[1 + r, :, 128:] = roll(packed[r % 2][64:], -16 * r, 1).astype(BF16)
    for r, place in enumerate((0, band_rows + 1)):
        wide_ref[place, :, 128:] = roll(packed[r][:64], -16 * r, 1).astype(BF16)
    wide_ref[0, :, :128] = above_ref[...]
    wide_ref[1 : band_rows + 1, :, :128] = x_ref[...]
    wide_ref[band_rows + 1, :, :128] = below_ref[...]
    weights = w_ref[...]
    rows = slope_ref.shape[0]
    halves, held = [], None
    for h in range(rows):
        y = dot(weights, wide_ref[h : h + 3].reshape(192, 256), (1, 0))
        pre = roll(y[:64], 1, 1) + y[64:128] + roll(y[128:], -1, 1)
        sig = sigmoid(pre)
        slope_ref[h] = slope_of(pre, sig).astype(BF16)
        active = pre * sig
        if h % 2:
            halves.append((held + active).astype(BF16))
        else:
            held = active
    pooled = dot(pool_ref[...], jnp.concatenate(halves, 0), (1, 1))
    stacked = jnp.concatenate(
        [
            jnp.concatenate(
                [pooled[:PITCH, u * 128 : u * 128 + 128], pooled[PITCH:, u * 128 : u * 128 + 128]], 1
            )
            for u in range(2)
        ],
        0,
    ).astype(BF16)
    ordered = dot(stacked, order_ref[...], (1, 0)).astype(BF16)
    for u in range(2):
        pooled_ref[u] = ordered[u * PITCH : u * PITCH + SENT]


def layer_two(og_ref, w_ref, *refs, bands):
    pieces, refs = refs[:bands], refs[bands:]
    terms, refs = refs[:bands], refs[bands:]
    map_ref, grad_ref, pack_ref = refs
    band = lax.axis_index("row")
    rows, _, filters = og_ref.shape
    count = rows * PITCH
    map_ref[0] = jnp.zeros((PITCH, 256), BF16)
    map_ref[rows + 1] = jnp.zeros((PITCH, 256), BF16)
    blank = jnp.zeros((PITCH - SENT, 256), BF16)
    for k, piece in zip(row_order(bands, near_first=True), pieces):
        for t in range(2):
            map_ref[1 + 2 * (band ^ k) + t] = jnp.concatenate([piece[t], blank], 0)
    near = jnp.concatenate([map_ref[i : i + rows].reshape(count, 256) for i in range(3)], 1)
    y = dot(near, jnp.concatenate([w_ref[i] for i in range(3)], 1), (1, 1))
    pre = roll(y[:, :filters], 1, 0) + y[:, filters : 2 * filters] + roll(y[:, 2 * filters :], -1, 0)
    grad = og_ref[...].reshape(count, filters).astype(F32) * slope_of(pre, sigmoid(pre))
    grad = grad.astype(BF16)
    grad_ref[0] = jnp.zeros((PITCH, filters), BF16)
    grad_ref[rows + 1] = jnp.zeros((PITCH, filters), BF16)
    grad_ref[1 : rows + 1] = grad.reshape(rows, PITCH, filters)
    near = jnp.concatenate([grad_ref[2 - i : 2 - i + rows].reshape(count, filters) for i in range(3)], 1)
    weights = [
        jnp.concatenate([w_ref[i, j * filters : (j + 1) * filters] for j in range(3)], 1) for i in range(3)
    ]
    z = dot(near, jnp.concatenate(weights, 0), (1, 0))
    spread = roll(z[:, :256], -1 - REACH, 0) + roll(z[:, 256:512], -REACH, 0) + roll(z[:, 512:], 1 - REACH, 0)
    spread = spread.reshape(rows, PITCH, 256)
    odd = (lax.broadcasted_iota(jnp.int32, (8, 256), 1) & 1) == 1
    row = lax.broadcasted_iota(jnp.int32, (8, 256), 0)
    ends = [jnp.where(odd, spread[u - 1, 47:48], spread[u, 32:33]) for u in range(rows)]
    for p in range(rows // 2):
        shared = jnp.where(row == 0, ends[2 * p], jnp.where(row == 1, ends[2 * p + 1], 0.0))
        pack_ref[p] = jnp.concatenate([spread[2 * p, :32], shared, spread[2 * p + 1, :32]], 0).astype(BF16)
    for k in range(bands):
        terms[k][...] = pack_ref[band ^ k]


def filter_two_grads(map_ref, grad_ref, keep_ref, send_ref, all_ref):
    pair = lax.axis_index("pair")
    rows = map_ref.shape[0] - 2
    filters = grad_ref.shape[2]
    v = lax.broadcasted_iota(jnp.int32, (rows, PITCH, filters), 1)
    own = (v >= REACH) & (v < REACH + 32)
    wide = jnp.where(own, grad_ref[1 : rows + 1].astype(F32), 0.0).reshape(rows * PITCH, filters)
    cat = jnp.concatenate([roll(wide, -1, 0), wide, roll(wide, 1, 0)], 1).astype(BF16)
    taps = 3 * filters
    for i in range(3):
        part = dot(cat, map_ref[i : i + rows].reshape(rows * PITCH, 256), (0, 0))
        all_ref[i * taps : (i + 1) * taps] = part.astype(BF16)
    half = keep_ref.shape[0]
    keep_ref[...] = all_ref[pl.ds(pl.multiple_of(pair * half, 16), half)]
    send_ref[...] = all_ref[pl.ds(pl.multiple_of((1 - pair) * half, 16), half)]


def add_after(a_ref, b_ref, *refs):
    refs[-1][...] = (a_ref[...].astype(F32) + b_ref[...].astype(F32)).astype(BF16)


def add_halves(a_ref, b_ref, border_ref, two_ref, one_ref, joined_ref):
    half, border = two_ref.shape[0], border_ref.shape[0]
    total = (a_ref[...].astype(F32) + b_ref[...].astype(F32)).astype(BF16)
    two_ref[...] = total[:half]
    one_ref[...] = total[half:]
    joined_ref[:border] = border_ref[...]
    joined_ref[border:] = total[half:]


def sum_rows(*refs):
    *refs, _, out_ref = refs
    rows = out_ref.shape[0]
    terms = dict(zip(row_order(len(refs), near_first=True, by_half=False), (ref[-rows:].astype(F32) for ref in refs)))
    terms = [terms[k] for k in range(len(refs))]
    while len(terms) > 1:
        terms = [a + b for a, b in zip(terms[::2], terms[1::2])]
    out_ref[...] = terms[0].astype(BF16)


def grad_pre_one(*refs, bands):
    terms, refs = refs[:bands], refs[bands:]
    slope_ref, wide_ref, pool_ref, order_ref, keep_two_ref, send_two_ref, *refs = refs
    g_ref, a_ref, b_ref, keep_ref, send_ref, part_ref = refs
    pair = lax.axis_index("pair")
    summed = terms[0][...].astype(F32)
    for k in range(1, bands):
        summed = summed + terms[k][...].astype(F32)
    blank = jnp.zeros((8, 256), F32)
    ends = summed[32:40]
    blocks = [summed[:32], ends, blank, summed[40:], roll(ends, -1, 0), blank]
    ordered = dot(jnp.concatenate(blocks, 0).astype(BF16), order_ref[...], (1, 1)).astype(BF16)
    pool = pool_ref[...]
    cats = []
    own = lax.broadcasted_iota(jnp.int32, (64, 256), 1) < 128
    for u in range(2):
        block = ordered[u * PITCH : (u + 1) * PITCH]
        up = dot(jnp.concatenate([block[:, :128], block[:, 128:]], 0), pool, (0, 0))
        for i in range(4):
            h = 4 * u + i
            g = (up[64 * (i // 2) : 64 * (i // 2) + 64] * slope_ref[h].astype(F32)).astype(BF16)
            g_ref[h] = g
            mine = jnp.where(own, g.astype(F32), 0.0)
            cats.append(jnp.concatenate([roll(mine, -1, 1), mine, roll(mine, 1, 1)], 0).astype(BF16))
    around = jnp.concatenate([wide_ref[h : h + 3].reshape(192, 256) for h in range(8)], 1)
    acc = dot(jnp.concatenate(cats, 1), around, (1, 1))
    even = (lax.axis_index("row") & 1) == 0
    first, last = g_ref[0].astype(F32), g_ref[7].astype(F32)
    a_ref[...] = jnp.where(even, last, first).astype(BF16)
    b_ref[...] = jnp.where(even, first, last).astype(BF16)
    part_ref[:96] = jnp.concatenate([acc[:96, :128], acc[96:, :128]], 1)
    part_ref[96:] = jnp.concatenate([acc[48 * q : 48 * q + 48, 128:] for q in range(4)], 1)
    half = keep_two_ref.shape[0]
    for ref, two_ref, place in ((keep_ref, keep_two_ref, pair), (send_ref, send_two_ref, 1 - pair)):
        ref[:half] = two_ref[...]
        ref[half:] = part_ref[pl.ds(pl.multiple_of(place * HALF_ONE, 8), HALF_ONE)].astype(BF16)


def layer_one_back(g_ref, a_ref, b_ref, w_ref, out_ref, done_ref, *, bands):
    above, below = beside(a_ref.at[: b_ref.shape[0]], b_ref, lax.axis_index("row"), bands)
    done_ref[...] = jnp.zeros(done_ref.shape, F32)
    lines = [above] + [g_ref[h] for h in range(8)] + [below]
    rows = []
    for h in range(8):
        z = dot(w_ref[...], jnp.concatenate(lines[h : h + 3], 0), (1, 0))
        rows.append((roll(z[:64], -1, 1) + z[64:128] + roll(z[128:], 1, 1))[:, :128])
    out_ref[...] = jnp.swapaxes(jnp.stack(rows, 0), 0, 1).astype(BF16)


def finish_two(mine_ref, other_ref, two_hbm, done_ref, two_ref, sems, *, scale):
    pair, half = lax.axis_index("pair"), mine_ref.shape[0]
    done_ref[...] = jnp.zeros(done_ref.shape, F32)
    copies = []
    for n, (ref, place) in enumerate(((mine_ref, pair), (other_ref, 1 - pair))):
        rows = pl.ds(pl.multiple_of(place * half, 16), half)
        two_ref[n] = ref[...].astype(F32) * scale
        copies.append(pltpu.make_async_copy(two_ref.at[n], two_hbm.at[rows], sems.at[n]))
        copies[-1].start()
    for copy in copies:
        copy.wait()


def finish_one(mine_ref, beside_ref, corner_ref, across_ref, _, __, out_ref, flat_ref, *, scale):
    pair = lax.axis_index("pair")
    for refs, place in (((mine_ref, across_ref), pair), ((beside_ref, corner_ref), 1 - pair)):
        total = refs[0][...].astype(F32) + refs[1][...].astype(F32)
        flat_ref[pl.ds(pl.multiple_of(place * HALF_ONE, 8), HALF_ONE)] = total * scale
    out_ref[0, :96] = flat_ref[:96, :64]
    out_ref[1, :96] = flat_ref[:96, 64:128]
    out_ref[0, 96:] = flat_ref[:96, 128:192]
    out_ref[1, 96:] = flat_ref[:96, 192:]
    for q in range(4):
        out_ref[2, 48 * q : 48 * q + 48] = flat_ref[96:, 64 * q : 64 * q + 64]


def even_swap(values, axis, count):
    return lax.ppermute(values, axis, [(n, n ^ 1) for n in range(count)])


def odd_partner(place):
    return place - 1 if place % 2 == 0 else place + 1


def odd_row_swap(values):
    bands, cores = lax.axis_size("row"), lax.axis_size("pair")
    steps = []
    for n in range(bands):
        for p in range(cores):
            to = (n, p ^ 1) if n in (0, bands - 1) else (odd_partner(n), p)
            steps.append((n * cores + p, to[0] * cores + to[1]))
    return lax.ppermute(values, ("row", "pair"), steps)


def odd_strip_swap(values):
    groups, strips = lax.axis_size("grp"), lax.axis_size(COLS)
    steps = []
    for g in range(groups):
        for n in range(strips):
            to = ((g + 1) % groups, n) if n in (0, strips - 1) else (g, odd_partner(n))
            steps.append((g * strips + n, to[0] * strips + to[1]))
    return lax.ppermute(values, ("grp",) + COLS, steps)


def xor_swap(values, axis, count, k):
    return lax.ppermute(values, axis, [(n, n ^ k) for n in range(count)])


def corner_swap(values, k):
    columns, cores = lax.axis_size("col"), lax.axis_size("pair")
    steps = [(c * cores + p, (c ^ k) * cores + (p ^ 1)) for c in range(columns) for p in range(cores)]
    return lax.ppermute(values, COLS, steps)


def row_order(bands, near_first=False, by_half=False):
    far_first = sorted(range(1, bands), key=lambda k: (k < bands // 2, k if by_half else -k))
    return [0] + (far_first[::-1] if near_first else far_first)


def row_swaps(values, bands, near_first=False, by_half=False):
    order = row_order(bands, near_first, by_half)
    return [values[0]] + [xor_swap(values[k], "row", bands, k) for k in order[1:]]


def added(a, b, *after):
    (total,) = whole_call(add_after, [shaped(a.shape)], [a, b, *after], 0, after=len(after))
    return total


def sum_but_last(part, axis, count):
    step = 1
    while 2 * step < count:
        part = added(part, xor_swap(part, axis, count, step))
        step *= 2
    return part, xor_swap(part, axis, count, step)


def local(features_in, filters_one, filters_two, out_grad):
    channels, band_rows, strip_cols = features_in.shape
    filters, own_cols, pooled_rows = out_grad.shape
    bands = lax.axis_size("row")
    strips = lax.axis_size(COLS)
    band = lax.axis_index("row")
    strip = lax.axis_index(COLS)
    pair = lax.axis_index("pair")
    height, width = band_rows * bands, strip_cols * strips
    total = own_cols * strips

    taps_one = jnp.transpose(filters_one, (1, 2, 0, 3)).reshape(3, 3 * channels, channels)
    taps_two = jnp.transpose(filters_two, (1, 2, 0, 3)).reshape(3, 3 * filters, 4 * channels)

    og = jnp.transpose(out_grad, (1, 2, 0))
    edge = REACH - 1
    x = jnp.transpose(features_in, (1, 0, 2))
    even = band % 2 == 0
    to_a, to_b = jnp.where(even, x[-1], x[0]), jnp.where(even, x[0], x[-1])
    head, tail = og[:edge], og[-edge:]
    joined_one, back_one, pool, pool_back, order = whole_call(
        functools.partial(constants, total=total),
        [shaped((3 * channels, 3 * channels))] * 2 + [shaped((2 * PITCH, 256))] * 2 + [shaped((256, 256))],
        [taps_one],
        10**8,
    )
    head, tail = head.reshape(-1, 128), tail.reshape(-1, 128)
    own_a, own_b = whole_call(
        pack_own, [shaped((channels + head.shape[0], 128))] * 2, [x, head, tail], 10**8
    )
    to_a, to_b, above, below = whole_call(
        functools.partial(pack_borders, bands=bands),
        [shaped((2 * channels + head.shape[0], 128))] * 2 + [shaped((channels, strip_cols))] * 2,
        [odd_row_swap(to_b), even_swap(to_a, "row", bands), own_a, own_b],
        1,
    )
    side_a, side_b = even_swap(to_a, COLS, strips), odd_strip_swap(to_b)
    pooled, slope, wide = whole_call(
        functools.partial(layer_one, strips=strips),
        [
            shaped((2, SENT, 4 * channels)),
            shaped((band_rows, channels, 256)),
            shaped((band_rows + 2, channels, 256)),
        ],
        [x, above, below, side_a, side_b, joined_one, pool, order],
        2 * band_rows * 192 * 192 * 256,
    )
    pieces = row_swaps([pooled] * bands, bands, near_first=True)

    even = strip % 2 == 0
    ends = [side[2 * channels :].reshape(og[:edge].shape) for side in (side_a, side_b)]
    ends[1] = jnp.where((strip == 0) | (strip == strips - 1), 0, ends[1])
    before, after = jnp.where(even, ends[1], ends[0]), jnp.where(even, ends[0], ends[1])
    og = jnp.concatenate([before, og, after], 0)
    og = jnp.pad(og, ((1, PITCH - own_cols - 2 * REACH + 1), (0, 0), (0, 0)))
    og = jnp.transpose(og, (1, 0, 2))

    count = pooled_rows * PITCH
    *terms, pooled_map, grad_map = whole_call(
        functools.partial(layer_two, bands=bands),
        [shaped((72, 4 * channels))] * bands
        + [shaped((pooled_rows + 2, PITCH, 4 * channels)), shaped((pooled_rows + 2, PITCH, filters))],
        [og, taps_two] + pieces,
        4 * count * 9 * filters * 4 * channels,
        scratch=[pltpu.VMEM((bands, 72, 4 * channels), BF16)],
    )
    received = row_swaps(terms, bands)

    half = 9 * filters // 2
    keep_two, send_two = whole_call(
        filter_two_grads,
        [shaped((half, 4 * channels))] * 2,
        [pooled_map, grad_map],
        2 * count * 9 * filters * 4 * channels,
        scratch=[pltpu.VMEM((2 * half, 4 * channels), BF16)],
    )
    g, up_a, up_b, keep, send = whole_call(
        functools.partial(grad_pre_one, bands=bands),
        [shaped((band_rows, channels, 256))]
        + [shaped((channels, 256))] * 2
        + [shaped((half + HALF_ONE, 256))] * 2,
        received + [slope, wide, pool_back, order, keep_two, send_two],
        2 * 8 * 192 * 192 * 256,
        scratch=[pltpu.VMEM((144, 256), F32)],
    )
    two, one, joined = whole_call(
        add_halves,
        [shaped((half, 256)), shaped((HALF_ONE, 256)), shaped((channels + HALF_ONE, 256))],
        [keep, even_swap(send, "pair", 2), up_a],
        0,
    )
    columns = lax.axis_size("col")
    two, two_more = sum_but_last(two, "col", columns)
    ones = row_swaps([one, joined] + [one] * (bands - 2), bands, near_first=True, by_half=False)
    near = ones[row_order(bands, near_first=True, by_half=False).index(1)]
    up_b = odd_row_swap(up_b)
    (one,) = whole_call(sum_rows, [shaped(one.shape)], ones + [up_b], 0, after=1)
    input_grad, done = whole_call(
        functools.partial(layer_one_back, bands=bands),
        [shaped(features_in.shape), shaped((8, 128), F32)],
        [g, near, up_b, back_one],
        2 * band_rows * 192 * 192 * 256,
    )
    mine_two = added(two, two_more, one)
    grad_two, wrote = whole_call(
        functools.partial(finish_two, scale=1.0 / math.sqrt(pooled_rows * total)),
        [shaped((2 * half, 256), F32), shaped((8, 128), F32)],
        [mine_two, even_swap(mine_two, "pair", 2)],
        10**8,
        scratch=[pltpu.VMEM((2, half, 256), F32), pltpu.SemaphoreType.DMA((2,))],
        out_spaces=[pl.ANY, pltpu.VMEM],
    )
    one, across = sum_but_last(one, "col", columns)
    beside_one = even_swap(one, "pair", 2)
    corner = corner_swap(one, columns // 2)
    (grad_one,) = whole_call(
        functools.partial(finish_one, scale=1.0 / math.sqrt(height * width)),
        [shaped((3, 3 * channels, channels), F32)],
        [one, beside_one, corner, across, wrote, done],
        1,
        scratch=[pltpu.VMEM((144, 256), F32)],
        after=2,
    )
    grad_two = jnp.transpose(grad_two.reshape(3, 3, filters, 4 * channels), (2, 0, 1, 3))
    grad_one = jnp.transpose(grad_one.reshape(3, 3, channels, channels), (2, 0, 1, 3))
    return (input_grad, grad_one, grad_two)


def solution(mesh):
    in_specs = (
        P("grp", "row", ("col", "pair")),
        P(),
        P("row", None, None, None),
        P(("grp", "row"), ("col", "pair"), None),
    )
    out_specs = (
        P("grp", "row", ("col", "pair")),
        P("grp", None, None, None),
        P(("grp", "row"), None, None, None),
    )
    return jax.shard_map(local, mesh=mesh, in_specs=in_specs, out_specs=out_specs, check_vma=False)
```

```python
import functools
import math

import jax
import jax.numpy as jnp
from jax import lax
from jax.experimental import pallas as pl
from jax.experimental.pallas import tpu as pltpu
from jax.sharding import PartitionSpec as P

BF16 = jnp.bfloat16
F32 = jnp.float32
COLS = ("col", "pair")
REACH = 3
HALF_ONE = 72
PITCH = 48
SENT = 40


def dot(a, b, contract):
    return lax.dot_general(a, b, ((contract[:1], contract[1:]), ((), ())), preferred_element_type=F32)


def whole_call(body, outs, operands, flops, scratch=(), after=0, out_spaces=None):
    specs = [
        pl.BlockSpec(memory_space=pltpu.VMEM) for _ in range(len(operands) - after)
    ] + [pl.BlockSpec(memory_space=pl.ANY)] * after
    sizes = [math.prod(a.shape) * a.dtype.itemsize for a in tuple(operands) + tuple(outs)]
    moved = sum(sizes) if flops else 0
    return pl.pallas_call(
        body,
        out_shape=outs,
        in_specs=specs,
        out_specs=[pl.BlockSpec(memory_space=space) for space in out_spaces or [pltpu.VMEM] * len(outs)],
        scratch_shapes=list(scratch),
        cost_estimate=pl.CostEstimate(flops=flops, bytes_accessed=moved, transcendentals=0),
        compiler_params=pltpu.CompilerParams(vmem_limit_bytes=40 * 1024 * 1024),
    )(*operands)


def strip_index():
    return lax.axis_index("col") * lax.axis_size("pair") + lax.axis_index("pair")


def shaped(shape, dtype=BF16):
    return jax.ShapeDtypeStruct(shape, dtype)


def roll(values, amount, axis):
    return pltpu.roll(values, amount % values.shape[axis], axis)


def sigmoid(values):
    return 0.5 + 0.5 * jnp.tanh(0.5 * values)


def slope_of(values, sig):
    return sig * (1.0 + values * (1.0 - sig))


def pool_matrix(strip, total, back=False):
    row = lax.broadcasted_iota(jnp.int32, (2 * PITCH, 256), 0)
    lane = lax.broadcasted_iota(jnp.int32, (2 * PITCH, 256), 1)
    half = (row >= PITCH).astype(jnp.int32)
    n = row - half * PITCH
    if back:
        v, most = jnp.where((n == 32) & (half == 1), -1, n), 33
    else:
        v, most = n - REACH, 32 + 2 * REACH
    near = jnp.bitwise_and(lane - 4 * v - 2 * half, 255) < 2
    place = strip * 32 + v
    keep = near & (n < most) & (place >= 0) & (place < total)
    return jnp.where(keep, 0.25, 0.0).astype(BF16)


def order_matrix():
    row = lax.broadcasted_iota(jnp.int32, (256, 256), 0)
    lane = lax.broadcasted_iota(jnp.int32, (256, 256), 1)
    j, i, c = row >> 7, (row >> 6) & 1, row & 63
    return jnp.where(lane == 4 * c + 2 * i + j, 1.0, 0.0).astype(BF16)


def constants(w_ref, joined_ref, back_w_ref, pool_ref, back_ref, order_ref, *, total):
    turned = [w_ref[2 - i].astype(F32).T for i in range(3)]
    back_w_ref[...] = jnp.concatenate(
        [jnp.concatenate([t[:, 64 * j : 64 * j + 64] for t in turned], 1) for j in range(3)], 0
    ).astype(BF16)
    joined_ref[...] = jnp.concatenate([w_ref[0], w_ref[1], w_ref[2]], axis=1)
    pool_ref[...] = pool_matrix(strip_index(), total)
    back_ref[...] = pool_matrix(strip_index(), total, back=True)
    order_ref[...] = order_matrix()


def beside(a_ref, b_ref, place, count):
    even = (place & 1) == 0
    a = a_ref[...].astype(F32)
    b = jnp.where((place > 0) & (place < count - 1), b_ref[...].astype(F32), 0.0)
    return jnp.where(even, b, a).astype(BF16), jnp.where(even, a, b).astype(BF16)


def pack_row(row, r, slot, head, tail):
    turned = roll(row.astype(F32), 16 * r, 1)
    return jnp.where(slot == r, turned, head), jnp.where(slot == (r - 1) % 8, turned, tail)


def pack_own(x_ref, head_ref, tail_ref, a_ref, b_ref):
    even = (strip_index() & 1) == 0
    slot = lax.broadcasted_iota(jnp.int32, (64, 128), 1) >> 4
    head = tail = jnp.zeros((64, 128), F32)
    for r in range(x_ref.shape[0]):
        head, tail = pack_row(x_ref[r], r, slot, head, tail)
    a_ref[:64] = jnp.where(even, tail, head).astype(BF16)
    b_ref[:64] = jnp.where(even, head, tail).astype(BF16)
    first, last = head_ref[...].astype(F32), tail_ref[...].astype(F32)
    a_ref[64:] = jnp.where(even, last, first).astype(BF16)
    b_ref[64:] = jnp.where(even, first, last).astype(BF16)


def pack_borders(up_b_ref, up_a_ref, own_a_ref, own_b_ref, a_ref, b_ref, above_ref, below_ref, *, bands):
    even = (strip_index() & 1) == 0
    above_ref[...], below_ref[...] = beside(up_a_ref, up_b_ref, lax.axis_index("row"), bands)
    slot = lax.broadcasted_iota(jnp.int32, (64, 128), 1) >> 4
    head = tail = jnp.zeros((64, 128), F32)
    for r, ref in enumerate((above_ref, below_ref)):
        head, tail = pack_row(ref[...], r, slot, head, tail)
    a_ref[:64] = jnp.where(even, tail, head).astype(BF16)
    b_ref[:64] = jnp.where(even, head, tail).astype(BF16)
    a_ref[64:] = own_a_ref[...]
    b_ref[64:] = own_b_ref[...]


def layer_one(
    x_ref,
    above_ref,
    below_ref,
    b_ref,
    a_ref,
    w_ref,
    pool_ref,
    order_ref,
    pooled_ref,
    slope_ref,
    wide_ref,
    *,
    strips,
):
    strip = strip_index()
    band_rows = x_ref.shape[0]
    slot = lax.broadcasted_iota(jnp.int32, (128, 128), 1) >> 4
    inner = (strip > 0) & (strip < strips - 1)
    sides = a_ref[:128].astype(F32), jnp.where(inner, b_ref[:128].astype(F32), 0.0)
    from_a = ((slot ^ strip) & 1) == 0
    packed = jnp.where(from_a, *sides), jnp.where(from_a, *sides[::-1])
    for r in range(band_rows):
        wide_ref[1 + r, :, 128:] = roll(packed[r % 2][64:], -16 * r, 1).astype(BF16)
    for r, place in enumerate((0, band_rows + 1)):
        wide_ref[place, :, 128:] = roll(packed[r][:64], -16 * r, 1).astype(BF16)
    wide_ref[0, :, :128] = above_ref[...]
    wide_ref[1 : band_rows + 1, :, :128] = x_ref[...]
    wide_ref[band_rows + 1, :, :128] = below_ref[...]
    weights = w_ref[...]
    rows = slope_ref.shape[0]
    halves, held = [], None
    for h in range(rows):
        y = dot(weights, wide_ref[h : h + 3].reshape(192, 256), (1, 0))
        pre = roll(y[:64], 1, 1) + y[64:128] + roll(y[128:], -1, 1)
        sig = sigmoid(pre)
        slope_ref[h] = slope_of(pre, sig).astype(BF16)
        active = pre * sig
        if h % 2:
            halves.append((held + active).astype(BF16))
        else:
            held = active
    pooled = dot(pool_ref[...], jnp.concatenate(halves, 0), (1, 1))
    stacked = jnp.concatenate(
        [
            jnp.concatenate(
                [pooled[:PITCH, u * 128 : u * 128 + 128], pooled[PITCH:, u * 128 : u * 128 + 128]], 1
            )
            for u in range(2)
        ],
        0,
    ).astype(BF16)
    ordered = dot(stacked, order_ref[...], (1, 0)).astype(BF16)
    for u in range(2):
        pooled_ref[u] = ordered[u * PITCH : u * PITCH + SENT]


def layer_two(og_ref, w_ref, *refs, bands):
    pieces, refs = refs[:bands], refs[bands:]
    terms, refs = refs[:bands], refs[bands:]
    map_ref, grad_ref, pack_ref = refs
    band = lax.axis_index("row")
    rows, _, filters = og_ref.shape
    count = rows * PITCH
    map_ref[0] = jnp.zeros((PITCH, 256), BF16)
    map_ref[rows + 1] = jnp.zeros((PITCH, 256), BF16)
    blank = jnp.zeros((PITCH - SENT, 256), BF16)
    for k, piece in zip(row_order(bands, near_first=True), pieces):
        for t in range(2):
            map_ref[1 + 2 * (band ^ k) + t] = jnp.concatenate([piece[t], blank], 0)
    near = jnp.concatenate([map_ref[i : i + rows].reshape(count, 256) for i in range(3)], 1)
    y = dot(near, jnp.concatenate([w_ref[i] for i in range(3)], 1), (1, 1))
    pre = roll(y[:, :filters], 1, 0) + y[:, filters : 2 * filters] + roll(y[:, 2 * filters :], -1, 0)
    grad = og_ref[...].reshape(count, filters).astype(F32) * slope_of(pre, sigmoid(pre))
    grad = grad.astype(BF16)
    grad_ref[0] = jnp.zeros((PITCH, filters), BF16)
    grad_ref[rows + 1] = jnp.zeros((PITCH, filters), BF16)
    grad_ref[1 : rows + 1] = grad.reshape(rows, PITCH, filters)
    near = jnp.concatenate([grad_ref[2 - i : 2 - i + rows].reshape(count, filters) for i in range(3)], 1)
    weights = [
        jnp.concatenate([w_ref[i, j * filters : (j + 1) * filters] for j in range(3)], 1) for i in range(3)
    ]
    z = dot(near, jnp.concatenate(weights, 0), (1, 0))
    spread = roll(z[:, :256], -1 - REACH, 0) + roll(z[:, 256:512], -REACH, 0) + roll(z[:, 512:], 1 - REACH, 0)
    spread = spread.reshape(rows, PITCH, 256)
    odd = (lax.broadcasted_iota(jnp.int32, (8, 256), 1) & 1) == 1
    row = lax.broadcasted_iota(jnp.int32, (8, 256), 0)
    ends = [jnp.where(odd, spread[u - 1, 47:48], spread[u, 32:33]) for u in range(rows)]
    for p in range(rows // 2):
        shared = jnp.where(row == 0, ends[2 * p], jnp.where(row == 1, ends[2 * p + 1], 0.0))
        pack_ref[p] = jnp.concatenate([spread[2 * p, :32], shared, spread[2 * p + 1, :32]], 0).astype(BF16)
    for k in range(bands):
        terms[k][...] = pack_ref[band ^ k]


def filter_two_grads(map_ref, grad_ref, keep_ref, send_ref, all_ref):
    pair = lax.axis_index("pair")
    rows = map_ref.shape[0] - 2
    filters = grad_ref.shape[2]
    v = lax.broadcasted_iota(jnp.int32, (rows, PITCH, filters), 1)
    own = (v >= REACH) & (v < REACH + 32)
    wide = jnp.where(own, grad_ref[1 : rows + 1].astype(F32), 0.0).reshape(rows * PITCH, filters)
    cat = jnp.concatenate([roll(wide, -1, 0), wide, roll(wide, 1, 0)], 1).astype(BF16)
    taps = 3 * filters
    for i in range(3):
        part = dot(cat, map_ref[i : i + rows].reshape(rows * PITCH, 256), (0, 0))
        all_ref[i * taps : (i + 1) * taps] = part.astype(BF16)
    half = keep_ref.shape[0]
    keep_ref[...] = all_ref[pl.ds(pl.multiple_of(pair * half, 16), half)]
    send_ref[...] = all_ref[pl.ds(pl.multiple_of((1 - pair) * half, 16), half)]


def add_after(a_ref, b_ref, *refs):
    refs[-1][...] = (a_ref[...].astype(F32) + b_ref[...].astype(F32)).astype(BF16)


def add_halves(a_ref, b_ref, border_ref, two_ref, one_ref, joined_ref):
    half, border = two_ref.shape[0], border_ref.shape[0]
    total = (a_ref[...].astype(F32) + b_ref[...].astype(F32)).astype(BF16)
    two_ref[...] = total[:half]
    one_ref[...] = total[half:]
    joined_ref[:border] = border_ref[...]
    joined_ref[border:] = total[half:]


def sum_rows(*refs):
    *refs, _, out_ref = refs
    rows = out_ref.shape[0]
    terms = dict(zip(row_order(len(refs), near_first=True, by_half=True), (ref[-rows:].astype(F32) for ref in refs)))
    terms = [terms[k] for k in range(len(refs))]
    while len(terms) > 1:
        terms = [a + b for a, b in zip(terms[::2], terms[1::2])]
    out_ref[...] = terms[0].astype(BF16)


def grad_pre_one(*refs, bands):
    terms, refs = refs[:bands], refs[bands:]
    slope_ref, wide_ref, pool_ref, order_ref, keep_two_ref, send_two_ref, *refs = refs
    g_ref, a_ref, b_ref, keep_ref, send_ref, part_ref = refs
    pair = lax.axis_index("pair")
    summed = terms[0][...].astype(F32)
    for k in range(1, bands):
        summed = summed + terms[k][...].astype(F32)
    blank = jnp.zeros((8, 256), F32)
    ends = summed[32:40]
    blocks = [summed[:32], ends, blank, summed[40:], roll(ends, -1, 0), blank]
    ordered = dot(jnp.concatenate(blocks, 0).astype(BF16), order_ref[...], (1, 1)).astype(BF16)
    pool = pool_ref[...]
    cats = []
    own = lax.broadcasted_iota(jnp.int32, (64, 256), 1) < 128
    for u in range(2):
        block = ordered[u * PITCH : (u + 1) * PITCH]
        up = dot(jnp.concatenate([block[:, :128], block[:, 128:]], 0), pool, (0, 0))
        for i in range(4):
            h = 4 * u + i
            g = (up[64 * (i // 2) : 64 * (i // 2) + 64] * slope_ref[h].astype(F32)).astype(BF16)
            g_ref[h] = g
            mine = jnp.where(own, g.astype(F32), 0.0)
            cats.append(jnp.concatenate([roll(mine, -1, 1), mine, roll(mine, 1, 1)], 0).astype(BF16))
    around = jnp.concatenate([wide_ref[h : h + 3].reshape(192, 256) for h in range(8)], 1)
    acc = dot(jnp.concatenate(cats, 1), around, (1, 1))
    even = (lax.axis_index("row") & 1) == 0
    first, last = g_ref[0].astype(F32), g_ref[7].astype(F32)
    a_ref[...] = jnp.where(even, last, first).astype(BF16)
    b_ref[...] = jnp.where(even, first, last).astype(BF16)
    part_ref[:96] = jnp.concatenate([acc[:96, :128], acc[96:, :128]], 1)
    part_ref[96:] = jnp.concatenate([acc[48 * q : 48 * q + 48, 128:] for q in range(4)], 1)
    half = keep_two_ref.shape[0]
    for ref, two_ref, place in ((keep_ref, keep_two_ref, pair), (send_ref, send_two_ref, 1 - pair)):
        ref[:half] = two_ref[...]
        ref[half:] = part_ref[pl.ds(pl.multiple_of(place * HALF_ONE, 8), HALF_ONE)].astype(BF16)


def layer_one_back(g_ref, a_ref, b_ref, w_ref, out_ref, done_ref, *, bands):
    above, below = beside(a_ref.at[: b_ref.shape[0]], b_ref, lax.axis_index("row"), bands)
    done_ref[...] = jnp.zeros(done_ref.shape, F32)
    lines = [above] + [g_ref[h] for h in range(8)] + [below]
    rows = []
    for h in range(8):
        z = dot(w_ref[...], jnp.concatenate(lines[h : h + 3], 0), (1, 0))
        rows.append((roll(z[:64], -1, 1) + z[64:128] + roll(z[128:], 1, 1))[:, :128])
    out_ref[...] = jnp.swapaxes(jnp.stack(rows, 0), 0, 1).astype(BF16)


def finish_two(mine_ref, other_ref, two_hbm, done_ref, two_ref, sems, *, scale):
    pair, half = lax.axis_index("pair"), mine_ref.shape[0]
    done_ref[...] = jnp.zeros(done_ref.shape, F32)
    copies = []
    for n, (ref, place) in enumerate(((mine_ref, pair), (other_ref, 1 - pair))):
        rows = pl.ds(pl.multiple_of(place * half, 16), half)
        two_ref[n] = ref[...].astype(F32) * scale
        copies.append(pltpu.make_async_copy(two_ref.at[n], two_hbm.at[rows], sems.at[n]))
        copies[-1].start()
    for copy in copies:
        copy.wait()


def finish_one(mine_ref, beside_ref, corner_ref, across_ref, _, __, out_ref, flat_ref, *, scale):
    pair = lax.axis_index("pair")
    for refs, place in (((mine_ref, across_ref), pair), ((beside_ref, corner_ref), 1 - pair)):
        total = refs[0][...].astype(F32) + refs[1][...].astype(F32)
        flat_ref[pl.ds(pl.multiple_of(place * HALF_ONE, 8), HALF_ONE)] = total * scale
    out_ref[0, :96] = flat_ref[:96, :64]
    out_ref[1, :96] = flat_ref[:96, 64:128]
    out_ref[0, 96:] = flat_ref[:96, 128:192]
    out_ref[1, 96:] = flat_ref[:96, 192:]
    for q in range(4):
        out_ref[2, 48 * q : 48 * q + 48] = flat_ref[96:, 64 * q : 64 * q + 64]


def even_swap(values, axis, count):
    return lax.ppermute(values, axis, [(n, n ^ 1) for n in range(count)])


def odd_partner(place):
    return place - 1 if place % 2 == 0 else place + 1


def odd_row_swap(values):
    bands, cores = lax.axis_size("row"), lax.axis_size("pair")
    steps = []
    for n in range(bands):
        for p in range(cores):
            to = (n, p ^ 1) if n in (0, bands - 1) else (odd_partner(n), p)
            steps.append((n * cores + p, to[0] * cores + to[1]))
    return lax.ppermute(values, ("row", "pair"), steps)


def odd_strip_swap(values):
    groups, strips = lax.axis_size("grp"), lax.axis_size(COLS)
    steps = []
    for g in range(groups):
        for n in range(strips):
            to = ((g + 1) % groups, n) if n in (0, strips - 1) else (g, odd_partner(n))
            steps.append((g * strips + n, to[0] * strips + to[1]))
    return lax.ppermute(values, ("grp",) + COLS, steps)


def xor_swap(values, axis, count, k):
    return lax.ppermute(values, axis, [(n, n ^ k) for n in range(count)])


def corner_swap(values, k):
    columns, cores = lax.axis_size("col"), lax.axis_size("pair")
    steps = [(c * cores + p, (c ^ k) * cores + (p ^ 1)) for c in range(columns) for p in range(cores)]
    return lax.ppermute(values, COLS, steps)


def row_order(bands, near_first=False, by_half=False):
    far_first = sorted(range(1, bands), key=lambda k: (k < bands // 2, k if by_half else -k))
    return [0] + (far_first[::-1] if near_first else far_first)


def row_swaps(values, bands, near_first=False, by_half=False):
    order = row_order(bands, near_first, by_half)
    return [values[0]] + [xor_swap(values[k], "row", bands, k) for k in order[1:]]


def added(a, b, *after):
    (total,) = whole_call(add_after, [shaped(a.shape)], [a, b, *after], 0, after=len(after))
    return total


def sum_but_last(part, axis, count):
    step = 1
    while 2 * step < count:
        part = added(part, xor_swap(part, axis, count, step))
        step *= 2
    return part, xor_swap(part, axis, count, step)


def local(features_in, filters_one, filters_two, out_grad):
    channels, band_rows, strip_cols = features_in.shape
    filters, own_cols, pooled_rows = out_grad.shape
    bands = lax.axis_size("row")
    strips = lax.axis_size(COLS)
    band = lax.axis_index("row")
    strip = lax.axis_index(COLS)
    pair = lax.axis_index("pair")
    height, width = band_rows * bands, strip_cols * strips
    total = own_cols * strips

    taps_one = jnp.transpose(filters_one, (1, 2, 0, 3)).reshape(3, 3 * channels, channels)
    taps_two = jnp.transpose(filters_two, (1, 2, 0, 3)).reshape(3, 3 * filters, 4 * channels)

    og = jnp.transpose(out_grad, (1, 2, 0))
    edge = REACH - 1
    x = jnp.transpose(features_in, (1, 0, 2))
    even = band % 2 == 0
    to_a, to_b = jnp.where(even, x[-1], x[0]), jnp.where(even, x[0], x[-1])
    head, tail = og[:edge], og[-edge:]
    joined_one, back_one, pool, pool_back, order = whole_call(
        functools.partial(constants, total=total),
        [shaped((3 * channels, 3 * channels))] * 2 + [shaped((2 * PITCH, 256))] * 2 + [shaped((256, 256))],
        [taps_one],
        10**8,
    )
    head, tail = head.reshape(-1, 128), tail.reshape(-1, 128)
    own_a, own_b = whole_call(
        pack_own, [shaped((channels + head.shape[0], 128))] * 2, [x, head, tail], 10**8
    )
    to_a, to_b, above, below = whole_call(
        functools.partial(pack_borders, bands=bands),
        [shaped((2 * channels + head.shape[0], 128))] * 2 + [shaped((channels, strip_cols))] * 2,
        [odd_row_swap(to_b), even_swap(to_a, "row", bands), own_a, own_b],
        1,
    )
    side_a, side_b = even_swap(to_a, COLS, strips), odd_strip_swap(to_b)
    pooled, slope, wide = whole_call(
        functools.partial(layer_one, strips=strips),
        [
            shaped((2, SENT, 4 * channels)),
            shaped((band_rows, channels, 256)),
            shaped((band_rows + 2, channels, 256)),
        ],
        [x, above, below, side_b, side_a, joined_one, pool, order],
        2 * band_rows * 192 * 192 * 256,
    )
    pieces = row_swaps([pooled] * bands, bands, near_first=True)

    even = strip % 2 == 0
    ends = [side[2 * channels :].reshape(og[:edge].shape) for side in (side_a, side_b)]
    ends[1] = jnp.where((strip == 0) | (strip == strips - 1), 0, ends[1])
    before, after = jnp.where(even, ends[1], ends[0]), jnp.where(even, ends[0], ends[1])
    og = jnp.concatenate([before, og, after], 0)
    og = jnp.pad(og, ((1, PITCH - own_cols - 2 * REACH + 1), (0, 0), (0, 0)))
    og = jnp.transpose(og, (1, 0, 2))

    count = pooled_rows * PITCH
    *terms, pooled_map, grad_map = whole_call(
        functools.partial(layer_two, bands=bands),
        [shaped((72, 4 * channels))] * bands
        + [shaped((pooled_rows + 2, PITCH, 4 * channels)), shaped((pooled_rows + 2, PITCH, filters))],
        [og, taps_two] + pieces,
        4 * count * 9 * filters * 4 * channels,
        scratch=[pltpu.VMEM((bands, 72, 4 * channels), BF16)],
    )
    received = row_swaps(terms, bands)

    half = 9 * filters // 2
    keep_two, send_two = whole_call(
        filter_two_grads,
        [shaped((half, 4 * channels))] * 2,
        [pooled_map, grad_map],
        2 * count * 9 * filters * 4 * channels,
        scratch=[pltpu.VMEM((2 * half, 4 * channels), BF16)],
    )
    g, up_a, up_b, keep, send = whole_call(
        functools.partial(grad_pre_one, bands=bands),
        [shaped((band_rows, channels, 256))]
        + [shaped((channels, 256))] * 2
        + [shaped((half + HALF_ONE, 256))] * 2,
        received + [slope, wide, pool_back, order, keep_two, send_two],
        2 * 8 * 192 * 192 * 256,
        scratch=[pltpu.VMEM((144, 256), F32)],
    )
    two, one, joined = whole_call(
        add_halves,
        [shaped((half, 256)), shaped((HALF_ONE, 256)), shaped((channels + HALF_ONE, 256))],
        [keep, even_swap(send, "pair", 2), up_a],
        0,
    )
    columns = lax.axis_size("col")
    two, two_more = sum_but_last(two, "col", columns)
    ones = row_swaps([one, joined] + [one] * (bands - 2), bands, near_first=True, by_half=True)
    near = ones[row_order(bands, near_first=True, by_half=True).index(1)]
    up_b = odd_row_swap(up_b)
    (one,) = whole_call(sum_rows, [shaped(one.shape)], ones + [up_b], 0, after=1)
    input_grad, done = whole_call(
        functools.partial(layer_one_back, bands=bands),
        [shaped(features_in.shape), shaped((8, 128), F32)],
        [g, near, up_b, back_one],
        2 * band_rows * 192 * 192 * 256,
    )
    mine_two = added(two, two_more, one)
    grad_two, wrote = whole_call(
        functools.partial(finish_two, scale=1.0 / math.sqrt(pooled_rows * total)),
        [shaped((2 * half, 256), F32), shaped((8, 128), F32)],
        [mine_two, even_swap(mine_two, "pair", 2)],
        10**8,
        scratch=[pltpu.VMEM((2, half, 256), F32), pltpu.SemaphoreType.DMA((2,))],
        out_spaces=[pl.ANY, pltpu.VMEM],
    )
    one, across = sum_but_last(one, "col", columns)
    beside_one = even_swap(one, "pair", 2)
    corner = corner_swap(one, columns // 2)
    (grad_one,) = whole_call(
        functools.partial(finish_one, scale=1.0 / math.sqrt(height * width)),
        [shaped((3, 3 * channels, channels), F32)],
        [one, beside_one, corner, across, wrote, done],
        1,
        scratch=[pltpu.VMEM((144, 256), F32)],
        after=2,
    )
    grad_two = jnp.transpose(grad_two.reshape(3, 3, filters, 4 * channels), (2, 0, 1, 3))
    grad_one = jnp.transpose(grad_one.reshape(3, 3, channels, channels), (2, 0, 1, 3))
    return (input_grad, grad_one, grad_two)


def solution(mesh):
    in_specs = (
        P("grp", "row", ("col", "pair")),
        P(),
        P("row", None, None, None),
        P(("grp", "row"), ("col", "pair"), None),
    )
    out_specs = (
        P("grp", "row", ("col", "pair")),
        P("grp", None, None, None),
        P(("grp", "row"), None, None, None),
    )
    return jax.shard_map(local, mesh=mesh, in_specs=in_specs, out_specs=out_specs, check_vma=False)
```
